32 devices in a mesh: dp: 8 (over z, x), tensor: 4 (over y, core).
Axes of the slice: x: 2, y: 2, z: 4, core: 2. Of those that a mesh axis runs over, the one named last changes fastest.
Arguments:
- inputs: bfloat16 [32, 196, 768], P('dp'), may hold values from -6 to 6
- target: bfloat16 [32, 196, 768], P('dp'), may hold values from -6 to 6
- valid: int32 [32, 196], P('dp'), may hold values from 0 to 1, as said below
- first_gain: float32 [768], replicated, may hold values from 0.5 to 1.5
- first_shift: float32 [768], replicated, may hold values from -3 to 3
- triple_weight: bfloat16 [3, 768, 768], P(None, 'dp', 'tensor'), may hold values from -0.21875 to 0.21875
- query_value_bias: float32 [2, 768], P(None, 'tensor'), may hold values from -3 to 3
- output_weight: bfloat16 [768, 768], P('tensor', 'dp'), may hold values from -0.875 to 0.875
- output_bias: float32 [768], replicated, may hold values from -3 to 3
- second_gain: float32 [768], replicated, may hold values from 0.5 to 1.5
- second_shift: float32 [768], replicated, may hold values from -3 to 3
- expand_weight: bfloat16 [768, 3072], P('dp', 'tensor'), may hold values from -0.21875 to 0.21875
- expand_bias: float32 [3072], P('tensor'), may hold values from -3 to 3
- shrink_weight: bfloat16 [3072, 768], P('tensor', 'dp'), may hold values from -0.109375 to 0.109375
- shrink_bias: float32 [768], replicated, may hold values from -3 to 3
- rows_table: float32 [27, 64], replicated, may hold values from -0.6 to 0.6
- columns_table: float32 [27, 64], replicated, may hold values from -0.6 to 0.6
Outputs:
- block_output: bfloat16 [32, 196, 768], P('dp')
- loss: float32 [], replicated
- input_grad: float32 [32, 196, 768], P('dp')
- first_gain_grad: float32 [768], replicated
- first_shift_grad: float32 [768], replicated
- triple_weight_grad: float32 [3, 768, 768], P(None, 'dp', 'tensor')
- query_value_bias_grad: float32 [2, 768], P(None, 'tensor')
- output_weight_grad: float32 [768, 768], P('tensor', 'dp')
- output_bias_grad: float32 [768], replicated
- second_gain_grad: float32 [768], replicated
- second_shift_grad: float32 [768], replicated
- expand_weight_grad: float32 [768, 3072], P('dp', 'tensor')
- expand_bias_grad: float32 [3072], P('tensor')
- shrink_weight_grad: float32 [3072, 768], P('tensor', 'dp')
- shrink_bias_grad: float32 [768], replicated
- rows_table_grad: float32 [27, 64], replicated
- columns_table_grad: float32 [27, 64], replicated
The draws below stay inside these ranges and needn't reach their ends.
Inputs may be any that keep to these rules, and one draw needn't show every extreme that they name: `valid`: 1 marks an image token and 0 a padding token; the image tokens of a window fill a rectangle of its first rows and first columns, and every window holds at least one.
All inputs are finite; a program needn't handle non-finite values.
Results may differ from the reference program's by a relative error of at most 0.012.
Values may be sent and summed in bfloat16 or wider, within the bound.
A program may use at most 128 MiB of HBM per device.

```python
import math
import jax
import jax.numpy as jnp
from jax import lax

D = 768
HEADS = 12
HEAD = 64
FF = 3072
WIN = 14
WIN_TOK = 196
REL = 27
W_DEV = 4
WINDOWS = 32
TOKENS = 6272


def draw_valid(key, part):
    devices = WINDOWS // W_DEV
    spread = max(devices - 1, 1)
    window_ids = jnp.arange(WINDOWS, dtype=jnp.int32)
    owners = window_ids // W_DEV
    base_rows = WIN * (spread + 2 * owners) // (3 * spread)
    first_key, second_key = jax.random.split(key)
    jitter = jax.random.randint(first_key, (WINDOWS,), 0, 2, dtype=jnp.int32)
    live_rows = jnp.clip(base_rows - jitter, 1, WIN)
    live_cols = jax.random.randint(second_key, (WINDOWS,), WIN // 2, WIN + 1, dtype=jnp.int32)
    places = jnp.arange(WIN_TOK, dtype=jnp.int32)
    grid_row = places // WIN
    grid_col = places % WIN
    inside = (grid_row[None, :] < live_rows[:, None]) & (grid_col[None, :] < live_cols[:, None])
    return inside.astype(jnp.int32)


def levels(key, shape, shards, smallest, top_value):
    level, own = 1.0, jax.random.fold_in(key, 6)
    for dim, shards_of in shards:
        draws = jnp.exp(jax.random.uniform(jax.random.fold_in(own, dim), (shards_of,), jnp.float32, smallest / len(shards), top_value / len(shards)))
        level = level * jnp.repeat(draws, shape[dim] // shards_of).reshape([-1 if axis == dim else 1 for axis in range(len(shape))])
    return level


def centred(own_key, shape, scale, most, pieces=(), kind=jnp.bfloat16):
    entries = jax.random.normal(own_key, shape, jnp.float32) * scale
    if len(pieces) > 0:
        entries = levels(own_key, shape, pieces, -0.22, 0.18) * entries
    return jnp.clip(entries, min=-most, max=most).astype(kind)


def setup_inputs(seed: int = 0) -> dict:
    streams_of = jax.random.split(jax.random.key(seed), 18)
    inputs = centred(streams_of[0], (WINDOWS, WIN_TOK, D), 1.0, 6.0, ((0, 8),))
    target = centred(streams_of[1], (WINDOWS, WIN_TOK, D), 1.0, 6.0, ((0, 8),))
    valid = draw_valid(jax.random.fold_in(streams_of[17], 71), 0)
    first_gain = jnp.clip(1.0 + 0.1 * jax.random.normal(streams_of[3], (D,), jnp.float32), 0.5, 1.5)
    first_shift = centred(streams_of[4], (D,), 0.5, 3.0, (), jnp.float32)
    triple_weight = centred(streams_of[5], (3, D, D), D ** -0.5, 0.21875, ((1, 8), (2, 4)))
    query_value_bias = centred(streams_of[6], (2, D), 0.5, 3.0, ((1, 4),), jnp.float32)
    output_weight = centred(streams_of[7], (D, D), (D // 16) ** -0.5, 0.875, ((0, 4), (1, 8)))
    output_bias = centred(streams_of[8], (D,), 0.5, 3.0, (), jnp.float32)
    second_gain = jnp.clip(1.0 + 0.1 * jax.random.normal(streams_of[9], (D,), jnp.float32), 0.5, 1.5)
    second_shift = centred(streams_of[10], (D,), 0.5, 3.0, (), jnp.float32)
    expand_weight = centred(streams_of[11], (D, FF), D ** -0.5, 0.21875, ((0, 8), (1, 4)))
    expand_bias = centred(streams_of[12], (FF,), 0.5, 3.0, ((0, 4),), jnp.float32)
    shrink_weight = centred(streams_of[13], (FF, D), FF ** -0.5, 0.109375, ((0, 4), (1, 8)))
    shrink_bias = centred(streams_of[14], (D,), 0.5, 3.0, (), jnp.float32)
    rows_table = centred(streams_of[15], (REL, HEAD), 0.1, 0.6, (), jnp.float32)
    columns_table = centred(streams_of[16], (REL, HEAD), 0.1, 0.6, (), jnp.float32)
    return {"inputs": inputs, "target": target, "valid": valid, "first_gain": first_gain, "first_shift": first_shift, "triple_weight": triple_weight, "query_value_bias": query_value_bias, "output_weight": output_weight, "output_bias": output_bias, "second_gain": second_gain, "second_shift": second_shift, "expand_weight": expand_weight, "expand_bias": expand_bias, "shrink_weight": shrink_weight, "shrink_bias": shrink_bias, "rows_table": rows_table, "columns_table": columns_table}


@jax.custom_vjp
def low(v):
    return lax.optimization_barrier(v.astype(jnp.bfloat16)).astype(jnp.float32)

@jax.custom_vjp
def low_back(v):
    return v

def low_keep(v):
    return (low(v), None)

def low_pass(kept, grad):
    return (grad,)

def back_keep(v):
    return (v, None)

def back_low(kept, grad):
    return (low(grad),)
low.defvjp(low_keep, low_pass)
low_back.defvjp(back_keep, back_low)

def layer_norm(values, gain, shift):
    center = lax.optimization_barrier(jnp.mean(values, axis=-1, keepdims=True))
    centered = values - center
    spread = lax.optimization_barrier(jnp.mean(centered * centered, axis=-1, keepdims=True))
    return centered * lax.rsqrt(spread + 1e-06) * gain + shift

def position_table(table):
    offsets = jnp.arange(WIN)[:, None] - jnp.arange(WIN)[None, :] + (WIN - 1)
    return table[offsets]

def window_block(windows_in, params):
    first_gain, first_shift, triple_weight, query_value_bias, output_weight, output_bias, second_gain, second_shift, expand_weight, expand_bias, shrink_weight, shrink_bias, rows_table, columns_table = params
    groups = windows_in.shape[0]
    scale_factor = 1.0 / math.sqrt(HEAD)
    highest = lax.Precision.HIGHEST
    flat_rows = windows_in.reshape(-1, D)
    normed = low(layer_norm(flat_rows, first_gain, first_shift))
    biases = jnp.stack([query_value_bias[0], jnp.zeros_like(query_value_bias[0]), query_value_bias[1]])
    projected = jnp.einsum('rd,tde->rte', normed, triple_weight, precision=highest) + biases
    projected = low_back(low(projected))
    projected = projected.reshape(groups, WIN, WIN, 3, HEADS, HEAD)
    queries = projected[:, :, :, 0]
    keys = projected[:, :, :, 1]
    values = projected[:, :, :, 2].reshape(groups, WIN_TOK, HEADS, HEAD)
    table_rows = position_table(low(rows_table))
    table_cols = position_table(low(columns_table))
    along_rows = jnp.einsum('gabnc,aec->gnabe', queries, table_rows, precision=highest)
    along_cols = jnp.einsum('gabnc,bfc->gnabf', queries, table_cols, precision=highest)
    scores = jnp.einsum('gabnc,gefnc->gnabef', queries, keys, precision=highest) * scale_factor
    scores = scores + along_rows[..., :, None] + along_cols[..., None, :]
    scores = low_back(scores.reshape(groups, HEADS, WIN_TOK, WIN_TOK))
    softmaxed = jax.nn.softmax(scores, axis=-1)
    mixed = jnp.einsum('gnqk,gknc->gqnc', low(softmaxed), values, precision=highest)
    mixed = low_back(low(mixed.reshape(-1, D)))
    attended = low_back(jnp.dot(mixed, output_weight, precision=highest)) + output_bias
    middle = flat_rows + attended
    normed_two = low(layer_norm(middle, second_gain, second_shift))
    before = low_back(jnp.dot(normed_two, expand_weight, precision=highest) + expand_bias)
    hidden = low(jax.nn.gelu(before, approximate=False))
    shrunk = low_back(jnp.dot(hidden, shrink_weight, precision=highest)) + shrink_bias
    return (middle + shrunk).reshape(windows_in.shape)

def reference(inputs, target, valid, first_gain, first_shift, triple_weight, query_value_bias, output_weight, output_bias, second_gain, second_shift, expand_weight, expand_bias, shrink_weight, shrink_bias, rows_table, columns_table):
    params = tuple((item.astype(jnp.float32) for item in (first_gain, first_shift, triple_weight, query_value_bias, output_weight, output_bias, second_gain, second_shift, expand_weight, expand_bias, shrink_weight, shrink_bias, rows_table, columns_table)))
    flat_in = inputs.astype(jnp.float32)
    goal = target.astype(jnp.float32)
    marks_all = valid.astype(jnp.float32)
    count = jnp.sum(marks_all)
    groups = WINDOWS // W_DEV
    block_step = jax.checkpoint(window_block)

    def forward(flat_in, params):

        def advance(carry, item):
            piece, aim, marks = item
            result = block_step(piece, params)
            gap = result - aim
            return (carry + jnp.sum(marks[..., None] * gap * gap), result)
        summed, results = lax.scan(advance, jnp.zeros((), jnp.float32), (flat_in.reshape(groups, W_DEV, WIN_TOK, D), goal.reshape(groups, W_DEV, WIN_TOK, D), marks_all.reshape(groups, W_DEV, WIN_TOK)))
        return (summed / (count * D), results.reshape(WINDOWS, WIN_TOK, D))
    (loss, outputs), pullback = jax.vjp(forward, flat_in, params)
    input_grad, grads = pullback((jnp.asarray(TOKENS * D * 0.5, jnp.float32), jnp.zeros_like(outputs)))
    return (outputs.astype(jnp.bfloat16), loss, input_grad, grads[0], grads[1], grads[2], grads[3], grads[4], grads[5], grads[6], grads[7], grads[8], grads[9], grads[10], grads[11], grads[12], grads[13])
```

```python
import math

import jax
import jax.numpy as jnp
from jax import lax
from jax.experimental import pallas as pl
from jax.experimental.pallas import tpu as pltpu
from jax.sharding import PartitionSpec as P

MESH = pl.DeviceIdType.MESH

D = 768
HEADS = 12
HEAD = 64
WIN = 14
WIN_TOK = 196
MICRO = 2


def normalize(values):
    center = jnp.mean(values, axis=-1, keepdims=True)
    centered = values - center
    spread = jnp.mean(centered * centered, axis=-1, keepdims=True)
    inverse = lax.rsqrt(spread + 1e-06)
    return (centered * inverse, inverse)


def normalize_back(grad_out, unit, inverse, gain):
    scaled = grad_out * gain
    mean_one = jnp.mean(scaled, axis=-1, keepdims=True)
    mean_two = jnp.mean(scaled * unit, axis=-1, keepdims=True)
    return inverse * (scaled - mean_one - unit * mean_two)


def position_select(side):
    shape = (side, side, 2 * side - 1)
    first = lax.broadcasted_iota(jnp.int32, shape, 0)
    second = lax.broadcasted_iota(jnp.int32, shape, 1)
    slots = lax.broadcasted_iota(jnp.int32, shape, 2)
    return (slots == first - second + side - 1).astype(jnp.bfloat16)


def score_block(queries, keys, table_rows, table_cols, scale_factor):
    groups = queries.shape[0]
    side = queries.shape[1]
    heads = queries.shape[3]
    along_rows = jnp.einsum(
        "gabnc,aec->gnabe", queries, table_rows, preferred_element_type=jnp.float32
    )
    along_cols = jnp.einsum(
        "gabnc,bfc->gnabf", queries, table_cols, preferred_element_type=jnp.float32
    )
    scores = (
        jnp.einsum("gabnc,gefnc->gnabef", queries, keys, preferred_element_type=jnp.float32)
        * scale_factor
    )
    scores = scores + along_rows[..., :, None] + along_cols[..., None, :]
    return scores.reshape(groups, heads, side * side, side * side)


def gelu_exact(inner):
    return jax.nn.gelu(inner, approximate=False)


def row_total(partial_value):
    return lax.psum(partial_value, "tensor")


def share_of(values):
    share_rows = values.shape[0] // lax.axis_size("tensor")
    return lax.dynamic_slice_in_dim(values, lax.axis_index("tensor") * share_rows, share_rows, 0)


def z_mate(z, k):
    if k == 1:
        return z + 1 - 2 * (z % 2)
    if k == 2:
        return (z + 2) % 4
    return 3 - z


def gather_kernel(a_in, e_in, s_in, a_out, e_out, s_out, send_sem, recv_sem, local_sem):
    dp = lax.axis_index("dp")
    t = lax.axis_index("tensor")
    z = dp // 2
    x = dp % 2
    mates = [(z_mate(z, k) * 2 + x, t) for k in (1, 2, 3)]
    x_mate = (z * 2 + 1 - x, t)
    barrier = pltpu.get_barrier_semaphore()
    for mate in mates + [x_mate]:
        pl.semaphore_signal(barrier, inc=1, device_id=mate, device_id_type=MESH)
    pl.semaphore_wait(barrier, 4)
    ins = (a_in, e_in, s_in)
    outs = (a_out, e_out, s_out)
    started = []
    local = []
    for g in range(3):
        for k in (1, 2, 3):
            copy = pltpu.make_async_remote_copy(
                src_ref=ins[g],
                dst_ref=outs[g].at[dp],
                send_sem=send_sem.at[g, k - 1],
                recv_sem=recv_sem.at[g, k - 1],
                device_id=mates[k - 1],
                device_id_type=MESH,
            )
            copy.start()
            started.append(copy)
        copy = pltpu.make_async_remote_copy(
            src_ref=ins[g],
            dst_ref=outs[g].at[dp],
            send_sem=send_sem.at[g, 3],
            recv_sem=recv_sem.at[g, 3],
            device_id=x_mate,
            device_id_type=MESH,
        )
        copy.start()
        started.append(copy)
        own = pltpu.make_async_copy(ins[g], outs[g].at[dp], local_sem.at[g])
        own.start()
        local.append(own)
    for g in range(3):
        for k in (1, 2, 3):
            row = z_mate(z, k) * 2 + x
            started[4 * g + k - 1].wait_recv()
            copy = pltpu.make_async_remote_copy(
                src_ref=outs[g].at[row],
                dst_ref=outs[g].at[row],
                send_sem=send_sem.at[g, 3 + k],
                recv_sem=recv_sem.at[g, 3 + k],
                device_id=x_mate,
                device_id_type=MESH,
            )
            copy.start()
            started.append(copy)
    for g in range(3):
        started[4 * g + 3].wait_recv()
        local[g].wait()
    for copy in started[12:]:
        copy.wait_recv()
    for copy in started:
        copy.wait_send()


def gather_weights(triple_weight, output_weight, expand_weight, shrink_weight):
    rows = triple_weight.shape[1]
    width = triple_weight.shape[2]
    attention = jnp.concatenate(
        [triple_weight[0], triple_weight[1], triple_weight[2], output_weight.T], axis=1
    )
    shapes = [
        jax.ShapeDtypeStruct((8,) + part.shape, jnp.bfloat16)
        for part in (attention, expand_weight, shrink_weight.T)
    ]
    spec = pl.BlockSpec(memory_space=pltpu.VMEM)
    full = pl.pallas_call(
        gather_kernel,
        out_shape=shapes,
        in_specs=[spec] * 3,
        out_specs=[spec] * 3,
        scratch_shapes=[
            pltpu.SemaphoreType.DMA((3, 7)),
            pltpu.SemaphoreType.DMA((3, 7)),
            pltpu.SemaphoreType.DMA((3,)),
        ],
        compiler_params=pltpu.CompilerParams(
            collective_id=0, has_side_effects=True, vmem_limit_bytes=32 << 20
        ),
    )(attention, expand_weight, shrink_weight.T)
    attention, expand, shrink_t = (part.reshape(8 * rows, -1) for part in full)
    triple = jnp.stack([attention[:, i * width : (i + 1) * width] for i in range(3)])
    return triple, attention[:, 3 * width :].T, expand, shrink_t.T


def shards(
    inputs,
    target,
    valid,
    first_gain,
    first_shift,
    triple_weight,
    query_value_bias,
    output_weight,
    output_bias,
    second_gain,
    second_shift,
    expand_weight,
    expand_bias,
    shrink_weight,
    shrink_bias,
    rows_table,
    columns_table,
):
    local_heads = HEADS // lax.axis_size("tensor")
    local_width = local_heads * HEAD
    local_windows = inputs.shape[0]
    win_micro = local_windows // MICRO
    micro_rows = win_micro * WIN_TOK
    scale_factor = 1.0 / math.sqrt(HEAD)
    highest = lax.Precision.HIGHEST
    live = valid.astype(jnp.float32)
    select = position_select(WIN)
    table_rows = jnp.einsum(
        "aej,jc->aec", select, rows_table.astype(jnp.bfloat16), preferred_element_type=jnp.float32
    ).astype(jnp.bfloat16)
    table_cols = jnp.einsum(
        "aej,jc->aec",
        select,
        columns_table.astype(jnp.bfloat16),
        preferred_element_type=jnp.float32,
    ).astype(jnp.bfloat16)
    rows_float = table_rows.astype(jnp.float32)
    cols_float = table_cols.astype(jnp.float32)
    triple_bias = jnp.stack(
        [query_value_bias[0], jnp.zeros_like(query_value_bias[0]), query_value_bias[1]]
    )
    if lax.axis_size("dp") == 8 and lax.axis_size("tensor") == 4:
        gathered = gather_weights(triple_weight, output_weight, expand_weight, shrink_weight)
    else:
        gathered = (
            lax.all_gather(triple_weight, "dp", axis=1, tiled=True),
            lax.all_gather(output_weight, "dp", axis=1, tiled=True),
            lax.all_gather(expand_weight, "dp", axis=0, tiled=True),
            lax.all_gather(shrink_weight, "dp", axis=1, tiled=True),
        )
    saved = []
    outputs = []
    local_loss = jnp.zeros((), jnp.float32)
    for micro in range(MICRO):
        full_triple, full_output, full_expand, full_shrink = gathered
        lower = micro * win_micro
        flat_rows = inputs[lower : lower + win_micro].reshape(micro_rows, D).astype(jnp.float32)
        unit_one, inverse_one = normalize(flat_rows)
        normed = (unit_one * first_gain + first_shift).astype(jnp.bfloat16)
        projected = (
            jnp.einsum("rd,tde->rte", normed, full_triple, preferred_element_type=jnp.float32)
            + triple_bias
        )
        projected = projected.astype(jnp.bfloat16)
        split = projected.reshape(win_micro, WIN, WIN, 3, local_heads, HEAD)
        queries = split[:, :, :, 0]
        keys = split[:, :, :, 1]
        values = split[:, :, :, 2].reshape(win_micro, WIN_TOK, local_heads, HEAD)
        scores = score_block(queries, keys, table_rows, table_cols, scale_factor)
        peak = jnp.max(scores, axis=-1, keepdims=True)
        raised = jnp.exp(scores - peak)
        denominator = jnp.sum(raised, axis=-1, keepdims=True)
        log_total = peak + jnp.log(denominator)
        softmaxed = (raised / denominator).astype(jnp.bfloat16)
        mixed = jnp.einsum("gnqk,gknc->gqnc", softmaxed, values, preferred_element_type=jnp.float32)
        mixed = mixed.reshape(micro_rows, local_width).astype(jnp.bfloat16)
        partial_attended = jnp.dot(mixed, full_output, preferred_element_type=jnp.float32)
        middle = flat_rows + (row_total(partial_attended) + output_bias)
        unit_two, inverse_two = normalize(middle)
        normed_two = (unit_two * second_gain + second_shift).astype(jnp.bfloat16)
        before = jnp.dot(normed_two, full_expand, preferred_element_type=jnp.float32) + expand_bias
        hidden = gelu_exact(before).astype(jnp.bfloat16)
        partial_shrunk = jnp.dot(hidden, full_shrink, preferred_element_type=jnp.float32)
        result = middle + (row_total(partial_shrunk) + shrink_bias)
        aim = target[lower : lower + win_micro].reshape(micro_rows, D).astype(jnp.float32)
        marks = live[lower : lower + win_micro].reshape(micro_rows, 1)
        weighted_gap = marks * (result - aim)
        local_loss = local_loss + jnp.sum(weighted_gap * (result - aim))
        outputs.append(result.astype(jnp.bfloat16).reshape(win_micro, WIN_TOK, D))
        saved.append(
            (
                unit_one,
                inverse_one,
                normed,
                projected,
                log_total,
                mixed,
                unit_two,
                inverse_two,
                normed_two,
                before,
                hidden,
                weighted_gap,
            )
        )
    loss_total, count = lax.psum((local_loss, jnp.sum(live)), "dp")
    loss = loss_total / (count * D)
    grad_scale = local_windows * WIN_TOK * lax.axis_size("dp") / count
    triple_acc = jnp.zeros((3, D, local_width), jnp.float32)
    output_acc = jnp.zeros((local_width, D), jnp.float32)
    expand_acc = jnp.zeros((D, full_expand.shape[1]), jnp.float32)
    shrink_acc = jnp.zeros((full_shrink.shape[0], D), jnp.float32)
    first_gain_acc = jnp.zeros((D,), jnp.float32)
    first_shift_acc = jnp.zeros((D,), jnp.float32)
    second_gain_acc = jnp.zeros((D,), jnp.float32)
    second_shift_acc = jnp.zeros((D,), jnp.float32)
    output_bias_acc = jnp.zeros((D,), jnp.float32)
    shrink_bias_acc = jnp.zeros((D,), jnp.float32)
    expand_bias_acc = jnp.zeros((full_expand.shape[1],), jnp.float32)
    query_value_acc = jnp.zeros((2, local_width), jnp.float32)
    rows_expanded_acc = jnp.zeros((WIN, WIN, HEAD), jnp.float32)
    cols_expanded_acc = jnp.zeros((WIN, WIN, HEAD), jnp.float32)
    input_grads = []
    for micro in range(MICRO):
        full_triple, full_output, full_expand, full_shrink = gathered
        (
            unit_one,
            inverse_one,
            normed,
            projected,
            log_total,
            mixed,
            unit_two,
            inverse_two,
            normed_two,
            before,
            hidden,
            weighted_gap,
        ) = saved[micro]
        grad_result = grad_scale * weighted_gap
        shrink_bias_acc = shrink_bias_acc + jnp.sum(share_of(grad_result), axis=0)
        grad_result_low = grad_result.astype(jnp.bfloat16)
        shrink_acc = shrink_acc + jnp.einsum(
            "rf,rd->fd", hidden, grad_result_low, preferred_element_type=jnp.float32
        )
        grad_hidden = jnp.einsum(
            "rd,fd->rf", grad_result_low, full_shrink, preferred_element_type=jnp.float32
        )
        unused, gelu_pull = jax.vjp(gelu_exact, before)
        grad_before = gelu_pull(grad_hidden)[0].astype(jnp.bfloat16)
        expand_bias_acc = expand_bias_acc + jnp.sum(grad_before.astype(jnp.float32), axis=0)
        expand_acc = expand_acc + jnp.einsum(
            "rd,rf->df", normed_two, grad_before, preferred_element_type=jnp.float32
        )
        partial_two = jnp.einsum(
            "rf,df->rd", grad_before, full_expand, preferred_element_type=jnp.float32
        )
        grad_normed_two = row_total(partial_two)
        grad_middle = grad_result + normalize_back(
            grad_normed_two, unit_two, inverse_two, second_gain
        )
        second_gain_acc = second_gain_acc + jnp.sum(share_of(grad_normed_two * unit_two), axis=0)
        second_shift_acc = second_shift_acc + jnp.sum(share_of(grad_normed_two), axis=0)
        output_bias_acc = output_bias_acc + jnp.sum(share_of(grad_middle), axis=0)
        grad_middle_low = grad_middle.astype(jnp.bfloat16)
        output_acc = output_acc + jnp.einsum(
            "rc,rd->cd", mixed, grad_middle_low, preferred_element_type=jnp.float32
        )
        grad_mixed = jnp.einsum(
            "rd,cd->rc", grad_middle_low, full_output, preferred_element_type=jnp.float32
        )
        grad_mixed = grad_mixed.astype(jnp.bfloat16).reshape(win_micro, WIN_TOK, local_heads, HEAD)
        split = projected.reshape(win_micro, WIN, WIN, 3, local_heads, HEAD)
        queries = split[:, :, :, 0]
        keys = split[:, :, :, 1]
        queries_flat = queries.reshape(win_micro, WIN_TOK, local_heads, HEAD)
        keys_flat = keys.reshape(win_micro, WIN_TOK, local_heads, HEAD)
        values = split[:, :, :, 2].reshape(win_micro, WIN_TOK, local_heads, HEAD)
        scores = score_block(queries, keys, table_rows, table_cols, scale_factor)
        softmax_exact = jnp.exp(scores - log_total)
        grad_soft = jnp.einsum(
            "gqnc,gknc->gnqk", grad_mixed, values, preferred_element_type=jnp.float32
        )
        delta = jnp.sum(softmax_exact * grad_soft, axis=-1, keepdims=True)
        grad_scores = (softmax_exact * (grad_soft - delta)).astype(jnp.bfloat16)
        grad_values = jnp.einsum(
            "gnqk,gqnc->gknc",
            softmax_exact.astype(jnp.bfloat16),
            grad_mixed,
            preferred_element_type=jnp.float32,
        )
        grad_keys = (
            jnp.einsum(
                "gnqk,gqnc->gknc", grad_scores, queries_flat, preferred_element_type=jnp.float32
            )
            * scale_factor
        )
        grad_queries = (
            jnp.einsum(
                "gnqk,gknc->gqnc", grad_scores, keys_flat, preferred_element_type=jnp.float32
            )
            * scale_factor
        )
        grad_grid = grad_scores.astype(jnp.float32).reshape(
            win_micro, local_heads, WIN, WIN, WIN, WIN
        )
        row_part = jnp.sum(grad_grid, axis=5)
        col_part = jnp.sum(grad_grid, axis=4)
        queries_float = queries.astype(jnp.float32)
        rel_queries = jnp.einsum("gnabe,aec->gabnc", row_part, rows_float, precision=highest)
        rel_queries = rel_queries + jnp.einsum(
            "gnabf,bfc->gabnc", col_part, cols_float, precision=highest
        )
        grad_queries = grad_queries + rel_queries.reshape(win_micro, WIN_TOK, local_heads, HEAD)
        rows_expanded_acc = rows_expanded_acc + jnp.einsum(
            "gnabe,gabnc->aec", row_part, queries_float, precision=highest
        )
        cols_expanded_acc = cols_expanded_acc + jnp.einsum(
            "gnabf,gabnc->bfc", col_part, queries_float, precision=highest
        )
        grad_projected = jnp.stack(
            [
                grad_queries.reshape(micro_rows, local_width),
                grad_keys.reshape(micro_rows, local_width),
                grad_values.reshape(micro_rows, local_width),
            ],
            axis=1,
        ).astype(jnp.bfloat16)
        projected_float_sums = jnp.sum(grad_projected.astype(jnp.float32), axis=0)
        query_value_acc = query_value_acc + jnp.stack(
            [projected_float_sums[0], projected_float_sums[2]]
        )
        triple_acc = triple_acc + jnp.einsum(
            "rd,rte->tde", normed, grad_projected, preferred_element_type=jnp.float32
        )
        partial_one = jnp.einsum(
            "rte,tde->rd", grad_projected, full_triple, preferred_element_type=jnp.float32
        )
        grad_normed = row_total(partial_one)
        grad_tokens = grad_middle + normalize_back(grad_normed, unit_one, inverse_one, first_gain)
        first_gain_acc = first_gain_acc + jnp.sum(share_of(grad_normed * unit_one), axis=0)
        first_shift_acc = first_shift_acc + jnp.sum(share_of(grad_normed), axis=0)
        input_grads.append(grad_tokens.reshape(win_micro, WIN_TOK, D))
    select_float = select.astype(jnp.float32)
    rows_table_part = jnp.einsum("aej,aec->jc", select_float, rows_expanded_acc, precision=highest)
    cols_table_part = jnp.einsum("aej,aec->jc", select_float, cols_expanded_acc, precision=highest)
    triple_grad, output_grad, expand_grad, shrink_grad = (
        lax.psum_scatter(triple_acc, "dp", scatter_dimension=1, tiled=True),
        lax.psum_scatter(output_acc, "dp", scatter_dimension=1, tiled=True),
        lax.psum_scatter(expand_acc, "dp", scatter_dimension=0, tiled=True),
        lax.psum_scatter(shrink_acc, "dp", scatter_dimension=1, tiled=True),
    )
    over_heads = lax.psum(
        (
            rows_table_part,
            cols_table_part,
            first_gain_acc,
            first_shift_acc,
            output_bias_acc,
            second_gain_acc,
            second_shift_acc,
            shrink_bias_acc,
        ),
        "tensor",
    )
    summed_small = lax.psum(
        (
            over_heads[0],
            over_heads[1],
            over_heads[2],
            over_heads[3],
            over_heads[4],
            over_heads[5],
            over_heads[6],
            over_heads[7],
            query_value_acc,
            expand_bias_acc,
        ),
        "dp",
    )
    return (
        jnp.concatenate(outputs, axis=0),
        loss,
        jnp.concatenate(input_grads, axis=0),
        summed_small[2],
        summed_small[3],
        triple_grad,
        summed_small[8],
        output_grad,
        summed_small[4],
        summed_small[5],
        summed_small[6],
        expand_grad,
        summed_small[9],
        shrink_grad,
        summed_small[7],
        summed_small[0],
        summed_small[1],
    )


def solution(mesh):
    placed = (
        P("dp", None, None),
        P("dp", None, None),
        P("dp", None),
        P(),
        P(),
        P(None, "dp", "tensor"),
        P(None, "tensor"),
        P("tensor", "dp"),
        P(),
        P(),
        P(),
        P("dp", "tensor"),
        P("tensor"),
        P("tensor", "dp"),
        P(),
        P(),
        P(),
    )
    return jax.shard_map(
        shards,
        mesh=mesh,
        in_specs=placed,
        out_specs=(
            P("dp", None, None),
            P(),
            P("dp", None, None),
            P(),
            P(),
            P(None, "dp", "tensor"),
            P(None, "tensor"),
            P("tensor", "dp"),
            P(),
            P(),
            P(),
            P("dp", "tensor"),
            P("tensor"),
            P("tensor", "dp"),
            P(),
            P(),
            P(),
        ),
        check_vma=False,
    )
```

```python
import math

import jax
import jax.numpy as jnp
import numpy as np
from jax import lax
from jax.experimental import pallas as pl
from jax.experimental.pallas import tpu as pltpu
from jax.sharding import PartitionSpec as P

MESH = pl.DeviceIdType.MESH

D = 768
HEADS = 12
HEAD = 64
WIN = 14
WIN_TOK = 196
MICRO = 2


def normalize(values):
    center = jnp.mean(values, axis=-1, keepdims=True)
    centered = values - center
    spread = jnp.mean(centered * centered, axis=-1, keepdims=True)
    inverse = lax.rsqrt(spread + 1e-06)
    return (centered * inverse, inverse)


def normalize_back(grad_out, unit, inverse, gain):
    scaled = grad_out * gain
    mean_one = jnp.mean(scaled, axis=-1, keepdims=True)
    mean_two = jnp.mean(scaled * unit, axis=-1, keepdims=True)
    return inverse * (scaled - mean_one - unit * mean_two)


def position_select(side):
    shape = (side, side, 2 * side - 1)
    first = lax.broadcasted_iota(jnp.int32, shape, 0)
    second = lax.broadcasted_iota(jnp.int32, shape, 1)
    slots = lax.broadcasted_iota(jnp.int32, shape, 2)
    return (slots == first - second + side - 1).astype(jnp.bfloat16)


def score_block(queries, keys, table_rows, table_cols, scale_factor):
    groups = queries.shape[0]
    side = queries.shape[1]
    heads = queries.shape[3]
    along_rows = jnp.einsum(
        "gabnc,aec->gnabe", queries, table_rows, preferred_element_type=jnp.float32
    )
    along_cols = jnp.einsum(
        "gabnc,bfc->gnabf", queries, table_cols, preferred_element_type=jnp.float32
    )
    scores = (
        jnp.einsum("gabnc,gefnc->gnabef", queries, keys, preferred_element_type=jnp.float32)
        * scale_factor
    )
    scores = scores + along_rows[..., :, None] + along_cols[..., None, :]
    return scores.reshape(groups, heads, side * side, side * side)


def gelu_exact(inner):
    return jax.nn.gelu(inner, approximate=False)


def row_total(partial_value):
    return lax.psum(partial_value, "tensor")


def share_of(values):
    share_rows = values.shape[0] // lax.axis_size("tensor")
    return lax.dynamic_slice_in_dim(values, lax.axis_index("tensor") * share_rows, share_rows, 0)


def shards(
    inputs,
    target,
    valid,
    first_gain,
    first_shift,
    triple_weight,
    query_value_bias,
    output_weight,
    output_bias,
    second_gain,
    second_shift,
    expand_weight,
    expand_bias,
    shrink_weight,
    shrink_bias,
    rows_table,
    columns_table,
):
    local_heads = HEADS // lax.axis_size("tensor")
    local_width = local_heads * HEAD
    local_windows = inputs.shape[0]
    win_micro = local_windows // MICRO
    micro_rows = win_micro * WIN_TOK
    scale_factor = 1.0 / math.sqrt(HEAD)
    highest = lax.Precision.HIGHEST
    live = valid.astype(jnp.float32)
    select = position_select(WIN)
    table_rows = jnp.einsum(
        "aej,jc->aec", select, rows_table.astype(jnp.bfloat16), preferred_element_type=jnp.float32
    ).astype(jnp.bfloat16)
    table_cols = jnp.einsum(
        "aej,jc->aec",
        select,
        columns_table.astype(jnp.bfloat16),
        preferred_element_type=jnp.float32,
    ).astype(jnp.bfloat16)
    rows_float = table_rows.astype(jnp.float32)
    cols_float = table_cols.astype(jnp.float32)
    triple_bias = jnp.stack(
        [query_value_bias[0], jnp.zeros_like(query_value_bias[0]), query_value_bias[1]]
    )
    saved = []
    outputs = []
    local_loss = jnp.zeros((), jnp.float32)
    for micro in range(MICRO):
        gathered = (
            lax.all_gather(triple_weight, "dp", axis=1, tiled=True),
            lax.all_gather(output_weight, "dp", axis=1, tiled=True),
            lax.all_gather(expand_weight, "dp", axis=0, tiled=True),
            lax.all_gather(shrink_weight, "dp", axis=1, tiled=True),
        )
        full_triple, full_output, full_expand, full_shrink = gathered
        lower = micro * win_micro
        flat_rows = inputs[lower : lower + win_micro].reshape(micro_rows, D).astype(jnp.float32)
        unit_one, inverse_one = normalize(flat_rows)
        normed = (unit_one * first_gain + first_shift).astype(jnp.bfloat16)
        projected = (
            jnp.einsum("rd,tde->rte", normed, full_triple, preferred_element_type=jnp.float32)
            + triple_bias
        )
        projected = projected.astype(jnp.bfloat16)
        split = projected.reshape(win_micro, WIN, WIN, 3, local_heads, HEAD)
        queries = split[:, :, :, 0]
        keys = split[:, :, :, 1]
        values = split[:, :, :, 2].reshape(win_micro, WIN_TOK, local_heads, HEAD)
        scores = score_block(queries, keys, table_rows, table_cols, scale_factor)
        peak = jnp.max(scores, axis=-1, keepdims=True)
        raised = jnp.exp(scores - peak)
        denominator = jnp.sum(raised, axis=-1, keepdims=True)
        log_total = peak + jnp.log(denominator)
        softmaxed = (raised / denominator).astype(jnp.bfloat16)
        mixed = jnp.einsum("gnqk,gknc->gqnc", softmaxed, values, preferred_element_type=jnp.float32)
        mixed = mixed.reshape(micro_rows, local_width).astype(jnp.bfloat16)
        partial_attended = jnp.dot(mixed, full_output, preferred_element_type=jnp.float32)
        middle = flat_rows + (row_total(partial_attended) + output_bias)
        unit_two, inverse_two = normalize(middle)
        normed_two = (unit_two * second_gain + second_shift).astype(jnp.bfloat16)
        before = jnp.dot(normed_two, full_expand, preferred_element_type=jnp.float32) + expand_bias
        hidden = gelu_exact(before).astype(jnp.bfloat16)
        partial_shrunk = jnp.dot(hidden, full_shrink, preferred_element_type=jnp.float32)
        result = middle + (row_total(partial_shrunk) + shrink_bias)
        aim = target[lower : lower + win_micro].reshape(micro_rows, D).astype(jnp.float32)
        marks = live[lower : lower + win_micro].reshape(micro_rows, 1)
        weighted_gap = marks * (result - aim)
        local_loss = local_loss + jnp.sum(weighted_gap * (result - aim))
        outputs.append(result.astype(jnp.bfloat16).reshape(win_micro, WIN_TOK, D))
        saved.append(
            (
                unit_one,
                inverse_one,
                normed,
                projected,
                log_total,
                mixed,
                unit_two,
                inverse_two,
                normed_two,
                before,
                hidden,
                weighted_gap,
            )
        )
    loss_total, count = lax.psum((local_loss, jnp.sum(live)), "dp")
    loss = loss_total / (count * D)
    grad_scale = local_windows * WIN_TOK * lax.axis_size("dp") / count
    triple_acc = jnp.zeros((3, D, local_width), jnp.float32)
    output_acc = jnp.zeros((local_width, D), jnp.float32)
    expand_acc = jnp.zeros((D, full_expand.shape[1]), jnp.float32)
    shrink_acc = jnp.zeros((full_shrink.shape[0], D), jnp.float32)
    first_gain_acc = jnp.zeros((D,), jnp.float32)
    first_shift_acc = jnp.zeros((D,), jnp.float32)
    second_gain_acc = jnp.zeros((D,), jnp.float32)
    second_shift_acc = jnp.zeros((D,), jnp.float32)
    output_bias_acc = jnp.zeros((D,), jnp.float32)
    shrink_bias_acc = jnp.zeros((D,), jnp.float32)
    expand_bias_acc = jnp.zeros((full_expand.shape[1],), jnp.float32)
    query_value_acc = jnp.zeros((2, local_width), jnp.float32)
    rows_expanded_acc = jnp.zeros((WIN, WIN, HEAD), jnp.float32)
    cols_expanded_acc = jnp.zeros((WIN, WIN, HEAD), jnp.float32)
    input_grads = []
    for micro in range(MICRO):
        gathered = (
            lax.all_gather(triple_weight, "dp", axis=1, tiled=True),
            lax.all_gather(output_weight, "dp", axis=1, tiled=True),
            lax.all_gather(expand_weight, "dp", axis=0, tiled=True),
            lax.all_gather(shrink_weight, "dp", axis=1, tiled=True),
        )
        full_triple, full_output, full_expand, full_shrink = gathered
        (
            unit_one,
            inverse_one,
            normed,
            projected,
            log_total,
            mixed,
            unit_two,
            inverse_two,
            normed_two,
            before,
            hidden,
            weighted_gap,
        ) = saved[micro]
        grad_result = grad_scale * weighted_gap
        shrink_bias_acc = shrink_bias_acc + jnp.sum(share_of(grad_result), axis=0)
        grad_result_low = grad_result.astype(jnp.bfloat16)
        shrink_acc = shrink_acc + jnp.einsum(
            "rf,rd->fd", hidden, grad_result_low, preferred_element_type=jnp.float32
        )
        grad_hidden = jnp.einsum(
            "rd,fd->rf", grad_result_low, full_shrink, preferred_element_type=jnp.float32
        )
        unused, gelu_pull = jax.vjp(gelu_exact, before)
        grad_before = gelu_pull(grad_hidden)[0].astype(jnp.bfloat16)
        expand_bias_acc = expand_bias_acc + jnp.sum(grad_before.astype(jnp.float32), axis=0)
        expand_acc = expand_acc + jnp.einsum(
            "rd,rf->df", normed_two, grad_before, preferred_element_type=jnp.float32
        )
        partial_two = jnp.einsum(
            "rf,df->rd", grad_before, full_expand, preferred_element_type=jnp.float32
        )
        grad_normed_two = row_total(partial_two)
        grad_middle = grad_result + normalize_back(
            grad_normed_two, unit_two, inverse_two, second_gain
        )
        second_gain_acc = second_gain_acc + jnp.sum(share_of(grad_normed_two * unit_two), axis=0)
        second_shift_acc = second_shift_acc + jnp.sum(share_of(grad_normed_two), axis=0)
        output_bias_acc = output_bias_acc + jnp.sum(share_of(grad_middle), axis=0)
        grad_middle_low = grad_middle.astype(jnp.bfloat16)
        output_acc = output_acc + jnp.einsum(
            "rc,rd->cd", mixed, grad_middle_low, preferred_element_type=jnp.float32
        )
        grad_mixed = jnp.einsum(
            "rd,cd->rc", grad_middle_low, full_output, preferred_element_type=jnp.float32
        )
        grad_mixed = grad_mixed.astype(jnp.bfloat16).reshape(win_micro, WIN_TOK, local_heads, HEAD)
        split = projected.reshape(win_micro, WIN, WIN, 3, local_heads, HEAD)
        queries = split[:, :, :, 0]
        keys = split[:, :, :, 1]
        queries_flat = queries.reshape(win_micro, WIN_TOK, local_heads, HEAD)
        keys_flat = keys.reshape(win_micro, WIN_TOK, local_heads, HEAD)
        values = split[:, :, :, 2].reshape(win_micro, WIN_TOK, local_heads, HEAD)
        scores = score_block(queries, keys, table_rows, table_cols, scale_factor)
        softmax_exact = jnp.exp(scores - log_total)
        grad_soft = jnp.einsum(
            "gqnc,gknc->gnqk", grad_mixed, values, preferred_element_type=jnp.float32
        )
        delta = jnp.sum(softmax_exact * grad_soft, axis=-1, keepdims=True)
        grad_scores = (softmax_exact * (grad_soft - delta)).astype(jnp.bfloat16)
        grad_values = jnp.einsum(
            "gnqk,gqnc->gknc",
            softmax_exact.astype(jnp.bfloat16),
            grad_mixed,
            preferred_element_type=jnp.float32,
        )
        grad_keys = (
            jnp.einsum(
                "gnqk,gqnc->gknc", grad_scores, queries_flat, preferred_element_type=jnp.float32
            )
            * scale_factor
        )
        grad_queries = (
            jnp.einsum(
                "gnqk,gknc->gqnc", grad_scores, keys_flat, preferred_element_type=jnp.float32
            )
            * scale_factor
        )
        grad_grid = grad_scores.astype(jnp.float32).reshape(
            win_micro, local_heads, WIN, WIN, WIN, WIN
        )
        row_part = jnp.sum(grad_grid, axis=5)
        col_part = jnp.sum(grad_grid, axis=4)
        queries_float = queries.astype(jnp.float32)
        rel_queries = jnp.einsum("gnabe,aec->gabnc", row_part, rows_float, precision=highest)
        rel_queries = rel_queries + jnp.einsum(
            "gnabf,bfc->gabnc", col_part, cols_float, precision=highest
        )
        grad_queries = grad_queries + rel_queries.reshape(win_micro, WIN_TOK, local_heads, HEAD)
        rows_expanded_acc = rows_expanded_acc + jnp.einsum(
            "gnabe,gabnc->aec", row_part, queries_float, precision=highest
        )
        cols_expanded_acc = cols_expanded_acc + jnp.einsum(
            "gnabf,gabnc->bfc", col_part, queries_float, precision=highest
        )
        grad_projected = jnp.stack(
            [
                grad_queries.reshape(micro_rows, local_width),
                grad_keys.reshape(micro_rows, local_width),
                grad_values.reshape(micro_rows, local_width),
            ],
            axis=1,
        ).astype(jnp.bfloat16)
        projected_float_sums = jnp.sum(grad_projected.astype(jnp.float32), axis=0)
        query_value_acc = query_value_acc + jnp.stack(
            [projected_float_sums[0], projected_float_sums[2]]
        )
        triple_acc = triple_acc + jnp.einsum(
            "rd,rte->tde", normed, grad_projected, preferred_element_type=jnp.float32
        )
        partial_one = jnp.einsum(
            "rte,tde->rd", grad_projected, full_triple, preferred_element_type=jnp.float32
        )
        grad_normed = row_total(partial_one)
        grad_tokens = grad_middle + normalize_back(grad_normed, unit_one, inverse_one, first_gain)
        first_gain_acc = first_gain_acc + jnp.sum(share_of(grad_normed * unit_one), axis=0)
        first_shift_acc = first_shift_acc + jnp.sum(share_of(grad_normed), axis=0)
        input_grads.append(grad_tokens.reshape(win_micro, WIN_TOK, D))
    select_float = select.astype(jnp.float32)
    rows_table_part = jnp.einsum("aej,aec->jc", select_float, rows_expanded_acc, precision=highest)
    cols_table_part = jnp.einsum("aej,aec->jc", select_float, cols_expanded_acc, precision=highest)
    triple_grad, output_grad, expand_grad, shrink_grad = (
        lax.psum_scatter(triple_acc, "dp", scatter_dimension=1, tiled=True),
        lax.psum_scatter(output_acc, "dp", scatter_dimension=1, tiled=True),
        lax.psum_scatter(expand_acc, "dp", scatter_dimension=0, tiled=True),
        lax.psum_scatter(shrink_acc, "dp", scatter_dimension=1, tiled=True),
    )
    over_heads = lax.psum(
        (
            rows_table_part,
            cols_table_part,
            first_gain_acc,
            first_shift_acc,
            output_bias_acc,
            second_gain_acc,
            second_shift_acc,
            shrink_bias_acc,
        ),
        "tensor",
    )
    summed_small = lax.psum(
        (
            over_heads[0],
            over_heads[1],
            over_heads[2],
            over_heads[3],
            over_heads[4],
            over_heads[5],
            over_heads[6],
            over_heads[7],
            query_value_acc,
            expand_bias_acc,
        ),
        "dp",
    )
    return (
        jnp.concatenate(outputs, axis=0),
        loss,
        jnp.concatenate(input_grads, axis=0),
        summed_small[2],
        summed_small[3],
        triple_grad,
        summed_small[8],
        output_grad,
        summed_small[4],
        summed_small[5],
        summed_small[6],
        expand_grad,
        summed_small[9],
        shrink_grad,
        summed_small[7],
        summed_small[0],
        summed_small[1],
    )


ROWS = 208
KEYS = 256
CHUNKS = ((0, 112), (112, 96))
F32 = jnp.float32
BF16 = jnp.bfloat16


def z_mate(z, k):
    if k == 0:
        return z
    if k == 1:
        return z + 1 - 2 * (z % 2)
    if k == 2:
        return (z + 2) % 4
    return 3 - z


def dot_nn(a, b):
    return lax.dot_general(a, b, (((1,), (0,)), ((), ())), preferred_element_type=F32)


def dot_nt(a, b):
    return lax.dot_general(a, b, (((1,), (1,)), ((), ())), preferred_element_type=F32)


def dot_tn(a, b):
    return lax.dot_general(a, b, (((0,), (0,)), ((), ())), preferred_element_type=F32)


def column_sum(values):
    return jnp.sum(values, axis=0, keepdims=True)


UNITS = ((0, 1, 2, 0, 0), (0, 1, 2, 1, 1), (3, 5, 6, 0, 1))


def block_kernel(
    x_in,
    target_in,
    valid_in,
    vectors,
    side_in,
    wa_in,
    we_in,
    ws_in,
    tables_in,
    onehot,
    place,
    pick,
    block_out,
    grad_out,
    ga_out,
    ge_out,
    gs_out,
    small_out,
    table_out,
    wa,
    we,
    ws,
    side,
    xf,
    unit1,
    unit2,
    inv1,
    inv2,
    mid,
    acc,
    n1,
    n2,
    gr,
    gm,
    pj,
    ps,
    mx,
    mxr,
    hid,
    hidr,
    slope,
    gb,
    gbr,
    gmx,
    gp,
    gpr,
    t2,
    tg,
    es,
    er,
    gw,
    xs,
    xr,
    zs,
    zr,
    ig,
    cnt,
    cntr,
    sb,
    sbr,
    tb,
    tbr,
    send_sem,
    recv_sem,
):
    dp = lax.axis_index("dp")
    t = lax.axis_index("tensor")
    z = dp // 2
    x = dp % 2
    y = t // 2
    c = t % 2
    z_mates = [(z_mate(z, k) * 2 + x, t) for k in (1, 2, 3)]
    x_mate = (z * 2 + 1 - x, t)
    y_mate = (dp, (1 - y) * 2 + c)
    c_mate = (dp, y * 2 + 1 - c)
    peer_window = (1 - y) * 2 + c
    token_total = lax.axis_size("dp") * 4 * WIN_TOK

    started = []

    def send(src, dst, mate):
        i = len(started)
        copy = pltpu.make_async_remote_copy(
            src_ref=src,
            dst_ref=dst,
            send_sem=send_sem.at[i],
            recv_sem=recv_sem.at[i],
            device_id=mate,
            device_id_type=MESH,
        )
        copy.start()
        started.append(copy)
        return copy

    barrier = pltpu.get_barrier_semaphore()
    for mate in z_mates + [x_mate, y_mate, c_mate]:
        pl.semaphore_signal(barrier, inc=1, device_id=mate, device_id_type=MESH)
    pl.semaphore_wait(barrier, 6)

    w_in = (wa_in, we_in, ws_in)
    w_full = (wa, we, ws)
    from_z = {}
    from_x = {}
    from_c = {}

    def row_of(k, xx):
        return z_mate(z, k) * 2 + xx

    def gather_start(g):
        for k in (1, 2, 3):
            from_z[g, k] = send(w_in[g], w_full[g].at[0, dp], z_mates[k - 1])
        from_x[g, 0] = send(w_in[g], w_full[g].at[0, dp], x_mate)
        from_c[g, 0] = send(w_in[g], w_full[g].at[1, dp], c_mate)
        w_full[g][0, dp] = w_in[g][...]

    def gather_z(g, k):
        from_z[g, k].wait_recv()
        block = w_full[g].at[0, row_of(k, x)]
        from_x[g, k] = send(block, block, x_mate)
        from_c[g, k] = send(block, w_full[g].at[1, row_of(k, x)], c_mate)

    def gather_x(g, k):
        from_x[g, k].wait_recv()
        from_c[g, 4 + k] = send(
            w_full[g].at[0, row_of(k, 1 - x)], w_full[g].at[1, row_of(k, 1 - x)], c_mate
        )

    def gather_end(g):
        for k in range(8):
            from_c[g, k].wait_recv()

    gather_start(0)
    side_copy = send(side_in, side.at[1], c_mate)
    side[0] = side_in[...]
    marks_all = valid_in[...].astype(F32)
    cnt[0] = jnp.full((8, 128), jnp.sum(marks_all), F32)
    cnt_x = send(cnt.at[0], cntr.at[0], x_mate)

    gain1 = vectors[0:1, :]
    shift1 = vectors[1:2, :]
    bias_out = vectors[2:3, :]
    gain2 = vectors[3:4, :]
    shift2 = vectors[4:5, :]
    bias_shrink = vectors[5:6, :]

    lane = lax.broadcasted_iota(jnp.int32, (1, 128), 1)
    half = ((lane < 64).astype(F32), (lane >= 64).astype(F32))
    key_mask = [(m * 0.125).astype(BF16) for m in half]
    half = [m.astype(BF16) for m in half]
    key_lane = lax.broadcasted_iota(jnp.int32, (1, KEYS), 1)
    key_bias = jnp.where(key_lane < WIN_TOK, 0.0, -1e30).astype(F32)

    row_ids = lax.broadcasted_iota(jnp.int32, (4, WIN_TOK), 0)
    own_marks = column_sum(jnp.where(row_ids == t, marks_all, 0.0))
    eye = lax.broadcasted_iota(jnp.int32, (ROWS, WIN_TOK), 0) == lax.broadcasted_iota(
        jnp.int32, (ROWS, WIN_TOK), 1
    )
    live = jnp.sum(jnp.where(eye, own_marks, 0.0), axis=1, keepdims=True)

    xf[...] = jnp.zeros_like(xf)
    xf[0, 0:WIN_TOK, :] = x_in[t].astype(F32)
    xf[1, 0:WIN_TOK, :] = x_in[peer_window].astype(F32)
    for w in range(2):
        unit, inverse = normalize(xf[w])
        n1[0, w] = (unit * gain1 + shift1).astype(BF16)
        if w == 0:
            unit1[...] = unit
            inv1[...] = inverse
    n1_copy = send(n1.at[0], n1.at[1], c_mate)
    for p in range(2):
        t2[p] = dot_nn(onehot[...], tables_in[p]).astype(BF16)
    pj[:, :, ROWS:, :] = jnp.zeros((2, 2, KEYS - ROWS, 896), BF16)
    tg[...] = jnp.zeros_like(tg)

    for k in (1, 2, 3):
        gather_z(0, k)
    gather_start(1)
    for k in range(4):
        gather_x(0, k)
    cnt_x.wait_recv()
    cnt[1] = cnt[0] + cntr[0]
    cnt_z = [send(cnt.at[1], cntr.at[k], z_mates[k - 1]) for k in (1, 2, 3)]
    side_copy.wait_recv()
    gather_end(0)

    def project(w):
        def body(j, carry):
            value = dot_nn(n1[0, w], wa[j, :, :, 0:640].reshape(D, 640)) + side[j, 1:2, 0:640]
            pj[w, j, 0:ROWS, 0:640] = value.astype(BF16)
            rolled = pltpu.roll(value[:, 384:512], 64, 1)
            pj[w, j, 0:ROWS, 640:768] = rolled.astype(BF16)
            rolled = pltpu.roll(value[:, 512:640], 64, 1)
            pj[w, j, 0:ROWS, 768:896] = rolled.astype(BF16)
            return carry

        lax.fori_loop(0, 2, body, 0)

    def unit_of(w, j, h):
        q, k, v, p, pv = UNITS[h]
        query = pj[w, j, 0:ROWS, 128 * q : 128 * q + 128]
        key = pj[w, j, :, 128 * k : 128 * k + 128] * key_mask[p]
        value = pj[w, j, :, 128 * v : 128 * v + 128] * half[pv]
        return query, key, value

    def attend(w):
        def body(j, carry):
            mixes = []
            for h in range(3):
                query, key, value = unit_of(w, j, h)
                along = dot_nt(query, t2[UNITS[h][3]]) * place[...]
                high = along.astype(BF16)
                low = (along - high.astype(F32)).astype(BF16)
                scores = dot_nt(query, key) + dot_nn(high, pick[...]) + dot_nn(low, pick[...])
                scores = scores + key_bias
                raised = jnp.exp(scores - jnp.max(scores, axis=-1, keepdims=True))
                soft = raised * (1.0 / jnp.sum(raised, axis=-1, keepdims=True))
                ps[w, j, h] = soft
                mixes.append(dot_nn(soft.astype(BF16), value))
            mx[j, w, :, 0:128] = mixes[2].astype(BF16)
            mx[j, w, :, 128:256] = (mixes[0] + mixes[1]).astype(BF16)
            return carry

        lax.fori_loop(0, 2, body, 0)

    def attended(w, lo, n):
        return dot_nt(mx[0, w, lo : lo + n, :], wa[0, :, :, 512:768].reshape(D, 256)) + dot_nt(
            mx[1, w, lo : lo + n, :], wa[1, :, :, 512:768].reshape(D, 256)
        )

    project(1)
    attend(1)
    e1 = []
    for lo, n in CHUNKS:
        es[0, lo : lo + n, :] = attended(1, lo, n).astype(BF16)
        e1.append(send(es.at[0, pl.ds(lo, n)], er.at[0, pl.ds(lo, n)], y_mate))
    for k in (1, 2, 3):
        gather_z(1, k)
    gather_start(2)
    project(0)
    for k in range(4):
        gather_x(1, k)
    attend(0)
    mx_copy = send(mx.at[1], mxr, c_mate)
    mid[...] = xf[0] + bias_out + attended(0, 0, ROWS)
    gather_end(1)
    for k in (1, 2, 3):
        gather_z(2, k)

    e2 = []
    n2_c = []
    for i, (lo, n) in enumerate(CHUNKS):
        e1[i].wait_recv()
        middle = mid[lo : lo + n, :] + er[0, lo : lo + n, :].astype(F32)
        mid[lo : lo + n, :] = middle
        unit, inverse = normalize(middle)
        unit2[lo : lo + n, :] = unit
        inv2[lo : lo + n, :] = inverse
        n2[0, 0, lo : lo + n, :] = (unit * gain2 + shift2).astype(BF16)
        rows = pl.ds(lo, n)
        e2.append(send(n2.at[0, 0, rows], n2.at[0, 1, rows], y_mate))
        n2_c.append(send(n2.at[0, 0, rows], n2.at[1, 0, rows], c_mate))

    def feed(w, lo, n):
        def body(j, carry):
            before = dot_nn(n2[0, w, lo : lo + n, :], we[j].reshape(D, D)) + side[j, 0:1, :]
            phi = 0.5 * (1.0 + lax.erf(before * math.sqrt(0.5)))
            hid[j, w, lo : lo + n, :] = (before * phi).astype(BF16)
            bell = jnp.exp(-0.5 * before * before) * (1.0 / math.sqrt(2.0 * math.pi))
            slope[j, w, lo : lo + n, :] = phi + before * bell
            return carry

        lax.fori_loop(0, 2, body, 0)

    def shrunk(w, lo, n):
        return dot_nt(hid[0, w, lo : lo + n, :], ws[0].reshape(D, D)) + dot_nt(
            hid[1, w, lo : lo + n, :], ws[1].reshape(D, D)
        )

    for lo, n in CHUNKS:
        feed(0, lo, n)
    for k in range(4):
        gather_x(2, k)
    gather_end(2)
    e3 = []
    for i, (lo, n) in enumerate(CHUNKS):
        rows = pl.ds(lo, n)
        e2[i].wait_recv()
        n2_c.append(send(n2.at[0, 1, rows], n2.at[1, 1, rows], c_mate))
        feed(1, lo, n)
        es[1, lo : lo + n, :] = shrunk(1, lo, n).astype(BF16)
        e3.append(send(es.at[1, rows], er.at[1, rows], y_mate))
    hid_copy = send(hid.at[1], hidr, c_mate)
    acc[...] = mid[...] + bias_shrink + shrunk(0, 0, ROWS)

    for copy in cnt_z:
        copy.wait_recv()
    count = (cnt[1] + cntr[1]) + (cntr[2] + cntr[3])
    count = count[0:1, 0:1]
    scaled_live = live * (token_total / count)
    xf[1, 0:WIN_TOK, :] = target_in[t].astype(F32)
    xf[1, WIN_TOK:, :] = jnp.zeros((ROWS - WIN_TOK, D), F32)
    e4 = []
    gr_c = []
    loss_part = jnp.zeros((1, D), F32)
    shrink_bias_part = jnp.zeros((1, D), F32)
    for i, (lo, n) in enumerate(CHUNKS):
        rows = pl.ds(lo, n)
        e3[i].wait_recv()
        result = acc[lo : lo + n, :] + er[1, lo : lo + n, :].astype(F32)
        gap = result - xf[1, lo : lo + n, :]
        grad = gap * scaled_live[lo : lo + n, :]
        acc[lo : lo + n, :] = grad
        gr[0, 0, lo : lo + n, :] = grad.astype(BF16)
        e4.append(send(gr.at[0, 0, rows], gr.at[0, 1, rows], y_mate))
        gr_c.append(send(gr.at[0, 0, rows], gr.at[1, 0, rows], c_mate))
        block_out[t, lo : lo + n, :] = result.astype(BF16)
        loss_part = loss_part + column_sum(gap * gap * live[lo : lo + n, :])
        shrink_bias_part = shrink_bias_part + column_sum(grad)
    sb[0] = jnp.zeros((16, D), F32)
    sb[0, 6:7, :] = loss_part
    sb[0, 0:1, :] = shrink_bias_part

    def feed_back(w, lo, n):
        def body(j, carry):
            grad = dot_nn(gr[0, w, lo : lo + n, :], ws[j].reshape(D, D))
            grad = grad * slope[j, w, lo : lo + n, :]
            gb[j, w, lo : lo + n, :] = grad.astype(BF16)
            return carry

        lax.fori_loop(0, 2, body, 0)

    def expanded_back(w, lo, n):
        return dot_nt(gb[0, w, lo : lo + n, :], we[0].reshape(D, D)) + dot_nt(
            gb[1, w, lo : lo + n, :], we[1].reshape(D, D)
        )

    def rows_of(ref, width):
        return ref[...].reshape(2 * ROWS, width)

    def weight_grad(g, left, mine, theirs, width, at):
        value = dot_tn(rows_of(left.at[0], D), rows_of(mine, width)) + dot_tn(
            rows_of(left.at[1], D), rows_of(theirs, width)
        )
        gw[g, :, :, at : at + width] = value.reshape(8, 96, width)

    to_x = {}
    to_z = {}

    def scatter_x(g):
        for k in (1, 2, 3, 0):
            xs[g, k] = gw[g, row_of(k, 1 - x)].astype(BF16)
            to_x[g, k] = send(xs.at[g, k], xr.at[g, k], x_mate)

    def scatter_z(g):
        for k in (1, 2, 3):
            to_x[g, k].wait_recv()
            total = gw[g, row_of(k, x)] + xr[g, k].astype(F32)
            zs[g, k - 1] = total.astype(BF16)
            to_z[g, k] = send(zs.at[g, k - 1], zr.at[g, k - 1], z_mates[k - 1])

    def scatter_end(g, out):
        to_x[g, 0].wait_recv()
        total = gw[g, dp] + xr[g, 0].astype(F32)
        for k in (1, 2, 3):
            to_z[g, k].wait_recv()
            total = total + zr[g, k - 1].astype(F32)
        out[...] = total

    for lo, n in CHUNKS:
        feed_back(0, lo, n)
    e5 = []
    for i, (lo, n) in enumerate(CHUNKS):
        rows = pl.ds(lo, n)
        e4[i].wait_recv()
        gr_c.append(send(gr.at[0, 1, rows], gr.at[1, 1, rows], c_mate))
        feed_back(1, lo, n)
        es[2, lo : lo + n, :] = expanded_back(1, lo, n).astype(BF16)
        e5.append(send(es.at[2, rows], er.at[2, rows], y_mate))
    gb_copy = send(gb.at[1], gbr, c_mate)
    mid[...] = expanded_back(0, 0, ROWS)
    for copy in gr_c:
        copy.wait_recv()
    hid_copy.wait_recv()
    weight_grad(2, gr, hid.at[0], hidr, D, 0)
    scatter_x(2)

    e6 = []
    gm_c = []
    gain_part = jnp.zeros((1, D), F32)
    shift_part = jnp.zeros((1, D), F32)
    bias_part = jnp.zeros((1, D), F32)
    for i, (lo, n) in enumerate(CHUNKS):
        rows = pl.ds(lo, n)
        e5[i].wait_recv()
        grad = mid[lo : lo + n, :] + er[2, lo : lo + n, :].astype(F32)
        unit = unit2[lo : lo + n, :]
        gain_part = gain_part + column_sum(grad * unit)
        shift_part = shift_part + column_sum(grad)
        grad = acc[lo : lo + n, :] + normalize_back(grad, unit, inv2[lo : lo + n, :], gain2)
        acc[lo : lo + n, :] = grad
        gm[0, 0, lo : lo + n, :] = grad.astype(BF16)
        e6.append(send(gm.at[0, 0, rows], gm.at[0, 1, rows], y_mate))
        gm_c.append(send(gm.at[0, 0, rows], gm.at[1, 0, rows], c_mate))
        bias_part = bias_part + column_sum(grad)
    sb[0, 1:2, :] = gain_part
    sb[0, 2:3, :] = shift_part
    sb[0, 3:4, :] = bias_part

    bo_y = send(block_out.at[t], block_out.at[t], y_mate)
    bo_c = [send(block_out.at[t], block_out.at[t], c_mate)]
    gb_copy.wait_recv()
    for copy in n2_c:
        copy.wait_recv()
    weight_grad(1, n2, gb.at[0], gbr, D, 0)
    ones = jnp.ones((8, 2 * ROWS), BF16)
    sb[0, 8:9, :] = (dot_nn(ones, rows_of(gb.at[0], D)) + dot_nn(ones, rows_of(gbr, D)))[0:1]
    scatter_x(1)
    scatter_z(2)

    def mixed_back(w, lo, n):
        for j in range(2):
            grad = dot_nn(gm[0, w, lo : lo + n, :], wa[j, :, :, 512:768].reshape(D, 256))
            gmx[j, w, lo : lo + n, :] = grad.astype(BF16)

    def attend_back(w):
        def body(j, carry):
            grads_q = []
            grads_k = []
            grads_v = []
            for h in range(3):
                query, key, value = unit_of(w, j, h)
                p, pv = UNITS[h][3:]
                grad = gmx[j, w, :, 0:128] if h == 2 else gmx[j, w, :, 128:256]
                soft = ps[w, j, h]
                grad_soft = dot_nt(grad, value)
                delta = jnp.sum(soft * grad_soft, axis=-1, keepdims=True)
                grad_scores = (soft * (grad_soft - delta)).astype(BF16)
                grads_v.append(dot_tn(soft.astype(BF16), grad * half[pv])[0:ROWS])
                grads_k.append(dot_tn(grad_scores, query * key_mask[p])[0:ROWS])
                part = (dot_nt(grad_scores, pick[...]) * place[...]).astype(BF16)
                grads_q.append(dot_nn(grad_scores, key) + dot_nn(part, t2[p]))
                tg[...] += dot_tn(query * half[p], part)
            gp[j, w, :, 0:128] = (grads_q[0] + grads_q[1]).astype(BF16)
            gp[j, w, :, 128:256] = (grads_k[0] + grads_k[1]).astype(BF16)
            gp[j, w, :, 256:384] = (grads_v[0] + grads_v[1]).astype(BF16)
            gp[j, w, :, 384:512] = (grads_q[2] + pltpu.roll(grads_k[2], 64, 1)).astype(BF16)
            gp[j, w, :, 512:640] = pltpu.roll(grads_v[2], 64, 1).astype(BF16)
            return carry

        lax.fori_loop(0, 2, body, 0)

    def projected_back(w, lo, n):
        return dot_nt(gp[0, w, lo : lo + n, :], wa[0, :, :, 0:640].reshape(D, 640)) + dot_nt(
            gp[1, w, lo : lo + n, :], wa[1, :, :, 0:640].reshape(D, 640)
        )

    for i, (lo, n) in enumerate(CHUNKS):
        rows = pl.ds(lo, n)
        e6[i].wait_recv()
        gm_c.append(send(gm.at[0, 1, rows], gm.at[1, 1, rows], c_mate))
        mixed_back(1, lo, n)
    attend_back(1)
    e7 = []
    for lo, n in CHUNKS:
        rows = pl.ds(lo, n)
        es[3, lo : lo + n, :] = projected_back(1, lo, n).astype(BF16)
        e7.append(send(es.at[3, rows], er.at[3, rows], y_mate))
    scatter_z(1)
    mixed_back(0, 0, ROWS)
    attend_back(0)
    gp_copy = send(gp.at[1], gpr, c_mate)
    mid[...] = projected_back(0, 0, ROWS)
    for copy in gm_c:
        copy.wait_recv()
    mx_copy.wait_recv()
    n1_copy.wait_recv()
    gp_copy.wait_recv()
    weight_grad(0, n1, gp.at[0], gpr, 640, 0)
    value = dot_tn(rows_of(gm.at[0], D), rows_of(mx.at[0], 256)) + dot_tn(
        rows_of(gm.at[1], D), rows_of(mxr, 256)
    )
    value = value.reshape(8, 96, 256)
    gw[0, :, :, 512:640] += value[:, :, 0:128]
    gw[0, :, :, 640:768] = value[:, :, 128:256]
    scatter_x(0)
    sb[0, 9:10, 0:640] = (dot_nn(ones, rows_of(gp.at[0], 640)) + dot_nn(ones, rows_of(gpr, 640)))[
        0:1
    ]

    e8 = []
    ig_c = []
    gain_part = jnp.zeros((1, D), F32)
    shift_part = jnp.zeros((1, D), F32)
    for i, (lo, n) in enumerate(CHUNKS):
        rows = pl.ds(lo, n)
        e7[i].wait_recv()
        grad = mid[lo : lo + n, :] + er[3, lo : lo + n, :].astype(F32)
        unit = unit1[lo : lo + n, :]
        gain_part = gain_part + column_sum(grad * unit)
        shift_part = shift_part + column_sum(grad)
        grad = acc[lo : lo + n, :] + normalize_back(grad, unit, inv1[lo : lo + n, :], gain1)
        grad_out[t, lo : lo + n, :] = grad.astype(BF16)
        e8.append(send(grad_out.at[t, rows], grad_out.at[t, rows], y_mate))
        ig_c.append(send(grad_out.at[t, rows], grad_out.at[t, rows], c_mate))
    sb[0, 4:5, :] = gain_part
    sb[0, 5:6, :] = shift_part

    spread = tg[...]
    spread_high = spread.astype(BF16)
    spread_low = (spread - spread_high.astype(F32)).astype(BF16)
    table = dot_nn(spread_high, onehot[...]) + dot_nn(spread_low, onehot[...])
    tb[0] = table[0:64] + table[64:128]
    s_c = send(sb.at[0, pl.ds(0, 8)], sbr.at[0, pl.ds(0, 8)], c_mate)
    t_c = send(tb.at[0], tbr.at[0], c_mate)
    s_c.wait_recv()
    t_c.wait_recv()
    sb[1] = sb[0]
    sb[1, 0:8, :] = sb[0, 0:8, :] + sbr[0, 0:8, :]
    tb[1] = tb[0] + tbr[0]
    s_y = send(sb.at[1, pl.ds(0, 8)], sbr.at[1, pl.ds(0, 8)], y_mate)
    t_y = send(tb.at[1], tbr.at[1], y_mate)
    s_y.wait_recv()
    t_y.wait_recv()
    sb[2] = sb[1]
    sb[2, 0:8, :] = sb[1, 0:8, :] + sbr[1, 0:8, :]
    tb[2] = tb[1] + tbr[1]
    s_x = send(sb.at[2], sbr.at[2], x_mate)
    t_x = send(tb.at[2], tbr.at[2], x_mate)
    scatter_z(0)
    s_x.wait_recv()
    t_x.wait_recv()
    sb[3] = sb[2] + sbr[2]
    tb[3] = tb[2] + tbr[2]
    s_z = [send(sb.at[3], sbr.at[2 + k], z_mates[k - 1]) for k in (1, 2, 3)]
    t_z = [send(tb.at[3], tbr.at[2 + k], z_mates[k - 1]) for k in (1, 2, 3)]

    bo_y.wait_recv()
    bo_c.append(send(block_out.at[peer_window], block_out.at[peer_window], c_mate))
    for i, (lo, n) in enumerate(CHUNKS):
        rows = pl.ds(lo, n)
        e8[i].wait_recv()
        ig_c.append(send(grad_out.at[peer_window, rows], grad_out.at[peer_window, rows], c_mate))
    scatter_end(2, gs_out)
    scatter_end(1, ge_out)
    scatter_end(0, ga_out)
    for copy in s_z + t_z:
        copy.wait_recv()
    total = (sb[3] + sbr[3]) + (sbr[4] + sbr[5])
    small_out[...] = total
    small_out[6:7, :] = jnp.broadcast_to(
        jnp.sum(total[6:7, :], axis=1, keepdims=True) / (count * float(D)), (1, D)
    )
    table_out[...] = ((tb[3] + tbr[3]) + (tbr[4] + tbr[5])).T
    for copy in bo_c + ig_c:
        copy.wait_recv()
    for copy in started:
        copy.wait_send()


def constant_tables():
    onehot = np.zeros((512, 64), np.float32)
    place = np.zeros((ROWS, 512), np.float32)
    pick = np.zeros((512, KEYS), np.float32)
    for first in range(WIN):
        for second in range(WIN):
            at = first * WIN + second
            onehot[at, first - second + WIN - 1] = 1.0
            onehot[256 + at, 27 + first - second + WIN - 1] = 1.0
            for other in range(WIN):
                place[first * WIN + other, at] = 1.0
                place[other * WIN + first, 256 + at] = 1.0
                pick[at, second * WIN + other] = 1.0
                pick[256 + at, other * WIN + second] = 1.0
    return onehot, place, pick


def fused(
    inputs,
    target,
    valid,
    first_gain,
    first_shift,
    triple_weight,
    query_value_bias,
    output_weight,
    output_bias,
    second_gain,
    second_shift,
    expand_weight,
    expand_bias,
    shrink_weight,
    shrink_bias,
    rows_table,
    columns_table,
):
    onehot, place, pick = constant_tables()
    vectors = jnp.stack(
        [
            first_gain,
            first_shift,
            output_bias,
            second_gain,
            second_shift,
            shrink_bias,
            first_gain,
            first_gain,
        ]
    )
    q_bias, v_bias = query_value_bias[0], query_value_bias[1]
    none = jnp.zeros((128,), F32)
    bias_row = jnp.concatenate(
        [q_bias[:128], none, v_bias[:128], q_bias[128:], none[:64], v_bias[128:], none[:64], none]
    )
    side = jnp.concatenate([jnp.stack([expand_bias, bias_row]), jnp.zeros((6, D), F32)])
    out_t = output_weight.T
    q_w, k_w, v_w = triple_weight[0], triple_weight[1], triple_weight[2]
    attention = jnp.concatenate(
        [
            q_w[:, :128],
            k_w[:, :128],
            v_w[:, :128],
            q_w[:, 128:],
            k_w[:, 128:],
            v_w[:, 128:],
            out_t[:, 128:],
            out_t[:, :128],
        ],
        axis=1,
    )
    table = jnp.concatenate([rows_table, columns_table, jnp.zeros((10, HEAD), F32)]).astype(BF16)
    blank = jnp.zeros_like(table)
    tables = jnp.stack(
        [jnp.concatenate([table, blank], axis=1), jnp.concatenate([blank, table], axis=1)]
    )
    vmem = pl.BlockSpec(memory_space=pltpu.VMEM)
    big = jax.ShapeDtypeStruct((4, ROWS, D), BF16)
    part = jax.ShapeDtypeStruct((96, D), F32)
    copies = 224
    block, grad, ga, ge, gs, small, table_grad = pl.pallas_call(
        block_kernel,
        out_shape=[
            big,
            big,
            part,
            part,
            part,
            jax.ShapeDtypeStruct((16, D), F32),
            jax.ShapeDtypeStruct((64, 64), F32),
        ],
        in_specs=[vmem] * 12,
        out_specs=[vmem] * 7,
        scratch_shapes=[
            pltpu.VMEM((2, 8, 96, D), BF16),
            pltpu.VMEM((2, 8, 96, D), BF16),
            pltpu.VMEM((2, 8, 96, D), BF16),
            pltpu.VMEM((2, 8, D), F32),
            pltpu.VMEM((2, ROWS, D), F32),
            pltpu.VMEM((ROWS, D), F32),
            pltpu.VMEM((ROWS, D), F32),
            pltpu.VMEM((ROWS, 1), F32),
            pltpu.VMEM((ROWS, 1), F32),
            pltpu.VMEM((ROWS, D), F32),
            pltpu.VMEM((ROWS, D), F32),
            pltpu.VMEM((2, 2, ROWS, D), BF16),
            pltpu.VMEM((2, 2, ROWS, D), BF16),
            pltpu.VMEM((2, 2, ROWS, D), BF16),
            pltpu.VMEM((2, 2, ROWS, D), BF16),
            pltpu.VMEM((2, 2, KEYS, 896), BF16),
            pltpu.VMEM((2, 2, 3, ROWS, KEYS), F32),
            pltpu.VMEM((2, 2, ROWS, 256), BF16),
            pltpu.VMEM((2, ROWS, 256), BF16),
            pltpu.VMEM((2, 2, ROWS, D), BF16),
            pltpu.VMEM((2, ROWS, D), BF16),
            pltpu.VMEM((2, 2, ROWS, D), F32),
            pltpu.VMEM((2, 2, ROWS, D), BF16),
            pltpu.VMEM((2, ROWS, D), BF16),
            pltpu.VMEM((2, 2, ROWS, 256), BF16),
            pltpu.VMEM((2, 2, ROWS, 640), BF16),
            pltpu.VMEM((2, ROWS, 640), BF16),
            pltpu.VMEM((2, 512, 128), BF16),
            pltpu.VMEM((128, 512), F32),
            pltpu.VMEM((4, ROWS, D), BF16),
            pltpu.VMEM((4, ROWS, D), BF16),
            pltpu.VMEM((3, 8, 96, D), F32),
            pltpu.VMEM((3, 4, 96, D), BF16),
            pltpu.VMEM((3, 4, 96, D), BF16),
            pltpu.VMEM((3, 3, 96, D), BF16),
            pltpu.VMEM((3, 3, 96, D), BF16),
            pltpu.VMEM((8, 128), F32),
            pltpu.VMEM((2, 8, 128), F32),
            pltpu.VMEM((4, 8, 128), F32),
            pltpu.VMEM((4, 16, D), F32),
            pltpu.VMEM((6, 16, D), F32),
            pltpu.VMEM((4, 64, 64), F32),
            pltpu.VMEM((6, 64, 64), F32),
            pltpu.SemaphoreType.DMA((copies,)),
            pltpu.SemaphoreType.DMA((copies,)),
        ],
        compiler_params=pltpu.CompilerParams(
            collective_id=0, has_side_effects=True, vmem_limit_bytes=60 << 20
        ),
    )(
        inputs,
        target,
        valid,
        vectors,
        side,
        attention,
        expand_weight,
        shrink_weight.T,
        tables,
        jnp.asarray(onehot, BF16),
        jnp.asarray(place, F32),
        jnp.asarray(pick, BF16),
    )
    triple_grad = jnp.stack(
        [
            jnp.concatenate([ga[:, 0:128], ga[:, 384:448]], axis=1),
            jnp.concatenate([ga[:, 128:256], ga[:, 448:512]], axis=1),
            jnp.concatenate([ga[:, 256:384], ga[:, 512:576]], axis=1),
        ]
    )
    output_grad = jnp.concatenate([ga[:, 640:768], ga[:, 576:640]], axis=1).T
    bias_grad = small[9]
    query_value_grad = jnp.stack(
        [
            jnp.concatenate([bias_grad[0:128], bias_grad[384:448]]),
            jnp.concatenate([bias_grad[256:384], bias_grad[512:576]]),
        ]
    )
    return (
        block[:, :WIN_TOK],
        small[6, 0],
        grad[:, :WIN_TOK].astype(F32),
        small[4],
        small[5],
        triple_grad,
        query_value_grad,
        output_grad,
        small[3],
        small[1],
        small[2],
        ge,
        small[8],
        gs.T,
        small[0],
        table_grad[0:27],
        table_grad[27:54],
    )


def solution(mesh):
    placed = (
        P("dp", None, None),
        P("dp", None, None),
        P("dp", None),
        P(),
        P(),
        P(None, "dp", "tensor"),
        P(None, "tensor"),
        P("tensor", "dp"),
        P(),
        P(),
        P(),
        P("dp", "tensor"),
        P("tensor"),
        P("tensor", "dp"),
        P(),
        P(),
        P(),
    )
    on_slice = mesh.shape["dp"] == 8 and mesh.shape["tensor"] == 4
    return jax.shard_map(
        fused if on_slice else shards,
        mesh=mesh,
        in_specs=placed,
        out_specs=(
            P("dp", None, None),
            P(),
            P("dp", None, None),
            P(),
            P(),
            P(None, "dp", "tensor"),
            P(None, "tensor"),
            P("tensor", "dp"),
            P(),
            P(),
            P(),
            P("dp", "tensor"),
            P("tensor"),
            P("tensor", "dp"),
            P(),
            P(),
            P(),
        ),
        check_vma=False,
    )
```

```python
import math

import jax
import jax.numpy as jnp
import numpy as np
from jax import lax
from jax.experimental import pallas as pl
from jax.experimental.pallas import tpu as pltpu
from jax.sharding import PartitionSpec as P

MESH = pl.DeviceIdType.MESH

D = 768
HEADS = 12
HEAD = 64
WIN = 14
WIN_TOK = 196
MICRO = 2


def normalize(values):
    center = jnp.mean(values, axis=-1, keepdims=True)
    centered = values - center
    spread = jnp.mean(centered * centered, axis=-1, keepdims=True)
    inverse = lax.rsqrt(spread + 1e-06)
    return (centered * inverse, inverse)


def normalize_back(grad_out, unit, inverse, gain):
    scaled = grad_out * gain
    mean_one = jnp.mean(scaled, axis=-1, keepdims=True)
    mean_two = jnp.mean(scaled * unit, axis=-1, keepdims=True)
    return inverse * (scaled - mean_one - unit * mean_two)


def position_select(side):
    shape = (side, side, 2 * side - 1)
    first = lax.broadcasted_iota(jnp.int32, shape, 0)
    second = lax.broadcasted_iota(jnp.int32, shape, 1)
    slots = lax.broadcasted_iota(jnp.int32, shape, 2)
    return (slots == first - second + side - 1).astype(jnp.bfloat16)


def score_block(queries, keys, table_rows, table_cols, scale_factor):
    groups = queries.shape[0]
    side = queries.shape[1]
    heads = queries.shape[3]
    along_rows = jnp.einsum(
        "gabnc,aec->gnabe", queries, table_rows, preferred_element_type=jnp.float32
    )
    along_cols = jnp.einsum(
        "gabnc,bfc->gnabf", queries, table_cols, preferred_element_type=jnp.float32
    )
    scores = (
        jnp.einsum("gabnc,gefnc->gnabef", queries, keys, preferred_element_type=jnp.float32)
        * scale_factor
    )
    scores = scores + along_rows[..., :, None] + along_cols[..., None, :]
    return scores.reshape(groups, heads, side * side, side * side)


def gelu_exact(inner):
    return jax.nn.gelu(inner, approximate=False)


def row_total(partial_value):
    return lax.psum(partial_value, "tensor")


def share_of(values):
    share_rows = values.shape[0] // lax.axis_size("tensor")
    return lax.dynamic_slice_in_dim(values, lax.axis_index("tensor") * share_rows, share_rows, 0)


def shards(
    inputs,
    target,
    valid,
    first_gain,
    first_shift,
    triple_weight,
    query_value_bias,
    output_weight,
    output_bias,
    second_gain,
    second_shift,
    expand_weight,
    expand_bias,
    shrink_weight,
    shrink_bias,
    rows_table,
    columns_table,
):
    local_heads = HEADS // lax.axis_size("tensor")
    local_width = local_heads * HEAD
    local_windows = inputs.shape[0]
    win_micro = local_windows // MICRO
    micro_rows = win_micro * WIN_TOK
    scale_factor = 1.0 / math.sqrt(HEAD)
    highest = lax.Precision.HIGHEST
    live = valid.astype(jnp.float32)
    select = position_select(WIN)
    table_rows = jnp.einsum(
        "aej,jc->aec", select, rows_table.astype(jnp.bfloat16), preferred_element_type=jnp.float32
    ).astype(jnp.bfloat16)
    table_cols = jnp.einsum(
        "aej,jc->aec",
        select,
        columns_table.astype(jnp.bfloat16),
        preferred_element_type=jnp.float32,
    ).astype(jnp.bfloat16)
    rows_float = table_rows.astype(jnp.float32)
    cols_float = table_cols.astype(jnp.float32)
    triple_bias = jnp.stack(
        [query_value_bias[0], jnp.zeros_like(query_value_bias[0]), query_value_bias[1]]
    )
    saved = []
    outputs = []
    local_loss = jnp.zeros((), jnp.float32)
    for micro in range(MICRO):
        gathered = (
            lax.all_gather(triple_weight, "dp", axis=1, tiled=True),
            lax.all_gather(output_weight, "dp", axis=1, tiled=True),
            lax.all_gather(expand_weight, "dp", axis=0, tiled=True),
            lax.all_gather(shrink_weight, "dp", axis=1, tiled=True),
        )
        full_triple, full_output, full_expand, full_shrink = gathered
        lower = micro * win_micro
        flat_rows = inputs[lower : lower + win_micro].reshape(micro_rows, D).astype(jnp.float32)
        unit_one, inverse_one = normalize(flat_rows)
        normed = (unit_one * first_gain + first_shift).astype(jnp.bfloat16)
        projected = (
            jnp.einsum("rd,tde->rte", normed, full_triple, preferred_element_type=jnp.float32)
            + triple_bias
        )
        projected = projected.astype(jnp.bfloat16)
        split = projected.reshape(win_micro, WIN, WIN, 3, local_heads, HEAD)
        queries = split[:, :, :, 0]
        keys = split[:, :, :, 1]
        values = split[:, :, :, 2].reshape(win_micro, WIN_TOK, local_heads, HEAD)
        scores = score_block(queries, keys, table_rows, table_cols, scale_factor)
        peak = jnp.max(scores, axis=-1, keepdims=True)
        raised = jnp.exp(scores - peak)
        denominator = jnp.sum(raised, axis=-1, keepdims=True)
        log_total = peak + jnp.log(denominator)
        softmaxed = (raised / denominator).astype(jnp.bfloat16)
        mixed = jnp.einsum("gnqk,gknc->gqnc", softmaxed, values, preferred_element_type=jnp.float32)
        mixed = mixed.reshape(micro_rows, local_width).astype(jnp.bfloat16)
        partial_attended = jnp.dot(mixed, full_output, preferred_element_type=jnp.float32)
        middle = flat_rows + (row_total(partial_attended) + output_bias)
        unit_two, inverse_two = normalize(middle)
        normed_two = (unit_two * second_gain + second_shift).astype(jnp.bfloat16)
        before = jnp.dot(normed_two, full_expand, preferred_element_type=jnp.float32) + expand_bias
        hidden = gelu_exact(before).astype(jnp.bfloat16)
        partial_shrunk = jnp.dot(hidden, full_shrink, preferred_element_type=jnp.float32)
        result = middle + (row_total(partial_shrunk) + shrink_bias)
        aim = target[lower : lower + win_micro].reshape(micro_rows, D).astype(jnp.float32)
        marks = live[lower : lower + win_micro].reshape(micro_rows, 1)
        weighted_gap = marks * (result - aim)
        local_loss = local_loss + jnp.sum(weighted_gap * (result - aim))
        outputs.append(result.astype(jnp.bfloat16).reshape(win_micro, WIN_TOK, D))
        saved.append(
            (
                unit_one,
                inverse_one,
                normed,
                projected,
                log_total,
                mixed,
                unit_two,
                inverse_two,
                normed_two,
                before,
                hidden,
                weighted_gap,
            )
        )
    loss_total, count = lax.psum((local_loss, jnp.sum(live)), "dp")
    loss = loss_total / (count * D)
    grad_scale = local_windows * WIN_TOK * lax.axis_size("dp") / count
    triple_acc = jnp.zeros((3, D, local_width), jnp.float32)
    output_acc = jnp.zeros((local_width, D), jnp.float32)
    expand_acc = jnp.zeros((D, full_expand.shape[1]), jnp.float32)
    shrink_acc = jnp.zeros((full_shrink.shape[0], D), jnp.float32)
    first_gain_acc = jnp.zeros((D,), jnp.float32)
    first_shift_acc = jnp.zeros((D,), jnp.float32)
    second_gain_acc = jnp.zeros((D,), jnp.float32)
    second_shift_acc = jnp.zeros((D,), jnp.float32)
    output_bias_acc = jnp.zeros((D,), jnp.float32)
    shrink_bias_acc = jnp.zeros((D,), jnp.float32)
    expand_bias_acc = jnp.zeros((full_expand.shape[1],), jnp.float32)
    query_value_acc = jnp.zeros((2, local_width), jnp.float32)
    rows_expanded_acc = jnp.zeros((WIN, WIN, HEAD), jnp.float32)
    cols_expanded_acc = jnp.zeros((WIN, WIN, HEAD), jnp.float32)
    input_grads = []
    for micro in range(MICRO):
        gathered = (
            lax.all_gather(triple_weight, "dp", axis=1, tiled=True),
            lax.all_gather(output_weight, "dp", axis=1, tiled=True),
            lax.all_gather(expand_weight, "dp", axis=0, tiled=True),
            lax.all_gather(shrink_weight, "dp", axis=1, tiled=True),
        )
        full_triple, full_output, full_expand, full_shrink = gathered
        (
            unit_one,
            inverse_one,
            normed,
            projected,
            log_total,
            mixed,
            unit_two,
            inverse_two,
            normed_two,
            before,
            hidden,
            weighted_gap,
        ) = saved[micro]
        grad_result = grad_scale * weighted_gap
        shrink_bias_acc = shrink_bias_acc + jnp.sum(share_of(grad_result), axis=0)
        grad_result_low = grad_result.astype(jnp.bfloat16)
        shrink_acc = shrink_acc + jnp.einsum(
            "rf,rd->fd", hidden, grad_result_low, preferred_element_type=jnp.float32
        )
        grad_hidden = jnp.einsum(
            "rd,fd->rf", grad_result_low, full_shrink, preferred_element_type=jnp.float32
        )
        unused, gelu_pull = jax.vjp(gelu_exact, before)
        grad_before = gelu_pull(grad_hidden)[0].astype(jnp.bfloat16)
        expand_bias_acc = expand_bias_acc + jnp.sum(grad_before.astype(jnp.float32), axis=0)
        expand_acc = expand_acc + jnp.einsum(
            "rd,rf->df", normed_two, grad_before, preferred_element_type=jnp.float32
        )
        partial_two = jnp.einsum(
            "rf,df->rd", grad_before, full_expand, preferred_element_type=jnp.float32
        )
        grad_normed_two = row_total(partial_two)
        grad_middle = grad_result + normalize_back(
            grad_normed_two, unit_two, inverse_two, second_gain
        )
        second_gain_acc = second_gain_acc + jnp.sum(share_of(grad_normed_two * unit_two), axis=0)
        second_shift_acc = second_shift_acc + jnp.sum(share_of(grad_normed_two), axis=0)
        output_bias_acc = output_bias_acc + jnp.sum(share_of(grad_middle), axis=0)
        grad_middle_low = grad_middle.astype(jnp.bfloat16)
        output_acc = output_acc + jnp.einsum(
            "rc,rd->cd", mixed, grad_middle_low, preferred_element_type=jnp.float32
        )
        grad_mixed = jnp.einsum(
            "rd,cd->rc", grad_middle_low, full_output, preferred_element_type=jnp.float32
        )
        grad_mixed = grad_mixed.astype(jnp.bfloat16).reshape(win_micro, WIN_TOK, local_heads, HEAD)
        split = projected.reshape(win_micro, WIN, WIN, 3, local_heads, HEAD)
        queries = split[:, :, :, 0]
        keys = split[:, :, :, 1]
        queries_flat = queries.reshape(win_micro, WIN_TOK, local_heads, HEAD)
        keys_flat = keys.reshape(win_micro, WIN_TOK, local_heads, HEAD)
        values = split[:, :, :, 2].reshape(win_micro, WIN_TOK, local_heads, HEAD)
        scores = score_block(queries, keys, table_rows, table_cols, scale_factor)
        softmax_exact = jnp.exp(scores - log_total)
        grad_soft = jnp.einsum(
            "gqnc,gknc->gnqk", grad_mixed, values, preferred_element_type=jnp.float32
        )
        delta = jnp.sum(softmax_exact * grad_soft, axis=-1, keepdims=True)
        grad_scores = (softmax_exact * (grad_soft - delta)).astype(jnp.bfloat16)
        grad_values = jnp.einsum(
            "gnqk,gqnc->gknc",
            softmax_exact.astype(jnp.bfloat16),
            grad_mixed,
            preferred_element_type=jnp.float32,
        )
        grad_keys = (
            jnp.einsum(
                "gnqk,gqnc->gknc", grad_scores, queries_flat, preferred_element_type=jnp.float32
            )
            * scale_factor
        )
        grad_queries = (
            jnp.einsum(
                "gnqk,gknc->gqnc", grad_scores, keys_flat, preferred_element_type=jnp.float32
            )
            * scale_factor
        )
        grad_grid = grad_scores.astype(jnp.float32).reshape(
            win_micro, local_heads, WIN, WIN, WIN, WIN
        )
        row_part = jnp.sum(grad_grid, axis=5)
        col_part = jnp.sum(grad_grid, axis=4)
        queries_float = queries.astype(jnp.float32)
        rel_queries = jnp.einsum("gnabe,aec->gabnc", row_part, rows_float, precision=highest)
        rel_queries = rel_queries + jnp.einsum(
            "gnabf,bfc->gabnc", col_part, cols_float, precision=highest
        )
        grad_queries = grad_queries + rel_queries.reshape(win_micro, WIN_TOK, local_heads, HEAD)
        rows_expanded_acc = rows_expanded_acc + jnp.einsum(
            "gnabe,gabnc->aec", row_part, queries_float, precision=highest
        )
        cols_expanded_acc = cols_expanded_acc + jnp.einsum(
            "gnabf,gabnc->bfc", col_part, queries_float, precision=highest
        )
        grad_projected = jnp.stack(
            [
                grad_queries.reshape(micro_rows, local_width),
                grad_keys.reshape(micro_rows, local_width),
                grad_values.reshape(micro_rows, local_width),
            ],
            axis=1,
        ).astype(jnp.bfloat16)
        projected_float_sums = jnp.sum(grad_projected.astype(jnp.float32), axis=0)
        query_value_acc = query_value_acc + jnp.stack(
            [projected_float_sums[0], projected_float_sums[2]]
        )
        triple_acc = triple_acc + jnp.einsum(
            "rd,rte->tde", normed, grad_projected, preferred_element_type=jnp.float32
        )
        partial_one = jnp.einsum(
            "rte,tde->rd", grad_projected, full_triple, preferred_element_type=jnp.float32
        )
        grad_normed = row_total(partial_one)
        grad_tokens = grad_middle + normalize_back(grad_normed, unit_one, inverse_one, first_gain)
        first_gain_acc = first_gain_acc + jnp.sum(share_of(grad_normed * unit_one), axis=0)
        first_shift_acc = first_shift_acc + jnp.sum(share_of(grad_normed), axis=0)
        input_grads.append(grad_tokens.reshape(win_micro, WIN_TOK, D))
    select_float = select.astype(jnp.float32)
    rows_table_part = jnp.einsum("aej,aec->jc", select_float, rows_expanded_acc, precision=highest)
    cols_table_part = jnp.einsum("aej,aec->jc", select_float, cols_expanded_acc, precision=highest)
    triple_grad, output_grad, expand_grad, shrink_grad = (
        lax.psum_scatter(triple_acc, "dp", scatter_dimension=1, tiled=True),
        lax.psum_scatter(output_acc, "dp", scatter_dimension=1, tiled=True),
        lax.psum_scatter(expand_acc, "dp", scatter_dimension=0, tiled=True),
        lax.psum_scatter(shrink_acc, "dp", scatter_dimension=1, tiled=True),
    )
    over_heads = lax.psum(
        (
            rows_table_part,
            cols_table_part,
            first_gain_acc,
            first_shift_acc,
            output_bias_acc,
            second_gain_acc,
            second_shift_acc,
            shrink_bias_acc,
        ),
        "tensor",
    )
    summed_small = lax.psum(
        (
            over_heads[0],
            over_heads[1],
            over_heads[2],
            over_heads[3],
            over_heads[4],
            over_heads[5],
            over_heads[6],
            over_heads[7],
            query_value_acc,
            expand_bias_acc,
        ),
        "dp",
    )
    return (
        jnp.concatenate(outputs, axis=0),
        loss,
        jnp.concatenate(input_grads, axis=0),
        summed_small[2],
        summed_small[3],
        triple_grad,
        summed_small[8],
        output_grad,
        summed_small[4],
        summed_small[5],
        summed_small[6],
        expand_grad,
        summed_small[9],
        shrink_grad,
        summed_small[7],
        summed_small[0],
        summed_small[1],
    )


ROWS = 208
KEYS = 256
CHUNKS = ((0, 112), (112, 96))
F32 = jnp.float32
BF16 = jnp.bfloat16


def z_mate(z, k):
    if k == 0:
        return z
    if k == 1:
        return z + 1 - 2 * (z % 2)
    if k == 2:
        return (z + 2) % 4
    return 3 - z


def dot_nn(a, b):
    return lax.dot_general(a, b, (((1,), (0,)), ((), ())), preferred_element_type=F32)


def dot_nt(a, b):
    return lax.dot_general(a, b, (((1,), (1,)), ((), ())), preferred_element_type=F32)


def dot_tn(a, b):
    return lax.dot_general(a, b, (((0,), (0,)), ((), ())), preferred_element_type=F32)


def column_sum(values):
    return jnp.sum(values, axis=0, keepdims=True)


UNITS = ((0, 1, 2, 0, 0), (0, 1, 2, 1, 1), (3, 5, 6, 0, 1))


def block_kernel(
    x_in,
    target_in,
    valid_in,
    gain1_in,
    shift1_in,
    triple_in,
    qv_bias_in,
    out_w_in,
    bias_out_in,
    gain2_in,
    shift2_in,
    we_in,
    expand_bias_in,
    ws_in,
    bias_shrink_in,
    rows_in,
    columns_in,
    onehot_in,
    place_in,
    pick_in,
    block_out,
    grad_out,
    ga_out,
    ge_out,
    gs_out,
    small_out,
    table_out,
    wa_in,
    wa,
    we,
    ws,
    xt,
    tt,
    onehot,
    place,
    pick,
    tabs,
    bo,
    ig,
    mix,
    bo_low,
    ga,
    ge,
    gs,
    side,
    xf,
    unit1,
    unit2,
    inv1,
    inv2,
    mid,
    acc,
    n1,
    n2,
    gr,
    gm,
    pj,
    ps,
    mx,
    mxr,
    hid,
    hidr,
    slope,
    gb,
    gbr,
    gmx,
    gp,
    gpr,
    t2,
    tg,
    es,
    er,
    gw,
    xs,
    xr,
    zs,
    zr,
    cnt,
    cntr,
    sb,
    sbr,
    tb,
    tbr,
    load_sem,
    send_sem,
    recv_sem,
):
    dp = lax.axis_index("dp")
    t = lax.axis_index("tensor")
    z = dp // 2
    x = dp % 2
    y = t // 2
    c = t % 2
    z_mates = [(z_mate(z, k) * 2 + x, t) for k in (1, 2, 3)]
    x_mate = (z * 2 + 1 - x, t)
    y_mate = (dp, (1 - y) * 2 + c)
    c_mate = (dp, y * 2 + 1 - c)
    peer_window = (1 - y) * 2 + c
    token_total = lax.axis_size("dp") * 4 * WIN_TOK

    started = []

    def send(src, dst, mate):
        i = len(started)
        copy = pltpu.make_async_remote_copy(
            src_ref=src,
            dst_ref=dst,
            send_sem=send_sem.at[i],
            recv_sem=recv_sem.at[i],
            device_id=mate,
            device_id_type=MESH,
        )
        copy.start()
        started.append(copy)
        return copy

    loads = []

    def load(src, dst):
        copy = pltpu.make_async_copy(src, dst, load_sem.at[len(loads)])
        copy.start()
        loads.append(copy)
        return copy

    x_load = load(x_in, xt)
    onehot_load = load(onehot_in, onehot)
    place_load = load(place_in, place)
    pick_load = load(pick_in, pick)
    target_load = load(target_in, tt)
    barrier = pltpu.get_barrier_semaphore()
    for mate in z_mates + [x_mate, y_mate, c_mate]:
        pl.semaphore_signal(barrier, inc=1, device_id=mate, device_id_type=MESH)
    pl.semaphore_wait(barrier, 6)

    w_in = (wa_in, we_in, ws_in)
    w_full = (wa, we, ws)
    from_z = {}
    from_x = {}
    from_c = {}

    def row_of(k, xx):
        return z_mate(z, k) * 2 + xx

    def gather_start(g):
        for k in (1, 2, 3):
            from_z[g, k] = send(w_in[g], w_full[g].at[0, dp], z_mates[k - 1])
        from_x[g, 0] = send(w_in[g], w_full[g].at[0, dp], x_mate)
        from_c[g, 0] = send(w_in[g], w_full[g].at[1, dp], c_mate)
        w_full[g][0, dp] = w_in[g][...]

    def gather_z(g, k):
        from_z[g, k].wait_recv()
        block = w_full[g].at[0, row_of(k, x)]
        from_x[g, k] = send(block, block, x_mate)
        from_c[g, k] = send(block, w_full[g].at[1, row_of(k, x)], c_mate)

    def gather_x(g, k):
        from_x[g, k].wait_recv()
        from_c[g, 4 + k] = send(
            w_full[g].at[0, row_of(k, 1 - x)], w_full[g].at[1, row_of(k, 1 - x)], c_mate
        )

    def gather_end(g):
        for k in range(8):
            from_c[g, k].wait_recv()

    for i in range(3):
        wa_in[:, 128 * i : 128 * i + 128] = triple_in[i, :, 0:128]
    source = lax.broadcasted_iota(jnp.int32, (192, 256), 0)
    column = lax.broadcasted_iota(jnp.int32, (192, 256), 1)
    tail = sum(
        dot_nn(
            triple_in[i],
            ((source >= 128) & (source - 128 == column - 64 * i)).astype(F32).astype(BF16),
        )
        for i in range(3)
    )
    out_w = out_w_in[...]
    tail = tail + dot_tn(
        out_w, ((source >= 128) & (source + 64 == column)).astype(F32).astype(BF16)
    )
    wa_in[:, 384:640] = tail.astype(BF16)
    wa_in[:, 640:768] = dot_tn(
        out_w, (source == column).astype(F32).astype(BF16)[:, 0:128]
    ).astype(BF16)
    gather_start(0)
    gather_start(1)
    gather_start(2)
    side[0] = jnp.zeros((8, D), F32)
    side[0, 0:1, :] = expand_bias_in[...].reshape(1, D)
    side[0, 1:2, 0:128] = qv_bias_in[0:1, 0:128]
    side[0, 1:2, 256:384] = qv_bias_in[1:2, 0:128]
    side[0, 1:2, 384:448] = qv_bias_in[0:1, 128:192]
    side[0, 1:2, 512:576] = qv_bias_in[1:2, 128:192]
    side_copy = send(side.at[0], side.at[1], c_mate)
    marks_all = valid_in[...].astype(F32)
    cnt[0] = jnp.full((8, 128), jnp.sum(marks_all), F32)
    cnt_x = send(cnt.at[0], cntr.at[0], x_mate)

    gain1 = gain1_in[...].reshape(1, D)
    shift1 = shift1_in[...].reshape(1, D)
    bias_out = bias_out_in[...].reshape(1, D)
    gain2 = gain2_in[...].reshape(1, D)
    shift2 = shift2_in[...].reshape(1, D)
    bias_shrink = bias_shrink_in[...].reshape(1, D)

    lane = lax.broadcasted_iota(jnp.int32, (1, 128), 1)
    half = ((lane < 64).astype(F32), (lane >= 64).astype(F32))
    key_mask = [(m * 0.125).astype(BF16) for m in half]
    half = [m.astype(BF16) for m in half]
    key_lane = lax.broadcasted_iota(jnp.int32, (1, KEYS), 1)
    key_bias = jnp.where(key_lane < WIN_TOK, 0.0, -1e30).astype(F32)

    row_ids = lax.broadcasted_iota(jnp.int32, (4, WIN_TOK), 0)
    own_marks = column_sum(jnp.where(row_ids == t, marks_all, 0.0))
    eye = lax.broadcasted_iota(jnp.int32, (ROWS, WIN_TOK), 0) == lax.broadcasted_iota(
        jnp.int32, (ROWS, WIN_TOK), 1
    )
    live = jnp.sum(jnp.where(eye, own_marks, 0.0), axis=1, keepdims=True)

    window_ids = lax.broadcasted_iota(jnp.int32, (1, 4, 1), 1)

    def window_of(ref, window):
        return jnp.sum(ref[...].astype(F32) * (window_ids == window).astype(F32), axis=1)

    xf[...] = jnp.zeros_like(xf)
    x_load.wait()
    xf[0, 0:WIN_TOK, :] = window_of(xt, t)
    xf[1, 0:WIN_TOK, :] = window_of(xt, peer_window)
    for w in range(2):
        unit, inverse = normalize(xf[w])
        n1[0, w] = (unit * gain1 + shift1).astype(BF16)
        if w == 0:
            unit1[...] = unit
            inv1[...] = inverse
    n1_copy = send(n1.at[0], n1.at[1], c_mate)
    tabs[...] = jnp.zeros_like(tabs)
    tabs[0:27, 0:64] = rows_in[...]
    tabs[32:59, 0:64] = columns_in[...]
    onehot_load.wait()
    t2[0] = dot_nn(onehot[...], tabs[...].astype(BF16)).astype(BF16)
    t2[1] = dot_nn(onehot[...], pltpu.roll(tabs[...], 64, 1).astype(BF16)).astype(BF16)
    place_load.wait()
    pick_load.wait()
    pj[:, :, ROWS:, :] = jnp.zeros((2, 2, KEYS - ROWS, 896), BF16)
    tg[...] = jnp.zeros_like(tg)

    for k in (1, 2, 3):
        gather_z(0, k)
    for k in range(4):
        gather_x(0, k)
    cnt_x.wait_recv()
    cnt[1] = cnt[0] + cntr[0]
    cnt_z = [send(cnt.at[1], cntr.at[k], z_mates[k - 1]) for k in (1, 2, 3)]
    side_copy.wait_recv()
    gather_end(0)

    def project(w):
        def body(j, carry):
            value = dot_nn(n1[0, w], wa[j, :, :, 0:640].reshape(D, 640)) + side[j, 1:2, 0:640]
            pj[w, j, 0:ROWS, 0:640] = value.astype(BF16)
            rolled = pltpu.roll(value[:, 384:512], 64, 1)
            pj[w, j, 0:ROWS, 640:768] = rolled.astype(BF16)
            rolled = pltpu.roll(value[:, 512:640], 64, 1)
            pj[w, j, 0:ROWS, 768:896] = rolled.astype(BF16)
            return carry

        lax.fori_loop(0, 2, body, 0)

    def unit_of(w, j, h):
        q, k, v, p, pv = UNITS[h]
        query = pj[w, j, 0:ROWS, 128 * q : 128 * q + 128]
        key = pj[w, j, :, 128 * k : 128 * k + 128] * key_mask[p]
        value = pj[w, j, :, 128 * v : 128 * v + 128] * half[pv]
        return query, key, value

    def attend(w):
        def body(j, carry):
            mixes = []
            for h in range(3):
                query, key, value = unit_of(w, j, h)
                along = dot_nt(query, t2[UNITS[h][3]]) * place[...]
                high = along.astype(BF16)
                low = (along - high.astype(F32)).astype(BF16)
                scores = dot_nt(query, key) + dot_nn(high, pick[...]) + dot_nn(low, pick[...])
                scores = scores + key_bias
                raised = jnp.exp(scores - jnp.max(scores, axis=-1, keepdims=True))
                soft = raised * (1.0 / jnp.sum(raised, axis=-1, keepdims=True))
                ps[w, j, h] = soft
                mixes.append(dot_nn(soft.astype(BF16), value))
            mx[j, w, :, 0:128] = mixes[2].astype(BF16)
            mx[j, w, :, 128:256] = (mixes[0] + mixes[1]).astype(BF16)
            return carry

        lax.fori_loop(0, 2, body, 0)

    def attended(w, lo, n):
        return dot_nt(mx[0, w, lo : lo + n, :], wa[0, :, :, 512:768].reshape(D, 256)) + dot_nt(
            mx[1, w, lo : lo + n, :], wa[1, :, :, 512:768].reshape(D, 256)
        )

    project(1)
    attend(1)
    e1 = []
    for lo, n in CHUNKS:
        es[0, lo : lo + n, :] = attended(1, lo, n).astype(BF16)
        e1.append(send(es.at[0, pl.ds(lo, n)], er.at[0, pl.ds(lo, n)], y_mate))
    for k in (1, 2, 3):
        gather_z(1, k)
    project(0)
    for k in range(4):
        gather_x(1, k)
    attend(0)
    mx_copy = send(mx.at[1], mxr, c_mate)
    mid[...] = xf[0] + bias_out + attended(0, 0, ROWS)
    gather_end(1)
    for k in (1, 2, 3):
        gather_z(2, k)

    e2 = []
    n2_c = []
    for i, (lo, n) in enumerate(CHUNKS):
        e1[i].wait_recv()
        middle = mid[lo : lo + n, :] + er[0, lo : lo + n, :].astype(F32)
        mid[lo : lo + n, :] = middle
        unit, inverse = normalize(middle)
        unit2[lo : lo + n, :] = unit
        inv2[lo : lo + n, :] = inverse
        n2[0, 0, lo : lo + n, :] = (unit * gain2 + shift2).astype(BF16)
        rows = pl.ds(lo, n)
        e2.append(send(n2.at[0, 0, rows], n2.at[0, 1, rows], y_mate))
        n2_c.append(send(n2.at[0, 0, rows], n2.at[1, 0, rows], c_mate))

    def feed(w, lo, n):
        def body(j, carry):
            before = dot_nn(n2[0, w, lo : lo + n, :], we[j].reshape(D, D)) + side[j, 0:1, :]
            phi = 0.5 * (1.0 + lax.erf(before * math.sqrt(0.5)))
            hid[j, w, lo : lo + n, :] = (before * phi).astype(BF16)
            bell = jnp.exp(-0.5 * before * before) * (1.0 / math.sqrt(2.0 * math.pi))
            slope[j, w, lo : lo + n, :] = phi + before * bell
            return carry

        lax.fori_loop(0, 2, body, 0)

    def shrunk(w, lo, n):
        return dot_nt(hid[0, w, lo : lo + n, :], ws[0].reshape(D, D)) + dot_nt(
            hid[1, w, lo : lo + n, :], ws[1].reshape(D, D)
        )

    for lo, n in CHUNKS:
        feed(0, lo, n)
    for k in range(4):
        gather_x(2, k)
    gather_end(2)
    e3 = []
    for i, (lo, n) in enumerate(CHUNKS):
        rows = pl.ds(lo, n)
        e2[i].wait_recv()
        n2_c.append(send(n2.at[0, 1, rows], n2.at[1, 1, rows], c_mate))
        feed(1, lo, n)
        es[1, lo : lo + n, :] = shrunk(1, lo, n).astype(BF16)
        e3.append(send(es.at[1, rows], er.at[1, rows], y_mate))
    hid_copy = send(hid.at[1], hidr, c_mate)
    acc[...] = mid[...] + bias_shrink + shrunk(0, 0, ROWS)

    for copy in cnt_z:
        copy.wait_recv()
    count = (cnt[1] + cntr[1]) + (cntr[2] + cntr[3])
    count = count[0:1, 0:1]
    scaled_live = live * (token_total / count)
    target_load.wait()
    xf[1, 0:WIN_TOK, :] = window_of(tt, t)
    xf[1, WIN_TOK:, :] = jnp.zeros((ROWS - WIN_TOK, D), F32)
    e4 = []
    gr_c = []
    loss_part = jnp.zeros((1, D), F32)
    shrink_bias_part = jnp.zeros((1, D), F32)
    for i, (lo, n) in enumerate(CHUNKS):
        rows = pl.ds(lo, n)
        e3[i].wait_recv()
        result = acc[lo : lo + n, :] + er[1, lo : lo + n, :].astype(F32)
        gap = result - xf[1, lo : lo + n, :]
        grad = gap * scaled_live[lo : lo + n, :]
        acc[lo : lo + n, :] = grad
        gr[0, 0, lo : lo + n, :] = grad.astype(BF16)
        e4.append(send(gr.at[0, 0, rows], gr.at[0, 1, rows], y_mate))
        gr_c.append(send(gr.at[0, 0, rows], gr.at[1, 0, rows], c_mate))
        bo[t, lo : lo + n, :] = result.astype(BF16)
        loss_part = loss_part + column_sum(gap * gap * live[lo : lo + n, :])
        shrink_bias_part = shrink_bias_part + column_sum(grad)
    sb[0] = jnp.zeros((16, D), F32)
    sb[0, 6:7, :] = loss_part
    sb[0, 0:1, :] = shrink_bias_part

    def feed_back(w, lo, n):
        def body(j, carry):
            grad = dot_nn(gr[0, w, lo : lo + n, :], ws[j].reshape(D, D))
            grad = grad * slope[j, w, lo : lo + n, :]
            gb[j, w, lo : lo + n, :] = grad.astype(BF16)
            return carry

        lax.fori_loop(0, 2, body, 0)

    def expanded_back(w, lo, n):
        return dot_nt(gb[0, w, lo : lo + n, :], we[0].reshape(D, D)) + dot_nt(
            gb[1, w, lo : lo + n, :], we[1].reshape(D, D)
        )

    def rows_of(ref, width):
        return ref[...].reshape(2 * ROWS, width)

    def weight_grad(g, left, mine, theirs, width, at):
        value = dot_tn(rows_of(left.at[0], D), rows_of(mine, width)) + dot_tn(
            rows_of(left.at[1], D), rows_of(theirs, width)
        )
        gw[g, :, :, at : at + width] = value.reshape(8, 96, width)

    to_x = {}
    to_z = {}

    def scatter_x(g):
        for k in (1, 2, 3, 0):
            xs[g, k] = gw[g, row_of(k, 1 - x)].astype(BF16)
            to_x[g, k] = send(xs.at[g, k], xr.at[g, k], x_mate)

    def scatter_z(g):
        for k in (1, 2, 3):
            to_x[g, k].wait_recv()
            total = gw[g, row_of(k, x)] + xr[g, k].astype(F32)
            zs[g, k - 1] = total.astype(BF16)
            to_z[g, k] = send(zs.at[g, k - 1], zr.at[g, k - 1], z_mates[k - 1])

    def scatter_end(g, out):
        to_x[g, 0].wait_recv()
        total = gw[g, dp] + xr[g, 0].astype(F32)
        for k in (1, 2, 3):
            to_z[g, k].wait_recv()
            total = total + zr[g, k - 1].astype(F32)
        out[...] = total

    for lo, n in CHUNKS:
        feed_back(0, lo, n)
    e5 = []
    for i, (lo, n) in enumerate(CHUNKS):
        rows = pl.ds(lo, n)
        e4[i].wait_recv()
        gr_c.append(send(gr.at[0, 1, rows], gr.at[1, 1, rows], c_mate))
        feed_back(1, lo, n)
        es[2, lo : lo + n, :] = expanded_back(1, lo, n).astype(BF16)
        e5.append(send(es.at[2, rows], er.at[2, rows], y_mate))
    gb_copy = send(gb.at[1], gbr, c_mate)
    mid[...] = expanded_back(0, 0, ROWS)
    for copy in gr_c:
        copy.wait_recv()
    hid_copy.wait_recv()
    weight_grad(2, gr, hid.at[0], hidr, D, 0)
    scatter_x(2)

    e6 = []
    gm_c = []
    gain_part = jnp.zeros((1, D), F32)
    shift_part = jnp.zeros((1, D), F32)
    bias_part = jnp.zeros((1, D), F32)
    for i, (lo, n) in enumerate(CHUNKS):
        rows = pl.ds(lo, n)
        e5[i].wait_recv()
        grad = mid[lo : lo + n, :] + er[2, lo : lo + n, :].astype(F32)
        unit = unit2[lo : lo + n, :]
        gain_part = gain_part + column_sum(grad * unit)
        shift_part = shift_part + column_sum(grad)
        grad = acc[lo : lo + n, :] + normalize_back(grad, unit, inv2[lo : lo + n, :], gain2)
        acc[lo : lo + n, :] = grad
        gm[0, 0, lo : lo + n, :] = grad.astype(BF16)
        e6.append(send(gm.at[0, 0, rows], gm.at[0, 1, rows], y_mate))
        gm_c.append(send(gm.at[0, 0, rows], gm.at[1, 0, rows], c_mate))
        bias_part = bias_part + column_sum(grad)
    sb[0, 1:2, :] = gain_part
    sb[0, 2:3, :] = shift_part
    sb[0, 3:4, :] = bias_part

    bo_y = send(bo.at[t], bo.at[t], y_mate)
    bo_c = [send(bo.at[t], bo.at[t], c_mate)]
    gb_copy.wait_recv()
    for copy in n2_c:
        copy.wait_recv()
    weight_grad(1, n2, gb.at[0], gbr, D, 0)
    ones = jnp.ones((8, 2 * ROWS), BF16)
    sb[0, 8:9, :] = (dot_nn(ones, rows_of(gb.at[0], D)) + dot_nn(ones, rows_of(gbr, D)))[0:1]
    scatter_x(1)
    scatter_z(2)

    def mixed_back(w, lo, n):
        for j in range(2):
            grad = dot_nn(gm[0, w, lo : lo + n, :], wa[j, :, :, 512:768].reshape(D, 256))
            gmx[j, w, lo : lo + n, :] = grad.astype(BF16)

    def attend_back(w):
        def body(j, carry):
            grads_q = []
            grads_k = []
            grads_v = []
            for h in range(3):
                query, key, value = unit_of(w, j, h)
                p, pv = UNITS[h][3:]
                grad = gmx[j, w, :, 0:128] if h == 2 else gmx[j, w, :, 128:256]
                soft = ps[w, j, h]
                grad_soft = dot_nt(grad, value)
                delta = jnp.sum(soft * grad_soft, axis=-1, keepdims=True)
                grad_scores = (soft * (grad_soft - delta)).astype(BF16)
                grads_v.append(dot_tn(soft.astype(BF16), grad * half[pv])[0:ROWS])
                grads_k.append(dot_tn(grad_scores, query * key_mask[p])[0:ROWS])
                part = (dot_nt(grad_scores, pick[...]) * place[...]).astype(BF16)
                grads_q.append(dot_nn(grad_scores, key) + dot_nn(part, t2[p]))
                tg[...] += dot_tn(query * half[p], part)
            gp[j, w, :, 0:128] = (grads_q[0] + grads_q[1]).astype(BF16)
            gp[j, w, :, 128:256] = (grads_k[0] + grads_k[1]).astype(BF16)
            gp[j, w, :, 256:384] = (grads_v[0] + grads_v[1]).astype(BF16)
            gp[j, w, :, 384:512] = (grads_q[2] + pltpu.roll(grads_k[2], 64, 1)).astype(BF16)
            gp[j, w, :, 512:640] = pltpu.roll(grads_v[2], 64, 1).astype(BF16)
            return carry

        lax.fori_loop(0, 2, body, 0)

    def projected_back(w, lo, n):
        return dot_nt(gp[0, w, lo : lo + n, :], wa[0, :, :, 0:640].reshape(D, 640)) + dot_nt(
            gp[1, w, lo : lo + n, :], wa[1, :, :, 0:640].reshape(D, 640)
        )

    for i, (lo, n) in enumerate(CHUNKS):
        rows = pl.ds(lo, n)
        e6[i].wait_recv()
        gm_c.append(send(gm.at[0, 1, rows], gm.at[1, 1, rows], c_mate))
        mixed_back(1, lo, n)
    attend_back(1)
    e7 = []
    for lo, n in CHUNKS:
        rows = pl.ds(lo, n)
        es[3, lo : lo + n, :] = projected_back(1, lo, n).astype(BF16)
        e7.append(send(es.at[3, rows], er.at[3, rows], y_mate))
    scatter_z(1)
    mixed_back(0, 0, ROWS)
    attend_back(0)
    gp_copy = send(gp.at[1], gpr, c_mate)
    mid[...] = projected_back(0, 0, ROWS)
    for copy in gm_c:
        copy.wait_recv()
    mx_copy.wait_recv()
    n1_copy.wait_recv()
    gp_copy.wait_recv()
    weight_grad(0, n1, gp.at[0], gpr, 640, 0)
    value = dot_tn(rows_of(gm.at[0], D), rows_of(mx.at[0], 256)) + dot_tn(
        rows_of(gm.at[1], D), rows_of(mxr, 256)
    )
    value = value.reshape(8, 96, 256)
    gw[0, :, :, 512:640] += value[:, :, 0:128]
    gw[0, :, :, 640:768] = value[:, :, 128:256]
    scatter_x(0)
    sb[0, 9:10, 0:640] = (dot_nn(ones, rows_of(gp.at[0], 640)) + dot_nn(ones, rows_of(gpr, 640)))[
        0:1
    ]

    e8 = []
    ig_c = []
    gain_part = jnp.zeros((1, D), F32)
    shift_part = jnp.zeros((1, D), F32)
    for i, (lo, n) in enumerate(CHUNKS):
        rows = pl.ds(lo, n)
        e7[i].wait_recv()
        grad = mid[lo : lo + n, :] + er[3, lo : lo + n, :].astype(F32)
        unit = unit1[lo : lo + n, :]
        gain_part = gain_part + column_sum(grad * unit)
        shift_part = shift_part + column_sum(grad)
        grad = acc[lo : lo + n, :] + normalize_back(grad, unit, inv1[lo : lo + n, :], gain1)
        ig[t, lo : lo + n, :] = grad.astype(BF16)
        e8.append(send(ig.at[t, rows], ig.at[t, rows], y_mate))
        ig_c.append(send(ig.at[t, rows], ig.at[t, rows], c_mate))
    sb[0, 4:5, :] = gain_part
    sb[0, 5:6, :] = shift_part

    scatter_z(0)
    spread = tg[...]
    spread_high = spread.astype(BF16)
    spread_low = (spread - spread_high.astype(F32)).astype(BF16)
    table = dot_nn(spread_high, onehot[...]) + dot_nn(spread_low, onehot[...])
    tb[0] = table[0:64] + table[64:128]
    s_c = send(sb.at[0, pl.ds(0, 8)], sbr.at[0, pl.ds(0, 8)], c_mate)
    t_c = send(tb.at[0], tbr.at[0], c_mate)
    s_c.wait_recv()
    t_c.wait_recv()
    sb[1] = sb[0]
    sb[1, 0:8, :] = sb[0, 0:8, :] + sbr[0, 0:8, :]
    tb[1] = tb[0] + tbr[0]
    s_y = send(sb.at[1, pl.ds(0, 8)], sbr.at[1, pl.ds(0, 8)], y_mate)
    t_y = send(tb.at[1], tbr.at[1], y_mate)
    s_y.wait_recv()
    t_y.wait_recv()
    sb[2] = sb[1]
    sb[2, 0:8, :] = sb[1, 0:8, :] + sbr[1, 0:8, :]
    tb[2] = tb[1] + tbr[1]
    s_x = send(sb.at[2], sbr.at[2], x_mate)
    t_x = send(tb.at[2], tbr.at[2], x_mate)
    s_x.wait_recv()
    t_x.wait_recv()
    sb[3] = sb[2] + sbr[2]
    tb[3] = tb[2] + tbr[2]
    s_z = [send(sb.at[3], sbr.at[2 + k], z_mates[k - 1]) for k in (1, 2, 3)]
    t_z = [send(tb.at[3], tbr.at[2 + k], z_mates[k - 1]) for k in (1, 2, 3)]

    bo_y.wait_recv()
    bo_c.append(send(bo.at[peer_window], bo.at[peer_window], c_mate))
    scatter_end(2, gs)
    gs_store = load(gs, gs_out)
    scatter_end(1, ge)
    ge_store = load(ge, ge_out)
    for copy in bo_c:
        copy.wait_recv()
    for w in range(4):
        mix[:, w, :] = bo[w, 0:WIN_TOK, :].astype(F32)
    bo_low[...] = mix[...].astype(BF16)
    bo_store = load(bo_low, block_out)
    for i, (lo, n) in enumerate(CHUNKS):
        rows = pl.ds(lo, n)
        e8[i].wait_recv()
        ig_c.append(send(ig.at[peer_window, rows], ig.at[peer_window, rows], c_mate))
    for copy in ig_c:
        copy.wait_recv()
    for w in range(4):
        mix[:, w, :] = ig[w, 0:WIN_TOK, :].astype(F32)
    ig_store = load(mix, grad_out)
    scatter_end(0, ga)
    ga_store = load(ga, ga_out)
    for copy in s_z + t_z:
        copy.wait_recv()
    total = (sb[3] + sbr[3]) + (sbr[4] + sbr[5])
    small_out[...] = total
    small_out[6:7, :] = jnp.broadcast_to(
        jnp.sum(total[6:7, :], axis=1, keepdims=True) / (count * float(D)), (1, D)
    )
    table_out[...] = ((tb[3] + tbr[3]) + (tbr[4] + tbr[5])).T
    for copy in started:
        copy.wait_send()
    for copy in (gs_store, ge_store, bo_store, ig_store, ga_store):
        copy.wait()


def finish_kernel(
    block_in,
    grad_in,
    ga,
    ge,
    gs,
    small,
    table,
    block_out,
    loss_out,
    grad_out,
    gain1_out,
    shift1_out,
    triple_out,
    qv_out,
    out_w_out,
    out_b_out,
    gain2_out,
    shift2_out,
    we_out,
    expand_bias_out,
    ws_out,
    bias_shrink_out,
    rows_out,
    columns_out,
    block_hold,
    grad_hold,
    ge_hold,
    gs_hold,
    sems,
):
    moves = []
    at = 0
    for src, hold, dst, step in (
        (block_in, block_hold, block_out, 49),
        (grad_in, grad_hold, grad_out, 49),
        (ge, ge_hold, we_out, 96),
        (gs, gs_hold, ws_out, 96),
    ):
        for lo in range(0, src.shape[0], step):
            rows = pl.ds(lo, step)
            copy = pltpu.make_async_copy(src.at[rows], hold.at[rows], sems.at[at])
            copy.start()
            moves.append(
                (copy, pltpu.make_async_copy(hold.at[rows], dst.at[rows], sems.at[at + 1]))
            )
            at += 2
    for i in range(3):
        triple_out[i, :, 0:128] = ga[:, 128 * i : 128 * i + 128]
    triple_out[0, :, 128:192] = ga[:, 384:448]
    triple_out[1, :, 128:192] = pltpu.roll(ga[:, 384:512], 64, 1)[:, 0:64]
    triple_out[2, :, 128:192] = ga[:, 512:576]
    out_w_out[0:128, :] = ga[:, 640:768].T
    out_w_out[128:192, :] = ga[:, 512:640].T[64:128]
    loss_out[...] = small[6:7, 0:1]
    for i, out in enumerate(
        (bias_shrink_out, gain2_out, shift2_out, out_b_out, gain1_out, shift1_out)
    ):
        out[...] = small[i]
    expand_bias_out[...] = small[8]
    for i in range(2):
        qv_out[i : i + 1, 0:128] = small[9:10, 256 * i : 256 * i + 128]
        qv_out[i : i + 1, 128:192] = small[9:10, 384 + 128 * i : 448 + 128 * i]
    rows_out[...] = table[0:27]
    columns_out[...] = table[32:59]
    for arrive, leave in moves:
        arrive.wait()
        leave.start()
    for arrive, leave in moves:
        leave.wait()


def constant_tables():
    onehot = np.zeros((512, 64), np.float32)
    place = np.zeros((ROWS, 512), np.float32)
    pick = np.zeros((512, KEYS), np.float32)
    for first in range(WIN):
        for second in range(WIN):
            at = first * WIN + second
            onehot[at, first - second + WIN - 1] = 1.0
            onehot[256 + at, 32 + first - second + WIN - 1] = 1.0
            for other in range(WIN):
                place[first * WIN + other, at] = 1.0
                place[other * WIN + first, 256 + at] = 1.0
                pick[at, second * WIN + other] = 1.0
                pick[256 + at, other * WIN + second] = 1.0
    return onehot, place, pick


def fused(
    inputs,
    target,
    valid,
    first_gain,
    first_shift,
    triple_weight,
    query_value_bias,
    output_weight,
    output_bias,
    second_gain,
    second_shift,
    expand_weight,
    expand_bias,
    shrink_weight,
    shrink_bias,
    rows_table,
    columns_table,
):
    onehot, place, pick = constant_tables()
    vmem = pl.BlockSpec(memory_space=pltpu.VMEM)
    anywhere = pl.BlockSpec(memory_space=pl.ANY)
    mixed_shape = (WIN_TOK, 4, D)
    part = jax.ShapeDtypeStruct((96, D), F32)
    copies = 224
    parts = pl.pallas_call(
        block_kernel,
        out_shape=[
            jax.ShapeDtypeStruct(mixed_shape, BF16),
            jax.ShapeDtypeStruct(mixed_shape, F32),
            part,
            part,
            part,
            jax.ShapeDtypeStruct((16, D), F32),
            jax.ShapeDtypeStruct((64, 64), F32),
        ],
        in_specs=[anywhere] * 2 + [vmem] * 15 + [anywhere] * 3,
        out_specs=[anywhere] * 5 + [vmem] * 2,
        scratch_shapes=[
            pltpu.VMEM((96, D), BF16),
            pltpu.VMEM((2, 8, 96, D), BF16),
            pltpu.VMEM((2, 8, 96, D), BF16),
            pltpu.VMEM((2, 8, 96, D), BF16),
            pltpu.VMEM(mixed_shape, BF16),
            pltpu.VMEM(mixed_shape, BF16),
            pltpu.VMEM((512, 64), BF16),
            pltpu.VMEM((ROWS, 512), F32),
            pltpu.VMEM((512, KEYS), BF16),
            pltpu.VMEM((64, 128), F32),
            pltpu.VMEM((4, ROWS, D), BF16),
            pltpu.VMEM((4, ROWS, D), BF16),
            pltpu.VMEM(mixed_shape, F32),
            pltpu.VMEM(mixed_shape, BF16),
            pltpu.VMEM((96, D), F32),
            pltpu.VMEM((96, D), F32),
            pltpu.VMEM((96, D), F32),
            pltpu.VMEM((2, 8, D), F32),
            pltpu.VMEM((2, ROWS, D), F32),
            pltpu.VMEM((ROWS, D), F32),
            pltpu.VMEM((ROWS, D), F32),
            pltpu.VMEM((ROWS, 1), F32),
            pltpu.VMEM((ROWS, 1), F32),
            pltpu.VMEM((ROWS, D), F32),
            pltpu.VMEM((ROWS, D), F32),
            pltpu.VMEM((2, 2, ROWS, D), BF16),
            pltpu.VMEM((2, 2, ROWS, D), BF16),
            pltpu.VMEM((2, 2, ROWS, D), BF16),
            pltpu.VMEM((2, 2, ROWS, D), BF16),
            pltpu.VMEM((2, 2, KEYS, 896), BF16),
            pltpu.VMEM((2, 2, 3, ROWS, KEYS), F32),
            pltpu.VMEM((2, 2, ROWS, 256), BF16),
            pltpu.VMEM((2, ROWS, 256), BF16),
            pltpu.VMEM((2, 2, ROWS, D), BF16),
            pltpu.VMEM((2, ROWS, D), BF16),
            pltpu.VMEM((2, 2, ROWS, D), F32),
            pltpu.VMEM((2, 2, ROWS, D), BF16),
            pltpu.VMEM((2, ROWS, D), BF16),
            pltpu.VMEM((2, 2, ROWS, 256), BF16),
            pltpu.VMEM((2, 2, ROWS, 640), BF16),
            pltpu.VMEM((2, ROWS, 640), BF16),
            pltpu.VMEM((2, 512, 128), BF16),
            pltpu.VMEM((128, 512), F32),
            pltpu.VMEM((4, ROWS, D), BF16),
            pltpu.VMEM((4, ROWS, D), BF16),
            pltpu.VMEM((3, 8, 96, D), F32),
            pltpu.VMEM((3, 4, 96, D), BF16),
            pltpu.VMEM((3, 4, 96, D), BF16),
            pltpu.VMEM((3, 3, 96, D), BF16),
            pltpu.VMEM((3, 3, 96, D), BF16),
            pltpu.VMEM((2, 8, 128), F32),
            pltpu.VMEM((4, 8, 128), F32),
            pltpu.VMEM((4, 16, D), F32),
            pltpu.VMEM((6, 16, D), F32),
            pltpu.VMEM((4, 64, 64), F32),
            pltpu.VMEM((6, 64, 64), F32),
            pltpu.SemaphoreType.DMA((16,)),
            pltpu.SemaphoreType.DMA((copies,)),
            pltpu.SemaphoreType.DMA((copies,)),
        ],
        compiler_params=pltpu.CompilerParams(
            collective_id=0, has_side_effects=True, vmem_limit_bytes=60 << 20
        ),
    )(
        inputs.transpose(1, 0, 2),
        target.transpose(1, 0, 2),
        valid,
        first_gain,
        first_shift,
        triple_weight,
        query_value_bias,
        output_weight,
        output_bias,
        second_gain,
        second_shift,
        expand_weight,
        expand_bias,
        shrink_weight.T,
        shrink_bias,
        rows_table,
        columns_table,
        jnp.asarray(onehot, BF16),
        jnp.asarray(place, F32),
        jnp.asarray(pick, BF16),
    )
    vector = jax.ShapeDtypeStruct((D,), F32)
    relative = jax.ShapeDtypeStruct(rows_table.shape, F32)
    outs = pl.pallas_call(
        finish_kernel,
        out_shape=[
            jax.ShapeDtypeStruct(mixed_shape, BF16),
            jax.ShapeDtypeStruct((1, 1), F32),
            jax.ShapeDtypeStruct(mixed_shape, F32),
            vector,
            vector,
            jax.ShapeDtypeStruct(triple_weight.shape, F32),
            jax.ShapeDtypeStruct(query_value_bias.shape, F32),
            jax.ShapeDtypeStruct(output_weight.shape, F32),
            vector,
            vector,
            vector,
            part,
            jax.ShapeDtypeStruct(expand_bias.shape, F32),
            part,
            vector,
            relative,
            relative,
        ],
        in_specs=[anywhere] * 2 + [vmem, anywhere, anywhere] + [vmem] * 2,
        out_specs=[
            anywhere if i in (0, 2, 11, 13) else vmem for i in range(17)
        ],
        scratch_shapes=[
            pltpu.VMEM(mixed_shape, BF16),
            pltpu.VMEM(mixed_shape, F32),
            pltpu.VMEM((96, D), F32),
            pltpu.VMEM((96, D), F32),
            pltpu.SemaphoreType.DMA((20,)),
        ],
    )(*parts)
    outs = list(outs)
    outs[0] = outs[0].transpose(1, 0, 2)
    outs[1] = outs[1].reshape(())
    outs[2] = outs[2].transpose(1, 0, 2)
    outs[13] = outs[13].T
    return tuple(outs)


def solution(mesh):
    placed = (
        P("dp", None, None),
        P("dp", None, None),
        P("dp", None),
        P(),
        P(),
        P(None, "dp", "tensor"),
        P(None, "tensor"),
        P("tensor", "dp"),
        P(),
        P(),
        P(),
        P("dp", "tensor"),
        P("tensor"),
        P("tensor", "dp"),
        P(),
        P(),
        P(),
    )
    on_slice = mesh.shape["dp"] == 8 and mesh.shape["tensor"] == 4
    return jax.shard_map(
        fused if on_slice else shards,
        mesh=mesh,
        in_specs=placed,
        out_specs=(
            P("dp", None, None),
            P(),
            P("dp", None, None),
            P(),
            P(),
            P(None, "dp", "tensor"),
            P(None, "tensor"),
            P("tensor", "dp"),
            P(),
            P(),
            P(),
            P("dp", "tensor"),
            P("tensor"),
            P("tensor", "dp"),
            P(),
            P(),
            P(),
        ),
        check_vma=False,
    )
```

```python
import math

import jax
import jax.numpy as jnp
import numpy as np
from jax import lax
from jax.experimental import pallas as pl
from jax.experimental.pallas import tpu as pltpu
from jax.sharding import PartitionSpec as P

MESH = pl.DeviceIdType.MESH

D = 768
HEADS = 12
HEAD = 64
WIN = 14
WIN_TOK = 196
MICRO = 2


def normalize(values):
    center = jnp.mean(values, axis=-1, keepdims=True)
    centered = values - center
    spread = jnp.mean(centered * centered, axis=-1, keepdims=True)
    inverse = lax.rsqrt(spread + 1e-06)
    return (centered * inverse, inverse)


def normalize_back(grad_out, unit, inverse, gain):
    scaled = grad_out * gain
    mean_one = jnp.mean(scaled, axis=-1, keepdims=True)
    mean_two = jnp.mean(scaled * unit, axis=-1, keepdims=True)
    return inverse * (scaled - mean_one - unit * mean_two)


def position_select(side):
    shape = (side, side, 2 * side - 1)
    first = lax.broadcasted_iota(jnp.int32, shape, 0)
    second = lax.broadcasted_iota(jnp.int32, shape, 1)
    slots = lax.broadcasted_iota(jnp.int32, shape, 2)
    return (slots == first - second + side - 1).astype(jnp.bfloat16)


def score_block(queries, keys, table_rows, table_cols, scale_factor):
    groups = queries.shape[0]
    side = queries.shape[1]
    heads = queries.shape[3]
    along_rows = jnp.einsum(
        "gabnc,aec->gnabe", queries, table_rows, preferred_element_type=jnp.float32
    )
    along_cols = jnp.einsum(
        "gabnc,bfc->gnabf", queries, table_cols, preferred_element_type=jnp.float32
    )
    scores = (
        jnp.einsum("gabnc,gefnc->gnabef", queries, keys, preferred_element_type=jnp.float32)
        * scale_factor
    )
    scores = scores + along_rows[..., :, None] + along_cols[..., None, :]
    return scores.reshape(groups, heads, side * side, side * side)


def gelu_exact(inner):
    return jax.nn.gelu(inner, approximate=False)


def row_total(partial_value):
    return lax.psum(partial_value, "tensor")


def share_of(values):
    share_rows = values.shape[0] // lax.axis_size("tensor")
    return lax.dynamic_slice_in_dim(values, lax.axis_index("tensor") * share_rows, share_rows, 0)


def shards(
    inputs,
    target,
    valid,
    first_gain,
    first_shift,
    triple_weight,
    query_value_bias,
    output_weight,
    output_bias,
    second_gain,
    second_shift,
    expand_weight,
    expand_bias,
    shrink_weight,
    shrink_bias,
    rows_table,
    columns_table,
):
    local_heads = HEADS // lax.axis_size("tensor")
    local_width = local_heads * HEAD
    local_windows = inputs.shape[0]
    win_micro = local_windows // MICRO
    micro_rows = win_micro * WIN_TOK
    scale_factor = 1.0 / math.sqrt(HEAD)
    highest = lax.Precision.HIGHEST
    live = valid.astype(jnp.float32)
    select = position_select(WIN)
    table_rows = jnp.einsum(
        "aej,jc->aec", select, rows_table.astype(jnp.bfloat16), preferred_element_type=jnp.float32
    ).astype(jnp.bfloat16)
    table_cols = jnp.einsum(
        "aej,jc->aec",
        select,
        columns_table.astype(jnp.bfloat16),
        preferred_element_type=jnp.float32,
    ).astype(jnp.bfloat16)
    rows_float = table_rows.astype(jnp.float32)
    cols_float = table_cols.astype(jnp.float32)
    triple_bias = jnp.stack(
        [query_value_bias[0], jnp.zeros_like(query_value_bias[0]), query_value_bias[1]]
    )
    saved = []
    outputs = []
    local_loss = jnp.zeros((), jnp.float32)
    for micro in range(MICRO):
        gathered = (
            lax.all_gather(triple_weight, "dp", axis=1, tiled=True),
            lax.all_gather(output_weight, "dp", axis=1, tiled=True),
            lax.all_gather(expand_weight, "dp", axis=0, tiled=True),
            lax.all_gather(shrink_weight, "dp", axis=1, tiled=True),
        )
        full_triple, full_output, full_expand, full_shrink = gathered
        lower = micro * win_micro
        flat_rows = inputs[lower : lower + win_micro].reshape(micro_rows, D).astype(jnp.float32)
        unit_one, inverse_one = normalize(flat_rows)
        normed = (unit_one * first_gain + first_shift).astype(jnp.bfloat16)
        projected = (
            jnp.einsum("rd,tde->rte", normed, full_triple, preferred_element_type=jnp.float32)
            + triple_bias
        )
        projected = projected.astype(jnp.bfloat16)
        split = projected.reshape(win_micro, WIN, WIN, 3, local_heads, HEAD)
        queries = split[:, :, :, 0]
        keys = split[:, :, :, 1]
        values = split[:, :, :, 2].reshape(win_micro, WIN_TOK, local_heads, HEAD)
        scores = score_block(queries, keys, table_rows, table_cols, scale_factor)
        peak = jnp.max(scores, axis=-1, keepdims=True)
        raised = jnp.exp(scores - peak)
        denominator = jnp.sum(raised, axis=-1, keepdims=True)
        log_total = peak + jnp.log(denominator)
        softmaxed = (raised / denominator).astype(jnp.bfloat16)
        mixed = jnp.einsum("gnqk,gknc->gqnc", softmaxed, values, preferred_element_type=jnp.float32)
        mixed = mixed.reshape(micro_rows, local_width).astype(jnp.bfloat16)
        partial_attended = jnp.dot(mixed, full_output, preferred_element_type=jnp.float32)
        middle = flat_rows + (row_total(partial_attended) + output_bias)
        unit_two, inverse_two = normalize(middle)
        normed_two = (unit_two * second_gain + second_shift).astype(jnp.bfloat16)
        before = jnp.dot(normed_two, full_expand, preferred_element_type=jnp.float32) + expand_bias
        hidden = gelu_exact(before).astype(jnp.bfloat16)
        partial_shrunk = jnp.dot(hidden, full_shrink, preferred_element_type=jnp.float32)
        result = middle + (row_total(partial_shrunk) + shrink_bias)
        aim = target[lower : lower + win_micro].reshape(micro_rows, D).astype(jnp.float32)
        marks = live[lower : lower + win_micro].reshape(micro_rows, 1)
        weighted_gap = marks * (result - aim)
        local_loss = local_loss + jnp.sum(weighted_gap * (result - aim))
        outputs.append(result.astype(jnp.bfloat16).reshape(win_micro, WIN_TOK, D))
        saved.append(
            (
                unit_one,
                inverse_one,
                normed,
                projected,
                log_total,
                mixed,
                unit_two,
                inverse_two,
                normed_two,
                before,
                hidden,
                weighted_gap,
            )
        )
    loss_total, count = lax.psum((local_loss, jnp.sum(live)), "dp")
    loss = loss_total / (count * D)
    grad_scale = local_windows * WIN_TOK * lax.axis_size("dp") / count
    triple_acc = jnp.zeros((3, D, local_width), jnp.float32)
    output_acc = jnp.zeros((local_width, D), jnp.float32)
    expand_acc = jnp.zeros((D, full_expand.shape[1]), jnp.float32)
    shrink_acc = jnp.zeros((full_shrink.shape[0], D), jnp.float32)
    first_gain_acc = jnp.zeros((D,), jnp.float32)
    first_shift_acc = jnp.zeros((D,), jnp.float32)
    second_gain_acc = jnp.zeros((D,), jnp.float32)
    second_shift_acc = jnp.zeros((D,), jnp.float32)
    output_bias_acc = jnp.zeros((D,), jnp.float32)
    shrink_bias_acc = jnp.zeros((D,), jnp.float32)
    expand_bias_acc = jnp.zeros((full_expand.shape[1],), jnp.float32)
    query_value_acc = jnp.zeros((2, local_width), jnp.float32)
    rows_expanded_acc = jnp.zeros((WIN, WIN, HEAD), jnp.float32)
    cols_expanded_acc = jnp.zeros((WIN, WIN, HEAD), jnp.float32)
    input_grads = []
    for micro in range(MICRO):
        gathered = (
            lax.all_gather(triple_weight, "dp", axis=1, tiled=True),
            lax.all_gather(output_weight, "dp", axis=1, tiled=True),
            lax.all_gather(expand_weight, "dp", axis=0, tiled=True),
            lax.all_gather(shrink_weight, "dp", axis=1, tiled=True),
        )
        full_triple, full_output, full_expand, full_shrink = gathered
        (
            unit_one,
            inverse_one,
            normed,
            projected,
            log_total,
            mixed,
            unit_two,
            inverse_two,
            normed_two,
            before,
            hidden,
            weighted_gap,
        ) = saved[micro]
        grad_result = grad_scale * weighted_gap
        shrink_bias_acc = shrink_bias_acc + jnp.sum(share_of(grad_result), axis=0)
        grad_result_low = grad_result.astype(jnp.bfloat16)
        shrink_acc = shrink_acc + jnp.einsum(
            "rf,rd->fd", hidden, grad_result_low, preferred_element_type=jnp.float32
        )
        grad_hidden = jnp.einsum(
            "rd,fd->rf", grad_result_low, full_shrink, preferred_element_type=jnp.float32
        )
        unused, gelu_pull = jax.vjp(gelu_exact, before)
        grad_before = gelu_pull(grad_hidden)[0].astype(jnp.bfloat16)
        expand_bias_acc = expand_bias_acc + jnp.sum(grad_before.astype(jnp.float32), axis=0)
        expand_acc = expand_acc + jnp.einsum(
            "rd,rf->df", normed_two, grad_before, preferred_element_type=jnp.float32
        )
        partial_two = jnp.einsum(
            "rf,df->rd", grad_before, full_expand, preferred_element_type=jnp.float32
        )
        grad_normed_two = row_total(partial_two)
        grad_middle = grad_result + normalize_back(
            grad_normed_two, unit_two, inverse_two, second_gain
        )
        second_gain_acc = second_gain_acc + jnp.sum(share_of(grad_normed_two * unit_two), axis=0)
        second_shift_acc = second_shift_acc + jnp.sum(share_of(grad_normed_two), axis=0)
        output_bias_acc = output_bias_acc + jnp.sum(share_of(grad_middle), axis=0)
        grad_middle_low = grad_middle.astype(jnp.bfloat16)
        output_acc = output_acc + jnp.einsum(
            "rc,rd->cd", mixed, grad_middle_low, preferred_element_type=jnp.float32
        )
        grad_mixed = jnp.einsum(
            "rd,cd->rc", grad_middle_low, full_output, preferred_element_type=jnp.float32
        )
        grad_mixed = grad_mixed.astype(jnp.bfloat16).reshape(win_micro, WIN_TOK, local_heads, HEAD)
        split = projected.reshape(win_micro, WIN, WIN, 3, local_heads, HEAD)
        queries = split[:, :, :, 0]
        keys = split[:, :, :, 1]
        queries_flat = queries.reshape(win_micro, WIN_TOK, local_heads, HEAD)
        keys_flat = keys.reshape(win_micro, WIN_TOK, local_heads, HEAD)
        values = split[:, :, :, 2].reshape(win_micro, WIN_TOK, local_heads, HEAD)
        scores = score_block(queries, keys, table_rows, table_cols, scale_factor)
        softmax_exact = jnp.exp(scores - log_total)
        grad_soft = jnp.einsum(
            "gqnc,gknc->gnqk", grad_mixed, values, preferred_element_type=jnp.float32
        )
        delta = jnp.sum(softmax_exact * grad_soft, axis=-1, keepdims=True)
        grad_scores = (softmax_exact * (grad_soft - delta)).astype(jnp.bfloat16)
        grad_values = jnp.einsum(
            "gnqk,gqnc->gknc",
            softmax_exact.astype(jnp.bfloat16),
            grad_mixed,
            preferred_element_type=jnp.float32,
        )
        grad_keys = (
            jnp.einsum(
                "gnqk,gqnc->gknc", grad_scores, queries_flat, preferred_element_type=jnp.float32
            )
            * scale_factor
        )
        grad_queries = (
            jnp.einsum(
                "gnqk,gknc->gqnc", grad_scores, keys_flat, preferred_element_type=jnp.float32
            )
            * scale_factor
        )
        grad_grid = grad_scores.astype(jnp.float32).reshape(
            win_micro, local_heads, WIN, WIN, WIN, WIN
        )
        row_part = jnp.sum(grad_grid, axis=5)
        col_part = jnp.sum(grad_grid, axis=4)
        queries_float = queries.astype(jnp.float32)
        rel_queries = jnp.einsum("gnabe,aec->gabnc", row_part, rows_float, precision=highest)
        rel_queries = rel_queries + jnp.einsum(
            "gnabf,bfc->gabnc", col_part, cols_float, precision=highest
        )
        grad_queries = grad_queries + rel_queries.reshape(win_micro, WIN_TOK, local_heads, HEAD)
        rows_expanded_acc = rows_expanded_acc + jnp.einsum(
            "gnabe,gabnc->aec", row_part, queries_float, precision=highest
        )
        cols_expanded_acc = cols_expanded_acc + jnp.einsum(
            "gnabf,gabnc->bfc", col_part, queries_float, precision=highest
        )
        grad_projected = jnp.stack(
            [
                grad_queries.reshape(micro_rows, local_width),
                grad_keys.reshape(micro_rows, local_width),
                grad_values.reshape(micro_rows, local_width),
            ],
            axis=1,
        ).astype(jnp.bfloat16)
        projected_float_sums = jnp.sum(grad_projected.astype(jnp.float32), axis=0)
        query_value_acc = query_value_acc + jnp.stack(
            [projected_float_sums[0], projected_float_sums[2]]
        )
        triple_acc = triple_acc + jnp.einsum(
            "rd,rte->tde", normed, grad_projected, preferred_element_type=jnp.float32
        )
        partial_one = jnp.einsum(
            "rte,tde->rd", grad_projected, full_triple, preferred_element_type=jnp.float32
        )
        grad_normed = row_total(partial_one)
        grad_tokens = grad_middle + normalize_back(grad_normed, unit_one, inverse_one, first_gain)
        first_gain_acc = first_gain_acc + jnp.sum(share_of(grad_normed * unit_one), axis=0)
        first_shift_acc = first_shift_acc + jnp.sum(share_of(grad_normed), axis=0)
        input_grads.append(grad_tokens.reshape(win_micro, WIN_TOK, D))
    select_float = select.astype(jnp.float32)
    rows_table_part = jnp.einsum("aej,aec->jc", select_float, rows_expanded_acc, precision=highest)
    cols_table_part = jnp.einsum("aej,aec->jc", select_float, cols_expanded_acc, precision=highest)
    triple_grad, output_grad, expand_grad, shrink_grad = (
        lax.psum_scatter(triple_acc, "dp", scatter_dimension=1, tiled=True),
        lax.psum_scatter(output_acc, "dp", scatter_dimension=1, tiled=True),
        lax.psum_scatter(expand_acc, "dp", scatter_dimension=0, tiled=True),
        lax.psum_scatter(shrink_acc, "dp", scatter_dimension=1, tiled=True),
    )
    over_heads = lax.psum(
        (
            rows_table_part,
            cols_table_part,
            first_gain_acc,
            first_shift_acc,
            output_bias_acc,
            second_gain_acc,
            second_shift_acc,
            shrink_bias_acc,
        ),
        "tensor",
    )
    summed_small = lax.psum(
        (
            over_heads[0],
            over_heads[1],
            over_heads[2],
            over_heads[3],
            over_heads[4],
            over_heads[5],
            over_heads[6],
            over_heads[7],
            query_value_acc,
            expand_bias_acc,
        ),
        "dp",
    )
    return (
        jnp.concatenate(outputs, axis=0),
        loss,
        jnp.concatenate(input_grads, axis=0),
        summed_small[2],
        summed_small[3],
        triple_grad,
        summed_small[8],
        output_grad,
        summed_small[4],
        summed_small[5],
        summed_small[6],
        expand_grad,
        summed_small[9],
        shrink_grad,
        summed_small[7],
        summed_small[0],
        summed_small[1],
    )


ROWS = 208
KEYS = 256
CHUNKS = ((0, 112), (112, 96))
F32 = jnp.float32
BF16 = jnp.bfloat16


def z_mate(z, k):
    if k == 0:
        return z
    if k == 1:
        return z + 1 - 2 * (z % 2)
    if k == 2:
        return (z + 2) % 4
    return 3 - z


def dot_nn(a, b):
    return lax.dot_general(a, b, (((1,), (0,)), ((), ())), preferred_element_type=F32)


def dot_nt(a, b):
    return lax.dot_general(a, b, (((1,), (1,)), ((), ())), preferred_element_type=F32)


def dot_tn(a, b):
    return lax.dot_general(a, b, (((0,), (0,)), ((), ())), preferred_element_type=F32)


def column_sum(values):
    return jnp.sum(values, axis=0, keepdims=True)


UNITS = ((0, 1, 2, 0, 0), (0, 1, 2, 1, 1), (3, 5, 6, 0, 1))


PLAN = (0, 6, 1, 0, 0, 2, 0, 0, 1, 0, 0, 0, 5, 0, 0, 0, 1, 1, 1, 3, 0, 4, 0, 1, 0, 0, 1, 2, 0, 1, 1, 0, 0, 2, 1, 0, 2, 0, 1, 0, 1, 0, 0, 0, 0, 0, 0, 4, 0, 1, 0, 1)


def block_kernel(
    x_in,
    target_in,
    valid_in,
    gain1_in,
    shift1_in,
    triple_in,
    qv_bias_in,
    out_w_in,
    bias_out_in,
    gain2_in,
    shift2_in,
    we_in,
    expand_bias_in,
    ws_in,
    bias_shrink_in,
    rows_in,
    columns_in,
    onehot_in,
    place_in,
    pick_in,
    block_out,
    grad_out,
    ga_out,
    ge_out,
    gs_out,
    small_out,
    table_out,
    wa_in,
    wa,
    we,
    ws,
    xt,
    tt,
    onehot,
    place,
    pick,
    tabs,
    bo,
    ig,
    mix,
    ga,
    ge,
    gs,
    side,
    xf,
    unit1,
    unit2,
    inv1,
    inv2,
    mid,
    acc,
    n1,
    n2,
    gr,
    gm,
    pj,
    ps,
    mx,
    mxr,
    hid,
    hidr,
    slope,
    gb,
    gbr,
    gmx,
    gp,
    gpr,
    t2,
    tg,
    es,
    er,
    es3,
    er3,
    sums,
    shrink_row,
    gw,
    xs,
    xr,
    zs,
    zr,
    ps2,
    pr2,
    ptotal,
    pxs,
    pxr,
    cnt,
    cntr,
    sb,
    sbr,
    tb,
    tbr,
    load_sem,
    send_sem,
    recv_sem,
):
    dp = lax.axis_index("dp")
    t = lax.axis_index("tensor")
    z = dp // 2
    x = dp % 2
    y = t // 2
    c = t % 2
    z_mates = [(z_mate(z, k) * 2 + x, t) for k in (1, 2, 3)]
    x_mate = (z * 2 + 1 - x, t)
    y_mate = (dp, (1 - y) * 2 + c)
    c_mate = (dp, y * 2 + 1 - c)
    peer_window = (1 - y) * 2 + c
    token_total = lax.axis_size("dp") * 4 * WIN_TOK

    started = []

    def send(src, dst, mate):
        i = len(started)
        copy = pltpu.make_async_remote_copy(
            src_ref=src,
            dst_ref=dst,
            send_sem=send_sem.at[i],
            recv_sem=recv_sem.at[i],
            device_id=mate,
            device_id_type=MESH,
        )
        copy.start()
        started.append(copy)
        return copy

    barrier = pltpu.get_barrier_semaphore()
    for mate in z_mates + [x_mate, y_mate, c_mate]:
        pl.semaphore_signal(barrier, inc=1, device_id=mate, device_id_type=MESH)

    loads = []

    def load(src, dst):
        copy = pltpu.make_async_copy(src, dst, load_sem.at[len(loads)])
        copy.start()
        loads.append(copy)
        return copy

    x_load = load(x_in, xt)
    onehot_load = load(onehot_in, onehot)
    place_load = load(place_in, place)
    pick_load = load(pick_in, pick)
    target_load = load(target_in, tt)

    w_in = (wa_in, we_in, ws_in)
    w_full = (wa, we, ws)
    from_z = {}
    from_x = {}
    from_p = {}
    from_c = {}

    def row_of(k, xx):
        return z_mate(z, k) * 2 + xx

    first = pl.ds(0, 640)
    last = pl.ds(640, 128)

    def gather_start(g):
        full = w_full[g]
        from_p[g, 0] = send(w_in[g].at[:, last], full.at[0, dp, :, last], x_mate)
        for k in (3, 1):
            from_z[g, k] = send(w_in[g].at[:, first], full.at[0, dp, :, first], z_mates[k - 1])
        from_x[g, 0] = send(w_in[g].at[:, first], full.at[0, dp, :, first], x_mate)
        from_c[g, 0] = send(w_in[g], full.at[1, dp], c_mate)
        full[0, dp] = w_in[g][...]

    def to_core(g, i, *at):
        from_c[g, i] = send(w_full[g].at[(0,) + at], w_full[g].at[(1,) + at], c_mate)

    def gather_pair(g, k):
        from_p[g, k].wait_recv()
        pair = (pl.ds(2 * z_mate(z, k), 2), slice(None), last)
        block = w_full[g].at[(0,) + pair]
        if k == 0:
            for m in (3, 1):
                from_p[g, m] = send(block, block, z_mates[m - 1])
            to_core(g, 8, row_of(0, 1 - x), slice(None), last)
        else:
            if k == 3:
                from_p[g, 2] = send(block, block, z_mates[0])
            to_core(g, 8 + k, *pair)

    def gather_z(g, k):
        from_z[g, k].wait_recv()
        block = w_full[g].at[0, row_of(k, x), :, first]
        if k == 3:
            from_z[g, 2] = send(block, block, z_mates[0])
        else:
            from_x[g, k] = send(block, block, x_mate)
        to_core(g, k, row_of(k, x), slice(None), first)

    def gather_far(g):
        block = w_full[g].at[0, row_of(3, x), :, first]
        from_x[g, 3] = send(block, block, x_mate)

    def gather_x(g, k):
        from_x[g, k].wait_recv()
        to_core(g, 4 + k, row_of(k, 1 - x), slice(None), first)

    def gather_end(g, far):
        for k in (2, 3, 6, 7, 10, 11) if far else (0, 1, 4, 5, 8, 9):
            from_c[g, k].wait_recv()

    tasks = []
    done = set()
    plan = iter(PLAN)

    def add(key, step, *args):
        tasks.append((key, step, args))

    def serve():
        key, step, args = tasks.pop(0)
        step(*args)
        done.add(key)

    def point():
        for _ in range(next(plan, 0)):
            if tasks:
                serve()

    def need(key):
        while key not in done:
            serve()

    def gather_add(g):
        add(("pair", g, 0), gather_pair, g, 0)
        add(("z", g, 3), gather_z, g, 3)
        if g == 0:
            add(("start", 1), gather_start, 1)
        add(("z", g, 1), gather_z, g, 1)
        add(("far", g), gather_far, g)
        add(("pair", g, 3), gather_pair, g, 3)
        add(("x", g, 0), gather_x, g, 0)
        add(("pair", g, 1), gather_pair, g, 1)
        add(("z", g, 2), gather_z, g, 2)
        if g == 0:
            add(("count",), count_spread)
            add(("start", 2), gather_start, 2)
        add(("x", g, 1), gather_x, g, 1)
        add(("near", g), gather_end, g, False)
        add(("x", g, 3), gather_x, g, 3)
        add(("pair", g, 2), gather_pair, g, 2)
        add(("x", g, 2), gather_x, g, 2)
        add(("all", g), gather_end, g, True)

    cnt_z = []

    def count_spread():
        cnt_x.wait_recv()
        cnt[1] = cnt[0] + cntr[0]
        cnt_z.extend(send(cnt.at[1], cntr.at[k], z_mates[k - 1]) for k in (1, 2, 3))

    for i in range(3):
        wa_in[:, 128 * i : 128 * i + 128] = triple_in[i, :, 0:128]
    source = lax.broadcasted_iota(jnp.int32, (192, 256), 0)
    column = lax.broadcasted_iota(jnp.int32, (192, 256), 1)
    tail = sum(
        dot_nn(
            triple_in[i],
            ((source >= 128) & (source - 128 == column - 64 * i)).astype(F32).astype(BF16),
        )
        for i in range(3)
    )
    out_w = out_w_in[...]
    tail = tail + dot_tn(
        out_w, ((source >= 128) & (source + 64 == column)).astype(F32).astype(BF16)
    )
    wa_in[:, 384:640] = tail.astype(BF16)
    wa_in[:, 640:768] = dot_tn(
        out_w, (source == column).astype(F32).astype(BF16)[:, 0:128]
    ).astype(BF16)
    pl.semaphore_wait(barrier, 6)
    gather_start(0)
    side[0] = jnp.zeros((8, D), F32)
    side[0, 0:1, :] = expand_bias_in[...].reshape(1, D)
    side[0, 1:2, 0:128] = qv_bias_in[0:1, 0:128]
    side[0, 1:2, 256:384] = qv_bias_in[1:2, 0:128]
    side[0, 1:2, 384:448] = qv_bias_in[0:1, 128:192]
    side[0, 1:2, 512:576] = qv_bias_in[1:2, 128:192]
    side_copy = send(side.at[0], side.at[1], c_mate)
    marks_all = valid_in[...].astype(F32)
    cnt[0] = jnp.full((8, 128), jnp.sum(marks_all), F32)
    cnt_x = send(cnt.at[0], cntr.at[0], x_mate)
    for g in range(3):
        gather_add(g)

    gain1 = gain1_in[...].reshape(1, D)
    shift1 = shift1_in[...].reshape(1, D)
    bias_out = bias_out_in[...].reshape(1, D)
    gain2 = gain2_in[...].reshape(1, D)
    shift2 = shift2_in[...].reshape(1, D)
    shrink_row[...] = bias_shrink_in[...].reshape(1, D)

    lane = lax.broadcasted_iota(jnp.int32, (1, 128), 1)
    half = ((lane < 64).astype(F32), (lane >= 64).astype(F32))
    key_mask = [(m * 0.125).astype(BF16) for m in half]
    half = [m.astype(BF16) for m in half]
    key_lane = lax.broadcasted_iota(jnp.int32, (1, KEYS), 1)
    key_bias = jnp.where(key_lane < WIN_TOK, 0.0, -1e30).astype(F32)

    row_ids = lax.broadcasted_iota(jnp.int32, (4, WIN_TOK), 0)
    own_marks = column_sum(jnp.where(row_ids == t, marks_all, 0.0))
    eye = lax.broadcasted_iota(jnp.int32, (ROWS, WIN_TOK), 0) == lax.broadcasted_iota(
        jnp.int32, (ROWS, WIN_TOK), 1
    )
    live = jnp.sum(jnp.where(eye, own_marks, 0.0), axis=1, keepdims=True)

    window_ids = lax.broadcasted_iota(jnp.int32, (1, 4, 1), 1)

    def window_of(ref, window):
        return jnp.sum(ref[...].astype(F32) * (window_ids == window).astype(F32), axis=1)

    xf[...] = jnp.zeros_like(xf)
    x_load.wait()
    for w in range(2):
        xf[w, 0:WIN_TOK, :] = window_of(xt, peer_window if w else t)
        point()
        unit, inverse = normalize(xf[w])
        n1[0, w] = (unit * gain1 + shift1).astype(BF16)
        if w == 0:
            unit1[...] = unit
            inv1[...] = inverse
    n1_copy = send(n1.at[0], n1.at[1], c_mate)
    tabs[...] = jnp.zeros_like(tabs)
    tabs[0:27, 0:64] = rows_in[...]
    tabs[32:59, 0:64] = columns_in[...]
    onehot_load.wait()
    t2[0] = dot_nn(onehot[...], tabs[...].astype(BF16)).astype(BF16)
    t2[1] = dot_nn(onehot[...], pltpu.roll(tabs[...], 64, 1).astype(BF16)).astype(BF16)
    place_load.wait()
    pick_load.wait()
    pj[:, :, ROWS:, :] = jnp.zeros((2, 2, KEYS - ROWS, 896), BF16)
    tg[...] = jnp.zeros_like(tg)

    def project(w):
        def body(j, carry):
            value = dot_nn(n1[0, w], wa[j, :, :, 0:640].reshape(D, 640)) + side[j, 1:2, 0:640]
            pj[w, j, 0:ROWS, 0:640] = value.astype(BF16)
            rolled = pltpu.roll(value[:, 384:512], 64, 1)
            pj[w, j, 0:ROWS, 640:768] = rolled.astype(BF16)
            rolled = pltpu.roll(value[:, 512:640], 64, 1)
            pj[w, j, 0:ROWS, 768:896] = rolled.astype(BF16)
            return carry

        lax.fori_loop(0, 2, body, 0)

    def unit_of(w, j, h):
        q, k, v, p, pv = UNITS[h]
        query = pj[w, j, 0:ROWS, 128 * q : 128 * q + 128]
        key = pj[w, j, :, 128 * k : 128 * k + 128] * key_mask[p]
        value = pj[w, j, :, 128 * v : 128 * v + 128] * half[pv]
        return query, key, value

    def attend(w, j):
        mixes = []
        for h in range(3):
            query, key, value = unit_of(w, j, h)
            along = dot_nt(query, t2[UNITS[h][3]]) * place[...]
            high = along.astype(BF16)
            low = (along - high.astype(F32)).astype(BF16)
            scores = dot_nt(query, key) + dot_nn(high, pick[...]) + dot_nn(low, pick[...])
            scores = scores + key_bias
            raised = jnp.exp(scores - jnp.max(scores, axis=-1, keepdims=True))
            soft = raised * (1.0 / jnp.sum(raised, axis=-1, keepdims=True))
            ps[w, j, h] = soft
            mixes.append(dot_nn(soft.astype(BF16), value))
            point()
        mx[j, w, :, 0:128] = mixes[2].astype(BF16)
        mx[j, w, :, 128:256] = (mixes[0] + mixes[1]).astype(BF16)

    def attended(w, lo, n):
        return dot_nt(mx[0, w, lo : lo + n, :], wa[0, :, :, 512:768].reshape(D, 256)) + dot_nt(
            mx[1, w, lo : lo + n, :], wa[1, :, :, 512:768].reshape(D, 256)
        )

    side_copy.wait_recv()
    need(("all", 0))
    project(1)
    point()
    attend(1, 0)
    attend(1, 1)
    e1 = []
    for lo, n in CHUNKS:
        es[0, lo : lo + n, :] = attended(1, lo, n).astype(BF16)
        e1.append(send(es.at[0, pl.ds(lo, n)], er.at[0, pl.ds(lo, n)], y_mate))
    point()
    project(0)
    point()
    attend(0, 0)
    attend(0, 1)
    mx_copy = send(mx.at[1], mxr, c_mate)
    mid[...] = xf[0] + bias_out + attended(0, 0, ROWS)
    point()

    e2 = []
    n2_c = []
    for i, (lo, n) in enumerate(CHUNKS):
        point()
        e1[i].wait_recv()
        middle = mid[lo : lo + n, :] + er[0, lo : lo + n, :].astype(F32)
        mid[lo : lo + n, :] = middle
        unit, inverse = normalize(middle)
        unit2[lo : lo + n, :] = unit
        inv2[lo : lo + n, :] = inverse
        n2[0, 0, lo : lo + n, :] = (unit * gain2 + shift2).astype(BF16)
        rows = pl.ds(lo, n)
        e2.append(send(n2.at[0, 0, rows], n2.at[0, 1, rows], y_mate))
        n2_c.append(send(n2.at[0, 0, rows], n2.at[1, 0, rows], c_mate))

    def feed(w, lo, n):
        for j in range(2):
            before = dot_nn(n2[0, w, lo : lo + n, :], we[j].reshape(D, D)) + side[j, 0:1, :]
            phi = 0.5 * (1.0 + lax.erf(before * math.sqrt(0.5)))
            hid[j, w, lo : lo + n, :] = (before * phi).astype(BF16)
            bell = jnp.exp(-0.5 * before * before) * (1.0 / math.sqrt(2.0 * math.pi))
            slope[j, w, lo : lo + n, :] = phi + before * bell
            point()

    zone = z // 2
    zones = (zone, 1 - zone)
    halves = [pl.ds(pl.multiple_of(q * 384, 128), 384) for q in zones]

    def shrunk(w, i):
        rows = pl.ds(zones[i] * 4, 4)
        return dot_nt(hid[0, w], ws[0, rows].reshape(384, D)) + dot_nt(
            hid[1, w], ws[1, rows].reshape(384, D)
        )

    need(("all", 1))
    for lo, n in CHUNKS:
        feed(0, lo, n)
    for i, (lo, n) in enumerate(CHUNKS):
        rows = pl.ds(lo, n)
        point()
        e2[i].wait_recv()
        n2_c.append(send(n2.at[0, 1, rows], n2.at[1, 1, rows], c_mate))
        feed(1, lo, n)
    hid_copy = send(hid.at[1], hidr, c_mate)
    target_load.wait()
    xf[1, 0:WIN_TOK, :] = window_of(tt, t)
    point()
    xf[1, WIN_TOK:, :] = jnp.zeros((ROWS - WIN_TOK, D), F32)
    need(("near", 2))
    for copy in cnt_z:
        copy.wait_recv()
    count = (cnt[1] + cntr[1]) + (cntr[2] + cntr[3])
    count = count[0:1, 0:1]
    scaled_live = live * (token_total / count)
    e3 = []
    for i in range(2):
        if i == 1:
            need(("all", 2))
        es3[i] = shrunk(1, i).astype(BF16)
        e3.append(send(es3.at[i], er3.at[i], y_mate))
        acc[:, halves[i]] = mid[:, halves[i]] + shrink_row[:, halves[i]] + shrunk(0, i)

    e4 = []
    gr_c = []
    for i in range(2):
        cols = halves[i]
        e3[i].wait_recv()
        result = acc[:, cols] + er3[i].astype(F32)
        gap = result - xf[1, :, cols]
        grad = gap * scaled_live
        acc[:, cols] = grad
        gr[0, 0, :, cols] = grad.astype(BF16)
        e4.append(send(gr.at[0, 0, :, cols], gr.at[0, 1, :, cols], y_mate))
        gr_c.append(send(gr.at[0, 0, :, cols], gr.at[1, 0, :, cols], c_mate))
        bo[t, :, cols] = result.astype(BF16)
        sums[6:7, cols] = column_sum(gap * gap * live)
        sums[0:1, cols] = column_sum(grad)
    sb[0] = jnp.zeros((16, D), F32)
    sb[0, 6:7, :] = sums[6:7, :]
    sb[0, 0:1, :] = sums[0:1, :]

    def feed_back(w, lo, n):
        def body(j, carry):
            grad = dot_nn(gr[0, w, lo : lo + n, :], ws[j].reshape(D, D))
            grad = grad * slope[j, w, lo : lo + n, :]
            gb[j, w, lo : lo + n, :] = grad.astype(BF16)
            return carry

        lax.fori_loop(0, 2, body, 0)

    def expanded_back(w, lo, n):
        return dot_nt(gb[0, w, lo : lo + n, :], we[0].reshape(D, D)) + dot_nt(
            gb[1, w, lo : lo + n, :], we[1].reshape(D, D)
        )

    def rows_of(ref, width):
        return ref[...].reshape(2 * ROWS, width)

    def weight_grad(g, left, mine, theirs, width, at):
        value = dot_tn(rows_of(left.at[0], D), rows_of(mine, width)) + dot_tn(
            rows_of(left.at[1], D), rows_of(theirs, width)
        )
        gw[g, :, :, at : at + width] = value.reshape(8, 96, width)

    to_x = {}
    to_z = {}

    pair_of = {}

    def pair_rows(k):
        return pl.ds(2 * z_mate(z, k), 2)

    def scatter_pairs(g):
        for i, k in enumerate((2, 1)):
            ps2[g, i] = gw[g, pair_rows(k), :, 640:768].astype(BF16)
            pair_of[g, i] = send(ps2.at[g, i], pr2.at[g, i], z_mates[0])

    def scatter_blocks(g):
        for k in (2, 3, 1, 0):
            xs[g, k] = gw[g, row_of(k, 1 - x), :, 0:640].astype(BF16)
            to_x[g, k] = send(xs.at[g, k], xr.at[g, k], x_mate)

    def scatter_pair(g):
        pair_of[g, 0].wait_recv()
        total = gw[g, pair_rows(3), :, 640:768] + pr2[g, 0].astype(F32)
        ps2[g, 2] = total.astype(BF16)
        pair_of[g, 2] = send(ps2.at[g, 2], pr2.at[g, 2], z_mates[2])

    def scatter_turn(g):
        pair_of[g, 1].wait_recv()
        pair_of[g, 2].wait_recv()
        total = gw[g, pair_rows(0), :, 640:768] + pr2[g, 1].astype(F32)
        ptotal[g] = total + pr2[g, 2].astype(F32)
        pxs[g] = ptotal[g, 1 - x].astype(BF16)
        pair_of[g, 3] = send(pxs.at[g], pxr.at[g], x_mate)

    def scatter_z(g, k):
        to_x[g, k].wait_recv()
        total = gw[g, row_of(k, x), :, 0:640] + xr[g, k].astype(F32)
        if k == 3:
            to_z[g, 2].wait_recv()
            total = total + zr[g, 1].astype(F32)
        zs[g, k - 1] = total.astype(BF16)
        to_z[g, k] = send(zs.at[g, k - 1], zr.at[g, k - 1], z_mates[2 if k == 3 else 0])

    def scatter_end(g, out):
        to_x[g, 0].wait_recv()
        to_z[g, 1].wait_recv()
        to_z[g, 3].wait_recv()
        total = gw[g, dp, :, 0:640] + xr[g, 0].astype(F32)
        out[:, 0:640] = total + zr[g, 0].astype(F32) + zr[g, 2].astype(F32)
        pair_of[g, 3].wait_recv()
        out[:, 640:768] = ptotal[g, x] + pxr[g].astype(F32)

    def scatter_add(g, *keys):
        steps = {"pair": scatter_pair, "turn": scatter_turn}
        for key in keys:
            if key in steps:
                add((key + "s", g), steps[key], g)
            else:
                add(("zs", g, key), scatter_z, g, key)

    for lo, n in CHUNKS:
        feed_back(0, lo, n)
    for i in range(2):
        e4[i].wait_recv()
        gr_c.append(send(gr.at[0, 1, :, halves[i]], gr.at[1, 1, :, halves[i]], c_mate))
    e5 = []
    for lo, n in CHUNKS:
        rows = pl.ds(lo, n)
        feed_back(1, lo, n)
        es[1, lo : lo + n, :] = expanded_back(1, lo, n).astype(BF16)
        e5.append(send(es.at[1, rows], er.at[1, rows], y_mate))
    gb_copy = send(gb.at[1], gbr, c_mate)
    mid[...] = expanded_back(0, 0, ROWS)
    for copy in gr_c:
        copy.wait_recv()
    hid_copy.wait_recv()
    weight_grad(2, gr, hid.at[0], hidr, D, 0)
    scatter_pairs(2)
    scatter_blocks(2)
    scatter_add(2, "pair", 2, "turn", 3, 1)
    point()

    e6 = []
    gm_c = []
    gain_part = jnp.zeros((1, D), F32)
    shift_part = jnp.zeros((1, D), F32)
    bias_part = jnp.zeros((1, D), F32)
    for i, (lo, n) in enumerate(CHUNKS):
        rows = pl.ds(lo, n)
        point()
        e5[i].wait_recv()
        grad = mid[lo : lo + n, :] + er[1, lo : lo + n, :].astype(F32)
        unit = unit2[lo : lo + n, :]
        gain_part = gain_part + column_sum(grad * unit)
        shift_part = shift_part + column_sum(grad)
        grad = acc[lo : lo + n, :] + normalize_back(grad, unit, inv2[lo : lo + n, :], gain2)
        acc[lo : lo + n, :] = grad
        gm[0, 0, lo : lo + n, :] = grad.astype(BF16)
        e6.append(send(gm.at[0, 0, rows], gm.at[0, 1, rows], y_mate))
        gm_c.append(send(gm.at[0, 0, rows], gm.at[1, 0, rows], c_mate))
        bias_part = bias_part + column_sum(grad)
    sb[0, 1:2, :] = gain_part
    sb[0, 2:3, :] = shift_part
    sb[0, 3:4, :] = bias_part

    bo_y = send(bo.at[t], bo.at[t], y_mate)
    bo_c = [send(bo.at[t], bo.at[t], c_mate)]

    def block_pass():
        bo_y.wait_recv()
        bo_c.append(send(bo.at[peer_window], bo.at[peer_window], c_mate))

    def block_mix():
        for copy in bo_c:
            copy.wait_recv()
        for w in range(4):
            mix[:, w, :] = bo[w, 0:WIN_TOK, :].astype(F32)
        xt[...] = mix[...].astype(BF16)
        stores.append(load(xt, block_out))

    stores = []
    gb_copy.wait_recv()
    for copy in n2_c:
        copy.wait_recv()
    weight_grad(1, n2, gb.at[0], gbr, D, 0)
    ones = jnp.ones((8, 2 * ROWS), BF16)
    sb[0, 8:9, :] = (dot_nn(ones, rows_of(gb.at[0], D)) + dot_nn(ones, rows_of(gbr, D)))[0:1]
    scatter_pairs(1)
    scatter_blocks(1)
    scatter_add(1, "pair", 2, "turn", 3, 1)
    point()

    def mixed_back(w, lo, n):
        for j in range(2):
            grad = dot_nn(gm[0, w, lo : lo + n, :], wa[j, :, :, 512:768].reshape(D, 256))
            gmx[j, w, lo : lo + n, :] = grad.astype(BF16)

    def attend_back(w, j):
        grads_q = []
        grads_k = []
        grads_v = []
        for h in range(3):
            query, key, value = unit_of(w, j, h)
            p, pv = UNITS[h][3:]
            grad = gmx[j, w, :, 0:128] if h == 2 else gmx[j, w, :, 128:256]
            soft = ps[w, j, h]
            grad_soft = dot_nt(grad, value)
            delta = jnp.sum(soft * grad_soft, axis=-1, keepdims=True)
            grad_scores = (soft * (grad_soft - delta)).astype(BF16)
            grads_v.append(dot_tn(soft.astype(BF16), grad * half[pv])[0:ROWS])
            grads_k.append(dot_tn(grad_scores, query * key_mask[p])[0:ROWS])
            part = (dot_nt(grad_scores, pick[...]) * place[...]).astype(BF16)
            grads_q.append(dot_nn(grad_scores, key) + dot_nn(part, t2[p]))
            tg[...] += dot_tn(query * half[p], part)
            point()
        gp[j, w, :, 0:128] = (grads_q[0] + grads_q[1]).astype(BF16)
        gp[j, w, :, 128:256] = (grads_k[0] + grads_k[1]).astype(BF16)
        gp[j, w, :, 256:384] = (grads_v[0] + grads_v[1]).astype(BF16)
        gp[j, w, :, 384:512] = (grads_q[2] + pltpu.roll(grads_k[2], 64, 1)).astype(BF16)
        gp[j, w, :, 512:640] = pltpu.roll(grads_v[2], 64, 1).astype(BF16)

    def projected_back(w, lo, n):
        return dot_nt(gp[0, w, lo : lo + n, :], wa[0, :, :, 0:640].reshape(D, 640)) + dot_nt(
            gp[1, w, lo : lo + n, :], wa[1, :, :, 0:640].reshape(D, 640)
        )

    for i, (lo, n) in enumerate(CHUNKS):
        rows = pl.ds(lo, n)
        point()
        e6[i].wait_recv()
        gm_c.append(send(gm.at[0, 1, rows], gm.at[1, 1, rows], c_mate))
        mixed_back(1, lo, n)
    point()
    add(("block pass",), block_pass)
    add(("block mix",), block_mix)
    attend_back(1, 0)
    attend_back(1, 1)
    e7 = []
    for lo, n in CHUNKS:
        rows = pl.ds(lo, n)
        es[2, lo : lo + n, :] = projected_back(1, lo, n).astype(BF16)
        e7.append(send(es.at[2, rows], er.at[2, rows], y_mate))
    point()
    for copy in gm_c:
        copy.wait_recv()
    mx_copy.wait_recv()
    value = dot_tn(rows_of(gm.at[0], D), rows_of(mx.at[0], 256)) + dot_tn(
        rows_of(gm.at[1], D), rows_of(mxr, 256)
    )
    gw[0, :, :, 512:768] = value.reshape(8, 96, 256)
    scatter_pairs(0)
    scatter_add(0, "pair", "turn")
    point()
    mixed_back(0, 0, ROWS)
    attend_back(0, 0)
    attend_back(0, 1)
    gp_copy = send(gp.at[1], gpr, c_mate)
    mid[...] = projected_back(0, 0, ROWS)
    n1_copy.wait_recv()
    gp_copy.wait_recv()
    value = dot_tn(rows_of(n1.at[0], D), rows_of(gp.at[0], 640)) + dot_tn(
        rows_of(n1.at[1], D), rows_of(gpr, 640)
    )
    value = value.reshape(8, 96, 640)
    gw[0, :, :, 0:512] = value[:, :, 0:512]
    gw[0, :, :, 512:640] += value[:, :, 512:640]
    need(("turns", 0))
    scatter_blocks(0)

    small = {}

    def small_first():
        bias = dot_nn(ones, rows_of(gp.at[0], 640)) + dot_nn(ones, rows_of(gpr, 640))
        sb[0, 9:10, 0:640] = bias[0:1]
        spread = tg[...]
        spread_high = spread.astype(BF16)
        spread_low = (spread - spread_high.astype(F32)).astype(BF16)
        table = dot_nn(spread_high, onehot[...]) + dot_nn(spread_low, onehot[...])
        tb[0] = table[0:64] + table[64:128]

    def small_c():
        sums_now = sb.at[0, pl.ds(0, 8)]
        small["c"] = [send(sums_now, sbr.at[0, pl.ds(0, 8)], c_mate), send(tb.at[0], tbr.at[0], c_mate)]

    def small_wait(stage):
        for copy in small[stage]:
            copy.wait_recv()

    def small_y():
        small_wait("c")
        sb[1] = sb[0]
        sb[1, 0:8, :] = sb[0, 0:8, :] + sbr[0, 0:8, :]
        tb[1] = tb[0] + tbr[0]
        sums_now = sb.at[1, pl.ds(0, 8)]
        small["y"] = [send(sums_now, sbr.at[1, pl.ds(0, 8)], y_mate), send(tb.at[1], tbr.at[1], y_mate)]

    def small_x():
        small_wait("y")
        sb[2] = sb[1]
        sb[2, 0:8, :] = sb[1, 0:8, :] + sbr[1, 0:8, :]
        tb[2] = tb[1] + tbr[1]
        small["x"] = [send(sb.at[2], sbr.at[2], x_mate), send(tb.at[2], tbr.at[2], x_mate)]

    def small_z():
        small_wait("x")
        sb[3] = sb[2] + sbr[2]
        tb[3] = tb[2] + tbr[2]
        small["z"] = [send(sb.at[3], sbr.at[2 + k], z_mates[k - 1]) for k in (1, 2, 3)]
        small["z"] += [send(tb.at[3], tbr.at[2 + k], z_mates[k - 1]) for k in (1, 2, 3)]

    def small_end():
        small_wait("z")
        total = (sb[3] + sbr[3]) + (sbr[4] + sbr[5])
        small_out[...] = total
        small_out[6:7, :] = jnp.broadcast_to(
            jnp.sum(total[6:7, :], axis=1, keepdims=True) / (count * float(D)), (1, D)
        )
        table_out[...] = ((tb[3] + tbr[3]) + (tbr[4] + tbr[5])).T

    e8 = {}
    ig_c = {}

    def mix_in(window, i):
        lo, n = CHUNKS[i]
        top = min(lo + n, WIN_TOK)
        mix[lo:top, pl.ds(window, 1), :] = (
            ig[window, lo:top, :].astype(F32).reshape(top - lo, 1, D)
        )

    def own_grad(i):
        lo, n = CHUNKS[i]
        e7[i].wait_recv()
        grad = mid[lo : lo + n, :] + er[2, lo : lo + n, :].astype(F32)
        unit = unit1[lo : lo + n, :]
        gain_part = column_sum(grad * unit)
        shift_part = column_sum(grad)
        sb[0, 4:5, :] = gain_part if i == 0 else sb[0, 4:5, :] + gain_part
        sb[0, 5:6, :] = shift_part if i == 0 else sb[0, 5:6, :] + shift_part
        grad = acc[lo : lo + n, :] + normalize_back(grad, unit, inv1[lo : lo + n, :], gain1)
        ig[t, lo : lo + n, :] = grad.astype(BF16)
        rows = pl.ds(lo, n)
        ig_c[i, 0] = send(ig.at[t, rows], ig.at[t, rows], c_mate)
        e8[i] = send(ig.at[t, rows], ig.at[t, rows], y_mate)
        mix_in(t, i)

    def side_grad(i):
        ig_c[i, 0].wait_recv()
        mix_in(t + 1 - 2 * c, i)

    def peer_grad(i):
        lo, n = CHUNKS[i]
        rows = pl.ds(lo, n)
        e8[i].wait_recv()
        ig_c[i, 1] = send(ig.at[peer_window, rows], ig.at[peer_window, rows], c_mate)
        mix_in(peer_window, i)

    def last_grad(i):
        lo, n = CHUNKS[i]
        ig_c[i, 1].wait_recv()
        mix_in(peer_window + 1 - 2 * c, i)
        rows = pl.ds(lo, min(n, WIN_TOK - lo))
        stores.append(load(mix.at[rows], grad_out.at[rows]))

    def scatter_out(g, held, out):
        scatter_end(g, held)
        stores.append(load(held, out))

    need(("block mix",))
    add(("own", 0), own_grad, 0)
    add(("small first",), small_first)
    add(("own", 1), own_grad, 1)
    add(("small c",), small_c)
    scatter_add(0, 2)
    add(("small y",), small_y)
    add(("side", 0), side_grad, 0)
    add(("side", 1), side_grad, 1)
    add(("small x",), small_x)
    add(("out", 2), scatter_out, 2, gs, gs_out)
    add(("out", 1), scatter_out, 1, ge, ge_out)
    add(("peer", 0), peer_grad, 0)
    scatter_add(0, 3)
    add(("last", 0), last_grad, 0)
    scatter_add(0, 1)
    add(("peer", 1), peer_grad, 1)
    add(("small z",), small_z)
    add(("last", 1), last_grad, 1)
    add(("out", 0), scatter_out, 0, ga, ga_out)
    add(("small end",), small_end)
    need(("small end",))
    for copy in started:
        copy.wait_send()
    for copy in stores:
        copy.wait()


def finish_kernel(
    block_in,
    grad_in,
    ga,
    ge,
    gs,
    small,
    table,
    block_out,
    loss_out,
    grad_out,
    gain1_out,
    shift1_out,
    triple_out,
    qv_out,
    out_w_out,
    out_b_out,
    gain2_out,
    shift2_out,
    we_out,
    expand_bias_out,
    ws_out,
    bias_shrink_out,
    rows_out,
    columns_out,
    block_hold,
    grad_hold,
    ge_hold,
    gs_hold,
    sems,
):
    moves = []
    at = 0
    for src, hold, dst, step in (
        (block_in, block_hold, block_out, 49),
        (grad_in, grad_hold, grad_out, 49),
        (ge, ge_hold, we_out, 96),
        (gs, gs_hold, ws_out, 96),
    ):
        for lo in range(0, src.shape[0], step):
            rows = pl.ds(lo, step)
            copy = pltpu.make_async_copy(src.at[rows], hold.at[rows], sems.at[at])
            copy.start()
            moves.append(
                (copy, pltpu.make_async_copy(hold.at[rows], dst.at[rows], sems.at[at + 1]))
            )
            at += 2
    for i in range(3):
        triple_out[i, :, 0:128] = ga[:, 128 * i : 128 * i + 128]
    triple_out[0, :, 128:192] = ga[:, 384:448]
    triple_out[1, :, 128:192] = pltpu.roll(ga[:, 384:512], 64, 1)[:, 0:64]
    triple_out[2, :, 128:192] = ga[:, 512:576]
    out_w_out[0:128, :] = ga[:, 640:768].T
    out_w_out[128:192, :] = ga[:, 512:640].T[64:128]
    loss_out[...] = small[6:7, 0:1]
    for i, out in enumerate(
        (bias_shrink_out, gain2_out, shift2_out, out_b_out, gain1_out, shift1_out)
    ):
        out[...] = small[i]
    expand_bias_out[...] = small[8]
    for i in range(2):
        qv_out[i : i + 1, 0:128] = small[9:10, 256 * i : 256 * i + 128]
        qv_out[i : i + 1, 128:192] = small[9:10, 384 + 128 * i : 448 + 128 * i]
    rows_out[...] = table[0:27]
    columns_out[...] = table[32:59]
    for arrive, leave in moves:
        arrive.wait()
        leave.start()
    for arrive, leave in moves:
        leave.wait()


def constant_tables():
    onehot = np.zeros((512, 64), np.float32)
    place = np.zeros((ROWS, 512), np.float32)
    pick = np.zeros((512, KEYS), np.float32)
    for first in range(WIN):
        for second in range(WIN):
            at = first * WIN + second
            onehot[at, first - second + WIN - 1] = 1.0
            onehot[256 + at, 32 + first - second + WIN - 1] = 1.0
            for other in range(WIN):
                place[first * WIN + other, at] = 1.0
                place[other * WIN + first, 256 + at] = 1.0
                pick[at, second * WIN + other] = 1.0
                pick[256 + at, other * WIN + second] = 1.0
    return onehot, place, pick


def fused(
    inputs,
    target,
    valid,
    first_gain,
    first_shift,
    triple_weight,
    query_value_bias,
    output_weight,
    output_bias,
    second_gain,
    second_shift,
    expand_weight,
    expand_bias,
    shrink_weight,
    shrink_bias,
    rows_table,
    columns_table,
):
    onehot, place, pick = constant_tables()
    vmem = pl.BlockSpec(memory_space=pltpu.VMEM)
    anywhere = pl.BlockSpec(memory_space=pl.ANY)
    mixed_shape = (WIN_TOK, 4, D)
    part = jax.ShapeDtypeStruct((96, D), F32)
    copies = 224
    parts = pl.pallas_call(
        block_kernel,
        out_shape=[
            jax.ShapeDtypeStruct(mixed_shape, BF16),
            jax.ShapeDtypeStruct(mixed_shape, F32),
            part,
            part,
            part,
            jax.ShapeDtypeStruct((16, D), F32),
            jax.ShapeDtypeStruct((64, 64), F32),
        ],
        in_specs=[anywhere] * 2 + [vmem] * 15 + [anywhere] * 3,
        out_specs=[anywhere] * 5 + [vmem] * 2,
        scratch_shapes=[
            pltpu.VMEM((96, D), BF16),
            pltpu.VMEM((2, 8, 96, D), BF16),
            pltpu.VMEM((2, 8, 96, D), BF16),
            pltpu.VMEM((2, 8, 96, D), BF16),
            pltpu.VMEM(mixed_shape, BF16),
            pltpu.VMEM(mixed_shape, BF16),
            pltpu.VMEM((512, 64), BF16),
            pltpu.VMEM((ROWS, 512), F32),
            pltpu.VMEM((512, KEYS), BF16),
            pltpu.VMEM((64, 128), F32),
            pltpu.VMEM((4, ROWS, D), BF16),
            pltpu.VMEM((4, ROWS, D), BF16),
            pltpu.VMEM(mixed_shape, F32),
            pltpu.VMEM((96, D), F32),
            pltpu.VMEM((96, D), F32),
            pltpu.VMEM((96, D), F32),
            pltpu.VMEM((2, 8, D), F32),
            pltpu.VMEM((2, ROWS, D), F32),
            pltpu.VMEM((ROWS, D), F32),
            pltpu.VMEM((ROWS, D), F32),
            pltpu.VMEM((ROWS, 1), F32),
            pltpu.VMEM((ROWS, 1), F32),
            pltpu.VMEM((ROWS, D), F32),
            pltpu.VMEM((ROWS, D), F32),
            pltpu.VMEM((2, 2, ROWS, D), BF16),
            pltpu.VMEM((2, 2, ROWS, D), BF16),
            pltpu.VMEM((2, 2, ROWS, D), BF16),
            pltpu.VMEM((2, 2, ROWS, D), BF16),
            pltpu.VMEM((2, 2, KEYS, 896), BF16),
            pltpu.VMEM((2, 2, 3, ROWS, KEYS), F32),
            pltpu.VMEM((2, 2, ROWS, 256), BF16),
            pltpu.VMEM((2, ROWS, 256), BF16),
            pltpu.VMEM((2, 2, ROWS, D), BF16),
            pltpu.VMEM((2, ROWS, D), BF16),
            pltpu.VMEM((2, 2, ROWS, D), F32),
            pltpu.VMEM((2, 2, ROWS, D), BF16),
            pltpu.VMEM((2, ROWS, D), BF16),
            pltpu.VMEM((2, 2, ROWS, 256), BF16),
            pltpu.VMEM((2, 2, ROWS, 640), BF16),
            pltpu.VMEM((2, ROWS, 640), BF16),
            pltpu.VMEM((2, 512, 128), BF16),
            pltpu.VMEM((128, 512), F32),
            pltpu.VMEM((3, ROWS, D), BF16),
            pltpu.VMEM((3, ROWS, D), BF16),
            pltpu.VMEM((2, ROWS, 384), BF16),
            pltpu.VMEM((2, ROWS, 384), BF16),
            pltpu.VMEM((8, D), F32),
            pltpu.VMEM((1, D), F32),
            pltpu.VMEM((3, 8, 96, D), F32),
            pltpu.VMEM((3, 4, 96, 640), BF16),
            pltpu.VMEM((3, 4, 96, 640), BF16),
            pltpu.VMEM((3, 3, 96, 640), BF16),
            pltpu.VMEM((3, 3, 96, 640), BF16),
            pltpu.VMEM((3, 3, 2, 96, 128), BF16),
            pltpu.VMEM((3, 3, 2, 96, 128), BF16),
            pltpu.VMEM((3, 2, 96, 128), F32),
            pltpu.VMEM((3, 96, 128), BF16),
            pltpu.VMEM((3, 96, 128), BF16),
            pltpu.VMEM((2, 8, 128), F32),
            pltpu.VMEM((4, 8, 128), F32),
            pltpu.VMEM((4, 16, D), F32),
            pltpu.VMEM((6, 16, D), F32),
            pltpu.VMEM((4, 64, 64), F32),
            pltpu.VMEM((6, 64, 64), F32),
            pltpu.SemaphoreType.DMA((16,)),
            pltpu.SemaphoreType.DMA((copies,)),
            pltpu.SemaphoreType.DMA((copies,)),
        ],
        compiler_params=pltpu.CompilerParams(
            collective_id=0, has_side_effects=True, vmem_limit_bytes=60 << 20
        ),
    )(
        inputs.transpose(1, 0, 2),
        target.transpose(1, 0, 2),
        valid,
        first_gain,
        first_shift,
        triple_weight,
        query_value_bias,
        output_weight,
        output_bias,
        second_gain,
        second_shift,
        expand_weight,
        expand_bias,
        shrink_weight.T,
        shrink_bias,
        rows_table,
        columns_table,
        jnp.asarray(onehot, BF16),
        jnp.asarray(place, F32),
        jnp.asarray(pick, BF16),
    )
    vector = jax.ShapeDtypeStruct((D,), F32)
    relative = jax.ShapeDtypeStruct(rows_table.shape, F32)
    outs = pl.pallas_call(
        finish_kernel,
        out_shape=[
            jax.ShapeDtypeStruct(mixed_shape, BF16),
            jax.ShapeDtypeStruct((1, 1), F32),
            jax.ShapeDtypeStruct(mixed_shape, F32),
            vector,
            vector,
            jax.ShapeDtypeStruct(triple_weight.shape, F32),
            jax.ShapeDtypeStruct(query_value_bias.shape, F32),
            jax.ShapeDtypeStruct(output_weight.shape, F32),
            vector,
            vector,
            vector,
            part,
            jax.ShapeDtypeStruct(expand_bias.shape, F32),
            part,
            vector,
            relative,
            relative,
        ],
        in_specs=[anywhere] * 2 + [vmem, anywhere, anywhere] + [vmem] * 2,
        out_specs=[
            anywhere if i in (0, 2, 11, 13) else vmem for i in range(17)
        ],
        scratch_shapes=[
            pltpu.VMEM(mixed_shape, BF16),
            pltpu.VMEM(mixed_shape, F32),
            pltpu.VMEM((96, D), F32),
            pltpu.VMEM((96, D), F32),
            pltpu.SemaphoreType.DMA((20,)),
        ],
    )(*parts)
    outs = list(outs)
    outs[0] = outs[0].transpose(1, 0, 2)
    outs[1] = outs[1].reshape(())
    outs[2] = outs[2].transpose(1, 0, 2)
    outs[13] = outs[13].T
    return tuple(outs)


def solution(mesh):
    placed = (
        P("dp", None, None),
        P("dp", None, None),
        P("dp", None),
        P(),
        P(),
        P(None, "dp", "tensor"),
        P(None, "tensor"),
        P("tensor", "dp"),
        P(),
        P(),
        P(),
        P("dp", "tensor"),
        P("tensor"),
        P("tensor", "dp"),
        P(),
        P(),
        P(),
    )
    on_slice = mesh.shape["dp"] == 8 and mesh.shape["tensor"] == 4
    return jax.shard_map(
        fused if on_slice else shards,
        mesh=mesh,
        in_specs=placed,
        out_specs=(
            P("dp", None, None),
            P(),
            P("dp", None, None),
            P(),
            P(),
            P(None, "dp", "tensor"),
            P(None, "tensor"),
            P("tensor", "dp"),
            P(),
            P(),
            P(),
            P("dp", "tensor"),
            P("tensor"),
            P("tensor", "dp"),
            P(),
            P(),
            P(),
        ),
        check_vma=False,
    )
```

```python
import math

import jax
import jax.numpy as jnp
import numpy as np
from jax import lax
from jax.experimental import pallas as pl
from jax.experimental.pallas import tpu as pltpu
from jax.sharding import PartitionSpec as P

MESH = pl.DeviceIdType.MESH

D = 768
HEADS = 12
HEAD = 64
WIN = 14
WIN_TOK = 196
MICRO = 2


def normalize(values):
    center = jnp.mean(values, axis=-1, keepdims=True)
    centered = values - center
    spread = jnp.mean(centered * centered, axis=-1, keepdims=True)
    inverse = lax.rsqrt(spread + 1e-06)
    return (centered * inverse, inverse)


def normalize_back(grad_out, unit, inverse, gain):
    scaled = grad_out * gain
    mean_one = jnp.mean(scaled, axis=-1, keepdims=True)
    mean_two = jnp.mean(scaled * unit, axis=-1, keepdims=True)
    return inverse * (scaled - mean_one - unit * mean_two)


def position_select(side):
    shape = (side, side, 2 * side - 1)
    first = lax.broadcasted_iota(jnp.int32, shape, 0)
    second = lax.broadcasted_iota(jnp.int32, shape, 1)
    slots = lax.broadcasted_iota(jnp.int32, shape, 2)
    return (slots == first - second + side - 1).astype(jnp.bfloat16)


def score_block(queries, keys, table_rows, table_cols, scale_factor):
    groups = queries.shape[0]
    side = queries.shape[1]
    heads = queries.shape[3]
    along_rows = jnp.einsum(
        "gabnc,aec->gnabe", queries, table_rows, preferred_element_type=jnp.float32
    )
    along_cols = jnp.einsum(
        "gabnc,bfc->gnabf", queries, table_cols, preferred_element_type=jnp.float32
    )
    scores = (
        jnp.einsum("gabnc,gefnc->gnabef", queries, keys, preferred_element_type=jnp.float32)
        * scale_factor
    )
    scores = scores + along_rows[..., :, None] + along_cols[..., None, :]
    return scores.reshape(groups, heads, side * side, side * side)


def gelu_exact(inner):
    return jax.nn.gelu(inner, approximate=False)


def row_total(partial_value):
    return lax.psum(partial_value, "tensor")


def share_of(values):
    share_rows = values.shape[0] // lax.axis_size("tensor")
    return lax.dynamic_slice_in_dim(values, lax.axis_index("tensor") * share_rows, share_rows, 0)


def shards(
    inputs,
    target,
    valid,
    first_gain,
    first_shift,
    triple_weight,
    query_value_bias,
    output_weight,
    output_bias,
    second_gain,
    second_shift,
    expand_weight,
    expand_bias,
    shrink_weight,
    shrink_bias,
    rows_table,
    columns_table,
):
    local_heads = HEADS // lax.axis_size("tensor")
    local_width = local_heads * HEAD
    local_windows = inputs.shape[0]
    win_micro = local_windows // MICRO
    micro_rows = win_micro * WIN_TOK
    scale_factor = 1.0 / math.sqrt(HEAD)
    highest = lax.Precision.HIGHEST
    live = valid.astype(jnp.float32)
    select = position_select(WIN)
    table_rows = jnp.einsum(
        "aej,jc->aec", select, rows_table.astype(jnp.bfloat16), preferred_element_type=jnp.float32
    ).astype(jnp.bfloat16)
    table_cols = jnp.einsum(
        "aej,jc->aec",
        select,
        columns_table.astype(jnp.bfloat16),
        preferred_element_type=jnp.float32,
    ).astype(jnp.bfloat16)
    rows_float = table_rows.astype(jnp.float32)
    cols_float = table_cols.astype(jnp.float32)
    triple_bias = jnp.stack(
        [query_value_bias[0], jnp.zeros_like(query_value_bias[0]), query_value_bias[1]]
    )
    saved = []
    outputs = []
    local_loss = jnp.zeros((), jnp.float32)
    for micro in range(MICRO):
        gathered = (
            lax.all_gather(triple_weight, "dp", axis=1, tiled=True),
            lax.all_gather(output_weight, "dp", axis=1, tiled=True),
            lax.all_gather(expand_weight, "dp", axis=0, tiled=True),
            lax.all_gather(shrink_weight, "dp", axis=1, tiled=True),
        )
        full_triple, full_output, full_expand, full_shrink = gathered
        lower = micro * win_micro
        flat_rows = inputs[lower : lower + win_micro].reshape(micro_rows, D).astype(jnp.float32)
        unit_one, inverse_one = normalize(flat_rows)
        normed = (unit_one * first_gain + first_shift).astype(jnp.bfloat16)
        projected = (
            jnp.einsum("rd,tde->rte", normed, full_triple, preferred_element_type=jnp.float32)
            + triple_bias
        )
        projected = projected.astype(jnp.bfloat16)
        split = projected.reshape(win_micro, WIN, WIN, 3, local_heads, HEAD)
        queries = split[:, :, :, 0]
        keys = split[:, :, :, 1]
        values = split[:, :, :, 2].reshape(win_micro, WIN_TOK, local_heads, HEAD)
        scores = score_block(queries, keys, table_rows, table_cols, scale_factor)
        peak = jnp.max(scores, axis=-1, keepdims=True)
        raised = jnp.exp(scores - peak)
        denominator = jnp.sum(raised, axis=-1, keepdims=True)
        log_total = peak + jnp.log(denominator)
        softmaxed = (raised / denominator).astype(jnp.bfloat16)
        mixed = jnp.einsum("gnqk,gknc->gqnc", softmaxed, values, preferred_element_type=jnp.float32)
        mixed = mixed.reshape(micro_rows, local_width).astype(jnp.bfloat16)
        partial_attended = jnp.dot(mixed, full_output, preferred_element_type=jnp.float32)
        middle = flat_rows + (row_total(partial_attended) + output_bias)
        unit_two, inverse_two = normalize(middle)
        normed_two = (unit_two * second_gain + second_shift).astype(jnp.bfloat16)
        before = jnp.dot(normed_two, full_expand, preferred_element_type=jnp.float32) + expand_bias
        hidden = gelu_exact(before).astype(jnp.bfloat16)
        partial_shrunk = jnp.dot(hidden, full_shrink, preferred_element_type=jnp.float32)
        result = middle + (row_total(partial_shrunk) + shrink_bias)
        aim = target[lower : lower + win_micro].reshape(micro_rows, D).astype(jnp.float32)
        marks = live[lower : lower + win_micro].reshape(micro_rows, 1)
        weighted_gap = marks * (result - aim)
        local_loss = local_loss + jnp.sum(weighted_gap * (result - aim))
        outputs.append(result.astype(jnp.bfloat16).reshape(win_micro, WIN_TOK, D))
        saved.append(
            (
                unit_one,
                inverse_one,
                normed,
                projected,
                log_total,
                mixed,
                unit_two,
                inverse_two,
                normed_two,
                before,
                hidden,
                weighted_gap,
            )
        )
    loss_total, count = lax.psum((local_loss, jnp.sum(live)), "dp")
    loss = loss_total / (count * D)
    grad_scale = local_windows * WIN_TOK * lax.axis_size("dp") / count
    triple_acc = jnp.zeros((3, D, local_width), jnp.float32)
    output_acc = jnp.zeros((local_width, D), jnp.float32)
    expand_acc = jnp.zeros((D, full_expand.shape[1]), jnp.float32)
    shrink_acc = jnp.zeros((full_shrink.shape[0], D), jnp.float32)
    first_gain_acc = jnp.zeros((D,), jnp.float32)
    first_shift_acc = jnp.zeros((D,), jnp.float32)
    second_gain_acc = jnp.zeros((D,), jnp.float32)
    second_shift_acc = jnp.zeros((D,), jnp.float32)
    output_bias_acc = jnp.zeros((D,), jnp.float32)
    shrink_bias_acc = jnp.zeros((D,), jnp.float32)
    expand_bias_acc = jnp.zeros((full_expand.shape[1],), jnp.float32)
    query_value_acc = jnp.zeros((2, local_width), jnp.float32)
    rows_expanded_acc = jnp.zeros((WIN, WIN, HEAD), jnp.float32)
    cols_expanded_acc = jnp.zeros((WIN, WIN, HEAD), jnp.float32)
    input_grads = []
    for micro in range(MICRO):
        gathered = (
            lax.all_gather(triple_weight, "dp", axis=1, tiled=True),
            lax.all_gather(output_weight, "dp", axis=1, tiled=True),
            lax.all_gather(expand_weight, "dp", axis=0, tiled=True),
            lax.all_gather(shrink_weight, "dp", axis=1, tiled=True),
        )
        full_triple, full_output, full_expand, full_shrink = gathered
        (
            unit_one,
            inverse_one,
            normed,
            projected,
            log_total,
            mixed,
            unit_two,
            inverse_two,
            normed_two,
            before,
            hidden,
            weighted_gap,
        ) = saved[micro]
        grad_result = grad_scale * weighted_gap
        shrink_bias_acc = shrink_bias_acc + jnp.sum(share_of(grad_result), axis=0)
        grad_result_low = grad_result.astype(jnp.bfloat16)
        shrink_acc = shrink_acc + jnp.einsum(
            "rf,rd->fd", hidden, grad_result_low, preferred_element_type=jnp.float32
        )
        grad_hidden = jnp.einsum(
            "rd,fd->rf", grad_result_low, full_shrink, preferred_element_type=jnp.float32
        )
        unused, gelu_pull = jax.vjp(gelu_exact, before)
        grad_before = gelu_pull(grad_hidden)[0].astype(jnp.bfloat16)
        expand_bias_acc = expand_bias_acc + jnp.sum(grad_before.astype(jnp.float32), axis=0)
        expand_acc = expand_acc + jnp.einsum(
            "rd,rf->df", normed_two, grad_before, preferred_element_type=jnp.float32
        )
        partial_two = jnp.einsum(
            "rf,df->rd", grad_before, full_expand, preferred_element_type=jnp.float32
        )
        grad_normed_two = row_total(partial_two)
        grad_middle = grad_result + normalize_back(
            grad_normed_two, unit_two, inverse_two, second_gain
        )
        second_gain_acc = second_gain_acc + jnp.sum(share_of(grad_normed_two * unit_two), axis=0)
        second_shift_acc = second_shift_acc + jnp.sum(share_of(grad_normed_two), axis=0)
        output_bias_acc = output_bias_acc + jnp.sum(share_of(grad_middle), axis=0)
        grad_middle_low = grad_middle.astype(jnp.bfloat16)
        output_acc = output_acc + jnp.einsum(
            "rc,rd->cd", mixed, grad_middle_low, preferred_element_type=jnp.float32
        )
        grad_mixed = jnp.einsum(
            "rd,cd->rc", grad_middle_low, full_output, preferred_element_type=jnp.float32
        )
        grad_mixed = grad_mixed.astype(jnp.bfloat16).reshape(win_micro, WIN_TOK, local_heads, HEAD)
        split = projected.reshape(win_micro, WIN, WIN, 3, local_heads, HEAD)
        queries = split[:, :, :, 0]
        keys = split[:, :, :, 1]
        queries_flat = queries.reshape(win_micro, WIN_TOK, local_heads, HEAD)
        keys_flat = keys.reshape(win_micro, WIN_TOK, local_heads, HEAD)
        values = split[:, :, :, 2].reshape(win_micro, WIN_TOK, local_heads, HEAD)
        scores = score_block(queries, keys, table_rows, table_cols, scale_factor)
        softmax_exact = jnp.exp(scores - log_total)
        grad_soft = jnp.einsum(
            "gqnc,gknc->gnqk", grad_mixed, values, preferred_element_type=jnp.float32
        )
        delta = jnp.sum(softmax_exact * grad_soft, axis=-1, keepdims=True)
        grad_scores = (softmax_exact * (grad_soft - delta)).astype(jnp.bfloat16)
        grad_values = jnp.einsum(
            "gnqk,gqnc->gknc",
            softmax_exact.astype(jnp.bfloat16),
            grad_mixed,
            preferred_element_type=jnp.float32,
        )
        grad_keys = (
            jnp.einsum(
                "gnqk,gqnc->gknc", grad_scores, queries_flat, preferred_element_type=jnp.float32
            )
            * scale_factor
        )
        grad_queries = (
            jnp.einsum(
                "gnqk,gknc->gqnc", grad_scores, keys_flat, preferred_element_type=jnp.float32
            )
            * scale_factor
        )
        grad_grid = grad_scores.astype(jnp.float32).reshape(
            win_micro, local_heads, WIN, WIN, WIN, WIN
        )
        row_part = jnp.sum(grad_grid, axis=5)
        col_part = jnp.sum(grad_grid, axis=4)
        queries_float = queries.astype(jnp.float32)
        rel_queries = jnp.einsum("gnabe,aec->gabnc", row_part, rows_float, precision=highest)
        rel_queries = rel_queries + jnp.einsum(
            "gnabf,bfc->gabnc", col_part, cols_float, precision=highest
        )
        grad_queries = grad_queries + rel_queries.reshape(win_micro, WIN_TOK, local_heads, HEAD)
        rows_expanded_acc = rows_expanded_acc + jnp.einsum(
            "gnabe,gabnc->aec", row_part, queries_float, precision=highest
        )
        cols_expanded_acc = cols_expanded_acc + jnp.einsum(
            "gnabf,gabnc->bfc", col_part, queries_float, precision=highest
        )
        grad_projected = jnp.stack(
            [
                grad_queries.reshape(micro_rows, local_width),
                grad_keys.reshape(micro_rows, local_width),
                grad_values.reshape(micro_rows, local_width),
            ],
            axis=1,
        ).astype(jnp.bfloat16)
        projected_float_sums = jnp.sum(grad_projected.astype(jnp.float32), axis=0)
        query_value_acc = query_value_acc + jnp.stack(
            [projected_float_sums[0], projected_float_sums[2]]
        )
        triple_acc = triple_acc + jnp.einsum(
            "rd,rte->tde", normed, grad_projected, preferred_element_type=jnp.float32
        )
        partial_one = jnp.einsum(
            "rte,tde->rd", grad_projected, full_triple, preferred_element_type=jnp.float32
        )
        grad_normed = row_total(partial_one)
        grad_tokens = grad_middle + normalize_back(grad_normed, unit_one, inverse_one, first_gain)
        first_gain_acc = first_gain_acc + jnp.sum(share_of(grad_normed * unit_one), axis=0)
        first_shift_acc = first_shift_acc + jnp.sum(share_of(grad_normed), axis=0)
        input_grads.append(grad_tokens.reshape(win_micro, WIN_TOK, D))
    select_float = select.astype(jnp.float32)
    rows_table_part = jnp.einsum("aej,aec->jc", select_float, rows_expanded_acc, precision=highest)
    cols_table_part = jnp.einsum("aej,aec->jc", select_float, cols_expanded_acc, precision=highest)
    triple_grad, output_grad, expand_grad, shrink_grad = (
        lax.psum_scatter(triple_acc, "dp", scatter_dimension=1, tiled=True),
        lax.psum_scatter(output_acc, "dp", scatter_dimension=1, tiled=True),
        lax.psum_scatter(expand_acc, "dp", scatter_dimension=0, tiled=True),
        lax.psum_scatter(shrink_acc, "dp", scatter_dimension=1, tiled=True),
    )
    over_heads = lax.psum(
        (
            rows_table_part,
            cols_table_part,
            first_gain_acc,
            first_shift_acc,
            output_bias_acc,
            second_gain_acc,
            second_shift_acc,
            shrink_bias_acc,
        ),
        "tensor",
    )
    summed_small = lax.psum(
        (
            over_heads[0],
            over_heads[1],
            over_heads[2],
            over_heads[3],
            over_heads[4],
            over_heads[5],
            over_heads[6],
            over_heads[7],
            query_value_acc,
            expand_bias_acc,
        ),
        "dp",
    )
    return (
        jnp.concatenate(outputs, axis=0),
        loss,
        jnp.concatenate(input_grads, axis=0),
        summed_small[2],
        summed_small[3],
        triple_grad,
        summed_small[8],
        output_grad,
        summed_small[4],
        summed_small[5],
        summed_small[6],
        expand_grad,
        summed_small[9],
        shrink_grad,
        summed_small[7],
        summed_small[0],
        summed_small[1],
    )


ROWS = 208
KEYS = 256
CHUNKS = ((0, 112), (112, 96))
F32 = jnp.float32
BF16 = jnp.bfloat16


def z_mate(z, k):
    if k == 0:
        return z
    if k == 1:
        return z + 1 - 2 * (z % 2)
    if k == 2:
        return (z + 2) % 4
    return 3 - z


def dot_nn(a, b):
    return lax.dot_general(a, b, (((1,), (0,)), ((), ())), preferred_element_type=F32)


def dot_nt(a, b):
    return lax.dot_general(a, b, (((1,), (1,)), ((), ())), preferred_element_type=F32)


def dot_tn(a, b):
    return lax.dot_general(a, b, (((0,), (0,)), ((), ())), preferred_element_type=F32)


def column_sum(values):
    return jnp.sum(values, axis=0, keepdims=True)


UNITS = ((0, 1, 2, 0, 0), (0, 1, 2, 1, 1), (3, 5, 6, 0, 1))


PLAN = (0, 6, 0, 1, 0, 2, 0, 0, 0, 1, 0, 0, 5, 0, 0, 0, 1, 1, 1, 3, 0, 3, 0, 0, 1, 0, 0, 2, 1, 1, 0, 1, 0, 1, 1, 1, 2, 0, 0, 0, 1, 0, 0, 0, 0, 0, 0, 3, 0, 1, 2, 0)


def block_kernel(
    x_in,
    target_in,
    valid_hbm,
    gain1_hbm,
    shift1_hbm,
    triple_hbm,
    qv_bias_hbm,
    out_w_hbm,
    bias_out_hbm,
    gain2_hbm,
    shift2_hbm,
    we_hbm,
    expand_bias_hbm,
    ws_hbm,
    bias_shrink_hbm,
    rows_hbm,
    columns_hbm,
    block_out,
    grad_out,
    ga_out,
    ge_out,
    gs_out,
    small_out,
    table_out,
    valid_in,
    gain1_in,
    shift1_in,
    triple_in,
    qv_bias_in,
    out_w_in,
    bias_out_in,
    gain2_in,
    shift2_in,
    we_in,
    expand_bias_in,
    ws_in,
    bias_shrink_in,
    rows_in,
    columns_in,
    wa_in,
    wa,
    we,
    ws,
    xt,
    tt,
    onehot,
    place,
    pick,
    tabs,
    bo,
    ig,
    mix,
    ga,
    ge,
    gs,
    side,
    xf,
    unit1,
    unit2,
    inv1,
    inv2,
    mid,
    acc,
    n1,
    n2,
    gr,
    gm,
    pj,
    ps,
    mx,
    mxr,
    hid,
    hidr,
    slope,
    gb,
    gbr,
    gmx,
    gp,
    gpr,
    t2,
    tg,
    es,
    er,
    es3,
    er3,
    sums,
    shrink_row,
    gw,
    xs,
    xr,
    zs,
    zr,
    ps2,
    pr2,
    ptotal,
    pxs,
    pxr,
    cnt,
    cntr,
    sb,
    sbr,
    tb,
    tbr,
    load_sem,
    send_sem,
    recv_sem,
):
    dp = lax.axis_index("dp")
    t = lax.axis_index("tensor")
    z = dp // 2
    x = dp % 2
    y = t // 2
    c = t % 2
    z_mates = [(z_mate(z, k) * 2 + x, t) for k in (1, 2, 3)]
    x_mate = (z * 2 + 1 - x, t)
    y_mate = (dp, (1 - y) * 2 + c)
    c_mate = (dp, y * 2 + 1 - c)
    peer_window = (1 - y) * 2 + c
    token_total = lax.axis_size("dp") * 4 * WIN_TOK

    started = []

    def send(src, dst, mate):
        i = len(started)
        copy = pltpu.make_async_remote_copy(
            src_ref=src,
            dst_ref=dst,
            send_sem=send_sem.at[i],
            recv_sem=recv_sem.at[i],
            device_id=mate,
            device_id_type=MESH,
        )
        copy.start()
        started.append(copy)
        return copy

    barrier = pltpu.get_barrier_semaphore()
    for mate in z_mates + [x_mate, y_mate, c_mate]:
        pl.semaphore_signal(barrier, inc=1, device_id=mate, device_id_type=MESH)

    loads = []

    def load(src, dst):
        copy = pltpu.make_async_copy(src, dst, load_sem.at[len(loads)])
        copy.start()
        loads.append(copy)
        return copy

    first_loads = [load(triple_hbm, triple_in), load(out_w_hbm, out_w_in)]
    group_loads = [load(we_hbm, we_in), load(ws_hbm, ws_in)]
    x_load = load(x_in, xt)
    side_loads = [
        load(src, dst)
        for src, dst in (
            (expand_bias_hbm, expand_bias_in),
            (qv_bias_hbm, qv_bias_in),
            (valid_hbm, valid_in),
            (gain1_hbm, gain1_in),
            (shift1_hbm, shift1_in),
            (bias_out_hbm, bias_out_in),
            (gain2_hbm, gain2_in),
            (shift2_hbm, shift2_in),
            (bias_shrink_hbm, bias_shrink_in),
            (rows_hbm, rows_in),
            (columns_hbm, columns_in),
        )
    ]
    target_load = load(target_in, tt)

    w_in = (wa_in, we_in, ws_in)
    w_full = (wa, we, ws)
    from_z = {}
    from_x = {}
    from_p = {}
    from_c = {}

    def row_of(k, xx):
        return z_mate(z, k) * 2 + xx

    first = pl.ds(0, 640)
    last = pl.ds(640, 128)

    def gather_start(g):
        full = w_full[g]
        from_p[g, 0] = send(w_in[g].at[:, last], full.at[0, dp, :, last], x_mate)
        for k in (3, 1):
            from_z[g, k] = send(w_in[g].at[:, first], full.at[0, dp, :, first], z_mates[k - 1])
        from_x[g, 0] = send(w_in[g].at[:, first], full.at[0, dp, :, first], x_mate)
        from_c[g, 0] = send(w_in[g], full.at[1, dp], c_mate)
        full[0, dp] = w_in[g][...]

    def to_core(g, i, *at):
        from_c[g, i] = send(w_full[g].at[(0,) + at], w_full[g].at[(1,) + at], c_mate)

    def gather_pair(g, k):
        from_p[g, k].wait_recv()
        pair = (pl.ds(2 * z_mate(z, k), 2), slice(None), last)
        block = w_full[g].at[(0,) + pair]
        if k == 0:
            for m in (3, 1):
                from_p[g, m] = send(block, block, z_mates[m - 1])
            to_core(g, 8, row_of(0, 1 - x), slice(None), last)
        else:
            if k == 3:
                from_p[g, 2] = send(block, block, z_mates[0])
            to_core(g, 8 + k, *pair)

    def gather_z(g, k):
        from_z[g, k].wait_recv()
        block = w_full[g].at[0, row_of(k, x), :, first]
        if k == 3:
            from_z[g, 2] = send(block, block, z_mates[0])
        else:
            from_x[g, k] = send(block, block, x_mate)
        to_core(g, k, row_of(k, x), slice(None), first)

    def gather_far(g):
        block = w_full[g].at[0, row_of(3, x), :, first]
        from_x[g, 3] = send(block, block, x_mate)

    def gather_x(g, k):
        from_x[g, k].wait_recv()
        to_core(g, 4 + k, row_of(k, 1 - x), slice(None), first)

    def gather_end(g, far):
        for k in (2, 3, 6, 7, 10, 11) if far else (0, 1, 4, 5, 8, 9):
            from_c[g, k].wait_recv()

    tasks = []
    done = set()
    plan = iter(PLAN)

    def add(key, step, *args):
        tasks.append((key, step, args))

    def serve():
        key, step, args = tasks.pop(0)
        step(*args)
        done.add(key)

    def point():
        for _ in range(next(plan, 0)):
            if tasks:
                serve()

    def need(key):
        while key not in done:
            serve()

    def gather_add(g):
        add(("pair", g, 0), gather_pair, g, 0)
        add(("z", g, 3), gather_z, g, 3)
        if g == 0:
            add(("start", 1), gather_start, 1)
        add(("z", g, 1), gather_z, g, 1)
        add(("far", g), gather_far, g)
        add(("pair", g, 3), gather_pair, g, 3)
        add(("x", g, 0), gather_x, g, 0)
        add(("pair", g, 1), gather_pair, g, 1)
        add(("z", g, 2), gather_z, g, 2)
        if g == 0:
            add(("count",), count_spread)
            add(("start", 2), gather_start, 2)
        add(("x", g, 1), gather_x, g, 1)
        add(("near", g), gather_end, g, False)
        add(("x", g, 3), gather_x, g, 3)
        add(("pair", g, 2), gather_pair, g, 2)
        add(("x", g, 2), gather_x, g, 2)
        add(("all", g), gather_end, g, True)

    cnt_z = []

    def count_spread():
        cnt_x.wait_recv()
        cnt[1] = cnt[0] + cntr[0]
        cnt_z.extend(send(cnt.at[1], cntr.at[k], z_mates[k - 1]) for k in (1, 2, 3))

    for copy in first_loads:
        copy.wait()
    for i in range(3):
        wa_in[:, 128 * i : 128 * i + 128] = triple_in[i, :, 0:128]
    source = lax.broadcasted_iota(jnp.int32, (192, 256), 0)
    column = lax.broadcasted_iota(jnp.int32, (192, 256), 1)
    tail = sum(
        dot_nn(
            triple_in[i],
            ((source >= 128) & (source - 128 == column - 64 * i)).astype(F32).astype(BF16),
        )
        for i in range(3)
    )
    out_w = out_w_in[...]
    tail = tail + dot_tn(
        out_w, ((source >= 128) & (source + 64 == column)).astype(F32).astype(BF16)
    )
    wa_in[:, 384:640] = tail.astype(BF16)
    wa_in[:, 640:768] = dot_tn(
        out_w, (source == column).astype(F32).astype(BF16)[:, 0:128]
    ).astype(BF16)
    def fourteens(at):
        whole = jnp.floor((at + 0.5) * (1.0 / WIN))
        return whole, at - WIN * whole

    def grid(shape, dim):
        return lax.broadcasted_iota(jnp.int32, shape, dim).astype(F32)

    def entries(shape, dim):
        at = grid(shape, dim)
        side = (at >= 256.0).astype(F32)
        at = at - 256.0 * side
        main, other = fourteens(at)
        return side, main, other, at < float(WIN_TOK)

    side_of, main, other, valid = entries((512, 64), 0)
    slot = main - other + (WIN - 1) + 32.0 * side_of
    onehot[...] = jnp.where(valid & (grid((512, 64), 1) == slot), 1.0, 0.0).astype(BF16)
    side_of, main, other, valid = entries((ROWS, 512), 1)
    token = grid((ROWS, 512), 0)
    down, across = fourteens(token)
    hit = valid & (main == jnp.where(side_of > 0.5, across, down)) & (token < float(WIN_TOK))
    place[...] = jnp.where(hit, 1.0, 0.0)
    side_of, main, other, valid = entries((512, KEYS), 0)
    token = grid((512, KEYS), 1)
    down, across = fourteens(token)
    hit = valid & (other == jnp.where(side_of > 0.5, across, down)) & (token < float(WIN_TOK))
    pick[...] = jnp.where(hit, 1.0, 0.0).astype(BF16)
    pl.semaphore_wait(barrier, 6)
    gather_start(0)
    for copy in group_loads + side_loads:
        copy.wait()
    side[0] = jnp.zeros((8, D), F32)
    side[0, 0:1, :] = expand_bias_in[...].reshape(1, D)
    side[0, 1:2, 0:128] = qv_bias_in[0:1, 0:128]
    side[0, 1:2, 256:384] = qv_bias_in[1:2, 0:128]
    side[0, 1:2, 384:448] = qv_bias_in[0:1, 128:192]
    side[0, 1:2, 512:576] = qv_bias_in[1:2, 128:192]
    side_copy = send(side.at[0], side.at[1], c_mate)
    marks_all = valid_in[...].astype(F32)
    cnt[0] = jnp.full((8, 128), jnp.sum(marks_all), F32)
    cnt_x = send(cnt.at[0], cntr.at[0], x_mate)
    for g in range(3):
        gather_add(g)

    gain1 = gain1_in[...].reshape(1, D)
    shift1 = shift1_in[...].reshape(1, D)
    bias_out = bias_out_in[...].reshape(1, D)
    gain2 = gain2_in[...].reshape(1, D)
    shift2 = shift2_in[...].reshape(1, D)
    shrink_row[...] = bias_shrink_in[...].reshape(1, D)

    lane = lax.broadcasted_iota(jnp.int32, (1, 128), 1)
    half = ((lane < 64).astype(F32), (lane >= 64).astype(F32))
    key_mask = [(m * 0.125).astype(BF16) for m in half]
    half = [m.astype(BF16) for m in half]
    key_lane = lax.broadcasted_iota(jnp.int32, (1, KEYS), 1)
    key_bias = jnp.where(key_lane < WIN_TOK, 0.0, -1e30).astype(F32)

    row_ids = lax.broadcasted_iota(jnp.int32, (4, WIN_TOK), 0)
    own_marks = column_sum(jnp.where(row_ids == t, marks_all, 0.0))
    eye = lax.broadcasted_iota(jnp.int32, (ROWS, WIN_TOK), 0) == lax.broadcasted_iota(
        jnp.int32, (ROWS, WIN_TOK), 1
    )
    live = jnp.sum(jnp.where(eye, own_marks, 0.0), axis=1, keepdims=True)

    window_ids = lax.broadcasted_iota(jnp.int32, (1, 4, 1), 1)

    def window_of(ref, window):
        return jnp.sum(ref[...].astype(F32) * (window_ids == window).astype(F32), axis=1)

    xf[...] = jnp.zeros_like(xf)
    x_load.wait()
    for w in range(2):
        xf[w, 0:WIN_TOK, :] = window_of(xt, peer_window if w else t)
        point()
        unit, inverse = normalize(xf[w])
        n1[0, w] = (unit * gain1 + shift1).astype(BF16)
        if w == 0:
            unit1[...] = unit
            inv1[...] = inverse
    n1_copy = send(n1.at[0], n1.at[1], c_mate)
    tabs[...] = jnp.zeros_like(tabs)
    tabs[0:27, 0:64] = rows_in[...]
    tabs[32:59, 0:64] = columns_in[...]
    t2[0] = dot_nn(onehot[...], tabs[...].astype(BF16)).astype(BF16)
    t2[1] = dot_nn(onehot[...], pltpu.roll(tabs[...], 64, 1).astype(BF16)).astype(BF16)
    pj[:, :, ROWS:, :] = jnp.zeros((2, 2, KEYS - ROWS, 896), BF16)
    tg[...] = jnp.zeros_like(tg)

    def project(w):
        def body(j, carry):
            value = dot_nn(n1[0, w], wa[j, :, :, 0:640].reshape(D, 640)) + side[j, 1:2, 0:640]
            pj[w, j, 0:ROWS, 0:640] = value.astype(BF16)
            rolled = pltpu.roll(value[:, 384:512], 64, 1)
            pj[w, j, 0:ROWS, 640:768] = rolled.astype(BF16)
            rolled = pltpu.roll(value[:, 512:640], 64, 1)
            pj[w, j, 0:ROWS, 768:896] = rolled.astype(BF16)
            return carry

        lax.fori_loop(0, 2, body, 0)

    def unit_of(w, j, h):
        q, k, v, p, pv = UNITS[h]
        query = pj[w, j, 0:ROWS, 128 * q : 128 * q + 128]
        key = pj[w, j, :, 128 * k : 128 * k + 128] * key_mask[p]
        value = pj[w, j, :, 128 * v : 128 * v + 128] * half[pv]
        return query, key, value

    def attend(w, j):
        mixes = []
        for h in range(3):
            query, key, value = unit_of(w, j, h)
            along = dot_nt(query, t2[UNITS[h][3]]) * place[...]
            high = along.astype(BF16)
            low = (along - high.astype(F32)).astype(BF16)
            scores = dot_nt(query, key) + dot_nn(high, pick[...]) + dot_nn(low, pick[...])
            scores = scores + key_bias
            raised = jnp.exp(scores - jnp.max(scores, axis=-1, keepdims=True))
            soft = raised * (1.0 / jnp.sum(raised, axis=-1, keepdims=True))
            ps[w, j, h] = soft
            mixes.append(dot_nn(soft.astype(BF16), value))
            point()
        mx[j, w, :, 0:128] = mixes[2].astype(BF16)
        mx[j, w, :, 128:256] = (mixes[0] + mixes[1]).astype(BF16)

    def attended(w, lo, n):
        return dot_nt(mx[0, w, lo : lo + n, :], wa[0, :, :, 512:768].reshape(D, 256)) + dot_nt(
            mx[1, w, lo : lo + n, :], wa[1, :, :, 512:768].reshape(D, 256)
        )

    side_copy.wait_recv()
    need(("all", 0))
    project(1)
    point()
    attend(1, 0)
    attend(1, 1)
    e1 = []
    for lo, n in CHUNKS:
        es[0, lo : lo + n, :] = attended(1, lo, n).astype(BF16)
        e1.append(send(es.at[0, pl.ds(lo, n)], er.at[0, pl.ds(lo, n)], y_mate))
    point()
    project(0)
    point()
    attend(0, 0)
    attend(0, 1)
    mx_copy = send(mx.at[1], mxr, c_mate)
    mid[...] = xf[0] + bias_out + attended(0, 0, ROWS)
    point()

    e2 = []
    n2_c = []
    for i, (lo, n) in enumerate(CHUNKS):
        point()
        e1[i].wait_recv()
        middle = mid[lo : lo + n, :] + er[0, lo : lo + n, :].astype(F32)
        mid[lo : lo + n, :] = middle
        unit, inverse = normalize(middle)
        unit2[lo : lo + n, :] = unit
        inv2[lo : lo + n, :] = inverse
        n2[0, 0, lo : lo + n, :] = (unit * gain2 + shift2).astype(BF16)
        rows = pl.ds(lo, n)
        e2.append(send(n2.at[0, 0, rows], n2.at[0, 1, rows], y_mate))
        n2_c.append(send(n2.at[0, 0, rows], n2.at[1, 0, rows], c_mate))

    def feed(w, lo, n):
        for j in range(2):
            before = dot_nn(n2[0, w, lo : lo + n, :], we[j].reshape(D, D)) + side[j, 0:1, :]
            phi = 0.5 * (1.0 + lax.erf(before * math.sqrt(0.5)))
            hid[j, w, lo : lo + n, :] = (before * phi).astype(BF16)
            bell = jnp.exp(-0.5 * before * before) * (1.0 / math.sqrt(2.0 * math.pi))
            slope[j, w, lo : lo + n, :] = phi + before * bell
            point()

    zone = z // 2
    zones = (zone, 1 - zone)
    halves = [pl.ds(pl.multiple_of(q * 384, 128), 384) for q in zones]

    def shrunk(w, i):
        rows = pl.ds(zones[i] * 4, 4)
        return dot_nt(hid[0, w], ws[0, rows].reshape(384, D)) + dot_nt(
            hid[1, w], ws[1, rows].reshape(384, D)
        )

    need(("all", 1))
    for lo, n in CHUNKS:
        feed(0, lo, n)
    for i, (lo, n) in enumerate(CHUNKS):
        rows = pl.ds(lo, n)
        point()
        e2[i].wait_recv()
        n2_c.append(send(n2.at[0, 1, rows], n2.at[1, 1, rows], c_mate))
        feed(1, lo, n)
    hid_copy = send(hid.at[1], hidr, c_mate)
    target_load.wait()
    xf[1, 0:WIN_TOK, :] = window_of(tt, t)
    point()
    xf[1, WIN_TOK:, :] = jnp.zeros((ROWS - WIN_TOK, D), F32)
    need(("near", 2))
    for copy in cnt_z:
        copy.wait_recv()
    count = (cnt[1] + cntr[1]) + (cntr[2] + cntr[3])
    count = count[0:1, 0:1]
    scaled_live = live * (token_total / count)
    e3 = []
    for i in range(2):
        if i == 1:
            need(("all", 2))
        es3[i] = shrunk(1, i).astype(BF16)
        e3.append(send(es3.at[i], er3.at[i], y_mate))
        acc[:, halves[i]] = mid[:, halves[i]] + shrink_row[:, halves[i]] + shrunk(0, i)

    e4 = []
    gr_c = []
    for i in range(2):
        cols = halves[i]
        e3[i].wait_recv()
        result = acc[:, cols] + er3[i].astype(F32)
        gap = result - xf[1, :, cols]
        grad = gap * scaled_live
        acc[:, cols] = grad
        gr[0, 0, :, cols] = grad.astype(BF16)
        e4.append(send(gr.at[0, 0, :, cols], gr.at[0, 1, :, cols], y_mate))
        gr_c.append(send(gr.at[0, 0, :, cols], gr.at[1, 0, :, cols], c_mate))
        bo[t, :, cols] = result.astype(BF16)
        sums[6:7, cols] = column_sum(gap * gap * live)
        sums[0:1, cols] = column_sum(grad)
    sb[0] = jnp.zeros((16, D), F32)
    sb[0, 6:7, :] = sums[6:7, :]
    sb[0, 0:1, :] = sums[0:1, :]

    def feed_back(w, lo, n):
        def body(j, carry):
            grad = dot_nn(gr[0, w, lo : lo + n, :], ws[j].reshape(D, D))
            grad = grad * slope[j, w, lo : lo + n, :]
            gb[j, w, lo : lo + n, :] = grad.astype(BF16)
            return carry

        lax.fori_loop(0, 2, body, 0)

    def expanded_back(w, lo, n):
        return dot_nt(gb[0, w, lo : lo + n, :], we[0].reshape(D, D)) + dot_nt(
            gb[1, w, lo : lo + n, :], we[1].reshape(D, D)
        )

    def rows_of(ref, width):
        return ref[...].reshape(2 * ROWS, width)

    def weight_grad(g, left, mine, theirs, width, at):
        value = dot_tn(rows_of(left.at[0], D), rows_of(mine, width)) + dot_tn(
            rows_of(left.at[1], D), rows_of(theirs, width)
        )
        gw[g, :, :, at : at + width] = value.reshape(8, 96, width)

    to_x = {}
    to_z = {}

    pair_of = {}

    def pair_rows(k):
        return pl.ds(2 * z_mate(z, k), 2)

    def scatter_pairs(g):
        for i, k in enumerate((2, 1)):
            ps2[g, i] = gw[g, pair_rows(k), :, 640:768].astype(BF16)
            pair_of[g, i] = send(ps2.at[g, i], pr2.at[g, i], z_mates[0])

    parts = {0: ((0, 384), (384, 256)), 1: ((0, 640),), 2: ((0, 640),)}

    def scatter_blocks(g, i, blocks):
        lo, n = parts[g][i]
        for k in blocks:
            xs[g, k, :, lo : lo + n] = gw[g, row_of(k, 1 - x), :, lo : lo + n].astype(BF16)
            at = (g, k, slice(None), pl.ds(lo, n))
            to_x[g, k, i] = send(xs.at[at], xr.at[at], x_mate)

    def scatter_pair(g):
        pair_of[g, 0].wait_recv()
        total = gw[g, pair_rows(3), :, 640:768] + pr2[g, 0].astype(F32)
        ps2[g, 2] = total.astype(BF16)
        pair_of[g, 2] = send(ps2.at[g, 2], pr2.at[g, 2], z_mates[2])

    def scatter_turn(g):
        pair_of[g, 1].wait_recv()
        pair_of[g, 2].wait_recv()
        total = gw[g, pair_rows(0), :, 640:768] + pr2[g, 1].astype(F32)
        ptotal[g] = total + pr2[g, 2].astype(F32)
        pxs[g] = ptotal[g, 1 - x].astype(BF16)
        pair_of[g, 3] = send(pxs.at[g], pxr.at[g], x_mate)

    def scatter_z(g, k, i):
        lo, n = parts[g][i]
        cols = slice(lo, lo + n)
        to_x[g, k, i].wait_recv()
        total = gw[g, row_of(k, x), :, cols] + xr[g, k, :, cols].astype(F32)
        if k == 3:
            to_z[g, 2, i].wait_recv()
            total = total + zr[g, 1, :, cols].astype(F32)
        zs[g, k - 1, :, cols] = total.astype(BF16)
        at = (g, k - 1, slice(None), pl.ds(lo, n))
        to_z[g, k, i] = send(zs.at[at], zr.at[at], z_mates[2 if k == 3 else 0])

    def scatter_end(g, i, out):
        lo, n = parts[g][i]
        cols = slice(lo, lo + n)
        to_x[g, 0, i].wait_recv()
        to_z[g, 1, i].wait_recv()
        to_z[g, 3, i].wait_recv()
        total = gw[g, dp, :, cols] + xr[g, 0, :, cols].astype(F32)
        out[:, cols] = total + zr[g, 0, :, cols].astype(F32) + zr[g, 2, :, cols].astype(F32)

    def scatter_last(g, out):
        pair_of[g, 3].wait_recv()
        out[:, 640:768] = ptotal[g, x] + pxr[g].astype(F32)

    def scatter_add(g, *keys):
        steps = {"pair": scatter_pair, "turn": scatter_turn}
        for key in keys:
            if key in steps:
                add((key + "s", g), steps[key], g)
            else:
                add(("zs", g, *key), scatter_z, g, *key)

    for lo, n in CHUNKS:
        feed_back(0, lo, n)
    for i in range(2):
        e4[i].wait_recv()
        gr_c.append(send(gr.at[0, 1, :, halves[i]], gr.at[1, 1, :, halves[i]], c_mate))
    e5 = []
    for lo, n in CHUNKS:
        rows = pl.ds(lo, n)
        feed_back(1, lo, n)
        es[1, lo : lo + n, :] = expanded_back(1, lo, n).astype(BF16)
        e5.append(send(es.at[1, rows], er.at[1, rows], y_mate))
    gb_copy = send(gb.at[1], gbr, c_mate)
    mid[...] = expanded_back(0, 0, ROWS)
    for copy in gr_c:
        copy.wait_recv()
    hid_copy.wait_recv()
    weight_grad(2, gr, hid.at[0], hidr, D, 0)
    scatter_pairs(2)
    scatter_blocks(2, 0, (2, 3, 1, 0))
    scatter_add(2, "pair", (2, 0), "turn", (3, 0), (1, 0))
    point()

    e6 = []
    gm_c = []
    gain_part = jnp.zeros((1, D), F32)
    shift_part = jnp.zeros((1, D), F32)
    bias_part = jnp.zeros((1, D), F32)
    for i, (lo, n) in enumerate(CHUNKS):
        rows = pl.ds(lo, n)
        point()
        e5[i].wait_recv()
        grad = mid[lo : lo + n, :] + er[1, lo : lo + n, :].astype(F32)
        unit = unit2[lo : lo + n, :]
        gain_part = gain_part + column_sum(grad * unit)
        shift_part = shift_part + column_sum(grad)
        grad = acc[lo : lo + n, :] + normalize_back(grad, unit, inv2[lo : lo + n, :], gain2)
        acc[lo : lo + n, :] = grad
        gm[0, 0, lo : lo + n, :] = grad.astype(BF16)
        e6.append(send(gm.at[0, 0, rows], gm.at[0, 1, rows], y_mate))
        gm_c.append(send(gm.at[0, 0, rows], gm.at[1, 0, rows], c_mate))
        bias_part = bias_part + column_sum(grad)
    sb[0, 1:2, :] = gain_part
    sb[0, 2:3, :] = shift_part
    sb[0, 3:4, :] = bias_part

    bo_y = send(bo.at[t], bo.at[t], y_mate)
    bo_c = [send(bo.at[t], bo.at[t], c_mate)]

    def block_pass():
        bo_y.wait_recv()
        bo_c.append(send(bo.at[peer_window], bo.at[peer_window], c_mate))

    def block_mix():
        for copy in bo_c:
            copy.wait_recv()
        for w in range(4):
            mix[:, w, :] = bo[w, 0:WIN_TOK, :].astype(F32)
        xt[...] = mix[...].astype(BF16)
        stores.append(load(xt, block_out))

    stores = []
    gb_copy.wait_recv()
    for copy in n2_c:
        copy.wait_recv()
    weight_grad(1, n2, gb.at[0], gbr, D, 0)
    ones = jnp.ones((8, 2 * ROWS), BF16)
    sb[0, 8:9, :] = (dot_nn(ones, rows_of(gb.at[0], D)) + dot_nn(ones, rows_of(gbr, D)))[0:1]
    scatter_pairs(1)
    scatter_blocks(1, 0, (2, 3, 1, 0))
    scatter_add(1, "pair", (2, 0), "turn", (3, 0), (1, 0))
    point()

    def mixed_back(w, lo, n):
        for j in range(2):
            grad = dot_nn(gm[0, w, lo : lo + n, :], wa[j, :, :, 512:768].reshape(D, 256))
            gmx[j, w, lo : lo + n, :] = grad.astype(BF16)

    def unit_back(w, j, h):
        query, key, value = unit_of(w, j, h)
        p, pv = UNITS[h][3:]
        grad = gmx[j, w, :, 0:128] if h == 2 else gmx[j, w, :, 128:256]
        soft = ps[w, j, h]
        grad_soft = dot_nt(grad, value)
        delta = jnp.sum(soft * grad_soft, axis=-1, keepdims=True)
        grad_scores = (soft * (grad_soft - delta)).astype(BF16)
        grad_v = dot_tn(soft.astype(BF16), grad * half[pv])[0:ROWS]
        grad_k = dot_tn(grad_scores, query * key_mask[p])[0:ROWS]
        part = (dot_nt(grad_scores, pick[...]) * place[...]).astype(BF16)
        grad_q = dot_nn(grad_scores, key) + dot_nn(part, t2[p])
        tg[...] += dot_tn(query * half[p], part)
        point()
        return grad_q, grad_k, grad_v

    def attend_back_pair(w, j):
        one, two = unit_back(w, j, 0), unit_back(w, j, 1)
        for i in range(3):
            gp[j, w, :, 128 * i : 128 * i + 128] = (one[i] + two[i]).astype(BF16)

    def attend_back_last(w, j):
        grad_q, grad_k, grad_v = unit_back(w, j, 2)
        gp[j, w, :, 384:512] = (grad_q + pltpu.roll(grad_k, 64, 1)).astype(BF16)
        gp[j, w, :, 512:640] = pltpu.roll(grad_v, 64, 1).astype(BF16)

    def projected_back(w, lo, n):
        return dot_nt(gp[0, w, lo : lo + n, :], wa[0, :, :, 0:640].reshape(D, 640)) + dot_nt(
            gp[1, w, lo : lo + n, :], wa[1, :, :, 0:640].reshape(D, 640)
        )

    for i, (lo, n) in enumerate(CHUNKS):
        rows = pl.ds(lo, n)
        point()
        e6[i].wait_recv()
        gm_c.append(send(gm.at[0, 1, rows], gm.at[1, 1, rows], c_mate))
        mixed_back(1, lo, n)
    point()
    add(("block pass",), block_pass)
    add(("block mix",), block_mix)
    for j in range(2):
        attend_back_pair(1, j)
        attend_back_last(1, j)
    gp_copies = [send(gp.at[1, 1], gpr.at[1], c_mate)]
    e7 = []
    for lo, n in CHUNKS:
        rows = pl.ds(lo, n)
        es[2, lo : lo + n, :] = projected_back(1, lo, n).astype(BF16)
        e7.append(send(es.at[2, rows], er.at[2, rows], y_mate))
    point()
    for copy in gm_c:
        copy.wait_recv()
    mx_copy.wait_recv()
    value = dot_tn(rows_of(gm.at[0], D), rows_of(mx.at[0], 256)) + dot_tn(
        rows_of(gm.at[1], D), rows_of(mxr, 256)
    )
    gw[0, :, :, 512:768] = value.reshape(8, 96, 256)
    scatter_pairs(0)
    scatter_add(0, "pair", "turn")
    point()
    mixed_back(0, 0, ROWS)
    for j in range(2):
        attend_back_pair(0, j)
    gp_copies.append(send(gp.at[1, 0, :, pl.ds(0, 384)], gpr.at[0, :, pl.ds(0, 384)], c_mate))
    attend_back_last(0, 0)
    n1_copy.wait_recv()
    for copy in gp_copies:
        copy.wait_recv()

    def triple_grad(lo, n):
        value = dot_tn(rows_of(n1.at[0], D), gp[0, :, :, lo : lo + n].reshape(2 * ROWS, n))
        value = value + dot_tn(rows_of(n1.at[1], D), gpr[:, :, lo : lo + n].reshape(2 * ROWS, n))
        return value.reshape(8, 96, n)

    gw[0, :, :, 0:384] = triple_grad(0, 384)
    scatter_blocks(0, 0, (2, 3, 1, 0))
    scatter_add(0, (2, 0))
    attend_back_last(0, 1)
    last_copy = send(gp.at[1, 0, :, pl.ds(384, 256)], gpr.at[0, :, pl.ds(384, 256)], c_mate)
    mid[...] = projected_back(0, 0, ROWS)
    last_copy.wait_recv()
    value = triple_grad(384, 256)
    gw[0, :, :, 384:512] = value[:, :, 0:128]
    gw[0, :, :, 512:640] += value[:, :, 128:256]
    need(("turns", 0))
    scatter_blocks(0, 1, (2, 3, 1, 0))

    small = {}

    def small_first():
        bias = dot_nn(ones, rows_of(gp.at[0], 640)) + dot_nn(ones, rows_of(gpr, 640))
        sb[0, 9:10, 0:640] = bias[0:1]
        spread = tg[...]
        spread_high = spread.astype(BF16)
        spread_low = (spread - spread_high.astype(F32)).astype(BF16)
        table = dot_nn(spread_high, onehot[...]) + dot_nn(spread_low, onehot[...])
        tb[0] = table[0:64] + table[64:128]

    top = pl.ds(0, 8)

    def small_send(stage, dst, mate, rows):
        return [
            send(sb.at[stage, rows], sbr.at[dst, rows], mate),
            send(tb.at[stage], tbr.at[dst], mate),
        ]

    def small_wait(stage):
        for copy in small[stage]:
            copy.wait_recv()

    def small_z():
        small[0] = sum((small_send(0, k - 1, z_mates[k - 1], pl.ds(0, 16)) for k in (1, 2, 3)), [])

    def small_c():
        small_wait(0)
        sb[1] = (sb[0] + sbr[0]) + (sbr[1] + sbr[2])
        tb[1] = (tb[0] + tbr[0]) + (tbr[1] + tbr[2])
        small[1] = small_send(1, 3, c_mate, top)

    def small_next(stage, mate, rows):
        small_wait(stage - 1)
        sb[stage] = sb[stage - 1]
        sb[stage, 0:8, :] = sb[stage - 1, 0:8, :] + sbr[stage + 1, 0:8, :]
        tb[stage] = tb[stage - 1] + tbr[stage + 1]
        small[stage] = small_send(stage, stage + 2, mate, rows)

    def small_end():
        small_wait(3)
        total = sb[3] + sbr[5]
        small_out[...] = total
        small_out[6:7, :] = jnp.broadcast_to(
            jnp.sum(total[6:7, :], axis=1, keepdims=True) / (count * float(D)), (1, D)
        )
        table_out[...] = (tb[3] + tbr[5]).T

    e8 = {}
    ig_c = {}

    def mix_in(window, i):
        lo, n = CHUNKS[i]
        top = min(lo + n, WIN_TOK)
        mix[lo:top, pl.ds(window, 1), :] = (
            ig[window, lo:top, :].astype(F32).reshape(top - lo, 1, D)
        )

    def own_grad(i):
        lo, n = CHUNKS[i]
        e7[i].wait_recv()
        grad = mid[lo : lo + n, :] + er[2, lo : lo + n, :].astype(F32)
        unit = unit1[lo : lo + n, :]
        gain_part = column_sum(grad * unit)
        shift_part = column_sum(grad)
        sb[0, 4:5, :] = gain_part if i == 0 else sb[0, 4:5, :] + gain_part
        sb[0, 5:6, :] = shift_part if i == 0 else sb[0, 5:6, :] + shift_part
        grad = acc[lo : lo + n, :] + normalize_back(grad, unit, inv1[lo : lo + n, :], gain1)
        ig[t, lo : lo + n, :] = grad.astype(BF16)
        rows = pl.ds(lo, n)
        ig_c[i, 0] = send(ig.at[t, rows], ig.at[t, rows], c_mate)
        e8[i] = send(ig.at[t, rows], ig.at[t, rows], y_mate)
        mix_in(t, i)

    def side_grad(i):
        ig_c[i, 0].wait_recv()
        mix_in(t + 1 - 2 * c, i)

    def peer_grad(i):
        lo, n = CHUNKS[i]
        rows = pl.ds(lo, n)
        e8[i].wait_recv()
        ig_c[i, 1] = send(ig.at[peer_window, rows], ig.at[peer_window, rows], c_mate)
        mix_in(peer_window, i)

    def last_grad(i):
        lo, n = CHUNKS[i]
        ig_c[i, 1].wait_recv()
        mix_in(peer_window + 1 - 2 * c, i)
        rows = pl.ds(lo, min(n, WIN_TOK - lo))
        stores.append(load(mix.at[rows], grad_out.at[rows]))

    def scatter_out(g, held, out):
        if g > 0:
            scatter_end(g, 0, held)
        else:
            scatter_end(0, 1, held)
        scatter_last(g, held)
        stores.append(load(held, out))

    need(("block mix",))
    add(("own", 0), own_grad, 0)
    add(("small first",), small_first)
    add(("own", 1), own_grad, 1)
    add(("small z",), small_z)
    scatter_add(0, (3, 0), (2, 1), (1, 0))
    add(("side", 0), side_grad, 0)
    add(("side", 1), side_grad, 1)
    add(("small c",), small_c)
    add(("out", 2), scatter_out, 2, gs, gs_out)
    add(("out", 1), scatter_out, 1, ge, ge_out)
    add(("small y",), small_next, 2, y_mate, top)
    add(("peer", 0), peer_grad, 0)
    scatter_add(0, (3, 1), (1, 1))
    add(("last", 0), last_grad, 0)
    add(("small x",), small_next, 3, x_mate, pl.ds(0, 16))
    add(("peer", 1), peer_grad, 1)
    add(("last", 1), last_grad, 1)
    add(("end", 0), scatter_end, 0, 0, ga)
    add(("out", 0), scatter_out, 0, ga, ga_out)
    add(("small end",), small_end)
    need(("small end",))
    for copy in started:
        copy.wait_send()
    for copy in stores:
        copy.wait()


def finish_kernel(
    block_in,
    grad_in,
    ga,
    ge,
    gs,
    small,
    table,
    block_out,
    loss_out,
    grad_out,
    gain1_out,
    shift1_out,
    triple_out,
    qv_out,
    out_w_out,
    out_b_out,
    gain2_out,
    shift2_out,
    we_out,
    expand_bias_out,
    ws_out,
    bias_shrink_out,
    rows_out,
    columns_out,
    block_hold,
    grad_hold,
    ge_hold,
    gs_hold,
    sems,
):
    moves = []
    at = 0
    for src, hold, dst, step in (
        (block_in, block_hold, block_out, 49),
        (grad_in, grad_hold, grad_out, 49),
        (ge, ge_hold, we_out, 96),
        (gs, gs_hold, ws_out, 96),
    ):
        for lo in range(0, src.shape[0], step):
            rows = pl.ds(lo, step)
            copy = pltpu.make_async_copy(src.at[rows], hold.at[rows], sems.at[at])
            copy.start()
            moves.append(
                (copy, pltpu.make_async_copy(hold.at[rows], dst.at[rows], sems.at[at + 1]))
            )
            at += 2
    for i in range(3):
        triple_out[i, :, 0:128] = ga[:, 128 * i : 128 * i + 128]
    triple_out[0, :, 128:192] = ga[:, 384:448]
    triple_out[1, :, 128:192] = pltpu.roll(ga[:, 384:512], 64, 1)[:, 0:64]
    triple_out[2, :, 128:192] = ga[:, 512:576]
    out_w_out[0:128, :] = ga[:, 640:768].T
    out_w_out[128:192, :] = ga[:, 512:640].T[64:128]
    loss_out[...] = small[6:7, 0:1]
    for i, out in enumerate(
        (bias_shrink_out, gain2_out, shift2_out, out_b_out, gain1_out, shift1_out)
    ):
        out[...] = small[i]
    expand_bias_out[...] = small[8]
    for i in range(2):
        qv_out[i : i + 1, 0:128] = small[9:10, 256 * i : 256 * i + 128]
        qv_out[i : i + 1, 128:192] = small[9:10, 384 + 128 * i : 448 + 128 * i]
    rows_out[...] = table[0:27]
    columns_out[...] = table[32:59]
    for arrive, leave in moves:
        arrive.wait()
        leave.start()
    for arrive, leave in moves:
        leave.wait()


def fused(
    inputs,
    target,
    valid,
    first_gain,
    first_shift,
    triple_weight,
    query_value_bias,
    output_weight,
    output_bias,
    second_gain,
    second_shift,
    expand_weight,
    expand_bias,
    shrink_weight,
    shrink_bias,
    rows_table,
    columns_table,
):
    vmem = pl.BlockSpec(memory_space=pltpu.VMEM)
    anywhere = pl.BlockSpec(memory_space=pl.ANY)
    mixed_shape = (WIN_TOK, 4, D)
    part = jax.ShapeDtypeStruct((96, D), F32)
    copies = 224
    parts = pl.pallas_call(
        block_kernel,
        out_shape=[
            jax.ShapeDtypeStruct(mixed_shape, BF16),
            jax.ShapeDtypeStruct(mixed_shape, F32),
            part,
            part,
            part,
            jax.ShapeDtypeStruct((16, D), F32),
            jax.ShapeDtypeStruct((64, 64), F32),
        ],
        in_specs=[anywhere] * 17,
        out_specs=[anywhere] * 5 + [vmem] * 2,
        scratch_shapes=[
            pltpu.VMEM(valid.shape, jnp.int32),
            pltpu.VMEM((D,), F32),
            pltpu.VMEM((D,), F32),
            pltpu.VMEM(triple_weight.shape, BF16),
            pltpu.VMEM(query_value_bias.shape, F32),
            pltpu.VMEM(output_weight.shape, BF16),
            pltpu.VMEM((D,), F32),
            pltpu.VMEM((D,), F32),
            pltpu.VMEM((D,), F32),
            pltpu.VMEM(expand_weight.shape, BF16),
            pltpu.VMEM(expand_bias.shape, F32),
            pltpu.VMEM(expand_weight.shape, BF16),
            pltpu.VMEM((D,), F32),
            pltpu.VMEM(rows_table.shape, F32),
            pltpu.VMEM(columns_table.shape, F32),
            pltpu.VMEM((96, D), BF16),
            pltpu.VMEM((2, 8, 96, D), BF16),
            pltpu.VMEM((2, 8, 96, D), BF16),
            pltpu.VMEM((2, 8, 96, D), BF16),
            pltpu.VMEM(mixed_shape, BF16),
            pltpu.VMEM(mixed_shape, BF16),
            pltpu.VMEM((512, 64), BF16),
            pltpu.VMEM((ROWS, 512), F32),
            pltpu.VMEM((512, KEYS), BF16),
            pltpu.VMEM((64, 128), F32),
            pltpu.VMEM((4, ROWS, D), BF16),
            pltpu.VMEM((4, ROWS, D), BF16),
            pltpu.VMEM(mixed_shape, F32),
            pltpu.VMEM((96, D), F32),
            pltpu.VMEM((96, D), F32),
            pltpu.VMEM((96, D), F32),
            pltpu.VMEM((2, 8, D), F32),
            pltpu.VMEM((2, ROWS, D), F32),
            pltpu.VMEM((ROWS, D), F32),
            pltpu.VMEM((ROWS, D), F32),
            pltpu.VMEM((ROWS, 1), F32),
            pltpu.VMEM((ROWS, 1), F32),
            pltpu.VMEM((ROWS, D), F32),
            pltpu.VMEM((ROWS, D), F32),
            pltpu.VMEM((2, 2, ROWS, D), BF16),
            pltpu.VMEM((2, 2, ROWS, D), BF16),
            pltpu.VMEM((2, 2, ROWS, D), BF16),
            pltpu.VMEM((2, 2, ROWS, D), BF16),
            pltpu.VMEM((2, 2, KEYS, 896), BF16),
            pltpu.VMEM((2, 2, 3, ROWS, KEYS), F32),
            pltpu.VMEM((2, 2, ROWS, 256), BF16),
            pltpu.VMEM((2, ROWS, 256), BF16),
            pltpu.VMEM((2, 2, ROWS, D), BF16),
            pltpu.VMEM((2, ROWS, D), BF16),
            pltpu.VMEM((2, 2, ROWS, D), F32),
            pltpu.VMEM((2, 2, ROWS, D), BF16),
            pltpu.VMEM((2, ROWS, D), BF16),
            pltpu.VMEM((2, 2, ROWS, 256), BF16),
            pltpu.VMEM((2, 2, ROWS, 640), BF16),
            pltpu.VMEM((2, ROWS, 640), BF16),
            pltpu.VMEM((2, 512, 128), BF16),
            pltpu.VMEM((128, 512), F32),
            pltpu.VMEM((3, ROWS, D), BF16),
            pltpu.VMEM((3, ROWS, D), BF16),
            pltpu.VMEM((2, ROWS, 384), BF16),
            pltpu.VMEM((2, ROWS, 384), BF16),
            pltpu.VMEM((8, D), F32),
            pltpu.VMEM((1, D), F32),
            pltpu.VMEM((3, 8, 96, D), F32),
            pltpu.VMEM((3, 4, 96, 640), BF16),
            pltpu.VMEM((3, 4, 96, 640), BF16),
            pltpu.VMEM((3, 3, 96, 640), BF16),
            pltpu.VMEM((3, 3, 96, 640), BF16),
            pltpu.VMEM((3, 3, 2, 96, 128), BF16),
            pltpu.VMEM((3, 3, 2, 96, 128), BF16),
            pltpu.VMEM((3, 2, 96, 128), F32),
            pltpu.VMEM((3, 96, 128), BF16),
            pltpu.VMEM((3, 96, 128), BF16),
            pltpu.VMEM((2, 8, 128), F32),
            pltpu.VMEM((4, 8, 128), F32),
            pltpu.VMEM((4, 16, D), F32),
            pltpu.VMEM((6, 16, D), F32),
            pltpu.VMEM((4, 64, 64), F32),
            pltpu.VMEM((6, 64, 64), F32),
            pltpu.SemaphoreType.DMA((32,)),
            pltpu.SemaphoreType.DMA((copies,)),
            pltpu.SemaphoreType.DMA((copies,)),
        ],
        compiler_params=pltpu.CompilerParams(
            collective_id=0, has_side_effects=True, vmem_limit_bytes=60 << 20
        ),
    )(
        inputs.transpose(1, 0, 2),
        target.transpose(1, 0, 2),
        valid,
        first_gain,
        first_shift,
        triple_weight,
        query_value_bias,
        output_weight,
        output_bias,
        second_gain,
        second_shift,
        expand_weight,
        expand_bias,
        shrink_weight.T,
        shrink_bias,
        rows_table,
        columns_table,
    )
    vector = jax.ShapeDtypeStruct((D,), F32)
    relative = jax.ShapeDtypeStruct(rows_table.shape, F32)
    outs = pl.pallas_call(
        finish_kernel,
        out_shape=[
            jax.ShapeDtypeStruct(mixed_shape, BF16),
            jax.ShapeDtypeStruct((1, 1), F32),
            jax.ShapeDtypeStruct(mixed_shape, F32),
            vector,
            vector,
            jax.ShapeDtypeStruct(triple_weight.shape, F32),
            jax.ShapeDtypeStruct(query_value_bias.shape, F32),
            jax.ShapeDtypeStruct(output_weight.shape, F32),
            vector,
            vector,
            vector,
            part,
            jax.ShapeDtypeStruct(expand_bias.shape, F32),
            part,
            vector,
            relative,
            relative,
        ],
        in_specs=[anywhere] * 2 + [vmem, anywhere, anywhere] + [vmem] * 2,
        out_specs=[
            anywhere if i in (0, 2, 11, 13) else vmem for i in range(17)
        ],
        scratch_shapes=[
            pltpu.VMEM(mixed_shape, BF16),
            pltpu.VMEM(mixed_shape, F32),
            pltpu.VMEM((96, D), F32),
            pltpu.VMEM((96, D), F32),
            pltpu.SemaphoreType.DMA((20,)),
        ],
    )(*parts)
    outs = list(outs)
    outs[0] = outs[0].transpose(1, 0, 2)
    outs[1] = outs[1].reshape(())
    outs[2] = outs[2].transpose(1, 0, 2)
    outs[13] = outs[13].T
    return tuple(outs)


def solution(mesh):
    placed = (
        P("dp", None, None),
        P("dp", None, None),
        P("dp", None),
        P(),
        P(),
        P(None, "dp", "tensor"),
        P(None, "tensor"),
        P("tensor", "dp"),
        P(),
        P(),
        P(),
        P("dp", "tensor"),
        P("tensor"),
        P("tensor", "dp"),
        P(),
        P(),
        P(),
    )
    on_slice = mesh.shape["dp"] == 8 and mesh.shape["tensor"] == 4
    return jax.shard_map(
        fused if on_slice else shards,
        mesh=mesh,
        in_specs=placed,
        out_specs=(
            P("dp", None, None),
            P(),
            P("dp", None, None),
            P(),
            P(),
            P(None, "dp", "tensor"),
            P(None, "tensor"),
            P("tensor", "dp"),
            P(),
            P(),
            P(),
            P("dp", "tensor"),
            P("tensor"),
            P("tensor", "dp"),
            P(),
            P(),
            P(),
        ),
        check_vma=False,
    )
```

```python
import math

import jax
import jax.numpy as jnp
import numpy as np
from jax import lax
from jax.experimental import pallas as pl
from jax.experimental.pallas import tpu as pltpu
from jax.sharding import PartitionSpec as P

MESH = pl.DeviceIdType.MESH

D = 768
HEADS = 12
HEAD = 64
WIN = 14
WIN_TOK = 196
MICRO = 2


def normalize(values):
    center = jnp.mean(values, axis=-1, keepdims=True)
    centered = values - center
    spread = jnp.mean(centered * centered, axis=-1, keepdims=True)
    inverse = lax.rsqrt(spread + 1e-06)
    return (centered * inverse, inverse)


def normalize_back(grad_out, unit, inverse, gain):
    scaled = grad_out * gain
    mean_one = jnp.mean(scaled, axis=-1, keepdims=True)
    mean_two = jnp.mean(scaled * unit, axis=-1, keepdims=True)
    return inverse * (scaled - mean_one - unit * mean_two)


def position_select(side):
    shape = (side, side, 2 * side - 1)
    first = lax.broadcasted_iota(jnp.int32, shape, 0)
    second = lax.broadcasted_iota(jnp.int32, shape, 1)
    slots = lax.broadcasted_iota(jnp.int32, shape, 2)
    return (slots == first - second + side - 1).astype(jnp.bfloat16)


def score_block(queries, keys, table_rows, table_cols, scale_factor):
    groups = queries.shape[0]
    side = queries.shape[1]
    heads = queries.shape[3]
    along_rows = jnp.einsum(
        "gabnc,aec->gnabe", queries, table_rows, preferred_element_type=jnp.float32
    )
    along_cols = jnp.einsum(
        "gabnc,bfc->gnabf", queries, table_cols, preferred_element_type=jnp.float32
    )
    scores = (
        jnp.einsum("gabnc,gefnc->gnabef", queries, keys, preferred_element_type=jnp.float32)
        * scale_factor
    )
    scores = scores + along_rows[..., :, None] + along_cols[..., None, :]
    return scores.reshape(groups, heads, side * side, side * side)


def gelu_exact(inner):
    return jax.nn.gelu(inner, approximate=False)


def row_total(partial_value):
    return lax.psum(partial_value, "tensor")


def share_of(values):
    share_rows = values.shape[0] // lax.axis_size("tensor")
    return lax.dynamic_slice_in_dim(values, lax.axis_index("tensor") * share_rows, share_rows, 0)


def shards(
    inputs,
    target,
    valid,
    first_gain,
    first_shift,
    triple_weight,
    query_value_bias,
    output_weight,
    output_bias,
    second_gain,
    second_shift,
    expand_weight,
    expand_bias,
    shrink_weight,
    shrink_bias,
    rows_table,
    columns_table,
):
    local_heads = HEADS // lax.axis_size("tensor")
    local_width = local_heads * HEAD
    local_windows = inputs.shape[0]
    win_micro = local_windows // MICRO
    micro_rows = win_micro * WIN_TOK
    scale_factor = 1.0 / math.sqrt(HEAD)
    highest = lax.Precision.HIGHEST
    live = valid.astype(jnp.float32)
    select = position_select(WIN)
    table_rows = jnp.einsum(
        "aej,jc->aec", select, rows_table.astype(jnp.bfloat16), preferred_element_type=jnp.float32
    ).astype(jnp.bfloat16)
    table_cols = jnp.einsum(
        "aej,jc->aec",
        select,
        columns_table.astype(jnp.bfloat16),
        preferred_element_type=jnp.float32,
    ).astype(jnp.bfloat16)
    rows_float = table_rows.astype(jnp.float32)
    cols_float = table_cols.astype(jnp.float32)
    triple_bias = jnp.stack(
        [query_value_bias[0], jnp.zeros_like(query_value_bias[0]), query_value_bias[1]]
    )
    saved = []
    outputs = []
    local_loss = jnp.zeros((), jnp.float32)
    for micro in range(MICRO):
        gathered = (
            lax.all_gather(triple_weight, "dp", axis=1, tiled=True),
            lax.all_gather(output_weight, "dp", axis=1, tiled=True),
            lax.all_gather(expand_weight, "dp", axis=0, tiled=True),
            lax.all_gather(shrink_weight, "dp", axis=1, tiled=True),
        )
        full_triple, full_output, full_expand, full_shrink = gathered
        lower = micro * win_micro
        flat_rows = inputs[lower : lower + win_micro].reshape(micro_rows, D).astype(jnp.float32)
        unit_one, inverse_one = normalize(flat_rows)
        normed = (unit_one * first_gain + first_shift).astype(jnp.bfloat16)
        projected = (
            jnp.einsum("rd,tde->rte", normed, full_triple, preferred_element_type=jnp.float32)
            + triple_bias
        )
        projected = projected.astype(jnp.bfloat16)
        split = projected.reshape(win_micro, WIN, WIN, 3, local_heads, HEAD)
        queries = split[:, :, :, 0]
        keys = split[:, :, :, 1]
        values = split[:, :, :, 2].reshape(win_micro, WIN_TOK, local_heads, HEAD)
        scores = score_block(queries, keys, table_rows, table_cols, scale_factor)
        peak = jnp.max(scores, axis=-1, keepdims=True)
        raised = jnp.exp(scores - peak)
        denominator = jnp.sum(raised, axis=-1, keepdims=True)
        log_total = peak + jnp.log(denominator)
        softmaxed = (raised / denominator).astype(jnp.bfloat16)
        mixed = jnp.einsum("gnqk,gknc->gqnc", softmaxed, values, preferred_element_type=jnp.float32)
        mixed = mixed.reshape(micro_rows, local_width).astype(jnp.bfloat16)
        partial_attended = jnp.dot(mixed, full_output, preferred_element_type=jnp.float32)
        middle = flat_rows + (row_total(partial_attended) + output_bias)
        unit_two, inverse_two = normalize(middle)
        normed_two = (unit_two * second_gain + second_shift).astype(jnp.bfloat16)
        before = jnp.dot(normed_two, full_expand, preferred_element_type=jnp.float32) + expand_bias
        hidden = gelu_exact(before).astype(jnp.bfloat16)
        partial_shrunk = jnp.dot(hidden, full_shrink, preferred_element_type=jnp.float32)
        result = middle + (row_total(partial_shrunk) + shrink_bias)
        aim = target[lower : lower + win_micro].reshape(micro_rows, D).astype(jnp.float32)
        marks = live[lower : lower + win_micro].reshape(micro_rows, 1)
        weighted_gap = marks * (result - aim)
        local_loss = local_loss + jnp.sum(weighted_gap * (result - aim))
        outputs.append(result.astype(jnp.bfloat16).reshape(win_micro, WIN_TOK, D))
        saved.append(
            (
                unit_one,
                inverse_one,
                normed,
                projected,
                log_total,
                mixed,
                unit_two,
                inverse_two,
                normed_two,
                before,
                hidden,
                weighted_gap,
            )
        )
    loss_total, count = lax.psum((local_loss, jnp.sum(live)), "dp")
    loss = loss_total / (count * D)
    grad_scale = local_windows * WIN_TOK * lax.axis_size("dp") / count
    triple_acc = jnp.zeros((3, D, local_width), jnp.float32)
    output_acc = jnp.zeros((local_width, D), jnp.float32)
    expand_acc = jnp.zeros((D, full_expand.shape[1]), jnp.float32)
    shrink_acc = jnp.zeros((full_shrink.shape[0], D), jnp.float32)
    first_gain_acc = jnp.zeros((D,), jnp.float32)
    first_shift_acc = jnp.zeros((D,), jnp.float32)
    second_gain_acc = jnp.zeros((D,), jnp.float32)
    second_shift_acc = jnp.zeros((D,), jnp.float32)
    output_bias_acc = jnp.zeros((D,), jnp.float32)
    shrink_bias_acc = jnp.zeros((D,), jnp.float32)
    expand_bias_acc = jnp.zeros((full_expand.shape[1],), jnp.float32)
    query_value_acc = jnp.zeros((2, local_width), jnp.float32)
    rows_expanded_acc = jnp.zeros((WIN, WIN, HEAD), jnp.float32)
    cols_expanded_acc = jnp.zeros((WIN, WIN, HEAD), jnp.float32)
    input_grads = []
    for micro in range(MICRO):
        gathered = (
            lax.all_gather(triple_weight, "dp", axis=1, tiled=True),
            lax.all_gather(output_weight, "dp", axis=1, tiled=True),
            lax.all_gather(expand_weight, "dp", axis=0, tiled=True),
            lax.all_gather(shrink_weight, "dp", axis=1, tiled=True),
        )
        full_triple, full_output, full_expand, full_shrink = gathered
        (
            unit_one,
            inverse_one,
            normed,
            projected,
            log_total,
            mixed,
            unit_two,
            inverse_two,
            normed_two,
            before,
            hidden,
            weighted_gap,
        ) = saved[micro]
        grad_result = grad_scale * weighted_gap
        shrink_bias_acc = shrink_bias_acc + jnp.sum(share_of(grad_result), axis=0)
        grad_result_low = grad_result.astype(jnp.bfloat16)
        shrink_acc = shrink_acc + jnp.einsum(
            "rf,rd->fd", hidden, grad_result_low, preferred_element_type=jnp.float32
        )
        grad_hidden = jnp.einsum(
            "rd,fd->rf", grad_result_low, full_shrink, preferred_element_type=jnp.float32
        )
        unused, gelu_pull = jax.vjp(gelu_exact, before)
        grad_before = gelu_pull(grad_hidden)[0].astype(jnp.bfloat16)
        expand_bias_acc = expand_bias_acc + jnp.sum(grad_before.astype(jnp.float32), axis=0)
        expand_acc = expand_acc + jnp.einsum(
            "rd,rf->df", normed_two, grad_before, preferred_element_type=jnp.float32
        )
        partial_two = jnp.einsum(
            "rf,df->rd", grad_before, full_expand, preferred_element_type=jnp.float32
        )
        grad_normed_two = row_total(partial_two)
        grad_middle = grad_result + normalize_back(
            grad_normed_two, unit_two, inverse_two, second_gain
        )
        second_gain_acc = second_gain_acc + jnp.sum(share_of(grad_normed_two * unit_two), axis=0)
        second_shift_acc = second_shift_acc + jnp.sum(share_of(grad_normed_two), axis=0)
        output_bias_acc = output_bias_acc + jnp.sum(share_of(grad_middle), axis=0)
        grad_middle_low = grad_middle.astype(jnp.bfloat16)
        output_acc = output_acc + jnp.einsum(
            "rc,rd->cd", mixed, grad_middle_low, preferred_element_type=jnp.float32
        )
        grad_mixed = jnp.einsum(
            "rd,cd->rc", grad_middle_low, full_output, preferred_element_type=jnp.float32
        )
        grad_mixed = grad_mixed.astype(jnp.bfloat16).reshape(win_micro, WIN_TOK, local_heads, HEAD)
        split = projected.reshape(win_micro, WIN, WIN, 3, local_heads, HEAD)
        queries = split[:, :, :, 0]
        keys = split[:, :, :, 1]
        queries_flat = queries.reshape(win_micro, WIN_TOK, local_heads, HEAD)
        keys_flat = keys.reshape(win_micro, WIN_TOK, local_heads, HEAD)
        values = split[:, :, :, 2].reshape(win_micro, WIN_TOK, local_heads, HEAD)
        scores = score_block(queries, keys, table_rows, table_cols, scale_factor)
        softmax_exact = jnp.exp(scores - log_total)
        grad_soft = jnp.einsum(
            "gqnc,gknc->gnqk", grad_mixed, values, preferred_element_type=jnp.float32
        )
        delta = jnp.sum(softmax_exact * grad_soft, axis=-1, keepdims=True)
        grad_scores = (softmax_exact * (grad_soft - delta)).astype(jnp.bfloat16)
        grad_values = jnp.einsum(
            "gnqk,gqnc->gknc",
            softmax_exact.astype(jnp.bfloat16),
            grad_mixed,
            preferred_element_type=jnp.float32,
        )
        grad_keys = (
            jnp.einsum(
                "gnqk,gqnc->gknc", grad_scores, queries_flat, preferred_element_type=jnp.float32
            )
            * scale_factor
        )
        grad_queries = (
            jnp.einsum(
                "gnqk,gknc->gqnc", grad_scores, keys_flat, preferred_element_type=jnp.float32
            )
            * scale_factor
        )
        grad_grid = grad_scores.astype(jnp.float32).reshape(
            win_micro, local_heads, WIN, WIN, WIN, WIN
        )
        row_part = jnp.sum(grad_grid, axis=5)
        col_part = jnp.sum(grad_grid, axis=4)
        queries_float = queries.astype(jnp.float32)
        rel_queries = jnp.einsum("gnabe,aec->gabnc", row_part, rows_float, precision=highest)
        rel_queries = rel_queries + jnp.einsum(
            "gnabf,bfc->gabnc", col_part, cols_float, precision=highest
        )
        grad_queries = grad_queries + rel_queries.reshape(win_micro, WIN_TOK, local_heads, HEAD)
        rows_expanded_acc = rows_expanded_acc + jnp.einsum(
            "gnabe,gabnc->aec", row_part, queries_float, precision=highest
        )
        cols_expanded_acc = cols_expanded_acc + jnp.einsum(
            "gnabf,gabnc->bfc", col_part, queries_float, precision=highest
        )
        grad_projected = jnp.stack(
            [
                grad_queries.reshape(micro_rows, local_width),
                grad_keys.reshape(micro_rows, local_width),
                grad_values.reshape(micro_rows, local_width),
            ],
            axis=1,
        ).astype(jnp.bfloat16)
        projected_float_sums = jnp.sum(grad_projected.astype(jnp.float32), axis=0)
        query_value_acc = query_value_acc + jnp.stack(
            [projected_float_sums[0], projected_float_sums[2]]
        )
        triple_acc = triple_acc + jnp.einsum(
            "rd,rte->tde", normed, grad_projected, preferred_element_type=jnp.float32
        )
        partial_one = jnp.einsum(
            "rte,tde->rd", grad_projected, full_triple, preferred_element_type=jnp.float32
        )
        grad_normed = row_total(partial_one)
        grad_tokens = grad_middle + normalize_back(grad_normed, unit_one, inverse_one, first_gain)
        first_gain_acc = first_gain_acc + jnp.sum(share_of(grad_normed * unit_one), axis=0)
        first_shift_acc = first_shift_acc + jnp.sum(share_of(grad_normed), axis=0)
        input_grads.append(grad_tokens.reshape(win_micro, WIN_TOK, D))
    select_float = select.astype(jnp.float32)
    rows_table_part = jnp.einsum("aej,aec->jc", select_float, rows_expanded_acc, precision=highest)
    cols_table_part = jnp.einsum("aej,aec->jc", select_float, cols_expanded_acc, precision=highest)
    triple_grad, output_grad, expand_grad, shrink_grad = (
        lax.psum_scatter(triple_acc, "dp", scatter_dimension=1, tiled=True),
        lax.psum_scatter(output_acc, "dp", scatter_dimension=1, tiled=True),
        lax.psum_scatter(expand_acc, "dp", scatter_dimension=0, tiled=True),
        lax.psum_scatter(shrink_acc, "dp", scatter_dimension=1, tiled=True),
    )
    over_heads = lax.psum(
        (
            rows_table_part,
            cols_table_part,
            first_gain_acc,
            first_shift_acc,
            output_bias_acc,
            second_gain_acc,
            second_shift_acc,
            shrink_bias_acc,
        ),
        "tensor",
    )
    summed_small = lax.psum(
        (
            over_heads[0],
            over_heads[1],
            over_heads[2],
            over_heads[3],
            over_heads[4],
            over_heads[5],
            over_heads[6],
            over_heads[7],
            query_value_acc,
            expand_bias_acc,
        ),
        "dp",
    )
    return (
        jnp.concatenate(outputs, axis=0),
        loss,
        jnp.concatenate(input_grads, axis=0),
        summed_small[2],
        summed_small[3],
        triple_grad,
        summed_small[8],
        output_grad,
        summed_small[4],
        summed_small[5],
        summed_small[6],
        expand_grad,
        summed_small[9],
        shrink_grad,
        summed_small[7],
        summed_small[0],
        summed_small[1],
    )


ROWS = 208
KEYS = 256
CHUNKS = ((0, 112), (112, 96))
F32 = jnp.float32
BF16 = jnp.bfloat16


def z_mate(z, k):
    if k == 0:
        return z
    if k == 1:
        return z + 1 - 2 * (z % 2)
    if k == 2:
        return (z + 2) % 4
    return 3 - z


def dot_nn(a, b):
    return lax.dot_general(a, b, (((1,), (0,)), ((), ())), preferred_element_type=F32)


def dot_nt(a, b):
    return lax.dot_general(a, b, (((1,), (1,)), ((), ())), preferred_element_type=F32)


def dot_tn(a, b):
    return lax.dot_general(a, b, (((0,), (0,)), ((), ())), preferred_element_type=F32)


def column_sum(values):
    return jnp.sum(values, axis=0, keepdims=True)


UNITS = ((0, 1, 2, 0, 0), (0, 1, 2, 1, 1), (3, 5, 6, 0, 1))


PLAN = (2, 1, 3, 0, 1, 4, 1, 1, 1, 6, 1, 2, 0, 1, 2, 0, 0, 0, 0, 2, 1, 1, 2, 0, 1, 0, 0, 4, 2)


def block_kernel(
    x_in,
    target_in,
    valid_hbm,
    gain1_hbm,
    shift1_hbm,
    triple_hbm,
    qv_bias_hbm,
    out_w_hbm,
    bias_out_hbm,
    gain2_hbm,
    shift2_hbm,
    we_hbm,
    expand_bias_hbm,
    ws_hbm,
    bias_shrink_hbm,
    rows_hbm,
    columns_hbm,
    block_out,
    grad_out,
    ga_out,
    ge_out,
    gs_out,
    small_out,
    table_out,
    valid_in,
    gain1_in,
    shift1_in,
    triple_in,
    qv_bias_in,
    out_w_in,
    bias_out_in,
    gain2_in,
    shift2_in,
    we_in,
    expand_bias_in,
    ws_in,
    bias_shrink_in,
    rows_in,
    columns_in,
    wa_in,
    wa,
    we,
    ws,
    xt,
    tt,
    onehot,
    place,
    pick,
    tabs,
    bo,
    ig,
    mix,
    ga,
    ge,
    gs,
    side,
    xf,
    unit1,
    unit2,
    inv1,
    inv2,
    mid,
    acc,
    n1,
    n2,
    gr,
    gm,
    pj,
    ps,
    mx,
    mxr,
    hid,
    hidr,
    slope,
    gb,
    gbr,
    gmx,
    gp,
    gpr,
    t2,
    tg,
    es,
    er,
    es3,
    er3,
    sums,
    shrink_row,
    gw,
    xs,
    xr,
    zs,
    zr,
    ps2,
    pr2,
    ptotal,
    pxs,
    pxr,
    cnt,
    cntr,
    sb,
    sbr,
    tb,
    tbr,
    load_sem,
    send_sem,
    recv_sem,
):
    dp = lax.axis_index("dp")
    t = lax.axis_index("tensor")
    z = dp // 2
    x = dp % 2
    y = t // 2
    c = t % 2
    z_mates = [(z_mate(z, k) * 2 + x, t) for k in (1, 2, 3)]
    x_mate = (z * 2 + 1 - x, t)
    y_mate = (dp, (1 - y) * 2 + c)
    c_mate = (dp, y * 2 + 1 - c)
    peer_window = (1 - y) * 2 + c
    token_total = lax.axis_size("dp") * 4 * WIN_TOK

    started = []

    def send(src, dst, mate):
        i = len(started)
        copy = pltpu.make_async_remote_copy(
            src_ref=src,
            dst_ref=dst,
            send_sem=send_sem.at[i],
            recv_sem=recv_sem.at[i],
            device_id=mate,
            device_id_type=MESH,
        )
        copy.start()
        started.append(copy)
        return copy

    barrier = pltpu.get_barrier_semaphore()
    for mate in z_mates + [x_mate, y_mate, c_mate]:
        pl.semaphore_signal(barrier, inc=1, device_id=mate, device_id_type=MESH)

    loads = []

    def load(src, dst):
        copy = pltpu.make_async_copy(src, dst, load_sem.at[len(loads)])
        copy.start()
        loads.append(copy)
        return copy

    first_loads = [load(triple_hbm, triple_in), load(out_w_hbm, out_w_in)]
    group_loads = [load(we_hbm, we_in), load(ws_hbm, ws_in)]
    x_load = load(x_in, xt)
    side_loads = [
        load(src, dst)
        for src, dst in (
            (expand_bias_hbm, expand_bias_in),
            (qv_bias_hbm, qv_bias_in),
            (valid_hbm, valid_in),
            (gain1_hbm, gain1_in),
            (shift1_hbm, shift1_in),
            (bias_out_hbm, bias_out_in),
            (gain2_hbm, gain2_in),
            (shift2_hbm, shift2_in),
            (bias_shrink_hbm, bias_shrink_in),
            (rows_hbm, rows_in),
            (columns_hbm, columns_in),
        )
    ]
    target_load = load(target_in, tt)

    w_in = (wa_in, we_in, ws_in)
    w_full = (wa, we, ws)
    from_z = {}
    from_x = {}
    from_p = {}
    from_c = {}

    def row_of(k, xx):
        return z_mate(z, k) * 2 + xx

    first = pl.ds(0, 640)
    last = pl.ds(640, 128)

    def gather_start(g):
        full = w_full[g]
        from_p[g, 0] = send(w_in[g].at[:, last], full.at[0, dp, :, last], x_mate)
        for k in (3, 1):
            from_z[g, k] = send(w_in[g].at[:, first], full.at[0, dp, :, first], z_mates[k - 1])
        from_x[g, 0] = send(w_in[g].at[:, first], full.at[0, dp, :, first], x_mate)
        from_c[g, 0] = send(w_in[g], full.at[1, dp], c_mate)
        full[0, dp] = w_in[g][...]

    def to_core(g, i, *at):
        from_c[g, i] = send(w_full[g].at[(0,) + at], w_full[g].at[(1,) + at], c_mate)

    def gather_pair(g, k):
        from_p[g, k].wait_recv()
        pair = (pl.ds(2 * z_mate(z, k), 2), slice(None), last)
        block = w_full[g].at[(0,) + pair]
        if k == 0:
            for m in (3, 1):
                from_p[g, m] = send(block, block, z_mates[m - 1])
            to_core(g, 8, row_of(0, 1 - x), slice(None), last)
        else:
            if k == 3:
                from_p[g, 2] = send(block, block, z_mates[0])
            to_core(g, 8 + k, *pair)

    def gather_z(g, k):
        from_z[g, k].wait_recv()
        block = w_full[g].at[0, row_of(k, x), :, first]
        if k == 3:
            from_z[g, 2] = send(block, block, z_mates[0])
        else:
            from_x[g, k] = send(block, block, x_mate)
        to_core(g, k, row_of(k, x), slice(None), first)

    def gather_far(g):
        block = w_full[g].at[0, row_of(3, x), :, first]
        from_x[g, 3] = send(block, block, x_mate)

    def gather_x(g, k):
        from_x[g, k].wait_recv()
        to_core(g, 4 + k, row_of(k, 1 - x), slice(None), first)

    def gather_end(g, far):
        for k in (2, 3, 6, 7, 10, 11) if far else (0, 1, 4, 5, 8, 9):
            from_c[g, k].wait_recv()

    tasks = []
    done = set()
    plan = iter(PLAN)

    def add(key, step, *args):
        tasks.append((key, step, args))

    def serve():
        key, step, args = tasks.pop(0)
        step(*args)
        done.add(key)

    def point():
        for _ in range(next(plan, 0)):
            if tasks:
                serve()

    def need(key):
        while key not in done:
            serve()

    def gather_add(g):
        add(("pair", g, 0), gather_pair, g, 0)
        add(("z", g, 3), gather_z, g, 3)
        if g == 0:
            add(("start", 1), gather_start, 1)
        add(("z", g, 1), gather_z, g, 1)
        add(("far", g), gather_far, g)
        add(("pair", g, 3), gather_pair, g, 3)
        add(("x", g, 0), gather_x, g, 0)
        add(("pair", g, 1), gather_pair, g, 1)
        add(("z", g, 2), gather_z, g, 2)
        if g == 0:
            add(("count",), count_spread)
            add(("start", 2), gather_start, 2)
        add(("x", g, 1), gather_x, g, 1)
        add(("near", g), gather_end, g, False)
        add(("x", g, 3), gather_x, g, 3)
        add(("pair", g, 2), gather_pair, g, 2)
        add(("x", g, 2), gather_x, g, 2)
        add(("all", g), gather_end, g, True)

    cnt_z = []

    def count_spread():
        cnt_x.wait_recv()
        cnt[1] = cnt[0] + cntr[0]
        cnt_z.extend(send(cnt.at[1], cntr.at[k], z_mates[k - 1]) for k in (1, 2, 3))

    for copy in first_loads:
        copy.wait()
    for i in range(3):
        wa_in[:, 128 * i : 128 * i + 128] = triple_in[i, :, 0:128]
    source = lax.broadcasted_iota(jnp.int32, (192, 256), 0)
    column = lax.broadcasted_iota(jnp.int32, (192, 256), 1)
    tail = sum(
        dot_nn(
            triple_in[i],
            ((source >= 128) & (source - 128 == column - 64 * i)).astype(F32).astype(BF16),
        )
        for i in range(3)
    )
    out_w = out_w_in[...]
    tail = tail + dot_tn(
        out_w, ((source >= 128) & (source + 64 == column)).astype(F32).astype(BF16)
    )
    wa_in[:, 384:640] = tail.astype(BF16)
    wa_in[:, 640:768] = dot_tn(
        out_w, (source == column).astype(F32).astype(BF16)[:, 0:128]
    ).astype(BF16)
    def fourteens(at):
        whole = jnp.floor((at + 0.5) * (1.0 / WIN))
        return whole, at - WIN * whole

    def grid(shape, dim):
        return lax.broadcasted_iota(jnp.int32, shape, dim).astype(F32)

    def entries(shape, dim):
        at = grid(shape, dim)
        side = (at >= 256.0).astype(F32)
        at = at - 256.0 * side
        main, other = fourteens(at)
        return side, main, other, at < float(WIN_TOK)

    side_of, main, other, valid = entries((512, 64), 0)
    slot = main - other + (WIN - 1) + 32.0 * side_of
    onehot[...] = jnp.where(valid & (grid((512, 64), 1) == slot), 1.0, 0.0).astype(BF16)
    side_of, main, other, valid = entries((ROWS, 512), 1)
    token = grid((ROWS, 512), 0)
    down, across = fourteens(token)
    hit = valid & (main == jnp.where(side_of > 0.5, across, down)) & (token < float(WIN_TOK))
    place[...] = jnp.where(hit, 1.0, 0.0)
    side_of, main, other, valid = entries((512, KEYS), 0)
    token = grid((512, KEYS), 1)
    down, across = fourteens(token)
    hit = valid & (other == jnp.where(side_of > 0.5, across, down)) & (token < float(WIN_TOK))
    pick[...] = jnp.where(hit, 1.0, 0.0).astype(BF16)
    pl.semaphore_wait(barrier, 6)
    gather_start(0)
    for copy in group_loads + side_loads:
        copy.wait()
    side[0] = jnp.zeros((8, D), F32)
    side[0, 0:1, :] = expand_bias_in[...].reshape(1, D)
    side[0, 1:2, 0:128] = qv_bias_in[0:1, 0:128]
    side[0, 1:2, 256:384] = qv_bias_in[1:2, 0:128]
    side[0, 1:2, 384:448] = qv_bias_in[0:1, 128:192]
    side[0, 1:2, 512:576] = qv_bias_in[1:2, 128:192]
    side_copy = send(side.at[0], side.at[1], c_mate)
    marks_all = valid_in[...].astype(F32)
    cnt[0] = jnp.full((8, 128), jnp.sum(marks_all), F32)
    cnt_x = send(cnt.at[0], cntr.at[0], x_mate)
    for g in range(3):
        gather_add(g)

    gain1 = gain1_in[...].reshape(1, D)
    shift1 = shift1_in[...].reshape(1, D)
    bias_out = bias_out_in[...].reshape(1, D)
    gain2 = gain2_in[...].reshape(1, D)
    shift2 = shift2_in[...].reshape(1, D)
    shrink_row[...] = bias_shrink_in[...].reshape(1, D)

    lane = lax.broadcasted_iota(jnp.int32, (1, 128), 1)
    half = ((lane < 64).astype(F32), (lane >= 64).astype(F32))
    key_mask = [(m * 0.125).astype(BF16) for m in half]
    half = [m.astype(BF16) for m in half]
    key_lane = lax.broadcasted_iota(jnp.int32, (1, KEYS), 1)
    key_bias = jnp.where(key_lane < WIN_TOK, 0.0, -1e30).astype(F32)

    row_ids = lax.broadcasted_iota(jnp.int32, (4, WIN_TOK), 0)
    own_marks = column_sum(jnp.where(row_ids == t, marks_all, 0.0))
    eye = lax.broadcasted_iota(jnp.int32, (ROWS, WIN_TOK), 0) == lax.broadcasted_iota(
        jnp.int32, (ROWS, WIN_TOK), 1
    )
    live = jnp.sum(jnp.where(eye, own_marks, 0.0), axis=1, keepdims=True)

    window_ids = lax.broadcasted_iota(jnp.int32, (1, 4, 1), 1)

    def window_of(ref, window):
        return jnp.sum(ref[...].astype(F32) * (window_ids == window).astype(F32), axis=1)

    xf[...] = jnp.zeros_like(xf)
    x_load.wait()
    for w in range(2):
        xf[w, 0:WIN_TOK, :] = window_of(xt, peer_window if w else t)
        point()
        unit, inverse = normalize(xf[w])
        n1[0, w] = (unit * gain1 + shift1).astype(BF16)
        if w == 0:
            unit1[...] = unit
            inv1[...] = inverse
    n1_copy = send(n1.at[0], n1.at[1], c_mate)
    tabs[...] = jnp.zeros_like(tabs)
    tabs[0:27, 0:64] = rows_in[...]
    tabs[32:59, 0:64] = columns_in[...]
    t2[0] = dot_nn(onehot[...], tabs[...].astype(BF16)).astype(BF16)
    t2[1] = dot_nn(onehot[...], pltpu.roll(tabs[...], 64, 1).astype(BF16)).astype(BF16)
    pj[:, :, ROWS:, :] = jnp.zeros((2, 2, KEYS - ROWS, 896), BF16)
    tg[...] = jnp.zeros_like(tg)

    def project(w):
        def body(j, carry):
            value = dot_nn(n1[0, w], wa[j, :, :, 0:640].reshape(D, 640)) + side[j, 1:2, 0:640]
            pj[w, j, 0:ROWS, 0:640] = value.astype(BF16)
            rolled = pltpu.roll(value[:, 384:512], 64, 1)
            pj[w, j, 0:ROWS, 640:768] = rolled.astype(BF16)
            rolled = pltpu.roll(value[:, 512:640], 64, 1)
            pj[w, j, 0:ROWS, 768:896] = rolled.astype(BF16)
            return carry

        lax.fori_loop(0, 2, body, 0)

    def unit_of(w, j, h):
        q, k, v, p, pv = UNITS[h]
        query = pj[w, j, 0:ROWS, 128 * q : 128 * q + 128]
        key = pj[w, j, :, 128 * k : 128 * k + 128] * key_mask[p]
        value = pj[w, j, :, 128 * v : 128 * v + 128] * half[pv]
        return query, key, value

    def attend(w):
        def body(j, carry):
            mixes = []
            for h in range(3):
                query, key, value = unit_of(w, j, h)
                along = dot_nt(query, t2[UNITS[h][3]]) * place[...]
                high = along.astype(BF16)
                low = (along - high.astype(F32)).astype(BF16)
                scores = dot_nt(query, key) + dot_nn(high, pick[...]) + dot_nn(low, pick[...])
                scores = scores + key_bias
                raised = jnp.exp(scores - jnp.max(scores, axis=-1, keepdims=True))
                soft = raised * (1.0 / jnp.sum(raised, axis=-1, keepdims=True))
                ps[w, j, h] = soft
                mixes.append(dot_nn(soft.astype(BF16), value))
            mx[j, w, :, 0:128] = mixes[2].astype(BF16)
            mx[j, w, :, 128:256] = (mixes[0] + mixes[1]).astype(BF16)
            return carry

        lax.fori_loop(0, 2, body, 0)
        point()

    def attended(w, lo, n):
        return dot_nt(mx[0, w, lo : lo + n, :], wa[0, :, :, 512:768].reshape(D, 256)) + dot_nt(
            mx[1, w, lo : lo + n, :], wa[1, :, :, 512:768].reshape(D, 256)
        )

    side_copy.wait_recv()
    need(("all", 0))
    project(1)
    point()
    attend(1)
    e1 = []
    for lo, n in CHUNKS:
        es[0, lo : lo + n, :] = attended(1, lo, n).astype(BF16)
        e1.append(send(es.at[0, pl.ds(lo, n)], er.at[0, pl.ds(lo, n)], y_mate))
    point()
    project(0)
    point()
    attend(0)
    mx_copy = send(mx.at[1], mxr, c_mate)
    mid[...] = xf[0] + bias_out + attended(0, 0, ROWS)
    point()

    e2 = []
    n2_c = []
    for i, (lo, n) in enumerate(CHUNKS):
        point()
        e1[i].wait_recv()
        middle = mid[lo : lo + n, :] + er[0, lo : lo + n, :].astype(F32)
        mid[lo : lo + n, :] = middle
        unit, inverse = normalize(middle)
        unit2[lo : lo + n, :] = unit
        inv2[lo : lo + n, :] = inverse
        n2[0, 0, lo : lo + n, :] = (unit * gain2 + shift2).astype(BF16)
        rows = pl.ds(lo, n)
        e2.append(send(n2.at[0, 0, rows], n2.at[0, 1, rows], y_mate))
        n2_c.append(send(n2.at[0, 0, rows], n2.at[1, 0, rows], c_mate))

    def feed(w, lo, n):
        def body(j, carry):
            before = dot_nn(n2[0, w, lo : lo + n, :], we[j].reshape(D, D)) + side[j, 0:1, :]
            phi = 0.5 * (1.0 + lax.erf(before * math.sqrt(0.5)))
            hid[j, w, lo : lo + n, :] = (before * phi).astype(BF16)
            bell = jnp.exp(-0.5 * before * before) * (1.0 / math.sqrt(2.0 * math.pi))
            slope[j, w, lo : lo + n, :] = phi + before * bell
            return carry

        lax.fori_loop(0, 2, body, 0)
        point()

    zone = z // 2
    zones = (zone, 1 - zone)
    halves = [pl.ds(pl.multiple_of(q * 384, 128), 384) for q in zones]

    def shrunk(w, i):
        rows = pl.ds(zones[i] * 4, 4)
        return dot_nt(hid[0, w], ws[0, rows].reshape(384, D)) + dot_nt(
            hid[1, w], ws[1, rows].reshape(384, D)
        )

    need(("all", 1))
    for lo, n in CHUNKS:
        feed(0, lo, n)
    for i, (lo, n) in enumerate(CHUNKS):
        rows = pl.ds(lo, n)
        point()
        e2[i].wait_recv()
        n2_c.append(send(n2.at[0, 1, rows], n2.at[1, 1, rows], c_mate))
        feed(1, lo, n)
    hid_copy = send(hid.at[1], hidr, c_mate)
    target_load.wait()
    xf[1, 0:WIN_TOK, :] = window_of(tt, t)
    point()
    xf[1, WIN_TOK:, :] = jnp.zeros((ROWS - WIN_TOK, D), F32)
    need(("near", 2))
    for copy in cnt_z:
        copy.wait_recv()
    count = (cnt[1] + cntr[1]) + (cntr[2] + cntr[3])
    count = count[0:1, 0:1]
    scaled_live = live * (token_total / count)
    e3 = []
    for i in range(2):
        if i == 1:
            need(("all", 2))
        es3[i] = shrunk(1, i).astype(BF16)
        e3.append(send(es3.at[i], er3.at[i], y_mate))
        acc[:, halves[i]] = mid[:, halves[i]] + shrink_row[:, halves[i]] + shrunk(0, i)

    e4 = []
    gr_c = []
    for i in range(2):
        cols = halves[i]
        e3[i].wait_recv()
        result = acc[:, cols] + er3[i].astype(F32)
        gap = result - xf[1, :, cols]
        grad = gap * scaled_live
        acc[:, cols] = grad
        gr[0, 0, :, cols] = grad.astype(BF16)
        e4.append(send(gr.at[0, 0, :, cols], gr.at[0, 1, :, cols], y_mate))
        gr_c.append(send(gr.at[0, 0, :, cols], gr.at[1, 0, :, cols], c_mate))
        bo[t, :, cols] = result.astype(BF16)
        sums[6:7, cols] = column_sum(gap * gap * live)
        sums[0:1, cols] = column_sum(grad)
    sb[0] = jnp.zeros((16, D), F32)
    sb[0, 6:7, :] = sums[6:7, :]
    sb[0, 0:1, :] = sums[0:1, :]

    def feed_back(w, lo, n):
        def body(j, carry):
            grad = dot_nn(gr[0, w, lo : lo + n, :], ws[j].reshape(D, D))
            grad = grad * slope[j, w, lo : lo + n, :]
            gb[j, w, lo : lo + n, :] = grad.astype(BF16)
            return carry

        lax.fori_loop(0, 2, body, 0)

    def expanded_back(w, lo, n):
        return dot_nt(gb[0, w, lo : lo + n, :], we[0].reshape(D, D)) + dot_nt(
            gb[1, w, lo : lo + n, :], we[1].reshape(D, D)
        )

    def rows_of(ref, width):
        return ref[...].reshape(2 * ROWS, width)

    def weight_grad(g, left, mine, theirs, width, at):
        def body(m, carry):
            cols = pl.ds(pl.multiple_of(m * 384, 128), 384)
            rows = pl.ds(m * 4, 4)
            value = dot_tn(left[0, :, :, cols].reshape(2 * ROWS, 384), mine.reshape(2 * ROWS, width))
            value = value + dot_tn(
                left[1, :, :, cols].reshape(2 * ROWS, 384), theirs.reshape(2 * ROWS, width)
            )
            gw[g, rows, :, at : at + width] = value.reshape(4, 96, width)
            return carry

        lax.fori_loop(0, 2, body, 0)

    to_x = {}
    to_z = {}

    pair_of = {}

    def pair_rows(k):
        return pl.ds(2 * z_mate(z, k), 2)

    def scatter_pairs(g):
        for i, k in enumerate((2, 1)):
            ps2[g, i] = gw[g, pair_rows(k), :, 640:768].astype(BF16)
            pair_of[g, i] = send(ps2.at[g, i], pr2.at[g, i], z_mates[0])

    parts = {0: ((0, 384), (384, 256)), 1: ((0, 640),), 2: ((0, 640),)}

    def scatter_blocks(g, i, blocks):
        lo, n = parts[g][i]
        for k in blocks:
            xs[g, k, :, lo : lo + n] = gw[g, row_of(k, 1 - x), :, lo : lo + n].astype(BF16)
            at = (g, k, slice(None), pl.ds(lo, n))
            to_x[g, k, i] = send(xs.at[at], xr.at[at], x_mate)

    def scatter_pair(g):
        pair_of[g, 0].wait_recv()
        total = gw[g, pair_rows(3), :, 640:768] + pr2[g, 0].astype(F32)
        ps2[g, 2] = total.astype(BF16)
        pair_of[g, 2] = send(ps2.at[g, 2], pr2.at[g, 2], z_mates[2])

    def scatter_turn(g):
        pair_of[g, 1].wait_recv()
        pair_of[g, 2].wait_recv()
        total = gw[g, pair_rows(0), :, 640:768] + pr2[g, 1].astype(F32)
        ptotal[g] = total + pr2[g, 2].astype(F32)
        pxs[g] = ptotal[g, 1 - x].astype(BF16)
        pair_of[g, 3] = send(pxs.at[g], pxr.at[g], x_mate)

    def scatter_z(g, k, i):
        lo, n = parts[g][i]
        cols = slice(lo, lo + n)
        to_x[g, k, i].wait_recv()
        total = gw[g, row_of(k, x), :, cols] + xr[g, k, :, cols].astype(F32)
        if k == 3:
            to_z[g, 2, i].wait_recv()
            total = total + zr[g, 1, :, cols].astype(F32)
        zs[g, k - 1, :, cols] = total.astype(BF16)
        at = (g, k - 1, slice(None), pl.ds(lo, n))
        to_z[g, k, i] = send(zs.at[at], zr.at[at], z_mates[2 if k == 3 else 0])

    def scatter_end(g, i, out):
        lo, n = parts[g][i]
        cols = slice(lo, lo + n)
        to_x[g, 0, i].wait_recv()
        to_z[g, 1, i].wait_recv()
        to_z[g, 3, i].wait_recv()
        total = gw[g, dp, :, cols] + xr[g, 0, :, cols].astype(F32)
        out[:, cols] = total + zr[g, 0, :, cols].astype(F32) + zr[g, 2, :, cols].astype(F32)

    def scatter_last(g, out):
        pair_of[g, 3].wait_recv()
        out[:, 640:768] = ptotal[g, x] + pxr[g].astype(F32)

    def scatter_add(g, *keys):
        steps = {"pair": scatter_pair, "turn": scatter_turn}
        for key in keys:
            if key in steps:
                add((key + "s", g), steps[key], g)
            else:
                add(("zs", g, *key), scatter_z, g, *key)

    for lo, n in CHUNKS:
        feed_back(0, lo, n)
    for i in range(2):
        e4[i].wait_recv()
        gr_c.append(send(gr.at[0, 1, :, halves[i]], gr.at[1, 1, :, halves[i]], c_mate))
    e5 = []
    for lo, n in CHUNKS:
        rows = pl.ds(lo, n)
        feed_back(1, lo, n)
        es[1, lo : lo + n, :] = expanded_back(1, lo, n).astype(BF16)
        e5.append(send(es.at[1, rows], er.at[1, rows], y_mate))
    gb_copy = send(gb.at[1], gbr, c_mate)
    mid[...] = expanded_back(0, 0, ROWS)
    for copy in gr_c:
        copy.wait_recv()
    hid_copy.wait_recv()
    weight_grad(2, gr, hid[0], hidr[...], D, 0)
    scatter_pairs(2)
    scatter_blocks(2, 0, (2, 3, 1, 0))
    scatter_add(2, "pair", (2, 0), "turn", (3, 0), (1, 0))
    point()

    e6 = []
    gm_c = []
    gain_part = jnp.zeros((1, D), F32)
    shift_part = jnp.zeros((1, D), F32)
    bias_part = jnp.zeros((1, D), F32)
    for i, (lo, n) in enumerate(CHUNKS):
        rows = pl.ds(lo, n)
        point()
        e5[i].wait_recv()
        grad = mid[lo : lo + n, :] + er[1, lo : lo + n, :].astype(F32)
        unit = unit2[lo : lo + n, :]
        gain_part = gain_part + column_sum(grad * unit)
        shift_part = shift_part + column_sum(grad)
        grad = acc[lo : lo + n, :] + normalize_back(grad, unit, inv2[lo : lo + n, :], gain2)
        acc[lo : lo + n, :] = grad
        gm[0, 0, lo : lo + n, :] = grad.astype(BF16)
        e6.append(send(gm.at[0, 0, rows], gm.at[0, 1, rows], y_mate))
        gm_c.append(send(gm.at[0, 0, rows], gm.at[1, 0, rows], c_mate))
        bias_part = bias_part + column_sum(grad)
    sb[0, 1:2, :] = gain_part
    sb[0, 2:3, :] = shift_part
    sb[0, 3:4, :] = bias_part

    bo_y = send(bo.at[t], bo.at[t], y_mate)
    bo_c = [send(bo.at[t], bo.at[t], c_mate)]

    def block_pass():
        bo_y.wait_recv()
        bo_c.append(send(bo.at[peer_window], bo.at[peer_window], c_mate))

    def block_mix():
        for copy in bo_c:
            copy.wait_recv()
        for w in range(4):
            mix[:, w, :] = bo[w, 0:WIN_TOK, :].astype(F32)
        xt[...] = mix[...].astype(BF16)
        stores.append(load(xt, block_out))

    stores = []
    gb_copy.wait_recv()
    for copy in n2_c:
        copy.wait_recv()
    weight_grad(1, n2, gb[0], gbr[...], D, 0)
    ones = jnp.ones((8, 2 * ROWS), BF16)
    sb[0, 8:9, :] = (dot_nn(ones, rows_of(gb.at[0], D)) + dot_nn(ones, rows_of(gbr, D)))[0:1]
    scatter_pairs(1)
    scatter_blocks(1, 0, (2, 3, 1, 0))
    scatter_add(1, "pair", (2, 0), "turn", (3, 0), (1, 0))
    point()

    def mixed_back(w, lo, n):
        for j in range(2):
            grad = dot_nn(gm[0, w, lo : lo + n, :], wa[j, :, :, 512:768].reshape(D, 256))
            gmx[j, w, lo : lo + n, :] = grad.astype(BF16)

    def unit_back(w, j, h):
        query, key, value = unit_of(w, j, h)
        p, pv = UNITS[h][3:]
        grad = gmx[j, w, :, 0:128] if h == 2 else gmx[j, w, :, 128:256]
        soft = ps[w, j, h]
        grad_soft = dot_nt(grad, value)
        delta = jnp.sum(soft * grad_soft, axis=-1, keepdims=True)
        grad_scores = (soft * (grad_soft - delta)).astype(BF16)
        grad_v = dot_tn(soft.astype(BF16), grad * half[pv])[0:ROWS]
        grad_k = dot_tn(grad_scores, query * key_mask[p])[0:ROWS]
        part = (dot_nt(grad_scores, pick[...]) * place[...]).astype(BF16)
        grad_q = dot_nn(grad_scores, key) + dot_nn(part, t2[p])
        tg[...] += dot_tn(query * half[p], part)
        return grad_q, grad_k, grad_v

    def attend_back_pair(w, j):
        one, two = unit_back(w, j, 0), unit_back(w, j, 1)
        for i in range(3):
            gp[j, w, :, 128 * i : 128 * i + 128] = (one[i] + two[i]).astype(BF16)

    def attend_back_last(w, j):
        grad_q, grad_k, grad_v = unit_back(w, j, 2)
        gp[j, w, :, 384:512] = (grad_q + pltpu.roll(grad_k, 64, 1)).astype(BF16)
        gp[j, w, :, 512:640] = pltpu.roll(grad_v, 64, 1).astype(BF16)

    def projected_back(w, lo, n):
        return dot_nt(gp[0, w, lo : lo + n, :], wa[0, :, :, 0:640].reshape(D, 640)) + dot_nt(
            gp[1, w, lo : lo + n, :], wa[1, :, :, 0:640].reshape(D, 640)
        )

    for i, (lo, n) in enumerate(CHUNKS):
        rows = pl.ds(lo, n)
        point()
        e6[i].wait_recv()
        gm_c.append(send(gm.at[0, 1, rows], gm.at[1, 1, rows], c_mate))
        mixed_back(1, lo, n)
    point()
    add(("block pass",), block_pass)
    add(("block mix",), block_mix)
    def both_back(j, carry):
        attend_back_pair(1, j)
        attend_back_last(1, j)
        return carry

    lax.fori_loop(0, 2, both_back, 0)
    point()
    gp_copies = [send(gp.at[1, 1], gpr.at[1], c_mate)]
    e7 = []
    for lo, n in CHUNKS:
        rows = pl.ds(lo, n)
        es[2, lo : lo + n, :] = projected_back(1, lo, n).astype(BF16)
        e7.append(send(es.at[2, rows], er.at[2, rows], y_mate))
    point()
    for copy in gm_c:
        copy.wait_recv()
    mx_copy.wait_recv()
    weight_grad(0, gm, mx[0], mxr[...], 256, 512)
    scatter_pairs(0)
    scatter_add(0, "pair", "turn")
    point()
    mixed_back(0, 0, ROWS)
    def pair_back(j, carry):
        attend_back_pair(0, j)
        return carry

    lax.fori_loop(0, 2, pair_back, 0)
    point()
    gp_copies.append(send(gp.at[1, 0, :, pl.ds(0, 384)], gpr.at[0, :, pl.ds(0, 384)], c_mate))
    attend_back_last(0, 0)
    point()
    n1_copy.wait_recv()
    for copy in gp_copies:
        copy.wait_recv()

    weight_grad(0, n1, gp[0, :, :, 0:384], gpr[:, :, 0:384], 384, 0)
    scatter_blocks(0, 0, (2, 3, 1, 0))
    scatter_add(0, (2, 0))
    attend_back_last(0, 1)
    last_copy = send(gp.at[1, 0, :, pl.ds(384, 256)], gpr.at[0, :, pl.ds(384, 256)], c_mate)
    mid[...] = projected_back(0, 0, ROWS)
    last_copy.wait_recv()
    held = gw[0, :, :, 512:640]
    weight_grad(0, n1, gp[0, :, :, 384:640], gpr[:, :, 384:640], 256, 384)
    gw[0, :, :, 512:640] += held
    need(("turns", 0))
    scatter_blocks(0, 1, (2, 3, 1, 0))

    small = {}

    def small_first():
        bias = dot_nn(ones, rows_of(gp.at[0], 640)) + dot_nn(ones, rows_of(gpr, 640))
        sb[0, 9:10, 0:640] = bias[0:1]
        spread = tg[...]
        spread_high = spread.astype(BF16)
        spread_low = (spread - spread_high.astype(F32)).astype(BF16)
        table = dot_nn(spread_high, onehot[...]) + dot_nn(spread_low, onehot[...])
        tb[0] = table[0:64] + table[64:128]

    top = pl.ds(0, 8)

    def small_send(stage, dst, mate, rows):
        return [
            send(sb.at[stage, rows], sbr.at[dst, rows], mate),
            send(tb.at[stage], tbr.at[dst], mate),
        ]

    def small_wait(stage):
        for copy in small[stage]:
            copy.wait_recv()

    def small_z():
        small[0] = sum((small_send(0, k - 1, z_mates[k - 1], pl.ds(0, 16)) for k in (1, 2, 3)), [])

    def small_c():
        small_wait(0)
        sb[1] = (sb[0] + sbr[0]) + (sbr[1] + sbr[2])
        tb[1] = (tb[0] + tbr[0]) + (tbr[1] + tbr[2])
        small[1] = small_send(1, 3, c_mate, top)

    def small_next(stage, mate, rows):
        small_wait(stage - 1)
        sb[stage] = sb[stage - 1]
        sb[stage, 0:8, :] = sb[stage - 1, 0:8, :] + sbr[stage + 1, 0:8, :]
        tb[stage] = tb[stage - 1] + tbr[stage + 1]
        small[stage] = small_send(stage, stage + 2, mate, rows)

    def small_end():
        small_wait(3)
        total = sb[3] + sbr[5]
        small_out[...] = total
        small_out[6:7, :] = jnp.broadcast_to(
            jnp.sum(total[6:7, :], axis=1, keepdims=True) / (count * float(D)), (1, D)
        )
        table_out[...] = (tb[3] + tbr[5]).T

    e8 = {}
    ig_c = {}

    def mix_in(window, i):
        lo, n = CHUNKS[i]
        top = min(lo + n, WIN_TOK)
        mix[lo:top, pl.ds(window, 1), :] = (
            ig[window, lo:top, :].astype(F32).reshape(top - lo, 1, D)
        )

    def own_grad(i):
        lo, n = CHUNKS[i]
        e7[i].wait_recv()
        grad = mid[lo : lo + n, :] + er[2, lo : lo + n, :].astype(F32)
        unit = unit1[lo : lo + n, :]
        gain_part = column_sum(grad * unit)
        shift_part = column_sum(grad)
        sb[0, 4:5, :] = gain_part if i == 0 else sb[0, 4:5, :] + gain_part
        sb[0, 5:6, :] = shift_part if i == 0 else sb[0, 5:6, :] + shift_part
        grad = acc[lo : lo + n, :] + normalize_back(grad, unit, inv1[lo : lo + n, :], gain1)
        ig[t, lo : lo + n, :] = grad.astype(BF16)
        rows = pl.ds(lo, n)
        ig_c[i, 0] = send(ig.at[t, rows], ig.at[t, rows], c_mate)
        e8[i] = send(ig.at[t, rows], ig.at[t, rows], y_mate)
        mix_in(t, i)

    def side_grad(i):
        ig_c[i, 0].wait_recv()
        mix_in(t + 1 - 2 * c, i)

    def peer_grad(i):
        lo, n = CHUNKS[i]
        rows = pl.ds(lo, n)
        e8[i].wait_recv()
        ig_c[i, 1] = send(ig.at[peer_window, rows], ig.at[peer_window, rows], c_mate)
        mix_in(peer_window, i)

    def last_grad(i):
        lo, n = CHUNKS[i]
        ig_c[i, 1].wait_recv()
        mix_in(peer_window + 1 - 2 * c, i)
        rows = pl.ds(lo, min(n, WIN_TOK - lo))
        stores.append(load(mix.at[rows], grad_out.at[rows]))

    def scatter_out(g, held, out):
        if g > 0:
            scatter_end(g, 0, held)
        else:
            scatter_end(0, 1, held)
        scatter_last(g, held)
        stores.append(load(held, out))

    need(("block mix",))
    add(("own", 0), own_grad, 0)
    add(("small first",), small_first)
    add(("own", 1), own_grad, 1)
    add(("small z",), small_z)
    scatter_add(0, (3, 0), (2, 1), (1, 0))
    add(("side", 0), side_grad, 0)
    add(("side", 1), side_grad, 1)
    add(("small c",), small_c)
    add(("out", 2), scatter_out, 2, gs, gs_out)
    add(("out", 1), scatter_out, 1, ge, ge_out)
    add(("small y",), small_next, 2, y_mate, top)
    add(("peer", 0), peer_grad, 0)
    scatter_add(0, (3, 1), (1, 1))
    add(("last", 0), last_grad, 0)
    add(("small x",), small_next, 3, x_mate, pl.ds(0, 16))
    add(("peer", 1), peer_grad, 1)
    add(("last", 1), last_grad, 1)
    add(("end", 0), scatter_end, 0, 0, ga)
    add(("out", 0), scatter_out, 0, ga, ga_out)
    add(("small end",), small_end)
    need(("small end",))
    for copy in started:
        copy.wait_send()
    for copy in stores:
        copy.wait()


def finish_kernel(
    block_in,
    grad_in,
    ga,
    ge,
    gs,
    small,
    table,
    block_out,
    loss_out,
    grad_out,
    gain1_out,
    shift1_out,
    triple_out,
    qv_out,
    out_w_out,
    out_b_out,
    gain2_out,
    shift2_out,
    we_out,
    expand_bias_out,
    ws_out,
    bias_shrink_out,
    rows_out,
    columns_out,
    block_hold,
    grad_hold,
    ge_hold,
    gs_hold,
    sems,
):
    moves = []
    at = 0
    for src, hold, dst, step in (
        (block_in, block_hold, block_out, 49),
        (grad_in, grad_hold, grad_out, 49),
        (ge, ge_hold, we_out, 96),
        (gs, gs_hold, ws_out, 96),
    ):
        for lo in range(0, src.shape[0], step):
            rows = pl.ds(lo, step)
            copy = pltpu.make_async_copy(src.at[rows], hold.at[rows], sems.at[at])
            copy.start()
            moves.append(
                (copy, pltpu.make_async_copy(hold.at[rows], dst.at[rows], sems.at[at + 1]))
            )
            at += 2
    for i in range(3):
        triple_out[i, :, 0:128] = ga[:, 128 * i : 128 * i + 128]
    triple_out[0, :, 128:192] = ga[:, 384:448]
    triple_out[1, :, 128:192] = pltpu.roll(ga[:, 384:512], 64, 1)[:, 0:64]
    triple_out[2, :, 128:192] = ga[:, 512:576]
    out_w_out[0:128, :] = ga[:, 640:768].T
    out_w_out[128:192, :] = ga[:, 512:640].T[64:128]
    loss_out[...] = small[6:7, 0:1]
    for i, out in enumerate(
        (bias_shrink_out, gain2_out, shift2_out, out_b_out, gain1_out, shift1_out)
    ):
        out[...] = small[i]
    expand_bias_out[...] = small[8]
    for i in range(2):
        qv_out[i : i + 1, 0:128] = small[9:10, 256 * i : 256 * i + 128]
        qv_out[i : i + 1, 128:192] = small[9:10, 384 + 128 * i : 448 + 128 * i]
    rows_out[...] = table[0:27]
    columns_out[...] = table[32:59]
    for arrive, leave in moves:
        arrive.wait()
        leave.start()
    for arrive, leave in moves:
        leave.wait()


def fused(
    inputs,
    target,
    valid,
    first_gain,
    first_shift,
    triple_weight,
    query_value_bias,
    output_weight,
    output_bias,
    second_gain,
    second_shift,
    expand_weight,
    expand_bias,
    shrink_weight,
    shrink_bias,
    rows_table,
    columns_table,
):
    vmem = pl.BlockSpec(memory_space=pltpu.VMEM)
    anywhere = pl.BlockSpec(memory_space=pl.ANY)
    mixed_shape = (WIN_TOK, 4, D)
    part = jax.ShapeDtypeStruct((96, D), F32)
    copies = 224
    parts = pl.pallas_call(
        block_kernel,
        out_shape=[
            jax.ShapeDtypeStruct(mixed_shape, BF16),
            jax.ShapeDtypeStruct(mixed_shape, F32),
            part,
            part,
            part,
            jax.ShapeDtypeStruct((16, D), F32),
            jax.ShapeDtypeStruct((64, 64), F32),
        ],
        in_specs=[anywhere] * 17,
        out_specs=[anywhere] * 5 + [vmem] * 2,
        scratch_shapes=[
            pltpu.VMEM(valid.shape, jnp.int32),
            pltpu.VMEM((D,), F32),
            pltpu.VMEM((D,), F32),
            pltpu.VMEM(triple_weight.shape, BF16),
            pltpu.VMEM(query_value_bias.shape, F32),
            pltpu.VMEM(output_weight.shape, BF16),
            pltpu.VMEM((D,), F32),
            pltpu.VMEM((D,), F32),
            pltpu.VMEM((D,), F32),
            pltpu.VMEM(expand_weight.shape, BF16),
            pltpu.VMEM(expand_bias.shape, F32),
            pltpu.VMEM(expand_weight.shape, BF16),
            pltpu.VMEM((D,), F32),
            pltpu.VMEM(rows_table.shape, F32),
            pltpu.VMEM(columns_table.shape, F32),
            pltpu.VMEM((96, D), BF16),
            pltpu.VMEM((2, 8, 96, D), BF16),
            pltpu.VMEM((2, 8, 96, D), BF16),
            pltpu.VMEM((2, 8, 96, D), BF16),
            pltpu.VMEM(mixed_shape, BF16),
            pltpu.VMEM(mixed_shape, BF16),
            pltpu.VMEM((512, 64), BF16),
            pltpu.VMEM((ROWS, 512), F32),
            pltpu.VMEM((512, KEYS), BF16),
            pltpu.VMEM((64, 128), F32),
            pltpu.VMEM((4, ROWS, D), BF16),
            pltpu.VMEM((4, ROWS, D), BF16),
            pltpu.VMEM(mixed_shape, F32),
            pltpu.VMEM((96, D), F32),
            pltpu.VMEM((96, D), F32),
            pltpu.VMEM((96, D), F32),
            pltpu.VMEM((2, 8, D), F32),
            pltpu.VMEM((2, ROWS, D), F32),
            pltpu.VMEM((ROWS, D), F32),
            pltpu.VMEM((ROWS, D), F32),
            pltpu.VMEM((ROWS, 1), F32),
            pltpu.VMEM((ROWS, 1), F32),
            pltpu.VMEM((ROWS, D), F32),
            pltpu.VMEM((ROWS, D), F32),
            pltpu.VMEM((2, 2, ROWS, D), BF16),
            pltpu.VMEM((2, 2, ROWS, D), BF16),
            pltpu.VMEM((2, 2, ROWS, D), BF16),
            pltpu.VMEM((2, 2, ROWS, D), BF16),
            pltpu.VMEM((2, 2, KEYS, 896), BF16),
            pltpu.VMEM((2, 2, 3, ROWS, KEYS), F32),
            pltpu.VMEM((2, 2, ROWS, 256), BF16),
            pltpu.VMEM((2, ROWS, 256), BF16),
            pltpu.VMEM((2, 2, ROWS, D), BF16),
            pltpu.VMEM((2, ROWS, D), BF16),
            pltpu.VMEM((2, 2, ROWS, D), F32),
            pltpu.VMEM((2, 2, ROWS, D), BF16),
            pltpu.VMEM((2, ROWS, D), BF16),
            pltpu.VMEM((2, 2, ROWS, 256), BF16),
            pltpu.VMEM((2, 2, ROWS, 640), BF16),
            pltpu.VMEM((2, ROWS, 640), BF16),
            pltpu.VMEM((2, 512, 128), BF16),
            pltpu.VMEM((128, 512), F32),
            pltpu.VMEM((3, ROWS, D), BF16),
            pltpu.VMEM((3, ROWS, D), BF16),
            pltpu.VMEM((2, ROWS, 384), BF16),
            pltpu.VMEM((2, ROWS, 384), BF16),
            pltpu.VMEM((8, D), F32),
            pltpu.VMEM((1, D), F32),
            pltpu.VMEM((3, 8, 96, D), F32),
            pltpu.VMEM((3, 4, 96, 640), BF16),
            pltpu.VMEM((3, 4, 96, 640), BF16),
            pltpu.VMEM((3, 3, 96, 640), BF16),
            pltpu.VMEM((3, 3, 96, 640), BF16),
            pltpu.VMEM((3, 3, 2, 96, 128), BF16),
            pltpu.VMEM((3, 3, 2, 96, 128), BF16),
            pltpu.VMEM((3, 2, 96, 128), F32),
            pltpu.VMEM((3, 96, 128), BF16),
            pltpu.VMEM((3, 96, 128), BF16),
            pltpu.VMEM((2, 8, 128), F32),
            pltpu.VMEM((4, 8, 128), F32),
            pltpu.VMEM((4, 16, D), F32),
            pltpu.VMEM((6, 16, D), F32),
            pltpu.VMEM((4, 64, 64), F32),
            pltpu.VMEM((6, 64, 64), F32),
            pltpu.SemaphoreType.DMA((32,)),
            pltpu.SemaphoreType.DMA((copies,)),
            pltpu.SemaphoreType.DMA((copies,)),
        ],
        compiler_params=pltpu.CompilerParams(
            collective_id=0, has_side_effects=True, vmem_limit_bytes=60 << 20
        ),
    )(
        inputs.transpose(1, 0, 2),
        target.transpose(1, 0, 2),
        valid,
        first_gain,
        first_shift,
        triple_weight,
        query_value_bias,
        output_weight,
        output_bias,
        second_gain,
        second_shift,
        expand_weight,
        expand_bias,
        shrink_weight.T,
        shrink_bias,
        rows_table,
        columns_table,
    )
    vector = jax.ShapeDtypeStruct((D,), F32)
    relative = jax.ShapeDtypeStruct(rows_table.shape, F32)
    outs = pl.pallas_call(
        finish_kernel,
        out_shape=[
            jax.ShapeDtypeStruct(mixed_shape, BF16),
            jax.ShapeDtypeStruct((1, 1), F32),
            jax.ShapeDtypeStruct(mixed_shape, F32),
            vector,
            vector,
            jax.ShapeDtypeStruct(triple_weight.shape, F32),
            jax.ShapeDtypeStruct(query_value_bias.shape, F32),
            jax.ShapeDtypeStruct(output_weight.shape, F32),
            vector,
            vector,
            vector,
            part,
            jax.ShapeDtypeStruct(expand_bias.shape, F32),
            part,
            vector,
            relative,
            relative,
        ],
        in_specs=[anywhere] * 2 + [vmem, anywhere, anywhere] + [vmem] * 2,
        out_specs=[
            anywhere if i in (0, 2, 11, 13) else vmem for i in range(17)
        ],
        scratch_shapes=[
            pltpu.VMEM(mixed_shape, BF16),
            pltpu.VMEM(mixed_shape, F32),
            pltpu.VMEM((96, D), F32),
            pltpu.VMEM((96, D), F32),
            pltpu.SemaphoreType.DMA((20,)),
        ],
    )(*parts)
    outs = list(outs)
    outs[0] = outs[0].transpose(1, 0, 2)
    outs[1] = outs[1].reshape(())
    outs[2] = outs[2].transpose(1, 0, 2)
    outs[13] = outs[13].T
    return tuple(outs)


def solution(mesh):
    placed = (
        P("dp", None, None),
        P("dp", None, None),
        P("dp", None),
        P(),
        P(),
        P(None, "dp", "tensor"),
        P(None, "tensor"),
        P("tensor", "dp"),
        P(),
        P(),
        P(),
        P("dp", "tensor"),
        P("tensor"),
        P("tensor", "dp"),
        P(),
        P(),
        P(),
    )
    on_slice = mesh.shape["dp"] == 8 and mesh.shape["tensor"] == 4
    return jax.shard_map(
        fused if on_slice else shards,
        mesh=mesh,
        in_specs=placed,
        out_specs=(
            P("dp", None, None),
            P(),
            P("dp", None, None),
            P(),
            P(),
            P(None, "dp", "tensor"),
            P(None, "tensor"),
            P("tensor", "dp"),
            P(),
            P(),
            P(),
            P("dp", "tensor"),
            P("tensor"),
            P("tensor", "dp"),
            P(),
            P(),
            P(),
        ),
        check_vma=False,
    )
```

```python
import math

import jax
import jax.numpy as jnp
import numpy as np
from jax import lax
from jax.experimental import pallas as pl
from jax.experimental.pallas import tpu as pltpu
from jax.sharding import PartitionSpec as P

MESH = pl.DeviceIdType.MESH

D = 768
HEADS = 12
HEAD = 64
WIN = 14
WIN_TOK = 196
MICRO = 2


def normalize(values):
    center = jnp.mean(values, axis=-1, keepdims=True)
    centered = values - center
    spread = jnp.mean(centered * centered, axis=-1, keepdims=True)
    inverse = lax.rsqrt(spread + 1e-06)
    return (centered * inverse, inverse)


def normalize_back(grad_out, unit, inverse, gain):
    scaled = grad_out * gain
    mean_one = jnp.mean(scaled, axis=-1, keepdims=True)
    mean_two = jnp.mean(scaled * unit, axis=-1, keepdims=True)
    return inverse * (scaled - mean_one - unit * mean_two)


def position_select(side):
    shape = (side, side, 2 * side - 1)
    first = lax.broadcasted_iota(jnp.int32, shape, 0)
    second = lax.broadcasted_iota(jnp.int32, shape, 1)
    slots = lax.broadcasted_iota(jnp.int32, shape, 2)
    return (slots == first - second + side - 1).astype(jnp.bfloat16)


def score_block(queries, keys, table_rows, table_cols, scale_factor):
    groups = queries.shape[0]
    side = queries.shape[1]
    heads = queries.shape[3]
    along_rows = jnp.einsum(
        "gabnc,aec->gnabe", queries, table_rows, preferred_element_type=jnp.float32
    )
    along_cols = jnp.einsum(
        "gabnc,bfc->gnabf", queries, table_cols, preferred_element_type=jnp.float32
    )
    scores = (
        jnp.einsum("gabnc,gefnc->gnabef", queries, keys, preferred_element_type=jnp.float32)
        * scale_factor
    )
    scores = scores + along_rows[..., :, None] + along_cols[..., None, :]
    return scores.reshape(groups, heads, side * side, side * side)


def gelu_exact(inner):
    return jax.nn.gelu(inner, approximate=False)


def row_total(partial_value):
    return lax.psum(partial_value, "tensor")


def share_of(values):
    share_rows = values.shape[0] // lax.axis_size("tensor")
    return lax.dynamic_slice_in_dim(values, lax.axis_index("tensor") * share_rows, share_rows, 0)


def shards(
    inputs,
    target,
    valid,
    first_gain,
    first_shift,
    triple_weight,
    query_value_bias,
    output_weight,
    output_bias,
    second_gain,
    second_shift,
    expand_weight,
    expand_bias,
    shrink_weight,
    shrink_bias,
    rows_table,
    columns_table,
):
    local_heads = HEADS // lax.axis_size("tensor")
    local_width = local_heads * HEAD
    local_windows = inputs.shape[0]
    win_micro = local_windows // MICRO
    micro_rows = win_micro * WIN_TOK
    scale_factor = 1.0 / math.sqrt(HEAD)
    highest = lax.Precision.HIGHEST
    live = valid.astype(jnp.float32)
    select = position_select(WIN)
    table_rows = jnp.einsum(
        "aej,jc->aec", select, rows_table.astype(jnp.bfloat16), preferred_element_type=jnp.float32
    ).astype(jnp.bfloat16)
    table_cols = jnp.einsum(
        "aej,jc->aec",
        select,
        columns_table.astype(jnp.bfloat16),
        preferred_element_type=jnp.float32,
    ).astype(jnp.bfloat16)
    rows_float = table_rows.astype(jnp.float32)
    cols_float = table_cols.astype(jnp.float32)
    triple_bias = jnp.stack(
        [query_value_bias[0], jnp.zeros_like(query_value_bias[0]), query_value_bias[1]]
    )
    saved = []
    outputs = []
    local_loss = jnp.zeros((), jnp.float32)
    for micro in range(MICRO):
        gathered = (
            lax.all_gather(triple_weight, "dp", axis=1, tiled=True),
            lax.all_gather(output_weight, "dp", axis=1, tiled=True),
            lax.all_gather(expand_weight, "dp", axis=0, tiled=True),
            lax.all_gather(shrink_weight, "dp", axis=1, tiled=True),
        )
        full_triple, full_output, full_expand, full_shrink = gathered
        lower = micro * win_micro
        flat_rows = inputs[lower : lower + win_micro].reshape(micro_rows, D).astype(jnp.float32)
        unit_one, inverse_one = normalize(flat_rows)
        normed = (unit_one * first_gain + first_shift).astype(jnp.bfloat16)
        projected = (
            jnp.einsum("rd,tde->rte", normed, full_triple, preferred_element_type=jnp.float32)
            + triple_bias
        )
        projected = projected.astype(jnp.bfloat16)
        split = projected.reshape(win_micro, WIN, WIN, 3, local_heads, HEAD)
        queries = split[:, :, :, 0]
        keys = split[:, :, :, 1]
        values = split[:, :, :, 2].reshape(win_micro, WIN_TOK, local_heads, HEAD)
        scores = score_block(queries, keys, table_rows, table_cols, scale_factor)
        peak = jnp.max(scores, axis=-1, keepdims=True)
        raised = jnp.exp(scores - peak)
        denominator = jnp.sum(raised, axis=-1, keepdims=True)
        log_total = peak + jnp.log(denominator)
        softmaxed = (raised / denominator).astype(jnp.bfloat16)
        mixed = jnp.einsum("gnqk,gknc->gqnc", softmaxed, values, preferred_element_type=jnp.float32)
        mixed = mixed.reshape(micro_rows, local_width).astype(jnp.bfloat16)
        partial_attended = jnp.dot(mixed, full_output, preferred_element_type=jnp.float32)
        middle = flat_rows + (row_total(partial_attended) + output_bias)
        unit_two, inverse_two = normalize(middle)
        normed_two = (unit_two * second_gain + second_shift).astype(jnp.bfloat16)
        before = jnp.dot(normed_two, full_expand, preferred_element_type=jnp.float32) + expand_bias
        hidden = gelu_exact(before).astype(jnp.bfloat16)
        partial_shrunk = jnp.dot(hidden, full_shrink, preferred_element_type=jnp.float32)
        result = middle + (row_total(partial_shrunk) + shrink_bias)
        aim = target[lower : lower + win_micro].reshape(micro_rows, D).astype(jnp.float32)
        marks = live[lower : lower + win_micro].reshape(micro_rows, 1)
        weighted_gap = marks * (result - aim)
        local_loss = local_loss + jnp.sum(weighted_gap * (result - aim))
        outputs.append(result.astype(jnp.bfloat16).reshape(win_micro, WIN_TOK, D))
        saved.append(
            (
                unit_one,
                inverse_one,
                normed,
                projected,
                log_total,
                mixed,
                unit_two,
                inverse_two,
                normed_two,
                before,
                hidden,
                weighted_gap,
            )
        )
    loss_total, count = lax.psum((local_loss, jnp.sum(live)), "dp")
    loss = loss_total / (count * D)
    grad_scale = local_windows * WIN_TOK * lax.axis_size("dp") / count
    triple_acc = jnp.zeros((3, D, local_width), jnp.float32)
    output_acc = jnp.zeros((local_width, D), jnp.float32)
    expand_acc = jnp.zeros((D, full_expand.shape[1]), jnp.float32)
    shrink_acc = jnp.zeros((full_shrink.shape[0], D), jnp.float32)
    first_gain_acc = jnp.zeros((D,), jnp.float32)
    first_shift_acc = jnp.zeros((D,), jnp.float32)
    second_gain_acc = jnp.zeros((D,), jnp.float32)
    second_shift_acc = jnp.zeros((D,), jnp.float32)
    output_bias_acc = jnp.zeros((D,), jnp.float32)
    shrink_bias_acc = jnp.zeros((D,), jnp.float32)
    expand_bias_acc = jnp.zeros((full_expand.shape[1],), jnp.float32)
    query_value_acc = jnp.zeros((2, local_width), jnp.float32)
    rows_expanded_acc = jnp.zeros((WIN, WIN, HEAD), jnp.float32)
    cols_expanded_acc = jnp.zeros((WIN, WIN, HEAD), jnp.float32)
    input_grads = []
    for micro in range(MICRO):
        gathered = (
            lax.all_gather(triple_weight, "dp", axis=1, tiled=True),
            lax.all_gather(output_weight, "dp", axis=1, tiled=True),
            lax.all_gather(expand_weight, "dp", axis=0, tiled=True),
            lax.all_gather(shrink_weight, "dp", axis=1, tiled=True),
        )
        full_triple, full_output, full_expand, full_shrink = gathered
        (
            unit_one,
            inverse_one,
            normed,
            projected,
            log_total,
            mixed,
            unit_two,
            inverse_two,
            normed_two,
            before,
            hidden,
            weighted_gap,
        ) = saved[micro]
        grad_result = grad_scale * weighted_gap
        shrink_bias_acc = shrink_bias_acc + jnp.sum(share_of(grad_result), axis=0)
        grad_result_low = grad_result.astype(jnp.bfloat16)
        shrink_acc = shrink_acc + jnp.einsum(
            "rf,rd->fd", hidden, grad_result_low, preferred_element_type=jnp.float32
        )
        grad_hidden = jnp.einsum(
            "rd,fd->rf", grad_result_low, full_shrink, preferred_element_type=jnp.float32
        )
        unused, gelu_pull = jax.vjp(gelu_exact, before)
        grad_before = gelu_pull(grad_hidden)[0].astype(jnp.bfloat16)
        expand_bias_acc = expand_bias_acc + jnp.sum(grad_before.astype(jnp.float32), axis=0)
        expand_acc = expand_acc + jnp.einsum(
            "rd,rf->df", normed_two, grad_before, preferred_element_type=jnp.float32
        )
        partial_two = jnp.einsum(
            "rf,df->rd", grad_before, full_expand, preferred_element_type=jnp.float32
        )
        grad_normed_two = row_total(partial_two)
        grad_middle = grad_result + normalize_back(
            grad_normed_two, unit_two, inverse_two, second_gain
        )
        second_gain_acc = second_gain_acc + jnp.sum(share_of(grad_normed_two * unit_two), axis=0)
        second_shift_acc = second_shift_acc + jnp.sum(share_of(grad_normed_two), axis=0)
        output_bias_acc = output_bias_acc + jnp.sum(share_of(grad_middle), axis=0)
        grad_middle_low = grad_middle.astype(jnp.bfloat16)
        output_acc = output_acc + jnp.einsum(
            "rc,rd->cd", mixed, grad_middle_low, preferred_element_type=jnp.float32
        )
        grad_mixed = jnp.einsum(
            "rd,cd->rc", grad_middle_low, full_output, preferred_element_type=jnp.float32
        )
        grad_mixed = grad_mixed.astype(jnp.bfloat16).reshape(win_micro, WIN_TOK, local_heads, HEAD)
        split = projected.reshape(win_micro, WIN, WIN, 3, local_heads, HEAD)
        queries = split[:, :, :, 0]
        keys = split[:, :, :, 1]
        queries_flat = queries.reshape(win_micro, WIN_TOK, local_heads, HEAD)
        keys_flat = keys.reshape(win_micro, WIN_TOK, local_heads, HEAD)
        values = split[:, :, :, 2].reshape(win_micro, WIN_TOK, local_heads, HEAD)
        scores = score_block(queries, keys, table_rows, table_cols, scale_factor)
        softmax_exact = jnp.exp(scores - log_total)
        grad_soft = jnp.einsum(
            "gqnc,gknc->gnqk", grad_mixed, values, preferred_element_type=jnp.float32
        )
        delta = jnp.sum(softmax_exact * grad_soft, axis=-1, keepdims=True)
        grad_scores = (softmax_exact * (grad_soft - delta)).astype(jnp.bfloat16)
        grad_values = jnp.einsum(
            "gnqk,gqnc->gknc",
            softmax_exact.astype(jnp.bfloat16),
            grad_mixed,
            preferred_element_type=jnp.float32,
        )
        grad_keys = (
            jnp.einsum(
                "gnqk,gqnc->gknc", grad_scores, queries_flat, preferred_element_type=jnp.float32
            )
            * scale_factor
        )
        grad_queries = (
            jnp.einsum(
                "gnqk,gknc->gqnc", grad_scores, keys_flat, preferred_element_type=jnp.float32
            )
            * scale_factor
        )
        grad_grid = grad_scores.astype(jnp.float32).reshape(
            win_micro, local_heads, WIN, WIN, WIN, WIN
        )
        row_part = jnp.sum(grad_grid, axis=5)
        col_part = jnp.sum(grad_grid, axis=4)
        queries_float = queries.astype(jnp.float32)
        rel_queries = jnp.einsum("gnabe,aec->gabnc", row_part, rows_float, precision=highest)
        rel_queries = rel_queries + jnp.einsum(
            "gnabf,bfc->gabnc", col_part, cols_float, precision=highest
        )
        grad_queries = grad_queries + rel_queries.reshape(win_micro, WIN_TOK, local_heads, HEAD)
        rows_expanded_acc = rows_expanded_acc + jnp.einsum(
            "gnabe,gabnc->aec", row_part, queries_float, precision=highest
        )
        cols_expanded_acc = cols_expanded_acc + jnp.einsum(
            "gnabf,gabnc->bfc", col_part, queries_float, precision=highest
        )
        grad_projected = jnp.stack(
            [
                grad_queries.reshape(micro_rows, local_width),
                grad_keys.reshape(micro_rows, local_width),
                grad_values.reshape(micro_rows, local_width),
            ],
            axis=1,
        ).astype(jnp.bfloat16)
        projected_float_sums = jnp.sum(grad_projected.astype(jnp.float32), axis=0)
        query_value_acc = query_value_acc + jnp.stack(
            [projected_float_sums[0], projected_float_sums[2]]
        )
        triple_acc = triple_acc + jnp.einsum(
            "rd,rte->tde", normed, grad_projected, preferred_element_type=jnp.float32
        )
        partial_one = jnp.einsum(
            "rte,tde->rd", grad_projected, full_triple, preferred_element_type=jnp.float32
        )
        grad_normed = row_total(partial_one)
        grad_tokens = grad_middle + normalize_back(grad_normed, unit_one, inverse_one, first_gain)
        first_gain_acc = first_gain_acc + jnp.sum(share_of(grad_normed * unit_one), axis=0)
        first_shift_acc = first_shift_acc + jnp.sum(share_of(grad_normed), axis=0)
        input_grads.append(grad_tokens.reshape(win_micro, WIN_TOK, D))
    select_float = select.astype(jnp.float32)
    rows_table_part = jnp.einsum("aej,aec->jc", select_float, rows_expanded_acc, precision=highest)
    cols_table_part = jnp.einsum("aej,aec->jc", select_float, cols_expanded_acc, precision=highest)
    triple_grad, output_grad, expand_grad, shrink_grad = (
        lax.psum_scatter(triple_acc, "dp", scatter_dimension=1, tiled=True),
        lax.psum_scatter(output_acc, "dp", scatter_dimension=1, tiled=True),
        lax.psum_scatter(expand_acc, "dp", scatter_dimension=0, tiled=True),
        lax.psum_scatter(shrink_acc, "dp", scatter_dimension=1, tiled=True),
    )
    over_heads = lax.psum(
        (
            rows_table_part,
            cols_table_part,
            first_gain_acc,
            first_shift_acc,
            output_bias_acc,
            second_gain_acc,
            second_shift_acc,
            shrink_bias_acc,
        ),
        "tensor",
    )
    summed_small = lax.psum(
        (
            over_heads[0],
            over_heads[1],
            over_heads[2],
            over_heads[3],
            over_heads[4],
            over_heads[5],
            over_heads[6],
            over_heads[7],
            query_value_acc,
            expand_bias_acc,
        ),
        "dp",
    )
    return (
        jnp.concatenate(outputs, axis=0),
        loss,
        jnp.concatenate(input_grads, axis=0),
        summed_small[2],
        summed_small[3],
        triple_grad,
        summed_small[8],
        output_grad,
        summed_small[4],
        summed_small[5],
        summed_small[6],
        expand_grad,
        summed_small[9],
        shrink_grad,
        summed_small[7],
        summed_small[0],
        summed_small[1],
    )


ROWS = 208
KEYS = 256
CHUNKS = ((0, 112), (112, 96))
F32 = jnp.float32
BF16 = jnp.bfloat16


def z_mate(z, k):
    if k == 0:
        return z
    if k == 1:
        return z + 1 - 2 * (z % 2)
    if k == 2:
        return (z + 2) % 4
    return 3 - z


def dot_nn(a, b):
    return lax.dot_general(a, b, (((1,), (0,)), ((), ())), preferred_element_type=F32)


def dot_nt(a, b):
    return lax.dot_general(a, b, (((1,), (1,)), ((), ())), preferred_element_type=F32)


def dot_tn(a, b):
    return lax.dot_general(a, b, (((0,), (0,)), ((), ())), preferred_element_type=F32)


def column_sum(values):
    return jnp.sum(values, axis=0, keepdims=True)


UNITS = ((0, 1, 2, 0, 0), (0, 1, 2, 1, 1), (3, 5, 6, 0, 1))


ORDER = (('pair', 0, 0), ('x', 0, 0), ('z', 0, 3), ('far', 0), ('z', 0, 1), ('pair', 0, 3), ('count',), ('x', 0, 3), ('z', 0, 2), ('start', 1), ('pair', 0, 1), ('x', 0, 1), ('near', 0), ('pair', 0, 2), ('x', 0, 2), ('pair', 1, 0), ('all', 0), ('start', 2), ('z', 1, 3), ('pair', 1, 3), ('z', 1, 1), ('far', 1), ('x', 1, 0), ('z', 2, 3), ('pair', 1, 1), ('z', 1, 2), ('x', 1, 1), ('x', 1, 3), ('pair', 1, 2), ('pair', 2, 0), ('near', 1), ('x', 1, 2), ('z', 2, 1), ('all', 1), ('far', 2), ('pair', 2, 3), ('z', 2, 2), ('pair', 2, 1), ('x', 2, 0), ('x', 2, 1), ('near', 2), ('x', 2, 3), ('pair', 2, 2), ('x', 2, 2), ('all', 2), ('pairs', 2), ('zs', 2, 2, 0), ('turns', 2), ('zs', 2, 3, 0), ('zs', 2, 1, 0), ('pairs', 1), ('zs', 1, 2, 0), ('block pass',), ('zs', 1, 1, 0), ('pairs', 0), ('zs', 1, 3, 0), ('block mix',), ('zs', 0, 2, 0), ('own', 0), ('small first',), ('own', 1), ('small z',), ('side', 0), ('turns', 0), ('turns', 1), ('zs', 0, 2, 1), ('zs', 0, 1, 0), ('small c',), ('zs', 0, 3, 0), ('out', 1), ('out', 2), ('small y',), ('side', 1), ('peer', 0), ('zs', 0, 1, 1), ('zs', 0, 3, 1), ('small x',), ('end', 0), ('last', 0), ('peer', 1), ('last', 1), ('out', 0), ('small end',))
PLAN = (0, 1, 1, 1, 2, 2, 3, 0, 0, 0, 1, 2, 1, 1, 1, 0, 0, 0, 0, 2, 0, 1, 3, 0, 1, 0, 1, 0, 3)


def block_kernel(
    x_in,
    target_in,
    valid_hbm,
    gain1_hbm,
    shift1_hbm,
    triple_hbm,
    qv_bias_hbm,
    out_w_hbm,
    bias_out_hbm,
    gain2_hbm,
    shift2_hbm,
    we_hbm,
    expand_bias_hbm,
    ws_hbm,
    bias_shrink_hbm,
    rows_hbm,
    columns_hbm,
    block_out,
    grad_out,
    ga_out,
    ge_out,
    gs_out,
    small_out,
    table_out,
    valid_in,
    gain1_in,
    shift1_in,
    triple_in,
    qv_bias_in,
    out_w_in,
    bias_out_in,
    gain2_in,
    shift2_in,
    we_in,
    expand_bias_in,
    ws_in,
    bias_shrink_in,
    rows_in,
    columns_in,
    wa_in,
    wa,
    we,
    ws,
    xt,
    tt,
    onehot,
    place,
    pick,
    tabs,
    bo,
    ig,
    mix,
    ga,
    ge,
    gs,
    side,
    xf,
    unit1,
    unit2,
    inv1,
    inv2,
    mid,
    acc,
    n1,
    n2,
    gr,
    gm,
    pj,
    ps,
    mx,
    mxr,
    hid,
    hidr,
    slope,
    gb,
    gbr,
    gmx,
    gp,
    gpr,
    t2,
    tg,
    es,
    er,
    es3,
    er3,
    sums,
    shrink_row,
    gw,
    xs,
    xr,
    zs,
    zr,
    ps2,
    pr2,
    ptotal,
    pxs,
    pxr,
    cnt,
    cntr,
    sb,
    sbr,
    tb,
    tbr,
    load_sem,
    send_sem,
    recv_sem,
):
    dp = lax.axis_index("dp")
    t = lax.axis_index("tensor")
    z = dp // 2
    x = dp % 2
    y = t // 2
    c = t % 2
    z_mates = [(z_mate(z, k) * 2 + x, t) for k in (1, 2, 3)]
    x_mate = (z * 2 + 1 - x, t)
    y_mate = (dp, (1 - y) * 2 + c)
    c_mate = (dp, y * 2 + 1 - c)
    peer_window = (1 - y) * 2 + c
    token_total = lax.axis_size("dp") * 4 * WIN_TOK

    started = []

    def send(src, dst, mate):
        i = len(started)
        copy = pltpu.make_async_remote_copy(
            src_ref=src,
            dst_ref=dst,
            send_sem=send_sem.at[i],
            recv_sem=recv_sem.at[i],
            device_id=mate,
            device_id_type=MESH,
        )
        copy.start()
        started.append(copy)
        return copy

    barrier = pltpu.get_barrier_semaphore()
    for mate in z_mates + [x_mate, y_mate, c_mate]:
        pl.semaphore_signal(barrier, inc=1, device_id=mate, device_id_type=MESH)

    loads = []

    def load(src, dst):
        copy = pltpu.make_async_copy(src, dst, load_sem.at[len(loads)])
        copy.start()
        loads.append(copy)
        return copy

    first_loads = [load(triple_hbm, triple_in), load(out_w_hbm, out_w_in)]
    group_loads = [load(we_hbm, we_in), load(ws_hbm, ws_in)]
    x_load = load(x_in, xt)
    side_loads = [
        load(src, dst)
        for src, dst in (
            (expand_bias_hbm, expand_bias_in),
            (qv_bias_hbm, qv_bias_in),
            (valid_hbm, valid_in),
            (gain1_hbm, gain1_in),
            (shift1_hbm, shift1_in),
            (bias_out_hbm, bias_out_in),
            (gain2_hbm, gain2_in),
            (shift2_hbm, shift2_in),
            (bias_shrink_hbm, bias_shrink_in),
            (rows_hbm, rows_in),
            (columns_hbm, columns_in),
        )
    ]
    target_load = load(target_in, tt)

    w_in = (wa_in, we_in, ws_in)
    w_full = (wa, we, ws)
    from_z = {}
    from_x = {}
    from_p = {}
    from_c = {}

    def row_of(k, xx):
        return z_mate(z, k) * 2 + xx

    first = pl.ds(0, 640)
    last = pl.ds(640, 128)

    def gather_start(g):
        full = w_full[g]
        from_p[g, 0] = send(w_in[g].at[:, last], full.at[0, dp, :, last], x_mate)
        for k in (3, 1):
            from_z[g, k] = send(w_in[g].at[:, first], full.at[0, dp, :, first], z_mates[k - 1])
        from_x[g, 0] = send(w_in[g].at[:, first], full.at[0, dp, :, first], x_mate)
        from_c[g, 0] = send(w_in[g], full.at[1, dp], c_mate)
        full[0, dp] = w_in[g][...]

    def to_core(g, i, *at):
        from_c[g, i] = send(w_full[g].at[(0,) + at], w_full[g].at[(1,) + at], c_mate)

    def gather_pair(g, k):
        from_p[g, k].wait_recv()
        pair = (pl.ds(2 * z_mate(z, k), 2), slice(None), last)
        block = w_full[g].at[(0,) + pair]
        if k == 0:
            for m in (3, 1):
                from_p[g, m] = send(block, block, z_mates[m - 1])
            to_core(g, 8, row_of(0, 1 - x), slice(None), last)
        else:
            if k == 3:
                from_p[g, 2] = send(block, block, z_mates[0])
            to_core(g, 8 + k, *pair)

    def gather_z(g, k):
        from_z[g, k].wait_recv()
        block = w_full[g].at[0, row_of(k, x), :, first]
        if k == 3:
            from_z[g, 2] = send(block, block, z_mates[0])
        else:
            from_x[g, k] = send(block, block, x_mate)
        to_core(g, k, row_of(k, x), slice(None), first)

    def gather_far(g):
        block = w_full[g].at[0, row_of(3, x), :, first]
        from_x[g, 3] = send(block, block, x_mate)

    def gather_x(g, k):
        from_x[g, k].wait_recv()
        to_core(g, 4 + k, row_of(k, 1 - x), slice(None), first)

    def gather_end(g, far):
        for k in (2, 3, 6, 7, 10, 11) if far else (0, 1, 4, 5, 8, 9):
            from_c[g, k].wait_recv()

    tasks = []
    done = set()
    plan = iter(PLAN)

    def add(key, step, *args):
        tasks.append((key, step, args))
        tasks.sort(key=lambda task: ORDER.index(task[0]))

    def serve():
        key, step, args = tasks.pop(0)
        step(*args)
        done.add(key)

    def point():
        for _ in range(next(plan, 0)):
            if tasks:
                serve()

    def need(key):
        while key not in done:
            serve()

    def gather_add(g):
        add(("pair", g, 0), gather_pair, g, 0)
        add(("z", g, 3), gather_z, g, 3)
        if g == 0:
            add(("start", 1), gather_start, 1)
        add(("z", g, 1), gather_z, g, 1)
        add(("far", g), gather_far, g)
        add(("pair", g, 3), gather_pair, g, 3)
        add(("x", g, 0), gather_x, g, 0)
        add(("pair", g, 1), gather_pair, g, 1)
        add(("z", g, 2), gather_z, g, 2)
        if g == 0:
            add(("count",), count_spread)
            add(("start", 2), gather_start, 2)
        add(("x", g, 1), gather_x, g, 1)
        add(("near", g), gather_end, g, False)
        add(("x", g, 3), gather_x, g, 3)
        add(("pair", g, 2), gather_pair, g, 2)
        add(("x", g, 2), gather_x, g, 2)
        add(("all", g), gather_end, g, True)

    cnt_z = []

    def count_spread():
        cnt_x.wait_recv()
        cnt[1] = cnt[0] + cntr[0]
        cnt_z.extend(send(cnt.at[1], cntr.at[k], z_mates[k - 1]) for k in (1, 2, 3))

    for copy in first_loads:
        copy.wait()
    for i in range(3):
        wa_in[:, 128 * i : 128 * i + 128] = triple_in[i, :, 0:128]
    source = lax.broadcasted_iota(jnp.int32, (192, 256), 0)
    column = lax.broadcasted_iota(jnp.int32, (192, 256), 1)
    tail = sum(
        dot_nn(
            triple_in[i],
            ((source >= 128) & (source - 128 == column - 64 * i)).astype(F32).astype(BF16),
        )
        for i in range(3)
    )
    out_w = out_w_in[...]
    tail = tail + dot_tn(
        out_w, ((source >= 128) & (source + 64 == column)).astype(F32).astype(BF16)
    )
    wa_in[:, 384:640] = tail.astype(BF16)
    wa_in[:, 640:768] = dot_tn(
        out_w, (source == column).astype(F32).astype(BF16)[:, 0:128]
    ).astype(BF16)
    def fourteens(at):
        whole = jnp.floor((at + 0.5) * (1.0 / WIN))
        return whole, at - WIN * whole

    def grid(shape, dim):
        return lax.broadcasted_iota(jnp.int32, shape, dim).astype(F32)

    def entries(shape, dim):
        at = grid(shape, dim)
        side = (at >= 256.0).astype(F32)
        at = at - 256.0 * side
        main, other = fourteens(at)
        return side, main, other, at < float(WIN_TOK)

    side_of, main, other, valid = entries((512, 64), 0)
    slot = main - other + (WIN - 1) + 32.0 * side_of
    onehot[...] = jnp.where(valid & (grid((512, 64), 1) == slot), 1.0, 0.0).astype(BF16)
    side_of, main, other, valid = entries((ROWS, 512), 1)
    token = grid((ROWS, 512), 0)
    down, across = fourteens(token)
    hit = valid & (main == jnp.where(side_of > 0.5, across, down)) & (token < float(WIN_TOK))
    place[...] = jnp.where(hit, 1.0, 0.0).astype(BF16)
    side_of, main, other, valid = entries((512, KEYS), 0)
    token = grid((512, KEYS), 1)
    down, across = fourteens(token)
    hit = valid & (other == jnp.where(side_of > 0.5, across, down)) & (token < float(WIN_TOK))
    pick[...] = jnp.where(hit, 1.0, 0.0).astype(BF16)
    pl.semaphore_wait(barrier, 6)
    gather_start(0)
    for copy in group_loads + side_loads:
        copy.wait()
    side[0] = jnp.zeros((8, D), F32)
    side[0, 0:1, :] = expand_bias_in[...].reshape(1, D)
    side[0, 1:2, 0:128] = qv_bias_in[0:1, 0:128]
    side[0, 1:2, 256:384] = qv_bias_in[1:2, 0:128]
    side[0, 1:2, 384:448] = qv_bias_in[0:1, 128:192]
    side[0, 1:2, 512:576] = qv_bias_in[1:2, 128:192]
    side_copy = send(side.at[0], side.at[1], c_mate)
    marks_all = valid_in[...].astype(F32)
    cnt[0] = jnp.full((8, 128), jnp.sum(marks_all), F32)
    cnt_x = send(cnt.at[0], cntr.at[0], x_mate)
    for g in range(3):
        gather_add(g)

    gain1 = gain1_in[...].reshape(1, D)
    shift1 = shift1_in[...].reshape(1, D)
    bias_out = bias_out_in[...].reshape(1, D)
    gain2 = gain2_in[...].reshape(1, D)
    shift2 = shift2_in[...].reshape(1, D)
    shrink_row[...] = bias_shrink_in[...].reshape(1, D)

    lane = lax.broadcasted_iota(jnp.int32, (1, 128), 1)
    half = ((lane < 64).astype(F32), (lane >= 64).astype(F32))
    key_mask = [(m * 0.125).astype(BF16) for m in half]
    half = [m.astype(BF16) for m in half]
    key_lane = lax.broadcasted_iota(jnp.int32, (1, KEYS), 1)
    key_bias = jnp.where(key_lane < WIN_TOK, 0.0, -1e30).astype(F32)

    row_ids = lax.broadcasted_iota(jnp.int32, (4, WIN_TOK), 0)
    own_marks = column_sum(jnp.where(row_ids == t, marks_all, 0.0))
    eye = lax.broadcasted_iota(jnp.int32, (ROWS, WIN_TOK), 0) == lax.broadcasted_iota(
        jnp.int32, (ROWS, WIN_TOK), 1
    )
    live = jnp.sum(jnp.where(eye, own_marks, 0.0), axis=1, keepdims=True)

    window_ids = lax.broadcasted_iota(jnp.int32, (1, 4, 1), 1)

    def window_of(ref, window):
        return jnp.sum(ref[...].astype(F32) * (window_ids == window).astype(F32), axis=1)

    xf[...] = jnp.zeros_like(xf)
    x_load.wait()
    for w in range(2):
        xf[w, 0:WIN_TOK, :] = window_of(xt, peer_window if w else t)
        point()
        unit, inverse = normalize(xf[w])
        n1[0, w] = (unit * gain1 + shift1).astype(BF16)
        if w == 0:
            unit1[...] = unit
            inv1[...] = inverse
    n1_copy = send(n1.at[0], n1.at[1], c_mate)
    tabs[...] = jnp.zeros_like(tabs)
    tabs[0:27, 0:64] = rows_in[...]
    tabs[32:59, 0:64] = columns_in[...]
    t2[0] = dot_nn(onehot[...], tabs[...].astype(BF16)).astype(BF16)
    t2[1] = dot_nn(onehot[...], pltpu.roll(tabs[...], 64, 1).astype(BF16)).astype(BF16)
    pj[:, :, ROWS:, :] = jnp.zeros((2, 2, KEYS - ROWS, 896), BF16)
    tg[...] = jnp.zeros_like(tg)

    def project(w):
        def body(j, carry):
            value = dot_nn(n1[0, w], wa[j, :, :, 0:640].reshape(D, 640)) + side[j, 1:2, 0:640]
            pj[w, j, 0:ROWS, 0:640] = value.astype(BF16)
            rolled = pltpu.roll(value[:, 384:512], 64, 1)
            pj[w, j, 0:ROWS, 640:768] = rolled.astype(BF16)
            rolled = pltpu.roll(value[:, 512:640], 64, 1)
            pj[w, j, 0:ROWS, 768:896] = rolled.astype(BF16)
            return carry

        lax.fori_loop(0, 2, body, 0)

    def unit_of(w, j, h):
        q, k, v, p, pv = UNITS[h]
        query = pj[w, j, 0:ROWS, 128 * q : 128 * q + 128]
        key = pj[w, j, :, 128 * k : 128 * k + 128] * key_mask[p]
        value = pj[w, j, :, 128 * v : 128 * v + 128] * half[pv]
        return query, key, value

    def attend(w):
        def body(j, carry):
            mixes = []
            for h in range(3):
                query, key, value = unit_of(w, j, h)
                along = dot_nt(query, t2[UNITS[h][3]])
                high = along.astype(BF16)
                low = (along - high.astype(F32)).astype(BF16) * place[...]
                high = high * place[...]
                scores = dot_nt(query, key) + dot_nn(high, pick[...]) + dot_nn(low, pick[...])
                scores = scores + key_bias
                raised = jnp.exp(scores - jnp.max(scores, axis=-1, keepdims=True))
                soft = raised * (1.0 / jnp.sum(raised, axis=-1, keepdims=True))
                ps[w, j, h] = soft
                mixes.append(dot_nn(soft.astype(BF16), value))
            mx[j, w, :, 0:128] = mixes[2].astype(BF16)
            mx[j, w, :, 128:256] = (mixes[0] + mixes[1]).astype(BF16)
            return carry

        lax.fori_loop(0, 2, body, 0)
        point()

    def attended(w, lo, n):
        return dot_nt(mx[0, w, lo : lo + n, :], wa[0, :, :, 512:768].reshape(D, 256)) + dot_nt(
            mx[1, w, lo : lo + n, :], wa[1, :, :, 512:768].reshape(D, 256)
        )

    side_copy.wait_recv()
    need(("all", 0))
    project(1)
    point()
    attend(1)
    e1 = []
    for lo, n in CHUNKS:
        es[0, lo : lo + n, :] = attended(1, lo, n).astype(BF16)
        e1.append(send(es.at[0, pl.ds(lo, n)], er.at[0, pl.ds(lo, n)], y_mate))
    point()
    project(0)
    point()
    attend(0)
    mx_copy = send(mx.at[1], mxr, c_mate)
    mid[...] = xf[0] + bias_out + attended(0, 0, ROWS)
    point()

    e2 = []
    n2_c = []
    for i, (lo, n) in enumerate(CHUNKS):
        point()
        e1[i].wait_recv()
        middle = mid[lo : lo + n, :] + er[0, lo : lo + n, :].astype(F32)
        mid[lo : lo + n, :] = middle
        unit, inverse = normalize(middle)
        unit2[lo : lo + n, :] = unit
        inv2[lo : lo + n, :] = inverse
        n2[0, 0, lo : lo + n, :] = (unit * gain2 + shift2).astype(BF16)
        rows = pl.ds(lo, n)
        e2.append(send(n2.at[0, 0, rows], n2.at[0, 1, rows], y_mate))
        n2_c.append(send(n2.at[0, 0, rows], n2.at[1, 0, rows], c_mate))

    def feed(w, lo, n):
        def body(j, carry):
            before = dot_nn(n2[0, w, lo : lo + n, :], we[j].reshape(D, D)) + side[j, 0:1, :]
            phi = 0.5 * (1.0 + lax.erf(before * math.sqrt(0.5)))
            hid[j, w, lo : lo + n, :] = (before * phi).astype(BF16)
            bell = jnp.exp(-0.5 * before * before) * (1.0 / math.sqrt(2.0 * math.pi))
            slope[j, w, lo : lo + n, :] = phi + before * bell
            return carry

        lax.fori_loop(0, 2, body, 0)
        point()

    zone = z // 2
    zones = (zone, 1 - zone)
    halves = [pl.ds(pl.multiple_of(q * 384, 128), 384) for q in zones]

    def shrunk(w, i):
        rows = pl.ds(zones[i] * 4, 4)
        return dot_nt(hid[0, w], ws[0, rows].reshape(384, D)) + dot_nt(
            hid[1, w], ws[1, rows].reshape(384, D)
        )

    need(("all", 1))
    for lo, n in CHUNKS:
        feed(0, lo, n)
    for i, (lo, n) in enumerate(CHUNKS):
        rows = pl.ds(lo, n)
        point()
        e2[i].wait_recv()
        n2_c.append(send(n2.at[0, 1, rows], n2.at[1, 1, rows], c_mate))
        feed(1, lo, n)
    hid_copy = send(hid.at[1], hidr, c_mate)
    target_load.wait()
    xf[1, 0:WIN_TOK, :] = window_of(tt, t)
    point()
    xf[1, WIN_TOK:, :] = jnp.zeros((ROWS - WIN_TOK, D), F32)
    need(("near", 2))
    for copy in cnt_z:
        copy.wait_recv()
    count = (cnt[1] + cntr[1]) + (cntr[2] + cntr[3])
    count = count[0:1, 0:1]
    scaled_live = live * (token_total / count)
    e3 = []
    for i in range(2):
        if i == 1:
            need(("all", 2))
        es3[i] = shrunk(1, i).astype(BF16)
        e3.append(send(es3.at[i], er3.at[i], y_mate))
        acc[:, halves[i]] = mid[:, halves[i]] + shrink_row[:, halves[i]] + shrunk(0, i)

    e4 = []
    gr_c = []
    for i in range(2):
        cols = halves[i]
        e3[i].wait_recv()
        result = acc[:, cols] + er3[i].astype(F32)
        gap = result - xf[1, :, cols]
        grad = gap * scaled_live
        acc[:, cols] = grad
        gr[0, 0, :, cols] = grad.astype(BF16)
        e4.append(send(gr.at[0, 0, :, cols], gr.at[0, 1, :, cols], y_mate))
        gr_c.append(send(gr.at[0, 0, :, cols], gr.at[1, 0, :, cols], c_mate))
        bo[t, :, cols] = result.astype(BF16)
        sums[6:7, cols] = column_sum(gap * gap * live)
        sums[0:1, cols] = column_sum(grad)
    sb[0] = jnp.zeros((16, D), F32)
    sb[0, 6:7, :] = sums[6:7, :]
    sb[0, 0:1, :] = sums[0:1, :]

    def feed_back(w, lo, n):
        def body(j, carry):
            grad = dot_nn(gr[0, w, lo : lo + n, :], ws[j].reshape(D, D))
            grad = grad * slope[j, w, lo : lo + n, :]
            gb[j, w, lo : lo + n, :] = grad.astype(BF16)
            return carry

        lax.fori_loop(0, 2, body, 0)

    def expanded_back(w, lo, n):
        return dot_nt(gb[0, w, lo : lo + n, :], we[0].reshape(D, D)) + dot_nt(
            gb[1, w, lo : lo + n, :], we[1].reshape(D, D)
        )

    def rows_of(ref, width):
        return ref[...].reshape(2 * ROWS, width)

    def weight_grad(g, left, mine, theirs, width, at):
        def body(m, carry):
            cols = pl.ds(pl.multiple_of(m * 384, 128), 384)
            rows = pl.ds(m * 4, 4)
            value = dot_tn(left[0, :, :, cols].reshape(2 * ROWS, 384), mine.reshape(2 * ROWS, width))
            value = value + dot_tn(
                left[1, :, :, cols].reshape(2 * ROWS, 384), theirs.reshape(2 * ROWS, width)
            )
            gw[g, rows, :, at : at + width] = value.reshape(4, 96, width)
            return carry

        lax.fori_loop(0, 2, body, 0)

    to_x = {}
    to_z = {}

    pair_of = {}

    def pair_rows(k):
        return pl.ds(2 * z_mate(z, k), 2)

    def scatter_pairs(g):
        for i, k in enumerate((2, 1)):
            ps2[g, i] = gw[g, pair_rows(k), :, 640:768].astype(BF16)
            pair_of[g, i] = send(ps2.at[g, i], pr2.at[g, i], z_mates[0])

    parts = {0: ((0, 384), (384, 256)), 1: ((0, 640),), 2: ((0, 640),)}

    def scatter_blocks(g, i, blocks):
        lo, n = parts[g][i]
        for k in blocks:
            xs[g, k, :, lo : lo + n] = gw[g, row_of(k, 1 - x), :, lo : lo + n].astype(BF16)
            at = (g, k, slice(None), pl.ds(lo, n))
            to_x[g, k, i] = send(xs.at[at], xr.at[at], x_mate)

    def scatter_pair(g):
        pair_of[g, 0].wait_recv()
        total = gw[g, pair_rows(3), :, 640:768] + pr2[g, 0].astype(F32)
        ps2[g, 2] = total.astype(BF16)
        pair_of[g, 2] = send(ps2.at[g, 2], pr2.at[g, 2], z_mates[2])

    def scatter_turn(g):
        pair_of[g, 1].wait_recv()
        pair_of[g, 2].wait_recv()
        total = gw[g, pair_rows(0), :, 640:768] + pr2[g, 1].astype(F32)
        ptotal[g] = total + pr2[g, 2].astype(F32)
        pxs[g] = ptotal[g, 1 - x].astype(BF16)
        pair_of[g, 3] = send(pxs.at[g], pxr.at[g], x_mate)

    def scatter_z(g, k, i):
        lo, n = parts[g][i]
        cols = slice(lo, lo + n)
        to_x[g, k, i].wait_recv()
        total = gw[g, row_of(k, x), :, cols] + xr[g, k, :, cols].astype(F32)
        if k == 3:
            to_z[g, 2, i].wait_recv()
            total = total + zr[g, 1, :, cols].astype(F32)
        zs[g, k - 1, :, cols] = total.astype(BF16)
        at = (g, k - 1, slice(None), pl.ds(lo, n))
        to_z[g, k, i] = send(zs.at[at], zr.at[at], z_mates[2 if k == 3 else 0])

    def scatter_end(g, i, out):
        lo, n = parts[g][i]
        cols = slice(lo, lo + n)
        to_x[g, 0, i].wait_recv()
        to_z[g, 1, i].wait_recv()
        to_z[g, 3, i].wait_recv()
        total = gw[g, dp, :, cols] + xr[g, 0, :, cols].astype(F32)
        out[:, cols] = total + zr[g, 0, :, cols].astype(F32) + zr[g, 2, :, cols].astype(F32)

    def scatter_last(g, out):
        pair_of[g, 3].wait_recv()
        out[:, 640:768] = ptotal[g, x] + pxr[g].astype(F32)

    def scatter_add(g, *keys):
        steps = {"pair": scatter_pair, "turn": scatter_turn}
        for key in keys:
            if key in steps:
                add((key + "s", g), steps[key], g)
            else:
                add(("zs", g, *key), scatter_z, g, *key)

    for lo, n in CHUNKS:
        feed_back(0, lo, n)
    for i in range(2):
        e4[i].wait_recv()
        gr_c.append(send(gr.at[0, 1, :, halves[i]], gr.at[1, 1, :, halves[i]], c_mate))
    e5 = []
    for lo, n in CHUNKS:
        rows = pl.ds(lo, n)
        feed_back(1, lo, n)
        es[1, lo : lo + n, :] = expanded_back(1, lo, n).astype(BF16)
        e5.append(send(es.at[1, rows], er.at[1, rows], y_mate))
    gb_copy = send(gb.at[1], gbr, c_mate)
    mid[...] = expanded_back(0, 0, ROWS)
    for copy in gr_c:
        copy.wait_recv()
    hid_copy.wait_recv()
    weight_grad(2, gr, hid[0], hidr[...], D, 0)
    scatter_pairs(2)
    scatter_blocks(2, 0, (2, 3, 1, 0))
    scatter_add(2, "pair", (2, 0), "turn", (3, 0), (1, 0))
    point()

    e6 = []
    gm_c = []
    gain_part = jnp.zeros((1, D), F32)
    shift_part = jnp.zeros((1, D), F32)
    bias_part = jnp.zeros((1, D), F32)
    for i, (lo, n) in enumerate(CHUNKS):
        rows = pl.ds(lo, n)
        point()
        e5[i].wait_recv()
        grad = mid[lo : lo + n, :] + er[1, lo : lo + n, :].astype(F32)
        unit = unit2[lo : lo + n, :]
        gain_part = gain_part + column_sum(grad * unit)
        shift_part = shift_part + column_sum(grad)
        grad = acc[lo : lo + n, :] + normalize_back(grad, unit, inv2[lo : lo + n, :], gain2)
        acc[lo : lo + n, :] = grad
        gm[0, 0, lo : lo + n, :] = grad.astype(BF16)
        e6.append(send(gm.at[0, 0, rows], gm.at[0, 1, rows], y_mate))
        gm_c.append(send(gm.at[0, 0, rows], gm.at[1, 0, rows], c_mate))
        bias_part = bias_part + column_sum(grad)
    sb[0, 1:2, :] = gain_part
    sb[0, 2:3, :] = shift_part
    sb[0, 3:4, :] = bias_part

    bo_y = send(bo.at[t], bo.at[t], y_mate)
    bo_c = [send(bo.at[t], bo.at[t], c_mate)]

    def block_pass():
        bo_y.wait_recv()
        bo_c.append(send(bo.at[peer_window], bo.at[peer_window], c_mate))

    def block_mix():
        for copy in bo_c:
            copy.wait_recv()
        for w in range(4):
            mix[:, w, :] = bo[w, 0:WIN_TOK, :].astype(F32)
        xt[...] = mix[...].astype(BF16)
        stores.append(load(xt, block_out))

    stores = []
    gb_copy.wait_recv()
    for copy in n2_c:
        copy.wait_recv()
    weight_grad(1, n2, gb[0], gbr[...], D, 0)
    ones = jnp.ones((8, 2 * ROWS), BF16)
    sb[0, 8:9, :] = (dot_nn(ones, rows_of(gb.at[0], D)) + dot_nn(ones, rows_of(gbr, D)))[0:1]
    scatter_pairs(1)
    scatter_blocks(1, 0, (2, 3, 1, 0))
    scatter_add(1, "pair", (2, 0), "turn", (3, 0), (1, 0))
    point()

    def mixed_back(w, lo, n):
        for j in range(2):
            grad = dot_nn(gm[0, w, lo : lo + n, :], wa[j, :, :, 512:768].reshape(D, 256))
            gmx[j, w, lo : lo + n, :] = grad.astype(BF16)

    def unit_back(w, j, h):
        query, key, value = unit_of(w, j, h)
        p, pv = UNITS[h][3:]
        grad = gmx[j, w, :, 0:128] if h == 2 else gmx[j, w, :, 128:256]
        soft = ps[w, j, h]
        grad_soft = dot_nt(grad, value)
        delta = jnp.sum(soft * grad_soft, axis=-1, keepdims=True)
        grad_scores = (soft * (grad_soft - delta)).astype(BF16)
        grad_v = dot_tn(soft.astype(BF16), grad * half[pv])[0:ROWS]
        grad_k = dot_tn(grad_scores, query * key_mask[p])[0:ROWS]
        part = dot_nt(grad_scores, pick[...]).astype(BF16) * place[...]
        grad_q = dot_nn(grad_scores, key) + dot_nn(part, t2[p])
        tg[...] += dot_tn(query * half[p], part)
        return grad_q, grad_k, grad_v

    def attend_back_pair(w, j):
        one, two = unit_back(w, j, 0), unit_back(w, j, 1)
        for i in range(3):
            gp[j, w, :, 128 * i : 128 * i + 128] = (one[i] + two[i]).astype(BF16)

    def attend_back_last(w, j):
        grad_q, grad_k, grad_v = unit_back(w, j, 2)
        gp[j, w, :, 384:512] = (grad_q + pltpu.roll(grad_k, 64, 1)).astype(BF16)
        gp[j, w, :, 512:640] = pltpu.roll(grad_v, 64, 1).astype(BF16)

    def projected_back(w, lo, n):
        return dot_nt(gp[0, w, lo : lo + n, :], wa[0, :, :, 0:640].reshape(D, 640)) + dot_nt(
            gp[1, w, lo : lo + n, :], wa[1, :, :, 0:640].reshape(D, 640)
        )

    for i, (lo, n) in enumerate(CHUNKS):
        rows = pl.ds(lo, n)
        point()
        e6[i].wait_recv()
        gm_c.append(send(gm.at[0, 1, rows], gm.at[1, 1, rows], c_mate))
        mixed_back(1, lo, n)
    point()
    add(("block pass",), block_pass)
    add(("block mix",), block_mix)
    def both_back(j, carry):
        attend_back_pair(1, j)
        attend_back_last(1, j)
        return carry

    lax.fori_loop(0, 2, both_back, 0)
    point()
    gp_copies = [send(gp.at[1, 1], gpr.at[1], c_mate)]
    e7 = []
    for lo, n in CHUNKS:
        rows = pl.ds(lo, n)
        es[2, lo : lo + n, :] = projected_back(1, lo, n).astype(BF16)
        e7.append(send(es.at[2, rows], er.at[2, rows], y_mate))
    point()
    for copy in gm_c:
        copy.wait_recv()
    mx_copy.wait_recv()
    weight_grad(0, gm, mx[0], mxr[...], 256, 512)
    scatter_pairs(0)
    scatter_add(0, "pair", "turn")
    point()
    mixed_back(0, 0, ROWS)
    def pair_back(j, carry):
        attend_back_pair(0, j)
        return carry

    lax.fori_loop(0, 2, pair_back, 0)
    point()
    gp_copies.append(send(gp.at[1, 0, :, pl.ds(0, 384)], gpr.at[0, :, pl.ds(0, 384)], c_mate))
    attend_back_last(0, 0)
    point()
    n1_copy.wait_recv()
    for copy in gp_copies:
        copy.wait_recv()

    weight_grad(0, n1, gp[0, :, :, 0:384], gpr[:, :, 0:384], 384, 0)
    scatter_blocks(0, 0, (2, 3, 1, 0))
    scatter_add(0, (2, 0))
    attend_back_last(0, 1)
    last_copy = send(gp.at[1, 0, :, pl.ds(384, 256)], gpr.at[0, :, pl.ds(384, 256)], c_mate)
    mid[...] = projected_back(0, 0, ROWS)
    last_copy.wait_recv()
    held = gw[0, :, :, 512:640]
    weight_grad(0, n1, gp[0, :, :, 384:640], gpr[:, :, 384:640], 256, 384)
    gw[0, :, :, 512:640] += held
    need(("turns", 0))
    scatter_blocks(0, 1, (2, 3, 1, 0))

    small = {}

    def small_first():
        bias = dot_nn(ones, rows_of(gp.at[0], 640)) + dot_nn(ones, rows_of(gpr, 640))
        sb[0, 9:10, 0:640] = bias[0:1]
        spread = tg[...]
        spread_high = spread.astype(BF16)
        spread_low = (spread - spread_high.astype(F32)).astype(BF16)
        table = dot_nn(spread_high, onehot[...]) + dot_nn(spread_low, onehot[...])
        tb[0] = table[0:64] + table[64:128]

    top = pl.ds(0, 8)

    def small_send(stage, dst, mate, rows):
        return [
            send(sb.at[stage, rows], sbr.at[dst, rows], mate),
            send(tb.at[stage], tbr.at[dst], mate),
        ]

    def small_wait(stage):
        for copy in small[stage]:
            copy.wait_recv()

    def small_z():
        small[0] = sum((small_send(0, k - 1, z_mates[k - 1], pl.ds(0, 16)) for k in (1, 2, 3)), [])

    def small_c():
        small_wait(0)
        sb[1] = (sb[0] + sbr[0]) + (sbr[1] + sbr[2])
        tb[1] = (tb[0] + tbr[0]) + (tbr[1] + tbr[2])
        small[1] = small_send(1, 3, c_mate, top)

    def small_next(stage, mate, rows):
        small_wait(stage - 1)
        sb[stage] = sb[stage - 1]
        sb[stage, 0:8, :] = sb[stage - 1, 0:8, :] + sbr[stage + 1, 0:8, :]
        tb[stage] = tb[stage - 1] + tbr[stage + 1]
        small[stage] = small_send(stage, stage + 2, mate, rows)

    def small_end():
        small_wait(3)
        total = sb[3] + sbr[5]
        small_out[...] = total
        small_out[6:7, :] = jnp.broadcast_to(
            jnp.sum(total[6:7, :], axis=1, keepdims=True) / (count * float(D)), (1, D)
        )
        table_out[...] = (tb[3] + tbr[5]).T

    e8 = {}
    ig_c = {}

    def mix_in(window, i):
        lo, n = CHUNKS[i]
        top = min(lo + n, WIN_TOK)
        mix[lo:top, pl.ds(window, 1), :] = (
            ig[window, lo:top, :].astype(F32).reshape(top - lo, 1, D)
        )

    def own_grad(i):
        lo, n = CHUNKS[i]
        e7[i].wait_recv()
        grad = mid[lo : lo + n, :] + er[2, lo : lo + n, :].astype(F32)
        unit = unit1[lo : lo + n, :]
        gain_part = column_sum(grad * unit)
        shift_part = column_sum(grad)
        sb[0, 4:5, :] = gain_part if i == 0 else sb[0, 4:5, :] + gain_part
        sb[0, 5:6, :] = shift_part if i == 0 else sb[0, 5:6, :] + shift_part
        grad = acc[lo : lo + n, :] + normalize_back(grad, unit, inv1[lo : lo + n, :], gain1)
        ig[t, lo : lo + n, :] = grad.astype(BF16)
        rows = pl.ds(lo, n)
        ig_c[i, 0] = send(ig.at[t, rows], ig.at[t, rows], c_mate)
        e8[i] = send(ig.at[t, rows], ig.at[t, rows], y_mate)
        mix_in(t, i)

    def side_grad(i):
        ig_c[i, 0].wait_recv()
        mix_in(t + 1 - 2 * c, i)

    def peer_grad(i):
        lo, n = CHUNKS[i]
        rows = pl.ds(lo, n)
        e8[i].wait_recv()
        ig_c[i, 1] = send(ig.at[peer_window, rows], ig.at[peer_window, rows], c_mate)
        mix_in(peer_window, i)

    def last_grad(i):
        lo, n = CHUNKS[i]
        ig_c[i, 1].wait_recv()
        mix_in(peer_window + 1 - 2 * c, i)
        rows = pl.ds(lo, min(n, WIN_TOK - lo))
        stores.append(load(mix.at[rows], grad_out.at[rows]))

    def scatter_out(g, held, out):
        if g > 0:
            scatter_end(g, 0, held)
        else:
            scatter_end(0, 1, held)
        scatter_last(g, held)
        stores.append(load(held, out))

    need(("block mix",))
    add(("own", 0), own_grad, 0)
    add(("small first",), small_first)
    add(("own", 1), own_grad, 1)
    add(("small z",), small_z)
    scatter_add(0, (3, 0), (2, 1), (1, 0))
    add(("side", 0), side_grad, 0)
    add(("side", 1), side_grad, 1)
    add(("small c",), small_c)
    add(("out", 2), scatter_out, 2, gs, gs_out)
    add(("out", 1), scatter_out, 1, ge, ge_out)
    add(("small y",), small_next, 2, y_mate, top)
    add(("peer", 0), peer_grad, 0)
    scatter_add(0, (3, 1), (1, 1))
    add(("last", 0), last_grad, 0)
    add(("small x",), small_next, 3, x_mate, pl.ds(0, 16))
    add(("peer", 1), peer_grad, 1)
    add(("last", 1), last_grad, 1)
    add(("end", 0), scatter_end, 0, 0, ga)
    add(("out", 0), scatter_out, 0, ga, ga_out)
    add(("small end",), small_end)
    need(("small end",))
    for copy in started:
        copy.wait_send()
    for copy in stores:
        copy.wait()


def finish_kernel(
    block_in,
    grad_in,
    ga,
    ge,
    gs,
    small,
    table,
    block_out,
    loss_out,
    grad_out,
    gain1_out,
    shift1_out,
    triple_out,
    qv_out,
    out_w_out,
    out_b_out,
    gain2_out,
    shift2_out,
    we_out,
    expand_bias_out,
    ws_out,
    bias_shrink_out,
    rows_out,
    columns_out,
    block_hold,
    grad_hold,
    ge_hold,
    gs_hold,
    sems,
):
    moves = []
    at = 0
    for src, hold, dst, step in (
        (block_in, block_hold, block_out, 49),
        (grad_in, grad_hold, grad_out, 49),
        (ge, ge_hold, we_out, 96),
        (gs, gs_hold, ws_out, 96),
    ):
        for lo in range(0, src.shape[0], step):
            rows = pl.ds(lo, step)
            copy = pltpu.make_async_copy(src.at[rows], hold.at[rows], sems.at[at])
            copy.start()
            moves.append(
                (copy, pltpu.make_async_copy(hold.at[rows], dst.at[rows], sems.at[at + 1]))
            )
            at += 2
    for i in range(3):
        triple_out[i, :, 0:128] = ga[:, 128 * i : 128 * i + 128]
    triple_out[0, :, 128:192] = ga[:, 384:448]
    triple_out[1, :, 128:192] = pltpu.roll(ga[:, 384:512], 64, 1)[:, 0:64]
    triple_out[2, :, 128:192] = ga[:, 512:576]
    out_w_out[0:128, :] = ga[:, 640:768].T
    out_w_out[128:192, :] = ga[:, 512:640].T[64:128]
    loss_out[...] = small[6:7, 0:1]
    for i, out in enumerate(
        (bias_shrink_out, gain2_out, shift2_out, out_b_out, gain1_out, shift1_out)
    ):
        out[...] = small[i]
    expand_bias_out[...] = small[8]
    for i in range(2):
        qv_out[i : i + 1, 0:128] = small[9:10, 256 * i : 256 * i + 128]
        qv_out[i : i + 1, 128:192] = small[9:10, 384 + 128 * i : 448 + 128 * i]
    rows_out[...] = table[0:27]
    columns_out[...] = table[32:59]
    for arrive, leave in moves:
        arrive.wait()
        leave.start()
    for arrive, leave in moves:
        leave.wait()


def fused(
    inputs,
    target,
    valid,
    first_gain,
    first_shift,
    triple_weight,
    query_value_bias,
    output_weight,
    output_bias,
    second_gain,
    second_shift,
    expand_weight,
    expand_bias,
    shrink_weight,
    shrink_bias,
    rows_table,
    columns_table,
):
    vmem = pl.BlockSpec(memory_space=pltpu.VMEM)
    anywhere = pl.BlockSpec(memory_space=pl.ANY)
    mixed_shape = (WIN_TOK, 4, D)
    part = jax.ShapeDtypeStruct((96, D), F32)
    copies = 224
    parts = pl.pallas_call(
        block_kernel,
        out_shape=[
            jax.ShapeDtypeStruct(mixed_shape, BF16),
            jax.ShapeDtypeStruct(mixed_shape, F32),
            part,
            part,
            part,
            jax.ShapeDtypeStruct((16, D), F32),
            jax.ShapeDtypeStruct((64, 64), F32),
        ],
        in_specs=[anywhere] * 17,
        out_specs=[anywhere] * 5 + [vmem] * 2,
        scratch_shapes=[
            pltpu.VMEM(valid.shape, jnp.int32),
            pltpu.VMEM((D,), F32),
            pltpu.VMEM((D,), F32),
            pltpu.VMEM(triple_weight.shape, BF16),
            pltpu.VMEM(query_value_bias.shape, F32),
            pltpu.VMEM(output_weight.shape, BF16),
            pltpu.VMEM((D,), F32),
            pltpu.VMEM((D,), F32),
            pltpu.VMEM((D,), F32),
            pltpu.VMEM(expand_weight.shape, BF16),
            pltpu.VMEM(expand_bias.shape, F32),
            pltpu.VMEM(expand_weight.shape, BF16),
            pltpu.VMEM((D,), F32),
            pltpu.VMEM(rows_table.shape, F32),
            pltpu.VMEM(columns_table.shape, F32),
            pltpu.VMEM((96, D), BF16),
            pltpu.VMEM((2, 8, 96, D), BF16),
            pltpu.VMEM((2, 8, 96, D), BF16),
            pltpu.VMEM((2, 8, 96, D), BF16),
            pltpu.VMEM(mixed_shape, BF16),
            pltpu.VMEM(mixed_shape, BF16),
            pltpu.VMEM((512, 64), BF16),
            pltpu.VMEM((ROWS, 512), BF16),
            pltpu.VMEM((512, KEYS), BF16),
            pltpu.VMEM((64, 128), F32),
            pltpu.VMEM((4, ROWS, D), BF16),
            pltpu.VMEM((4, ROWS, D), BF16),
            pltpu.VMEM(mixed_shape, F32),
            pltpu.VMEM((96, D), F32),
            pltpu.VMEM((96, D), F32),
            pltpu.VMEM((96, D), F32),
            pltpu.VMEM((2, 8, D), F32),
            pltpu.VMEM((2, ROWS, D), F32),
            pltpu.VMEM((ROWS, D), F32),
            pltpu.VMEM((ROWS, D), F32),
            pltpu.VMEM((ROWS, 1), F32),
            pltpu.VMEM((ROWS, 1), F32),
            pltpu.VMEM((ROWS, D), F32),
            pltpu.VMEM((ROWS, D), F32),
            pltpu.VMEM((2, 2, ROWS, D), BF16),
            pltpu.VMEM((2, 2, ROWS, D), BF16),
            pltpu.VMEM((2, 2, ROWS, D), BF16),
            pltpu.VMEM((2, 2, ROWS, D), BF16),
            pltpu.VMEM((2, 2, KEYS, 896), BF16),
            pltpu.VMEM((2, 2, 3, ROWS, KEYS), F32),
            pltpu.VMEM((2, 2, ROWS, 256), BF16),
            pltpu.VMEM((2, ROWS, 256), BF16),
            pltpu.VMEM((2, 2, ROWS, D), BF16),
            pltpu.VMEM((2, ROWS, D), BF16),
            pltpu.VMEM((2, 2, ROWS, D), F32),
            pltpu.VMEM((2, 2, ROWS, D), BF16),
            pltpu.VMEM((2, ROWS, D), BF16),
            pltpu.VMEM((2, 2, ROWS, 256), BF16),
            pltpu.VMEM((2, 2, ROWS, 640), BF16),
            pltpu.VMEM((2, ROWS, 640), BF16),
            pltpu.VMEM((2, 512, 128), BF16),
            pltpu.VMEM((128, 512), F32),
            pltpu.VMEM((3, ROWS, D), BF16),
            pltpu.VMEM((3, ROWS, D), BF16),
            pltpu.VMEM((2, ROWS, 384), BF16),
            pltpu.VMEM((2, ROWS, 384), BF16),
            pltpu.VMEM((8, D), F32),
            pltpu.VMEM((1, D), F32),
            pltpu.VMEM((3, 8, 96, D), F32),
            pltpu.VMEM((3, 4, 96, 640), BF16),
            pltpu.VMEM((3, 4, 96, 640), BF16),
            pltpu.VMEM((3, 3, 96, 640), BF16),
            pltpu.VMEM((3, 3, 96, 640), BF16),
            pltpu.VMEM((3, 3, 2, 96, 128), BF16),
            pltpu.VMEM((3, 3, 2, 96, 128), BF16),
            pltpu.VMEM((3, 2, 96, 128), F32),
            pltpu.VMEM((3, 96, 128), BF16),
            pltpu.VMEM((3, 96, 128), BF16),
            pltpu.VMEM((2, 8, 128), F32),
            pltpu.VMEM((4, 8, 128), F32),
            pltpu.VMEM((4, 16, D), F32),
            pltpu.VMEM((6, 16, D), F32),
            pltpu.VMEM((4, 64, 64), F32),
            pltpu.VMEM((6, 64, 64), F32),
            pltpu.SemaphoreType.DMA((32,)),
            pltpu.SemaphoreType.DMA((copies,)),
            pltpu.SemaphoreType.DMA((copies,)),
        ],
        compiler_params=pltpu.CompilerParams(
            collective_id=0, has_side_effects=True, vmem_limit_bytes=60 << 20
        ),
    )(
        inputs.transpose(1, 0, 2),
        target.transpose(1, 0, 2),
        valid,
        first_gain,
        first_shift,
        triple_weight,
        query_value_bias,
        output_weight,
        output_bias,
        second_gain,
        second_shift,
        expand_weight,
        expand_bias,
        shrink_weight.T,
        shrink_bias,
        rows_table,
        columns_table,
    )
    vector = jax.ShapeDtypeStruct((D,), F32)
    relative = jax.ShapeDtypeStruct(rows_table.shape, F32)
    outs = pl.pallas_call(
        finish_kernel,
        out_shape=[
            jax.ShapeDtypeStruct(mixed_shape, BF16),
            jax.ShapeDtypeStruct((1, 1), F32),
            jax.ShapeDtypeStruct(mixed_shape, F32),
            vector,
            vector,
            jax.ShapeDtypeStruct(triple_weight.shape, F32),
            jax.ShapeDtypeStruct(query_value_bias.shape, F32),
            jax.ShapeDtypeStruct(output_weight.shape, F32),
            vector,
            vector,
            vector,
            part,
            jax.ShapeDtypeStruct(expand_bias.shape, F32),
            part,
            vector,
            relative,
            relative,
        ],
        in_specs=[anywhere] * 2 + [vmem, anywhere, anywhere] + [vmem] * 2,
        out_specs=[
            anywhere if i in (0, 2, 11, 13) else vmem for i in range(17)
        ],
        scratch_shapes=[
            pltpu.VMEM(mixed_shape, BF16),
            pltpu.VMEM(mixed_shape, F32),
            pltpu.VMEM((96, D), F32),
            pltpu.VMEM((96, D), F32),
            pltpu.SemaphoreType.DMA((20,)),
        ],
    )(*parts)
    outs = list(outs)
    outs[0] = outs[0].transpose(1, 0, 2)
    outs[1] = outs[1].reshape(())
    outs[2] = outs[2].transpose(1, 0, 2)
    outs[13] = outs[13].T
    return tuple(outs)


def solution(mesh):
    placed = (
        P("dp", None, None),
        P("dp", None, None),
        P("dp", None),
        P(),
        P(),
        P(None, "dp", "tensor"),
        P(None, "tensor"),
        P("tensor", "dp"),
        P(),
        P(),
        P(),
        P("dp", "tensor"),
        P("tensor"),
        P("tensor", "dp"),
        P(),
        P(),
        P(),
    )
    on_slice = mesh.shape["dp"] == 8 and mesh.shape["tensor"] == 4
    return jax.shard_map(
        fused if on_slice else shards,
        mesh=mesh,
        in_specs=placed,
        out_specs=(
            P("dp", None, None),
            P(),
            P("dp", None, None),
            P(),
            P(),
            P(None, "dp", "tensor"),
            P(None, "tensor"),
            P("tensor", "dp"),
            P(),
            P(),
            P(),
            P("dp", "tensor"),
            P("tensor"),
            P("tensor", "dp"),
            P(),
            P(),
            P(),
        ),
        check_vma=False,
    )
```

```python
import math

import jax
import jax.numpy as jnp
import numpy as np
from jax import lax
from jax.experimental import pallas as pl
from jax.experimental.pallas import tpu as pltpu
from jax.sharding import PartitionSpec as P

MESH = pl.DeviceIdType.MESH

D = 768
HEADS = 12
HEAD = 64
WIN = 14
WIN_TOK = 196
MICRO = 2


def normalize(values):
    center = jnp.mean(values, axis=-1, keepdims=True)
    centered = values - center
    spread = jnp.mean(centered * centered, axis=-1, keepdims=True)
    inverse = lax.rsqrt(spread + 1e-06)
    return (centered * inverse, inverse)


def normalize_back(grad_out, unit, inverse, gain):
    scaled = grad_out * gain
    mean_one = jnp.mean(scaled, axis=-1, keepdims=True)
    mean_two = jnp.mean(scaled * unit, axis=-1, keepdims=True)
    return inverse * (scaled - mean_one - unit * mean_two)


def position_select(side):
    shape = (side, side, 2 * side - 1)
    first = lax.broadcasted_iota(jnp.int32, shape, 0)
    second = lax.broadcasted_iota(jnp.int32, shape, 1)
    slots = lax.broadcasted_iota(jnp.int32, shape, 2)
    return (slots == first - second + side - 1).astype(jnp.bfloat16)


def score_block(queries, keys, table_rows, table_cols, scale_factor):
    groups = queries.shape[0]
    side = queries.shape[1]
    heads = queries.shape[3]
    along_rows = jnp.einsum(
        "gabnc,aec->gnabe", queries, table_rows, preferred_element_type=jnp.float32
    )
    along_cols = jnp.einsum(
        "gabnc,bfc->gnabf", queries, table_cols, preferred_element_type=jnp.float32
    )
    scores = (
        jnp.einsum("gabnc,gefnc->gnabef", queries, keys, preferred_element_type=jnp.float32)
        * scale_factor
    )
    scores = scores + along_rows[..., :, None] + along_cols[..., None, :]
    return scores.reshape(groups, heads, side * side, side * side)


def gelu_exact(inner):
    return jax.nn.gelu(inner, approximate=False)


def row_total(partial_value):
    return lax.psum(partial_value, "tensor")


def share_of(values):
    share_rows = values.shape[0] // lax.axis_size("tensor")
    return lax.dynamic_slice_in_dim(values, lax.axis_index("tensor") * share_rows, share_rows, 0)


def shards(
    inputs,
    target,
    valid,
    first_gain,
    first_shift,
    triple_weight,
    query_value_bias,
    output_weight,
    output_bias,
    second_gain,
    second_shift,
    expand_weight,
    expand_bias,
    shrink_weight,
    shrink_bias,
    rows_table,
    columns_table,
):
    local_heads = HEADS // lax.axis_size("tensor")
    local_width = local_heads * HEAD
    local_windows = inputs.shape[0]
    win_micro = local_windows // MICRO
    micro_rows = win_micro * WIN_TOK
    scale_factor = 1.0 / math.sqrt(HEAD)
    highest = lax.Precision.HIGHEST
    live = valid.astype(jnp.float32)
    select = position_select(WIN)
    table_rows = jnp.einsum(
        "aej,jc->aec", select, rows_table.astype(jnp.bfloat16), preferred_element_type=jnp.float32
    ).astype(jnp.bfloat16)
    table_cols = jnp.einsum(
        "aej,jc->aec",
        select,
        columns_table.astype(jnp.bfloat16),
        preferred_element_type=jnp.float32,
    ).astype(jnp.bfloat16)
    rows_float = table_rows.astype(jnp.float32)
    cols_float = table_cols.astype(jnp.float32)
    triple_bias = jnp.stack(
        [query_value_bias[0], jnp.zeros_like(query_value_bias[0]), query_value_bias[1]]
    )
    saved = []
    outputs = []
    local_loss = jnp.zeros((), jnp.float32)
    for micro in range(MICRO):
        gathered = (
            lax.all_gather(triple_weight, "dp", axis=1, tiled=True),
            lax.all_gather(output_weight, "dp", axis=1, tiled=True),
            lax.all_gather(expand_weight, "dp", axis=0, tiled=True),
            lax.all_gather(shrink_weight, "dp", axis=1, tiled=True),
        )
        full_triple, full_output, full_expand, full_shrink = gathered
        lower = micro * win_micro
        flat_rows = inputs[lower : lower + win_micro].reshape(micro_rows, D).astype(jnp.float32)
        unit_one, inverse_one = normalize(flat_rows)
        normed = (unit_one * first_gain + first_shift).astype(jnp.bfloat16)
        projected = (
            jnp.einsum("rd,tde->rte", normed, full_triple, preferred_element_type=jnp.float32)
            + triple_bias
        )
        projected = projected.astype(jnp.bfloat16)
        split = projected.reshape(win_micro, WIN, WIN, 3, local_heads, HEAD)
        queries = split[:, :, :, 0]
        keys = split[:, :, :, 1]
        values = split[:, :, :, 2].reshape(win_micro, WIN_TOK, local_heads, HEAD)
        scores = score_block(queries, keys, table_rows, table_cols, scale_factor)
        peak = jnp.max(scores, axis=-1, keepdims=True)
        raised = jnp.exp(scores - peak)
        denominator = jnp.sum(raised, axis=-1, keepdims=True)
        log_total = peak + jnp.log(denominator)
        softmaxed = (raised / denominator).astype(jnp.bfloat16)
        mixed = jnp.einsum("gnqk,gknc->gqnc", softmaxed, values, preferred_element_type=jnp.float32)
        mixed = mixed.reshape(micro_rows, local_width).astype(jnp.bfloat16)
        partial_attended = jnp.dot(mixed, full_output, preferred_element_type=jnp.float32)
        middle = flat_rows + (row_total(partial_attended) + output_bias)
        unit_two, inverse_two = normalize(middle)
        normed_two = (unit_two * second_gain + second_shift).astype(jnp.bfloat16)
        before = jnp.dot(normed_two, full_expand, preferred_element_type=jnp.float32) + expand_bias
        hidden = gelu_exact(before).astype(jnp.bfloat16)
        partial_shrunk = jnp.dot(hidden, full_shrink, preferred_element_type=jnp.float32)
        result = middle + (row_total(partial_shrunk) + shrink_bias)
        aim = target[lower : lower + win_micro].reshape(micro_rows, D).astype(jnp.float32)
        marks = live[lower : lower + win_micro].reshape(micro_rows, 1)
        weighted_gap = marks * (result - aim)
        local_loss = local_loss + jnp.sum(weighted_gap * (result - aim))
        outputs.append(result.astype(jnp.bfloat16).reshape(win_micro, WIN_TOK, D))
        saved.append(
            (
                unit_one,
                inverse_one,
                normed,
                projected,
                log_total,
                mixed,
                unit_two,
                inverse_two,
                normed_two,
                before,
                hidden,
                weighted_gap,
            )
        )
    loss_total, count = lax.psum((local_loss, jnp.sum(live)), "dp")
    loss = loss_total / (count * D)
    grad_scale = local_windows * WIN_TOK * lax.axis_size("dp") / count
    triple_acc = jnp.zeros((3, D, local_width), jnp.float32)
    output_acc = jnp.zeros((local_width, D), jnp.float32)
    expand_acc = jnp.zeros((D, full_expand.shape[1]), jnp.float32)
    shrink_acc = jnp.zeros((full_shrink.shape[0], D), jnp.float32)
    first_gain_acc = jnp.zeros((D,), jnp.float32)
    first_shift_acc = jnp.zeros((D,), jnp.float32)
    second_gain_acc = jnp.zeros((D,), jnp.float32)
    second_shift_acc = jnp.zeros((D,), jnp.float32)
    output_bias_acc = jnp.zeros((D,), jnp.float32)
    shrink_bias_acc = jnp.zeros((D,), jnp.float32)
    expand_bias_acc = jnp.zeros((full_expand.shape[1],), jnp.float32)
    query_value_acc = jnp.zeros((2, local_width), jnp.float32)
    rows_expanded_acc = jnp.zeros((WIN, WIN, HEAD), jnp.float32)
    cols_expanded_acc = jnp.zeros((WIN, WIN, HEAD), jnp.float32)
    input_grads = []
    for micro in range(MICRO):
        gathered = (
            lax.all_gather(triple_weight, "dp", axis=1, tiled=True),
            lax.all_gather(output_weight, "dp", axis=1, tiled=True),
            lax.all_gather(expand_weight, "dp", axis=0, tiled=True),
            lax.all_gather(shrink_weight, "dp", axis=1, tiled=True),
        )
        full_triple, full_output, full_expand, full_shrink = gathered
        (
            unit_one,
            inverse_one,
            normed,
            projected,
            log_total,
            mixed,
            unit_two,
            inverse_two,
            normed_two,
            before,
            hidden,
            weighted_gap,
        ) = saved[micro]
        grad_result = grad_scale * weighted_gap
        shrink_bias_acc = shrink_bias_acc + jnp.sum(share_of(grad_result), axis=0)
        grad_result_low = grad_result.astype(jnp.bfloat16)
        shrink_acc = shrink_acc + jnp.einsum(
            "rf,rd->fd", hidden, grad_result_low, preferred_element_type=jnp.float32
        )
        grad_hidden = jnp.einsum(
            "rd,fd->rf", grad_result_low, full_shrink, preferred_element_type=jnp.float32
        )
        unused, gelu_pull = jax.vjp(gelu_exact, before)
        grad_before = gelu_pull(grad_hidden)[0].astype(jnp.bfloat16)
        expand_bias_acc = expand_bias_acc + jnp.sum(grad_before.astype(jnp.float32), axis=0)
        expand_acc = expand_acc + jnp.einsum(
            "rd,rf->df", normed_two, grad_before, preferred_element_type=jnp.float32
        )
        partial_two = jnp.einsum(
            "rf,df->rd", grad_before, full_expand, preferred_element_type=jnp.float32
        )
        grad_normed_two = row_total(partial_two)
        grad_middle = grad_result + normalize_back(
            grad_normed_two, unit_two, inverse_two, second_gain
        )
        second_gain_acc = second_gain_acc + jnp.sum(share_of(grad_normed_two * unit_two), axis=0)
        second_shift_acc = second_shift_acc + jnp.sum(share_of(grad_normed_two), axis=0)
        output_bias_acc = output_bias_acc + jnp.sum(share_of(grad_middle), axis=0)
        grad_middle_low = grad_middle.astype(jnp.bfloat16)
        output_acc = output_acc + jnp.einsum(
            "rc,rd->cd", mixed, grad_middle_low, preferred_element_type=jnp.float32
        )
        grad_mixed = jnp.einsum(
            "rd,cd->rc", grad_middle_low, full_output, preferred_element_type=jnp.float32
        )
        grad_mixed = grad_mixed.astype(jnp.bfloat16).reshape(win_micro, WIN_TOK, local_heads, HEAD)
        split = projected.reshape(win_micro, WIN, WIN, 3, local_heads, HEAD)
        queries = split[:, :, :, 0]
        keys = split[:, :, :, 1]
        queries_flat = queries.reshape(win_micro, WIN_TOK, local_heads, HEAD)
        keys_flat = keys.reshape(win_micro, WIN_TOK, local_heads, HEAD)
        values = split[:, :, :, 2].reshape(win_micro, WIN_TOK, local_heads, HEAD)
        scores = score_block(queries, keys, table_rows, table_cols, scale_factor)
        softmax_exact = jnp.exp(scores - log_total)
        grad_soft = jnp.einsum(
            "gqnc,gknc->gnqk", grad_mixed, values, preferred_element_type=jnp.float32
        )
        delta = jnp.sum(softmax_exact * grad_soft, axis=-1, keepdims=True)
        grad_scores = (softmax_exact * (grad_soft - delta)).astype(jnp.bfloat16)
        grad_values = jnp.einsum(
            "gnqk,gqnc->gknc",
            softmax_exact.astype(jnp.bfloat16),
            grad_mixed,
            preferred_element_type=jnp.float32,
        )
        grad_keys = (
            jnp.einsum(
                "gnqk,gqnc->gknc", grad_scores, queries_flat, preferred_element_type=jnp.float32
            )
            * scale_factor
        )
        grad_queries = (
            jnp.einsum(
                "gnqk,gknc->gqnc", grad_scores, keys_flat, preferred_element_type=jnp.float32
            )
            * scale_factor
        )
        grad_grid = grad_scores.astype(jnp.float32).reshape(
            win_micro, local_heads, WIN, WIN, WIN, WIN
        )
        row_part = jnp.sum(grad_grid, axis=5)
        col_part = jnp.sum(grad_grid, axis=4)
        queries_float = queries.astype(jnp.float32)
        rel_queries = jnp.einsum("gnabe,aec->gabnc", row_part, rows_float, precision=highest)
        rel_queries = rel_queries + jnp.einsum(
            "gnabf,bfc->gabnc", col_part, cols_float, precision=highest
        )
        grad_queries = grad_queries + rel_queries.reshape(win_micro, WIN_TOK, local_heads, HEAD)
        rows_expanded_acc = rows_expanded_acc + jnp.einsum(
            "gnabe,gabnc->aec", row_part, queries_float, precision=highest
        )
        cols_expanded_acc = cols_expanded_acc + jnp.einsum(
            "gnabf,gabnc->bfc", col_part, queries_float, precision=highest
        )
        grad_projected = jnp.stack(
            [
                grad_queries.reshape(micro_rows, local_width),
                grad_keys.reshape(micro_rows, local_width),
                grad_values.reshape(micro_rows, local_width),
            ],
            axis=1,
        ).astype(jnp.bfloat16)
        projected_float_sums = jnp.sum(grad_projected.astype(jnp.float32), axis=0)
        query_value_acc = query_value_acc + jnp.stack(
            [projected_float_sums[0], projected_float_sums[2]]
        )
        triple_acc = triple_acc + jnp.einsum(
            "rd,rte->tde", normed, grad_projected, preferred_element_type=jnp.float32
        )
        partial_one = jnp.einsum(
            "rte,tde->rd", grad_projected, full_triple, preferred_element_type=jnp.float32
        )
        grad_normed = row_total(partial_one)
        grad_tokens = grad_middle + normalize_back(grad_normed, unit_one, inverse_one, first_gain)
        first_gain_acc = first_gain_acc + jnp.sum(share_of(grad_normed * unit_one), axis=0)
        first_shift_acc = first_shift_acc + jnp.sum(share_of(grad_normed), axis=0)
        input_grads.append(grad_tokens.reshape(win_micro, WIN_TOK, D))
    select_float = select.astype(jnp.float32)
    rows_table_part = jnp.einsum("aej,aec->jc", select_float, rows_expanded_acc, precision=highest)
    cols_table_part = jnp.einsum("aej,aec->jc", select_float, cols_expanded_acc, precision=highest)
    triple_grad, output_grad, expand_grad, shrink_grad = (
        lax.psum_scatter(triple_acc, "dp", scatter_dimension=1, tiled=True),
        lax.psum_scatter(output_acc, "dp", scatter_dimension=1, tiled=True),
        lax.psum_scatter(expand_acc, "dp", scatter_dimension=0, tiled=True),
        lax.psum_scatter(shrink_acc, "dp", scatter_dimension=1, tiled=True),
    )
    over_heads = lax.psum(
        (
            rows_table_part,
            cols_table_part,
            first_gain_acc,
            first_shift_acc,
            output_bias_acc,
            second_gain_acc,
            second_shift_acc,
            shrink_bias_acc,
        ),
        "tensor",
    )
    summed_small = lax.psum(
        (
            over_heads[0],
            over_heads[1],
            over_heads[2],
            over_heads[3],
            over_heads[4],
            over_heads[5],
            over_heads[6],
            over_heads[7],
            query_value_acc,
            expand_bias_acc,
        ),
        "dp",
    )
    return (
        jnp.concatenate(outputs, axis=0),
        loss,
        jnp.concatenate(input_grads, axis=0),
        summed_small[2],
        summed_small[3],
        triple_grad,
        summed_small[8],
        output_grad,
        summed_small[4],
        summed_small[5],
        summed_small[6],
        expand_grad,
        summed_small[9],
        shrink_grad,
        summed_small[7],
        summed_small[0],
        summed_small[1],
    )


ROWS = 208
KEYS = 256
CHUNKS = ((0, 112), (112, 96))
F32 = jnp.float32
BF16 = jnp.bfloat16


def z_mate(z, k):
    if k == 0:
        return z
    if k == 1:
        return z + 1 - 2 * (z % 2)
    if k == 2:
        return (z + 2) % 4
    return 3 - z


def dot_nn(a, b):
    return lax.dot_general(a, b, (((1,), (0,)), ((), ())), preferred_element_type=F32)


def dot_nt(a, b):
    return lax.dot_general(a, b, (((1,), (1,)), ((), ())), preferred_element_type=F32)


def dot_tn(a, b):
    return lax.dot_general(a, b, (((0,), (0,)), ((), ())), preferred_element_type=F32)


def column_sum(values):
    return jnp.sum(values, axis=0, keepdims=True)


UNITS = ((0, 1, 2, 0, 0), (0, 1, 2, 1, 1), (3, 5, 6, 0, 1))


ORDER = (('pair', 0, 0), ('x', 0, 0), ('z', 0, 3), ('far', 0), ('z', 0, 1), ('pair', 0, 3), ('count',), ('x', 0, 3), ('z', 0, 2), ('start', 1), ('pair', 0, 1), ('x', 0, 1), ('near', 0), ('pair', 0, 2), ('x', 0, 2), ('pair', 1, 0), ('all', 0), ('start', 2), ('z', 1, 3), ('pair', 1, 3), ('z', 1, 1), ('far', 1), ('x', 1, 0), ('z', 2, 3), ('pair', 1, 1), ('z', 1, 2), ('x', 1, 1), ('x', 1, 3), ('pair', 1, 2), ('pair', 2, 0), ('near', 1), ('x', 1, 2), ('z', 2, 1), ('all', 1), ('far', 2), ('pair', 2, 3), ('z', 2, 2), ('pair', 2, 1), ('x', 2, 0), ('x', 2, 1), ('near', 2), ('x', 2, 3), ('pair', 2, 2), ('x', 2, 2), ('all', 2), ('pairs', 2), ('zs', 2, 2, 0), ('turns', 2), ('zs', 2, 3, 0), ('zs', 2, 1, 0), ('pairs', 1), ('zs', 1, 2, 0), ('block pass',), ('zs', 1, 1, 0), ('pairs', 0), ('zs', 1, 3, 0), ('block mix',), ('zs', 0, 2, 0), ('own', 0), ('small first',), ('own', 1), ('small z',), ('side', 0), ('turns', 0), ('turns', 1), ('zs', 0, 2, 1), ('zs', 0, 1, 0), ('small c',), ('zs', 0, 3, 0), ('out', 1), ('out', 2), ('small y',), ('side', 1), ('peer', 0), ('zs', 0, 1, 1), ('zs', 0, 3, 1), ('small x',), ('end', 0), ('last', 0), ('peer', 1), ('last', 1), ('out', 0), ('small end',))
PLAN = (0, 1, 1, 1, 2, 2, 3, 0, 0, 0, 1, 2, 1, 1, 1, 0, 0, 0, 0, 2, 0, 1, 3, 0, 1, 0, 1, 0, 3)


def block_kernel(
    x_in,
    target_in,
    valid_hbm,
    gain1_hbm,
    shift1_hbm,
    triple_hbm,
    qv_bias_hbm,
    out_w_hbm,
    bias_out_hbm,
    gain2_hbm,
    shift2_hbm,
    we_hbm,
    expand_bias_hbm,
    ws_hbm,
    bias_shrink_hbm,
    rows_hbm,
    columns_hbm,
    block_out,
    grad_out,
    ga_out,
    ge_out,
    gs_out,
    small_out,
    table_out,
    valid_in,
    gain1_in,
    shift1_in,
    triple_in,
    qv_bias_in,
    out_w_in,
    bias_out_in,
    gain2_in,
    shift2_in,
    we_in,
    expand_bias_in,
    ws_in,
    bias_shrink_in,
    rows_in,
    columns_in,
    wa_in,
    wa,
    we,
    ws,
    xt,
    tt,
    onehot,
    place,
    pick,
    tabs,
    bo,
    ig,
    mix,
    ga,
    ge,
    gs,
    side,
    xf,
    unit1,
    unit2,
    inv1,
    inv2,
    mid,
    acc,
    n1,
    n2,
    gr,
    gm,
    pj,
    ps,
    mx,
    mxr,
    hid,
    hidr,
    slope,
    gb,
    gbr,
    gmx,
    gp,
    gpr,
    t2,
    tg,
    es,
    er,
    es3,
    er3,
    sums,
    shrink_row,
    gw,
    xs,
    xr,
    zs,
    zr,
    ps2,
    pr2,
    ptotal,
    pxs,
    pxr,
    cnt,
    cntr,
    sb,
    sbr,
    tb,
    tbr,
    load_sem,
    send_sem,
    recv_sem,
):
    dp = lax.axis_index("dp")
    t = lax.axis_index("tensor")
    z = dp // 2
    x = dp % 2
    y = t // 2
    c = t % 2
    z_mates = [(z_mate(z, k) * 2 + x, t) for k in (1, 2, 3)]
    x_mate = (z * 2 + 1 - x, t)
    y_mate = (dp, (1 - y) * 2 + c)
    c_mate = (dp, y * 2 + 1 - c)
    peer_window = (1 - y) * 2 + c
    token_total = lax.axis_size("dp") * 4 * WIN_TOK

    started = []

    def send(src, dst, mate):
        i = len(started)
        copy = pltpu.make_async_remote_copy(
            src_ref=src,
            dst_ref=dst,
            send_sem=send_sem.at[i],
            recv_sem=recv_sem.at[i],
            device_id=mate,
            device_id_type=MESH,
        )
        copy.start()
        started.append(copy)
        return copy

    barrier = pltpu.get_barrier_semaphore()
    for mate in z_mates + [x_mate, y_mate, c_mate]:
        pl.semaphore_signal(barrier, inc=1, device_id=mate, device_id_type=MESH)

    loads = []

    def load(src, dst):
        copy = pltpu.make_async_copy(src, dst, load_sem.at[len(loads)])
        copy.start()
        loads.append(copy)
        return copy

    first_loads = [load(triple_hbm, triple_in), load(out_w_hbm, out_w_in)]
    group_loads = [load(we_hbm, we_in), load(ws_hbm, ws_in)]
    x_load = load(x_in, xt)
    side_loads = [
        load(src, dst)
        for src, dst in (
            (expand_bias_hbm, expand_bias_in),
            (qv_bias_hbm, qv_bias_in),
            (valid_hbm, valid_in),
            (gain1_hbm, gain1_in),
            (shift1_hbm, shift1_in),
            (bias_out_hbm, bias_out_in),
            (gain2_hbm, gain2_in),
            (shift2_hbm, shift2_in),
            (bias_shrink_hbm, bias_shrink_in),
            (rows_hbm, rows_in),
            (columns_hbm, columns_in),
        )
    ]
    target_load = load(target_in, tt)

    w_in = (wa_in, we_in, ws_in)
    w_full = (wa, we, ws)
    from_z = {}
    from_x = {}
    from_p = {}
    from_c = {}

    def row_of(k, xx):
        return z_mate(z, k) * 2 + xx

    first = pl.ds(0, 640)
    last = pl.ds(640, 128)

    def gather_start(g):
        full = w_full[g]
        from_p[g, 0] = send(w_in[g].at[:, last], full.at[0, dp, :, last], x_mate)
        for k in (3, 1):
            from_z[g, k] = send(w_in[g].at[:, first], full.at[0, dp, :, first], z_mates[k - 1])
        from_x[g, 0] = send(w_in[g].at[:, first], full.at[0, dp, :, first], x_mate)
        from_c[g, 0] = send(w_in[g], full.at[1, dp], c_mate)
        full[0, dp] = w_in[g][...]

    def to_core(g, i, *at):
        from_c[g, i] = send(w_full[g].at[(0,) + at], w_full[g].at[(1,) + at], c_mate)

    def gather_pair(g, k):
        from_p[g, k].wait_recv()
        pair = (pl.ds(2 * z_mate(z, k), 2), slice(None), last)
        block = w_full[g].at[(0,) + pair]
        if k == 0:
            for m in (3, 1):
                from_p[g, m] = send(block, block, z_mates[m - 1])
            to_core(g, 8, row_of(0, 1 - x), slice(None), last)
        else:
            if k == 3:
                from_p[g, 2] = send(block, block, z_mates[0])
            to_core(g, 8 + k, *pair)

    def gather_z(g, k):
        from_z[g, k].wait_recv()
        block = w_full[g].at[0, row_of(k, x), :, first]
        if k == 3:
            from_z[g, 2] = send(block, block, z_mates[0])
        else:
            from_x[g, k] = send(block, block, x_mate)
        to_core(g, k, row_of(k, x), slice(None), first)

    def gather_far(g):
        block = w_full[g].at[0, row_of(3, x), :, first]
        from_x[g, 3] = send(block, block, x_mate)

    def gather_x(g, k):
        from_x[g, k].wait_recv()
        to_core(g, 4 + k, row_of(k, 1 - x), slice(None), first)

    def gather_end(g, far):
        for k in (2, 3, 6, 7, 10, 11) if far else (0, 1, 4, 5, 8, 9):
            from_c[g, k].wait_recv()

    tasks = []
    done = set()
    plan = iter(PLAN)

    def add(key, step, *args):
        tasks.append((key, step, args))
        tasks.sort(key=lambda task: ORDER.index(task[0]))

    def serve():
        key, step, args = tasks.pop(0)
        step(*args)
        done.add(key)

    def point():
        for _ in range(next(plan, 0)):
            if tasks:
                serve()

    def need(key):
        while key not in done:
            serve()

    def gather_add(g):
        add(("pair", g, 0), gather_pair, g, 0)
        add(("z", g, 3), gather_z, g, 3)
        if g == 0:
            add(("start", 1), gather_start, 1)
        add(("z", g, 1), gather_z, g, 1)
        add(("far", g), gather_far, g)
        add(("pair", g, 3), gather_pair, g, 3)
        add(("x", g, 0), gather_x, g, 0)
        add(("pair", g, 1), gather_pair, g, 1)
        add(("z", g, 2), gather_z, g, 2)
        if g == 0:
            add(("count",), count_spread)
            add(("start", 2), gather_start, 2)
        add(("x", g, 1), gather_x, g, 1)
        add(("near", g), gather_end, g, False)
        add(("x", g, 3), gather_x, g, 3)
        add(("pair", g, 2), gather_pair, g, 2)
        add(("x", g, 2), gather_x, g, 2)
        add(("all", g), gather_end, g, True)

    cnt_z = []

    def count_spread():
        cnt_x.wait_recv()
        cnt[1] = cnt[0] + cntr[0]
        cnt_z.extend(send(cnt.at[1], cntr.at[k], z_mates[k - 1]) for k in (1, 2, 3))

    for copy in first_loads:
        copy.wait()
    for i in range(3):
        wa_in[:, 128 * i : 128 * i + 128] = triple_in[i, :, 0:128]
    source = lax.broadcasted_iota(jnp.int32, (192, 256), 0)
    column = lax.broadcasted_iota(jnp.int32, (192, 256), 1)
    tail = sum(
        dot_nn(
            triple_in[i],
            ((source >= 128) & (source - 128 == column - 64 * i)).astype(F32).astype(BF16),
        )
        for i in range(3)
    )
    out_w = out_w_in[...]
    tail = tail + dot_tn(
        out_w, ((source >= 128) & (source + 64 == column)).astype(F32).astype(BF16)
    )
    wa_in[:, 384:640] = tail.astype(BF16)
    wa_in[:, 640:768] = dot_tn(
        out_w, (source == column).astype(F32).astype(BF16)[:, 0:128]
    ).astype(BF16)
    def fourteens(at):
        whole = jnp.floor((at + 0.5) * (1.0 / WIN))
        return whole, at - WIN * whole

    def grid(shape, dim):
        return lax.broadcasted_iota(jnp.int32, shape, dim).astype(F32)

    def entries(shape, dim):
        at = grid(shape, dim)
        side = (at >= 256.0).astype(F32)
        at = at - 256.0 * side
        main, other = fourteens(at)
        return side, main, other, at < float(WIN_TOK)

    side_of, main, other, valid = entries((512, 64), 0)
    slot = main - other + (WIN - 1) + 32.0 * side_of
    onehot[...] = jnp.where(valid & (grid((512, 64), 1) == slot), 1.0, 0.0).astype(BF16)
    side_of, main, other, valid = entries((ROWS, 512), 1)
    token = grid((ROWS, 512), 0)
    down, across = fourteens(token)
    hit = valid & (main == jnp.where(side_of > 0.5, across, down)) & (token < float(WIN_TOK))
    place[...] = jnp.where(hit, 1.0, 0.0).astype(BF16)
    side_of, main, other, valid = entries((512, KEYS), 0)
    token = grid((512, KEYS), 1)
    down, across = fourteens(token)
    hit = valid & (other == jnp.where(side_of > 0.5, across, down)) & (token < float(WIN_TOK))
    pick[...] = jnp.where(hit, 1.0, 0.0).astype(BF16)
    pl.semaphore_wait(barrier, 6)
    gather_start(0)
    for copy in group_loads + side_loads:
        copy.wait()
    side[0] = jnp.zeros((8, D), F32)
    side[0, 0:1, :] = expand_bias_in[...].reshape(1, D)
    side[0, 1:2, 0:128] = qv_bias_in[0:1, 0:128]
    side[0, 1:2, 256:384] = qv_bias_in[1:2, 0:128]
    side[0, 1:2, 384:448] = qv_bias_in[0:1, 128:192]
    side[0, 1:2, 512:576] = qv_bias_in[1:2, 128:192]
    side_copy = send(side.at[0], side.at[1], c_mate)
    marks_all = valid_in[...].astype(F32)
    cnt[0] = jnp.full((8, 128), jnp.sum(marks_all), F32)
    cnt_x = send(cnt.at[0], cntr.at[0], x_mate)
    for g in range(3):
        gather_add(g)

    gain1 = gain1_in[...].reshape(1, D)
    shift1 = shift1_in[...].reshape(1, D)
    bias_out = bias_out_in[...].reshape(1, D)
    gain2 = gain2_in[...].reshape(1, D)
    shift2 = shift2_in[...].reshape(1, D)
    shrink_row[...] = bias_shrink_in[...].reshape(1, D)

    lane = lax.broadcasted_iota(jnp.int32, (1, 128), 1)
    half = ((lane < 64).astype(F32), (lane >= 64).astype(F32))
    key_mask = [(m * 0.125).astype(BF16) for m in half]
    half = [m.astype(BF16) for m in half]
    key_lane = lax.broadcasted_iota(jnp.int32, (1, KEYS), 1)
    key_bias = jnp.where(key_lane < WIN_TOK, 0.0, -1e30).astype(F32)

    row_ids = lax.broadcasted_iota(jnp.int32, (4, WIN_TOK), 0)
    own_marks = column_sum(jnp.where(row_ids == t, marks_all, 0.0))
    eye = lax.broadcasted_iota(jnp.int32, (ROWS, WIN_TOK), 0) == lax.broadcasted_iota(
        jnp.int32, (ROWS, WIN_TOK), 1
    )
    live = jnp.sum(jnp.where(eye, own_marks, 0.0), axis=1, keepdims=True)

    window_ids = lax.broadcasted_iota(jnp.int32, (1, 4, 1), 1)

    def window_of(ref, window):
        return jnp.sum(ref[...].astype(F32) * (window_ids == window).astype(F32), axis=1)

    xf[...] = jnp.zeros_like(xf)
    x_load.wait()
    for w in range(2):
        xf[w, 0:WIN_TOK, :] = window_of(xt, peer_window if w else t)
        point()
        unit, inverse = normalize(xf[w])
        n1[0, w] = (unit * gain1 + shift1).astype(BF16)
        if w == 0:
            unit1[...] = unit
            inv1[...] = inverse
    n1_copy = send(n1.at[0], n1.at[1], c_mate)
    tabs[...] = jnp.zeros_like(tabs)
    tabs[0:27, 0:64] = rows_in[...]
    tabs[32:59, 0:64] = columns_in[...]
    t2[0] = dot_nn(onehot[...], tabs[...].astype(BF16)).astype(BF16)
    t2[1] = dot_nn(onehot[...], pltpu.roll(tabs[...], 64, 1).astype(BF16)).astype(BF16)
    pj[:, :, ROWS:, :] = jnp.zeros((2, 2, KEYS - ROWS, 896), BF16)
    tg[...] = jnp.zeros_like(tg)

    def project(w):
        def body(j, carry):
            value = dot_nn(n1[0, w], wa[j, :, :, 0:640].reshape(D, 640)) + side[j, 1:2, 0:640]
            pj[w, j, 0:ROWS, 0:640] = value.astype(BF16)
            rolled = pltpu.roll(value[:, 384:512], 64, 1)
            pj[w, j, 0:ROWS, 640:768] = rolled.astype(BF16)
            rolled = pltpu.roll(value[:, 512:640], 64, 1)
            pj[w, j, 0:ROWS, 768:896] = rolled.astype(BF16)
            return carry

        lax.fori_loop(0, 2, body, 0)

    def unit_of(w, j, h):
        q, k, v, p, pv = UNITS[h]
        query = pj[w, j, 0:ROWS, 128 * q : 128 * q + 128]
        key = pj[w, j, :, 128 * k : 128 * k + 128] * key_mask[p]
        value = pj[w, j, :, 128 * v : 128 * v + 128] * half[pv]
        return query, key, value

    def attend(w):
        def body(j, carry):
            mixes = []
            for h in range(3):
                query, key, value = unit_of(w, j, h)
                along = dot_nt(query, t2[UNITS[h][3]])
                high = along.astype(BF16)
                low = (along - high.astype(F32)).astype(BF16) * place[...]
                high = high * place[...]
                scores = dot_nt(query, key) + dot_nn(high, pick[...]) + dot_nn(low, pick[...])
                scores = scores + key_bias
                raised = jnp.exp(scores - jnp.max(scores, axis=-1, keepdims=True))
                soft = raised * (1.0 / jnp.sum(raised, axis=-1, keepdims=True))
                ps[w, j, h] = soft
                mixes.append(dot_nn(soft.astype(BF16), value))
            mx[j, w, :, 0:128] = mixes[2].astype(BF16)
            mx[j, w, :, 128:256] = (mixes[0] + mixes[1]).astype(BF16)
            return carry

        lax.fori_loop(0, 2, body, 0)
        point()

    def attended(w, lo, n):
        return dot_nt(mx[0, w, lo : lo + n, :], wa[0, :, :, 512:768].reshape(D, 256)) + dot_nt(
            mx[1, w, lo : lo + n, :], wa[1, :, :, 512:768].reshape(D, 256)
        )

    side_copy.wait_recv()
    need(("all", 0))
    project(1)
    point()
    attend(1)
    e1 = []
    for lo, n in CHUNKS:
        es[0, lo : lo + n, :] = attended(1, lo, n).astype(BF16)
        e1.append(send(es.at[0, pl.ds(lo, n)], er.at[0, pl.ds(lo, n)], y_mate))
    point()
    project(0)
    point()
    attend(0)
    mx_copy = send(mx.at[1], mxr, c_mate)
    mid[...] = xf[0] + bias_out + attended(0, 0, ROWS)
    point()

    e2 = []
    n2_c = []
    for i, (lo, n) in enumerate(CHUNKS):
        point()
        e1[i].wait_recv()
        middle = mid[lo : lo + n, :] + er[0, lo : lo + n, :].astype(F32)
        mid[lo : lo + n, :] = middle
        unit, inverse = normalize(middle)
        unit2[lo : lo + n, :] = unit
        inv2[lo : lo + n, :] = inverse
        n2[0, 0, lo : lo + n, :] = (unit * gain2 + shift2).astype(BF16)
        rows = pl.ds(lo, n)
        e2.append(send(n2.at[0, 0, rows], n2.at[0, 1, rows], y_mate))
        n2_c.append(send(n2.at[0, 0, rows], n2.at[1, 0, rows], c_mate))

    def feed(w, lo, n):
        def body(j, carry):
            before = dot_nn(n2[0, w, lo : lo + n, :], we[j].reshape(D, D)) + side[j, 0:1, :]
            phi = 0.5 * (1.0 + lax.erf(before * math.sqrt(0.5)))
            hid[j, w, lo : lo + n, :] = (before * phi).astype(BF16)
            bell = jnp.exp(-0.5 * before * before) * (1.0 / math.sqrt(2.0 * math.pi))
            slope[j, w, lo : lo + n, :] = phi + before * bell
            return carry

        lax.fori_loop(0, 2, body, 0)
        point()

    zone = z // 2
    zones = (zone, 1 - zone)
    halves = [pl.ds(pl.multiple_of(q * 384, 128), 384) for q in zones]

    def shrunk(w, i):
        rows = pl.ds(zones[i] * 4, 4)
        return dot_nt(hid[0, w], ws[0, rows].reshape(384, D)) + dot_nt(
            hid[1, w], ws[1, rows].reshape(384, D)
        )

    need(("all", 1))
    for lo, n in CHUNKS:
        feed(0, lo, n)
    for i, (lo, n) in enumerate(CHUNKS):
        rows = pl.ds(lo, n)
        point()
        e2[i].wait_recv()
        n2_c.append(send(n2.at[0, 1, rows], n2.at[1, 1, rows], c_mate))
        feed(1, lo, n)
    hid_copy = send(hid.at[1], hidr, c_mate)
    target_load.wait()
    xf[1, 0:WIN_TOK, :] = window_of(tt, t)
    point()
    xf[1, WIN_TOK:, :] = jnp.zeros((ROWS - WIN_TOK, D), F32)
    need(("near", 2))
    for copy in cnt_z:
        copy.wait_recv()
    count = (cnt[1] + cntr[1]) + (cntr[2] + cntr[3])
    count = count[0:1, 0:1]
    scaled_live = live * (token_total / count)
    pieces = [(0, 0, ROWS)] + [(1, lo, n) for lo, n in CHUNKS]
    e3 = []
    for i in range(2):
        if i == 1:
            need(("all", 2))
        es3[i] = shrunk(1, i).astype(BF16)
        for half_at, lo, n in pieces[:1] if i == 0 else pieces[1:]:
            at = (i, pl.ds(lo, n))
            e3.append(send(es3.at[at], er3.at[at], y_mate))
        acc[:, halves[i]] = mid[:, halves[i]] + shrink_row[:, halves[i]] + shrunk(0, i)

    e4 = []
    gr_c = []
    for i, (half_at, lo, n) in enumerate(pieces):
        cols = halves[half_at]
        part = slice(lo, lo + n)
        rows = pl.ds(lo, n)
        e3[i].wait_recv()
        result = acc[part, cols] + er3[half_at, part, :].astype(F32)
        gap = result - xf[1, part, cols]
        grad = gap * scaled_live[part, :]
        acc[part, cols] = grad
        gr[0, 0, part, cols] = grad.astype(BF16)
        e4.append(send(gr.at[0, 0, rows, cols], gr.at[0, 1, rows, cols], y_mate))
        gr_c.append(send(gr.at[0, 0, rows, cols], gr.at[1, 0, rows, cols], c_mate))
        bo[t, part, cols] = result.astype(BF16)
        lost = column_sum(gap * gap * live[part, :])
        bias = column_sum(grad)
        sums[6:7, cols] = lost if lo == 0 else sums[6:7, cols] + lost
        sums[0:1, cols] = bias if lo == 0 else sums[0:1, cols] + bias
    sb[0] = jnp.zeros((16, D), F32)
    sb[0, 6:7, :] = sums[6:7, :]
    sb[0, 0:1, :] = sums[0:1, :]

    def feed_back(w, lo, n):
        def body(j, carry):
            grad = dot_nn(gr[0, w, lo : lo + n, :], ws[j].reshape(D, D))
            grad = grad * slope[j, w, lo : lo + n, :]
            gb[j, w, lo : lo + n, :] = grad.astype(BF16)
            return carry

        lax.fori_loop(0, 2, body, 0)

    def expanded_back(w, lo, n):
        return dot_nt(gb[0, w, lo : lo + n, :], we[0].reshape(D, D)) + dot_nt(
            gb[1, w, lo : lo + n, :], we[1].reshape(D, D)
        )

    def rows_of(ref, width):
        return ref[...].reshape(2 * ROWS, width)

    def weight_grad(g, left, mine, theirs, width, at):
        def body(m, carry):
            cols = pl.ds(pl.multiple_of(m * 384, 128), 384)
            rows = pl.ds(m * 4, 4)
            value = dot_tn(left[0, :, :, cols].reshape(2 * ROWS, 384), mine.reshape(2 * ROWS, width))
            value = value + dot_tn(
                left[1, :, :, cols].reshape(2 * ROWS, 384), theirs.reshape(2 * ROWS, width)
            )
            gw[g, rows, :, at : at + width] = value.reshape(4, 96, width)
            return carry

        lax.fori_loop(0, 2, body, 0)

    to_x = {}
    to_z = {}

    pair_of = {}

    def pair_rows(k):
        return pl.ds(2 * z_mate(z, k), 2)

    def scatter_pairs(g):
        for i, k in enumerate((2, 1)):
            ps2[g, i] = gw[g, pair_rows(k), :, 640:768].astype(BF16)
            pair_of[g, i] = send(ps2.at[g, i], pr2.at[g, i], z_mates[0])

    parts = {0: ((0, 384), (384, 256)), 1: ((0, 640),), 2: ((0, 640),)}

    def scatter_blocks(g, i, blocks):
        lo, n = parts[g][i]
        for k in blocks:
            xs[g, k, :, lo : lo + n] = gw[g, row_of(k, 1 - x), :, lo : lo + n].astype(BF16)
            at = (g, k, slice(None), pl.ds(lo, n))
            to_x[g, k, i] = send(xs.at[at], xr.at[at], x_mate)

    def scatter_pair(g):
        pair_of[g, 0].wait_recv()
        total = gw[g, pair_rows(3), :, 640:768] + pr2[g, 0].astype(F32)
        ps2[g, 2] = total.astype(BF16)
        pair_of[g, 2] = send(ps2.at[g, 2], pr2.at[g, 2], z_mates[2])

    def scatter_turn(g):
        pair_of[g, 1].wait_recv()
        pair_of[g, 2].wait_recv()
        total = gw[g, pair_rows(0), :, 640:768] + pr2[g, 1].astype(F32)
        ptotal[g] = total + pr2[g, 2].astype(F32)
        pxs[g] = ptotal[g, 1 - x].astype(BF16)
        pair_of[g, 3] = send(pxs.at[g], pxr.at[g], x_mate)

    def scatter_z(g, k, i):
        lo, n = parts[g][i]
        cols = slice(lo, lo + n)
        to_x[g, k, i].wait_recv()
        total = gw[g, row_of(k, x), :, cols] + xr[g, k, :, cols].astype(F32)
        if k == 3:
            to_z[g, 2, i].wait_recv()
            total = total + zr[g, 1, :, cols].astype(F32)
        zs[g, k - 1, :, cols] = total.astype(BF16)
        at = (g, k - 1, slice(None), pl.ds(lo, n))
        to_z[g, k, i] = send(zs.at[at], zr.at[at], z_mates[2 if k == 3 else 0])

    def scatter_end(g, i, out):
        lo, n = parts[g][i]
        cols = slice(lo, lo + n)
        to_x[g, 0, i].wait_recv()
        to_z[g, 1, i].wait_recv()
        to_z[g, 3, i].wait_recv()
        total = gw[g, dp, :, cols] + xr[g, 0, :, cols].astype(F32)
        out[:, cols] = total + zr[g, 0, :, cols].astype(F32) + zr[g, 2, :, cols].astype(F32)

    def scatter_last(g, out):
        pair_of[g, 3].wait_recv()
        out[:, 640:768] = ptotal[g, x] + pxr[g].astype(F32)

    def scatter_add(g, *keys):
        steps = {"pair": scatter_pair, "turn": scatter_turn}
        for key in keys:
            if key in steps:
                add((key + "s", g), steps[key], g)
            else:
                add(("zs", g, *key), scatter_z, g, *key)

    for lo, n in CHUNKS:
        feed_back(0, lo, n)
    e5 = []
    for i, (half_at, lo, n) in enumerate(pieces):
        rows = pl.ds(lo, n)
        cols = halves[half_at]
        e4[i].wait_recv()
        gr_c.append(send(gr.at[0, 1, rows, cols], gr.at[1, 1, rows, cols], c_mate))
        if i == 0:
            continue
        feed_back(1, lo, n)
        es[1, lo : lo + n, :] = expanded_back(1, lo, n).astype(BF16)
        e5.append(send(es.at[1, rows], er.at[1, rows], y_mate))
    gb_copy = send(gb.at[1], gbr, c_mate)
    mid[...] = expanded_back(0, 0, ROWS)
    for copy in gr_c:
        copy.wait_recv()
    hid_copy.wait_recv()
    weight_grad(2, gr, hid[0], hidr[...], D, 0)
    scatter_pairs(2)
    scatter_blocks(2, 0, (2, 3, 1, 0))
    scatter_add(2, "pair", (2, 0), "turn", (3, 0), (1, 0))
    point()

    e6 = []
    gm_c = []
    gain_part = jnp.zeros((1, D), F32)
    shift_part = jnp.zeros((1, D), F32)
    bias_part = jnp.zeros((1, D), F32)
    for i, (lo, n) in enumerate(CHUNKS):
        rows = pl.ds(lo, n)
        point()
        e5[i].wait_recv()
        grad = mid[lo : lo + n, :] + er[1, lo : lo + n, :].astype(F32)
        unit = unit2[lo : lo + n, :]
        gain_part = gain_part + column_sum(grad * unit)
        shift_part = shift_part + column_sum(grad)
        grad = acc[lo : lo + n, :] + normalize_back(grad, unit, inv2[lo : lo + n, :], gain2)
        acc[lo : lo + n, :] = grad
        gm[0, 0, lo : lo + n, :] = grad.astype(BF16)
        e6.append(send(gm.at[0, 0, rows], gm.at[0, 1, rows], y_mate))
        gm_c.append(send(gm.at[0, 0, rows], gm.at[1, 0, rows], c_mate))
        bias_part = bias_part + column_sum(grad)
    sb[0, 1:2, :] = gain_part
    sb[0, 2:3, :] = shift_part
    sb[0, 3:4, :] = bias_part

    bo_y = send(bo.at[t], bo.at[t], y_mate)
    bo_c = [send(bo.at[t], bo.at[t], c_mate)]

    def block_pass():
        bo_y.wait_recv()
        bo_c.append(send(bo.at[peer_window], bo.at[peer_window], c_mate))

    def block_mix():
        for copy in bo_c:
            copy.wait_recv()
        for w in range(4):
            mix[:, w, :] = bo[w, 0:WIN_TOK, :].astype(F32)
        xt[...] = mix[...].astype(BF16)
        stores.append(load(xt, block_out))

    stores = []
    gb_copy.wait_recv()
    for copy in n2_c:
        copy.wait_recv()
    weight_grad(1, n2, gb[0], gbr[...], D, 0)
    ones = jnp.ones((8, 2 * ROWS), BF16)
    sb[0, 8:9, :] = (dot_nn(ones, rows_of(gb.at[0], D)) + dot_nn(ones, rows_of(gbr, D)))[0:1]
    scatter_pairs(1)
    scatter_blocks(1, 0, (2, 3, 1, 0))
    scatter_add(1, "pair", (2, 0), "turn", (3, 0), (1, 0))
    point()

    def mixed_back(w, lo, n):
        for j in range(2):
            grad = dot_nn(gm[0, w, lo : lo + n, :], wa[j, :, :, 512:768].reshape(D, 256))
            gmx[j, w, lo : lo + n, :] = grad.astype(BF16)

    def unit_back(w, j, h):
        query, key, value = unit_of(w, j, h)
        p, pv = UNITS[h][3:]
        grad = gmx[j, w, :, 0:128] if h == 2 else gmx[j, w, :, 128:256]
        soft = ps[w, j, h]
        grad_soft = dot_nt(grad, value)
        delta = jnp.sum(soft * grad_soft, axis=-1, keepdims=True)
        grad_scores = (soft * (grad_soft - delta)).astype(BF16)
        grad_v = dot_tn(soft.astype(BF16), grad * half[pv])[0:ROWS]
        grad_k = dot_tn(grad_scores, query * key_mask[p])[0:ROWS]
        part = dot_nt(grad_scores, pick[...]).astype(BF16) * place[...]
        grad_q = dot_nn(grad_scores, key) + dot_nn(part, t2[p])
        tg[...] += dot_tn(query * half[p], part)
        return grad_q, grad_k, grad_v

    def attend_back_pair(w, j):
        one, two = unit_back(w, j, 0), unit_back(w, j, 1)
        for i in range(3):
            gp[j, w, :, 128 * i : 128 * i + 128] = (one[i] + two[i]).astype(BF16)

    def attend_back_last(w, j):
        grad_q, grad_k, grad_v = unit_back(w, j, 2)
        gp[j, w, :, 384:512] = (grad_q + pltpu.roll(grad_k, 64, 1)).astype(BF16)
        gp[j, w, :, 512:640] = pltpu.roll(grad_v, 64, 1).astype(BF16)

    def projected_back(w, lo, n):
        return dot_nt(gp[0, w, lo : lo + n, :], wa[0, :, :, 0:640].reshape(D, 640)) + dot_nt(
            gp[1, w, lo : lo + n, :], wa[1, :, :, 0:640].reshape(D, 640)
        )

    for i, (lo, n) in enumerate(CHUNKS):
        rows = pl.ds(lo, n)
        point()
        e6[i].wait_recv()
        gm_c.append(send(gm.at[0, 1, rows], gm.at[1, 1, rows], c_mate))
        mixed_back(1, lo, n)
    point()
    add(("block pass",), block_pass)
    add(("block mix",), block_mix)
    def both_back(j, carry):
        attend_back_pair(1, j)
        attend_back_last(1, j)
        return carry

    lax.fori_loop(0, 2, both_back, 0)
    point()
    gp_copies = [send(gp.at[1, 1], gpr.at[1], c_mate)]
    e7 = []
    for lo, n in CHUNKS:
        rows = pl.ds(lo, n)
        es[2, lo : lo + n, :] = projected_back(1, lo, n).astype(BF16)
        e7.append(send(es.at[2, rows], er.at[2, rows], y_mate))
    point()
    for copy in gm_c:
        copy.wait_recv()
    mx_copy.wait_recv()
    weight_grad(0, gm, mx[0], mxr[...], 256, 512)
    scatter_pairs(0)
    scatter_add(0, "pair", "turn")
    point()
    mixed_back(0, 0, ROWS)
    def pair_back(j, carry):
        attend_back_pair(0, j)
        return carry

    lax.fori_loop(0, 2, pair_back, 0)
    point()
    gp_copies.append(send(gp.at[1, 0, :, pl.ds(0, 384)], gpr.at[0, :, pl.ds(0, 384)], c_mate))
    attend_back_last(0, 0)
    point()
    n1_copy.wait_recv()
    for copy in gp_copies:
        copy.wait_recv()

    weight_grad(0, n1, gp[0, :, :, 0:384], gpr[:, :, 0:384], 384, 0)
    scatter_blocks(0, 0, (2, 3, 1, 0))
    scatter_add(0, (2, 0))
    attend_back_last(0, 1)
    last_copy = send(gp.at[1, 0, :, pl.ds(384, 256)], gpr.at[0, :, pl.ds(384, 256)], c_mate)
    mid[...] = projected_back(0, 0, ROWS)
    last_copy.wait_recv()
    held = gw[0, :, :, 512:640]
    weight_grad(0, n1, gp[0, :, :, 384:640], gpr[:, :, 384:640], 256, 384)
    gw[0, :, :, 512:640] += held
    need(("turns", 0))
    scatter_blocks(0, 1, (2, 3, 1, 0))

    small = {}

    def small_first():
        bias = dot_nn(ones, rows_of(gp.at[0], 640)) + dot_nn(ones, rows_of(gpr, 640))
        sb[0, 9:10, 0:640] = bias[0:1]
        spread = tg[...]
        spread_high = spread.astype(BF16)
        spread_low = (spread - spread_high.astype(F32)).astype(BF16)
        table = dot_nn(spread_high, onehot[...]) + dot_nn(spread_low, onehot[...])
        tb[0] = table[0:64] + table[64:128]

    top = pl.ds(0, 8)

    def small_send(stage, dst, mate, rows):
        return [
            send(sb.at[stage, rows], sbr.at[dst, rows], mate),
            send(tb.at[stage], tbr.at[dst], mate),
        ]

    def small_wait(stage):
        for copy in small[stage]:
            copy.wait_recv()

    def small_z():
        small[0] = sum((small_send(0, k - 1, z_mates[k - 1], pl.ds(0, 16)) for k in (1, 2, 3)), [])

    def small_c():
        small_wait(0)
        sb[1] = (sb[0] + sbr[0]) + (sbr[1] + sbr[2])
        tb[1] = (tb[0] + tbr[0]) + (tbr[1] + tbr[2])
        small[1] = small_send(1, 3, c_mate, top)

    def small_next(stage, mate, rows):
        small_wait(stage - 1)
        sb[stage] = sb[stage - 1]
        sb[stage, 0:8, :] = sb[stage - 1, 0:8, :] + sbr[stage + 1, 0:8, :]
        tb[stage] = tb[stage - 1] + tbr[stage + 1]
        small[stage] = small_send(stage, stage + 2, mate, rows)

    def small_end():
        small_wait(3)
        total = sb[3] + sbr[5]
        small_out[...] = total
        small_out[6:7, :] = jnp.broadcast_to(
            jnp.sum(total[6:7, :], axis=1, keepdims=True) / (count * float(D)), (1, D)
        )
        table_out[...] = (tb[3] + tbr[5]).T

    e8 = {}
    ig_c = {}

    def mix_in(window, i):
        lo, n = CHUNKS[i]
        top = min(lo + n, WIN_TOK)
        mix[lo:top, pl.ds(window, 1), :] = (
            ig[window, lo:top, :].astype(F32).reshape(top - lo, 1, D)
        )

    def own_grad(i):
        lo, n = CHUNKS[i]
        e7[i].wait_recv()
        grad = mid[lo : lo + n, :] + er[2, lo : lo + n, :].astype(F32)
        unit = unit1[lo : lo + n, :]
        gain_part = column_sum(grad * unit)
        shift_part = column_sum(grad)
        sb[0, 4:5, :] = gain_part if i == 0 else sb[0, 4:5, :] + gain_part
        sb[0, 5:6, :] = shift_part if i == 0 else sb[0, 5:6, :] + shift_part
        grad = acc[lo : lo + n, :] + normalize_back(grad, unit, inv1[lo : lo + n, :], gain1)
        ig[t, lo : lo + n, :] = grad.astype(BF16)
        rows = pl.ds(lo, n)
        ig_c[i, 0] = send(ig.at[t, rows], ig.at[t, rows], c_mate)
        e8[i] = send(ig.at[t, rows], ig.at[t, rows], y_mate)
        mix_in(t, i)

    def side_grad(i):
        ig_c[i, 0].wait_recv()
        mix_in(t + 1 - 2 * c, i)

    def peer_grad(i):
        lo, n = CHUNKS[i]
        rows = pl.ds(lo, n)
        e8[i].wait_recv()
        ig_c[i, 1] = send(ig.at[peer_window, rows], ig.at[peer_window, rows], c_mate)
        mix_in(peer_window, i)

    def last_grad(i):
        lo, n = CHUNKS[i]
        ig_c[i, 1].wait_recv()
        mix_in(peer_window + 1 - 2 * c, i)
        rows = pl.ds(lo, min(n, WIN_TOK - lo))
        stores.append(load(mix.at[rows], grad_out.at[rows]))

    def scatter_out(g, held, out):
        if g > 0:
            scatter_end(g, 0, held)
        else:
            scatter_end(0, 1, held)
        scatter_last(g, held)
        stores.append(load(held, out))

    need(("block mix",))
    add(("own", 0), own_grad, 0)
    add(("small first",), small_first)
    add(("own", 1), own_grad, 1)
    add(("small z",), small_z)
    scatter_add(0, (3, 0), (2, 1), (1, 0))
    add(("side", 0), side_grad, 0)
    add(("side", 1), side_grad, 1)
    add(("small c",), small_c)
    add(("out", 2), scatter_out, 2, gs, gs_out)
    add(("out", 1), scatter_out, 1, ge, ge_out)
    add(("small y",), small_next, 2, y_mate, top)
    add(("peer", 0), peer_grad, 0)
    scatter_add(0, (3, 1), (1, 1))
    add(("last", 0), last_grad, 0)
    add(("small x",), small_next, 3, x_mate, pl.ds(0, 16))
    add(("peer", 1), peer_grad, 1)
    add(("last", 1), last_grad, 1)
    add(("end", 0), scatter_end, 0, 0, ga)
    add(("out", 0), scatter_out, 0, ga, ga_out)
    add(("small end",), small_end)
    need(("small end",))
    for copy in started:
        copy.wait_send()
    for copy in stores:
        copy.wait()


def finish_kernel(*refs):
    block_in, grad_in, ga_in, ge, gs, small_in, table_in = refs[:7]
    outs = refs[7:24]
    block_hold, grad_hold, ge_hold, gs_hold, ga, small, table = refs[24:31]
    held = refs[31:44]
    sems = refs[44]
    count = [0]

    def move(src, dst):
        copy = pltpu.make_async_copy(src, dst, sems.at[count[0]])
        count[0] += 1
        copy.start()
        return copy

    little = [move(src, dst) for src, dst in ((ga_in, ga), (small_in, small), (table_in, table))]
    arrivals = []
    for src, hold, dst, step in (
        (grad_in, grad_hold, outs[2], 49),
        (block_in, block_hold, outs[0], 98),
        (ge, ge_hold, outs[11], 96),
        (gs, gs_hold, outs[13], 96),
    ):
        for lo in range(0, src.shape[0], step):
            rows = pl.ds(lo, step)
            arrivals.append((move(src.at[rows], hold.at[rows]), hold.at[rows], dst.at[rows]))
    for copy in little:
        copy.wait()
    loss, gain1, shift1, triple, qv, out_w, out_b, gain2, shift2, expand_bias, shrink_bias, by_row, by_column = held
    for i in range(3):
        triple[i, :, 0:128] = ga[:, 128 * i : 128 * i + 128]
    triple[0, :, 128:192] = ga[:, 384:448]
    triple[1, :, 128:192] = pltpu.roll(ga[:, 384:512], 64, 1)[:, 0:64]
    triple[2, :, 128:192] = ga[:, 512:576]
    out_w[0:128, :] = ga[:, 640:768].T
    out_w[128:192, :] = ga[:, 512:640].T[64:128]
    loss[...] = small[6:7, 0:1]
    for i, out in enumerate((shrink_bias, gain2, shift2, out_b, gain1, shift1)):
        out[...] = small[i]
    expand_bias[...] = small[8]
    for i in range(2):
        qv[i : i + 1, 0:128] = small[9:10, 256 * i : 256 * i + 128]
        qv[i : i + 1, 128:192] = small[9:10, 384 + 128 * i : 448 + 128 * i]
    by_row[...] = table[0:27]
    by_column[...] = table[32:59]
    others = [out for i, out in enumerate(outs) if i not in (0, 2, 11, 13)]
    leaving = [move(src, dst) for src, dst in zip(held, others, strict=True)]
    for copy, hold, dst in arrivals:
        copy.wait()
        leaving.append(move(hold, dst))
    for copy in leaving:
        copy.wait()


def fused(
    inputs,
    target,
    valid,
    first_gain,
    first_shift,
    triple_weight,
    query_value_bias,
    output_weight,
    output_bias,
    second_gain,
    second_shift,
    expand_weight,
    expand_bias,
    shrink_weight,
    shrink_bias,
    rows_table,
    columns_table,
):
    vmem = pl.BlockSpec(memory_space=pltpu.VMEM)
    anywhere = pl.BlockSpec(memory_space=pl.ANY)
    mixed_shape = (WIN_TOK, 4, D)
    part = jax.ShapeDtypeStruct((96, D), F32)
    copies = 224
    parts = pl.pallas_call(
        block_kernel,
        out_shape=[
            jax.ShapeDtypeStruct(mixed_shape, BF16),
            jax.ShapeDtypeStruct(mixed_shape, F32),
            part,
            part,
            part,
            jax.ShapeDtypeStruct((16, D), F32),
            jax.ShapeDtypeStruct((64, 64), F32),
        ],
        in_specs=[anywhere] * 17,
        out_specs=[anywhere] * 5 + [vmem] * 2,
        scratch_shapes=[
            pltpu.VMEM(valid.shape, jnp.int32),
            pltpu.VMEM((D,), F32),
            pltpu.VMEM((D,), F32),
            pltpu.VMEM(triple_weight.shape, BF16),
            pltpu.VMEM(query_value_bias.shape, F32),
            pltpu.VMEM(output_weight.shape, BF16),
            pltpu.VMEM((D,), F32),
            pltpu.VMEM((D,), F32),
            pltpu.VMEM((D,), F32),
            pltpu.VMEM(expand_weight.shape, BF16),
            pltpu.VMEM(expand_bias.shape, F32),
            pltpu.VMEM(expand_weight.shape, BF16),
            pltpu.VMEM((D,), F32),
            pltpu.VMEM(rows_table.shape, F32),
            pltpu.VMEM(columns_table.shape, F32),
            pltpu.VMEM((96, D), BF16),
            pltpu.VMEM((2, 8, 96, D), BF16),
            pltpu.VMEM((2, 8, 96, D), BF16),
            pltpu.VMEM((2, 8, 96, D), BF16),
            pltpu.VMEM(mixed_shape, BF16),
            pltpu.VMEM(mixed_shape, BF16),
            pltpu.VMEM((512, 64), BF16),
            pltpu.VMEM((ROWS, 512), BF16),
            pltpu.VMEM((512, KEYS), BF16),
            pltpu.VMEM((64, 128), F32),
            pltpu.VMEM((4, ROWS, D), BF16),
            pltpu.VMEM((4, ROWS, D), BF16),
            pltpu.VMEM(mixed_shape, F32),
            pltpu.VMEM((96, D), F32),
            pltpu.VMEM((96, D), F32),
            pltpu.VMEM((96, D), F32),
            pltpu.VMEM((2, 8, D), F32),
            pltpu.VMEM((2, ROWS, D), F32),
            pltpu.VMEM((ROWS, D), F32),
            pltpu.VMEM((ROWS, D), F32),
            pltpu.VMEM((ROWS, 1), F32),
            pltpu.VMEM((ROWS, 1), F32),
            pltpu.VMEM((ROWS, D), F32),
            pltpu.VMEM((ROWS, D), F32),
            pltpu.VMEM((2, 2, ROWS, D), BF16),
            pltpu.VMEM((2, 2, ROWS, D), BF16),
            pltpu.VMEM((2, 2, ROWS, D), BF16),
            pltpu.VMEM((2, 2, ROWS, D), BF16),
            pltpu.VMEM((2, 2, KEYS, 896), BF16),
            pltpu.VMEM((2, 2, 3, ROWS, KEYS), F32),
            pltpu.VMEM((2, 2, ROWS, 256), BF16),
            pltpu.VMEM((2, ROWS, 256), BF16),
            pltpu.VMEM((2, 2, ROWS, D), BF16),
            pltpu.VMEM((2, ROWS, D), BF16),
            pltpu.VMEM((2, 2, ROWS, D), F32),
            pltpu.VMEM((2, 2, ROWS, D), BF16),
            pltpu.VMEM((2, ROWS, D), BF16),
            pltpu.VMEM((2, 2, ROWS, 256), BF16),
            pltpu.VMEM((2, 2, ROWS, 640), BF16),
            pltpu.VMEM((2, ROWS, 640), BF16),
            pltpu.VMEM((2, 512, 128), BF16),
            pltpu.VMEM((128, 512), F32),
            pltpu.VMEM((3, ROWS, D), BF16),
            pltpu.VMEM((3, ROWS, D), BF16),
            pltpu.VMEM((2, ROWS, 384), BF16),
            pltpu.VMEM((2, ROWS, 384), BF16),
            pltpu.VMEM((8, D), F32),
            pltpu.VMEM((1, D), F32),
            pltpu.VMEM((3, 8, 96, D), F32),
            pltpu.VMEM((3, 4, 96, 640), BF16),
            pltpu.VMEM((3, 4, 96, 640), BF16),
            pltpu.VMEM((3, 3, 96, 640), BF16),
            pltpu.VMEM((3, 3, 96, 640), BF16),
            pltpu.VMEM((3, 3, 2, 96, 128), BF16),
            pltpu.VMEM((3, 3, 2, 96, 128), BF16),
            pltpu.VMEM((3, 2, 96, 128), F32),
            pltpu.VMEM((3, 96, 128), BF16),
            pltpu.VMEM((3, 96, 128), BF16),
            pltpu.VMEM((2, 8, 128), F32),
            pltpu.VMEM((4, 8, 128), F32),
            pltpu.VMEM((4, 16, D), F32),
            pltpu.VMEM((6, 16, D), F32),
            pltpu.VMEM((4, 64, 64), F32),
            pltpu.VMEM((6, 64, 64), F32),
            pltpu.SemaphoreType.DMA((32,)),
            pltpu.SemaphoreType.DMA((copies,)),
            pltpu.SemaphoreType.DMA((copies,)),
        ],
        compiler_params=pltpu.CompilerParams(
            collective_id=0, has_side_effects=True, vmem_limit_bytes=60 << 20
        ),
    )(
        inputs.transpose(1, 0, 2),
        target.transpose(1, 0, 2),
        valid,
        first_gain,
        first_shift,
        triple_weight,
        query_value_bias,
        output_weight,
        output_bias,
        second_gain,
        second_shift,
        expand_weight,
        expand_bias,
        shrink_weight.T,
        shrink_bias,
        rows_table,
        columns_table,
    )
    vector = jax.ShapeDtypeStruct((D,), F32)
    relative = jax.ShapeDtypeStruct(rows_table.shape, F32)
    shapes = [
        jax.ShapeDtypeStruct(mixed_shape, BF16),
        jax.ShapeDtypeStruct((1, 1), F32),
        jax.ShapeDtypeStruct(mixed_shape, F32),
        vector,
        vector,
        jax.ShapeDtypeStruct(triple_weight.shape, F32),
        jax.ShapeDtypeStruct(query_value_bias.shape, F32),
        jax.ShapeDtypeStruct(output_weight.shape, F32),
        vector,
        vector,
        vector,
        part,
        jax.ShapeDtypeStruct(expand_bias.shape, F32),
        part,
        vector,
        relative,
        relative,
    ]
    small_shapes = [shape for i, shape in enumerate(shapes) if i not in (0, 2, 11, 13)]
    outs = pl.pallas_call(
        finish_kernel,
        out_shape=shapes,
        in_specs=[anywhere] * 7,
        out_specs=[anywhere] * 17,
        scratch_shapes=[
            pltpu.VMEM(mixed_shape, BF16),
            pltpu.VMEM(mixed_shape, F32),
            pltpu.VMEM((96, D), F32),
            pltpu.VMEM((96, D), F32),
            pltpu.VMEM((96, D), F32),
            pltpu.VMEM((16, D), F32),
            pltpu.VMEM((64, 64), F32),
        ]
        + [pltpu.VMEM(shape.shape, shape.dtype) for shape in small_shapes]
        + [pltpu.SemaphoreType.DMA((40,))],
    )(*parts)
    outs = list(outs)
    outs[0] = outs[0].transpose(1, 0, 2)
    outs[1] = outs[1].reshape(())
    outs[2] = outs[2].transpose(1, 0, 2)
    outs[13] = outs[13].T
    return tuple(outs)


def solution(mesh):
    placed = (
        P("dp", None, None),
        P("dp", None, None),
        P("dp", None),
        P(),
        P(),
        P(None, "dp", "tensor"),
        P(None, "tensor"),
        P("tensor", "dp"),
        P(),
        P(),
        P(),
        P("dp", "tensor"),
        P("tensor"),
        P("tensor", "dp"),
        P(),
        P(),
        P(),
    )
    on_slice = mesh.shape["dp"] == 8 and mesh.shape["tensor"] == 4
    return jax.shard_map(
        fused if on_slice else shards,
        mesh=mesh,
        in_specs=placed,
        out_specs=(
            P("dp", None, None),
            P(),
            P("dp", None, None),
            P(),
            P(),
            P(None, "dp", "tensor"),
            P(None, "tensor"),
            P("tensor", "dp"),
            P(),
            P(),
            P(),
            P("dp", "tensor"),
            P("tensor"),
            P("tensor", "dp"),
            P(),
            P(),
            P(),
        ),
        check_vma=False,
    )
```

```python
import math

import jax
import jax.numpy as jnp
import numpy as np
from jax import lax
from jax.experimental import pallas as pl
from jax.experimental.pallas import tpu as pltpu
from jax.sharding import PartitionSpec as P

MESH = pl.DeviceIdType.MESH

D = 768
HEADS = 12
HEAD = 64
WIN = 14
WIN_TOK = 196
MICRO = 2


def normalize(values):
    center = jnp.mean(values, axis=-1, keepdims=True)
    centered = values - center
    spread = jnp.mean(centered * centered, axis=-1, keepdims=True)
    inverse = lax.rsqrt(spread + 1e-06)
    return (centered * inverse, inverse)


def normalize_back(grad_out, unit, inverse, gain):
    scaled = grad_out * gain
    mean_one = jnp.mean(scaled, axis=-1, keepdims=True)
    mean_two = jnp.mean(scaled * unit, axis=-1, keepdims=True)
    return inverse * (scaled - mean_one - unit * mean_two)


def position_select(side):
    shape = (side, side, 2 * side - 1)
    first = lax.broadcasted_iota(jnp.int32, shape, 0)
    second = lax.broadcasted_iota(jnp.int32, shape, 1)
    slots = lax.broadcasted_iota(jnp.int32, shape, 2)
    return (slots == first - second + side - 1).astype(jnp.bfloat16)


def score_block(queries, keys, table_rows, table_cols, scale_factor):
    groups = queries.shape[0]
    side = queries.shape[1]
    heads = queries.shape[3]
    along_rows = jnp.einsum(
        "gabnc,aec->gnabe", queries, table_rows, preferred_element_type=jnp.float32
    )
    along_cols = jnp.einsum(
        "gabnc,bfc->gnabf", queries, table_cols, preferred_element_type=jnp.float32
    )
    scores = (
        jnp.einsum("gabnc,gefnc->gnabef", queries, keys, preferred_element_type=jnp.float32)
        * scale_factor
    )
    scores = scores + along_rows[..., :, None] + along_cols[..., None, :]
    return scores.reshape(groups, heads, side * side, side * side)


def gelu_exact(inner):
    return jax.nn.gelu(inner, approximate=False)


def row_total(partial_value):
    return lax.psum(partial_value, "tensor")


def share_of(values):
    share_rows = values.shape[0] // lax.axis_size("tensor")
    return lax.dynamic_slice_in_dim(values, lax.axis_index("tensor") * share_rows, share_rows, 0)


def shards(
    inputs,
    target,
    valid,
    first_gain,
    first_shift,
    triple_weight,
    query_value_bias,
    output_weight,
    output_bias,
    second_gain,
    second_shift,
    expand_weight,
    expand_bias,
    shrink_weight,
    shrink_bias,
    rows_table,
    columns_table,
):
    local_heads = HEADS // lax.axis_size("tensor")
    local_width = local_heads * HEAD
    local_windows = inputs.shape[0]
    win_micro = local_windows // MICRO
    micro_rows = win_micro * WIN_TOK
    scale_factor = 1.0 / math.sqrt(HEAD)
    highest = lax.Precision.HIGHEST
    live = valid.astype(jnp.float32)
    select = position_select(WIN)
    table_rows = jnp.einsum(
        "aej,jc->aec", select, rows_table.astype(jnp.bfloat16), preferred_element_type=jnp.float32
    ).astype(jnp.bfloat16)
    table_cols = jnp.einsum(
        "aej,jc->aec",
        select,
        columns_table.astype(jnp.bfloat16),
        preferred_element_type=jnp.float32,
    ).astype(jnp.bfloat16)
    rows_float = table_rows.astype(jnp.float32)
    cols_float = table_cols.astype(jnp.float32)
    triple_bias = jnp.stack(
        [query_value_bias[0], jnp.zeros_like(query_value_bias[0]), query_value_bias[1]]
    )
    saved = []
    outputs = []
    local_loss = jnp.zeros((), jnp.float32)
    for micro in range(MICRO):
        gathered = (
            lax.all_gather(triple_weight, "dp", axis=1, tiled=True),
            lax.all_gather(output_weight, "dp", axis=1, tiled=True),
            lax.all_gather(expand_weight, "dp", axis=0, tiled=True),
            lax.all_gather(shrink_weight, "dp", axis=1, tiled=True),
        )
        full_triple, full_output, full_expand, full_shrink = gathered
        lower = micro * win_micro
        flat_rows = inputs[lower : lower + win_micro].reshape(micro_rows, D).astype(jnp.float32)
        unit_one, inverse_one = normalize(flat_rows)
        normed = (unit_one * first_gain + first_shift).astype(jnp.bfloat16)
        projected = (
            jnp.einsum("rd,tde->rte", normed, full_triple, preferred_element_type=jnp.float32)
            + triple_bias
        )
        projected = projected.astype(jnp.bfloat16)
        split = projected.reshape(win_micro, WIN, WIN, 3, local_heads, HEAD)
        queries = split[:, :, :, 0]
        keys = split[:, :, :, 1]
        values = split[:, :, :, 2].reshape(win_micro, WIN_TOK, local_heads, HEAD)
        scores = score_block(queries, keys, table_rows, table_cols, scale_factor)
        peak = jnp.max(scores, axis=-1, keepdims=True)
        raised = jnp.exp(scores - peak)
        denominator = jnp.sum(raised, axis=-1, keepdims=True)
        log_total = peak + jnp.log(denominator)
        softmaxed = (raised / denominator).astype(jnp.bfloat16)
        mixed = jnp.einsum("gnqk,gknc->gqnc", softmaxed, values, preferred_element_type=jnp.float32)
        mixed = mixed.reshape(micro_rows, local_width).astype(jnp.bfloat16)
        partial_attended = jnp.dot(mixed, full_output, preferred_element_type=jnp.float32)
        middle = flat_rows + (row_total(partial_attended) + output_bias)
        unit_two, inverse_two = normalize(middle)
        normed_two = (unit_two * second_gain + second_shift).astype(jnp.bfloat16)
        before = jnp.dot(normed_two, full_expand, preferred_element_type=jnp.float32) + expand_bias
        hidden = gelu_exact(before).astype(jnp.bfloat16)
        partial_shrunk = jnp.dot(hidden, full_shrink, preferred_element_type=jnp.float32)
        result = middle + (row_total(partial_shrunk) + shrink_bias)
        aim = target[lower : lower + win_micro].reshape(micro_rows, D).astype(jnp.float32)
        marks = live[lower : lower + win_micro].reshape(micro_rows, 1)
        weighted_gap = marks * (result - aim)
        local_loss = local_loss + jnp.sum(weighted_gap * (result - aim))
        outputs.append(result.astype(jnp.bfloat16).reshape(win_micro, WIN_TOK, D))
        saved.append(
            (
                unit_one,
                inverse_one,
                normed,
                projected,
                log_total,
                mixed,
                unit_two,
                inverse_two,
                normed_two,
                before,
                hidden,
                weighted_gap,
            )
        )
    loss_total, count = lax.psum((local_loss, jnp.sum(live)), "dp")
    loss = loss_total / (count * D)
    grad_scale = local_windows * WIN_TOK * lax.axis_size("dp") / count
    triple_acc = jnp.zeros((3, D, local_width), jnp.float32)
    output_acc = jnp.zeros((local_width, D), jnp.float32)
    expand_acc = jnp.zeros((D, full_expand.shape[1]), jnp.float32)
    shrink_acc = jnp.zeros((full_shrink.shape[0], D), jnp.float32)
    first_gain_acc = jnp.zeros((D,), jnp.float32)
    first_shift_acc = jnp.zeros((D,), jnp.float32)
    second_gain_acc = jnp.zeros((D,), jnp.float32)
    second_shift_acc = jnp.zeros((D,), jnp.float32)
    output_bias_acc = jnp.zeros((D,), jnp.float32)
    shrink_bias_acc = jnp.zeros((D,), jnp.float32)
    expand_bias_acc = jnp.zeros((full_expand.shape[1],), jnp.float32)
    query_value_acc = jnp.zeros((2, local_width), jnp.float32)
    rows_expanded_acc = jnp.zeros((WIN, WIN, HEAD), jnp.float32)
    cols_expanded_acc = jnp.zeros((WIN, WIN, HEAD), jnp.float32)
    input_grads = []
    for micro in range(MICRO):
        gathered = (
            lax.all_gather(triple_weight, "dp", axis=1, tiled=True),
            lax.all_gather(output_weight, "dp", axis=1, tiled=True),
            lax.all_gather(expand_weight, "dp", axis=0, tiled=True),
            lax.all_gather(shrink_weight, "dp", axis=1, tiled=True),
        )
        full_triple, full_output, full_expand, full_shrink = gathered
        (
            unit_one,
            inverse_one,
            normed,
            projected,
            log_total,
            mixed,
            unit_two,
            inverse_two,
            normed_two,
            before,
            hidden,
            weighted_gap,
        ) = saved[micro]
        grad_result = grad_scale * weighted_gap
        shrink_bias_acc = shrink_bias_acc + jnp.sum(share_of(grad_result), axis=0)
        grad_result_low = grad_result.astype(jnp.bfloat16)
        shrink_acc = shrink_acc + jnp.einsum(
            "rf,rd->fd", hidden, grad_result_low, preferred_element_type=jnp.float32
        )
        grad_hidden = jnp.einsum(
            "rd,fd->rf", grad_result_low, full_shrink, preferred_element_type=jnp.float32
        )
        unused, gelu_pull = jax.vjp(gelu_exact, before)
        grad_before = gelu_pull(grad_hidden)[0].astype(jnp.bfloat16)
        expand_bias_acc = expand_bias_acc + jnp.sum(grad_before.astype(jnp.float32), axis=0)
        expand_acc = expand_acc + jnp.einsum(
            "rd,rf->df", normed_two, grad_before, preferred_element_type=jnp.float32
        )
        partial_two = jnp.einsum(
            "rf,df->rd", grad_before, full_expand, preferred_element_type=jnp.float32
        )
        grad_normed_two = row_total(partial_two)
        grad_middle = grad_result + normalize_back(
            grad_normed_two, unit_two, inverse_two, second_gain
        )
        second_gain_acc = second_gain_acc + jnp.sum(share_of(grad_normed_two * unit_two), axis=0)
        second_shift_acc = second_shift_acc + jnp.sum(share_of(grad_normed_two), axis=0)
        output_bias_acc = output_bias_acc + jnp.sum(share_of(grad_middle), axis=0)
        grad_middle_low = grad_middle.astype(jnp.bfloat16)
        output_acc = output_acc + jnp.einsum(
            "rc,rd->cd", mixed, grad_middle_low, preferred_element_type=jnp.float32
        )
        grad_mixed = jnp.einsum(
            "rd,cd->rc", grad_middle_low, full_output, preferred_element_type=jnp.float32
        )
        grad_mixed = grad_mixed.astype(jnp.bfloat16).reshape(win_micro, WIN_TOK, local_heads, HEAD)
        split = projected.reshape(win_micro, WIN, WIN, 3, local_heads, HEAD)
        queries = split[:, :, :, 0]
        keys = split[:, :, :, 1]
        queries_flat = queries.reshape(win_micro, WIN_TOK, local_heads, HEAD)
        keys_flat = keys.reshape(win_micro, WIN_TOK, local_heads, HEAD)
        values = split[:, :, :, 2].reshape(win_micro, WIN_TOK, local_heads, HEAD)
        scores = score_block(queries, keys, table_rows, table_cols, scale_factor)
        softmax_exact = jnp.exp(scores - log_total)
        grad_soft = jnp.einsum(
            "gqnc,gknc->gnqk", grad_mixed, values, preferred_element_type=jnp.float32
        )
        delta = jnp.sum(softmax_exact * grad_soft, axis=-1, keepdims=True)
        grad_scores = (softmax_exact * (grad_soft - delta)).astype(jnp.bfloat16)
        grad_values = jnp.einsum(
            "gnqk,gqnc->gknc",
            softmax_exact.astype(jnp.bfloat16),
            grad_mixed,
            preferred_element_type=jnp.float32,
        )
        grad_keys = (
            jnp.einsum(
                "gnqk,gqnc->gknc", grad_scores, queries_flat, preferred_element_type=jnp.float32
            )
            * scale_factor
        )
        grad_queries = (
            jnp.einsum(
                "gnqk,gknc->gqnc", grad_scores, keys_flat, preferred_element_type=jnp.float32
            )
            * scale_factor
        )
        grad_grid = grad_scores.astype(jnp.float32).reshape(
            win_micro, local_heads, WIN, WIN, WIN, WIN
        )
        row_part = jnp.sum(grad_grid, axis=5)
        col_part = jnp.sum(grad_grid, axis=4)
        queries_float = queries.astype(jnp.float32)
        rel_queries = jnp.einsum("gnabe,aec->gabnc", row_part, rows_float, precision=highest)
        rel_queries = rel_queries + jnp.einsum(
            "gnabf,bfc->gabnc", col_part, cols_float, precision=highest
        )
        grad_queries = grad_queries + rel_queries.reshape(win_micro, WIN_TOK, local_heads, HEAD)
        rows_expanded_acc = rows_expanded_acc + jnp.einsum(
            "gnabe,gabnc->aec", row_part, queries_float, precision=highest
        )
        cols_expanded_acc = cols_expanded_acc + jnp.einsum(
            "gnabf,gabnc->bfc", col_part, queries_float, precision=highest
        )
        grad_projected = jnp.stack(
            [
                grad_queries.reshape(micro_rows, local_width),
                grad_keys.reshape(micro_rows, local_width),
                grad_values.reshape(micro_rows, local_width),
            ],
            axis=1,
        ).astype(jnp.bfloat16)
        projected_float_sums = jnp.sum(grad_projected.astype(jnp.float32), axis=0)
        query_value_acc = query_value_acc + jnp.stack(
            [projected_float_sums[0], projected_float_sums[2]]
        )
        triple_acc = triple_acc + jnp.einsum(
            "rd,rte->tde", normed, grad_projected, preferred_element_type=jnp.float32
        )
        partial_one = jnp.einsum(
            "rte,tde->rd", grad_projected, full_triple, preferred_element_type=jnp.float32
        )
        grad_normed = row_total(partial_one)
        grad_tokens = grad_middle + normalize_back(grad_normed, unit_one, inverse_one, first_gain)
        first_gain_acc = first_gain_acc + jnp.sum(share_of(grad_normed * unit_one), axis=0)
        first_shift_acc = first_shift_acc + jnp.sum(share_of(grad_normed), axis=0)
        input_grads.append(grad_tokens.reshape(win_micro, WIN_TOK, D))
    select_float = select.astype(jnp.float32)
    rows_table_part = jnp.einsum("aej,aec->jc", select_float, rows_expanded_acc, precision=highest)
    cols_table_part = jnp.einsum("aej,aec->jc", select_float, cols_expanded_acc, precision=highest)
    triple_grad, output_grad, expand_grad, shrink_grad = (
        lax.psum_scatter(triple_acc, "dp", scatter_dimension=1, tiled=True),
        lax.psum_scatter(output_acc, "dp", scatter_dimension=1, tiled=True),
        lax.psum_scatter(expand_acc, "dp", scatter_dimension=0, tiled=True),
        lax.psum_scatter(shrink_acc, "dp", scatter_dimension=1, tiled=True),
    )
    over_heads = lax.psum(
        (
            rows_table_part,
            cols_table_part,
            first_gain_acc,
            first_shift_acc,
            output_bias_acc,
            second_gain_acc,
            second_shift_acc,
            shrink_bias_acc,
        ),
        "tensor",
    )
    summed_small = lax.psum(
        (
            over_heads[0],
            over_heads[1],
            over_heads[2],
            over_heads[3],
            over_heads[4],
            over_heads[5],
            over_heads[6],
            over_heads[7],
            query_value_acc,
            expand_bias_acc,
        ),
        "dp",
    )
    return (
        jnp.concatenate(outputs, axis=0),
        loss,
        jnp.concatenate(input_grads, axis=0),
        summed_small[2],
        summed_small[3],
        triple_grad,
        summed_small[8],
        output_grad,
        summed_small[4],
        summed_small[5],
        summed_small[6],
        expand_grad,
        summed_small[9],
        shrink_grad,
        summed_small[7],
        summed_small[0],
        summed_small[1],
    )


ROWS = 208
KEYS = 256
CHUNKS = ((0, 112), (112, 96))
F32 = jnp.float32
BF16 = jnp.bfloat16


def z_mate(z, k):
    if k == 0:
        return z
    if k == 1:
        return z + 1 - 2 * (z % 2)
    if k == 2:
        return (z + 2) % 4
    return 3 - z


def dot_nn(a, b):
    return lax.dot_general(a, b, (((1,), (0,)), ((), ())), preferred_element_type=F32)


def dot_nt(a, b):
    return lax.dot_general(a, b, (((1,), (1,)), ((), ())), preferred_element_type=F32)


def dot_tn(a, b):
    return lax.dot_general(a, b, (((0,), (0,)), ((), ())), preferred_element_type=F32)


def column_sum(values):
    return jnp.sum(values, axis=0, keepdims=True)


UNITS = ((0, 1, 2, 0, 0), (0, 1, 2, 1, 1), (3, 5, 6, 0, 1))


ORDER = (('pair', 0, 0), ('x', 0, 0), ('z', 0, 3), ('far', 0), ('z', 0, 1), ('pair', 0, 3), ('count',), ('x', 0, 3), ('z', 0, 2), ('start', 1), ('pair', 0, 1), ('x', 0, 1), ('near', 0), ('pair', 0, 2), ('x', 0, 2), ('pair', 1, 0), ('all', 0), ('start', 2), ('z', 1, 3), ('pair', 1, 3), ('z', 1, 1), ('far', 1), ('x', 1, 0), ('z', 2, 3), ('pair', 1, 1), ('z', 1, 2), ('x', 1, 1), ('x', 1, 3), ('pair', 1, 2), ('pair', 2, 0), ('near', 1), ('x', 1, 2), ('z', 2, 1), ('all', 1), ('far', 2), ('pair', 2, 3), ('z', 2, 2), ('pair', 2, 1), ('x', 2, 0), ('x', 2, 1), ('near', 2), ('x', 2, 3), ('pair', 2, 2), ('x', 2, 2), ('all', 2), ('pairs', 2), ('zs', 2, 2, 0), ('turns', 2), ('zs', 2, 3, 0), ('zs', 2, 1, 0), ('pairs', 1), ('zs', 1, 2, 0), ('block pass',), ('zs', 1, 1, 0), ('pairs', 0), ('zs', 1, 3, 0), ('block mix',), ('zs', 0, 2, 0), ('own', 0), ('small first',), ('own', 1), ('small z',), ('side', 0), ('turns', 0), ('turns', 1), ('zs', 0, 2, 1), ('zs', 0, 1, 0), ('small c',), ('zs', 0, 3, 0), ('out', 1), ('out', 2), ('small y',), ('side', 1), ('peer', 0), ('zs', 0, 1, 1), ('zs', 0, 3, 1), ('small x',), ('end', 0), ('last', 0), ('peer', 1), ('last', 1), ('out', 0), ('small end',))
PLAN = (0, 1, 1, 1, 2, 2, 3, 0, 0, 0, 1, 2, 1, 1, 1, 0, 0, 0, 0, 2, 0, 1, 3, 0, 1, 0, 1, 0, 3)


def block_kernel(
    x_in,
    target_in,
    valid_hbm,
    gain1_hbm,
    shift1_hbm,
    triple_hbm,
    qv_bias_hbm,
    out_w_hbm,
    bias_out_hbm,
    gain2_hbm,
    shift2_hbm,
    we_hbm,
    expand_bias_hbm,
    ws_hbm,
    bias_shrink_hbm,
    rows_hbm,
    columns_hbm,
    block_out,
    grad_out,
    ga_out,
    ge_out,
    gs_out,
    small_out,
    table_out,
    valid_in,
    gain1_in,
    shift1_in,
    triple_in,
    qv_bias_in,
    out_w_in,
    bias_out_in,
    gain2_in,
    shift2_in,
    we_in,
    expand_bias_in,
    ws_in,
    bias_shrink_in,
    rows_in,
    columns_in,
    wa_in,
    wa,
    we,
    ws,
    xt,
    tt,
    onehot,
    place,
    pick,
    tabs,
    bo,
    ig,
    mix,
    ga,
    ge,
    gs,
    side,
    xf,
    unit1,
    unit2,
    inv1,
    inv2,
    mid,
    acc,
    n1,
    n2,
    gr,
    gm,
    pj,
    ps,
    mx,
    mxr,
    hid,
    hidr,
    slope,
    gb,
    gbr,
    gmx,
    gp,
    gpr,
    t2,
    tg,
    es,
    er,
    es3,
    er3,
    sums,
    shrink_row,
    gw,
    xs,
    xr,
    zs,
    zr,
    ps2,
    pr2,
    ptotal,
    pxs,
    pxr,
    cnt,
    cntr,
    sb,
    sbr,
    tb,
    tbr,
    load_sem,
    send_sem,
    recv_sem,
):
    dp = lax.axis_index("dp")
    t = lax.axis_index("tensor")
    z = dp // 2
    x = dp % 2
    y = t // 2
    c = t % 2
    z_mates = [(z_mate(z, k) * 2 + x, t) for k in (1, 2, 3)]
    x_mate = (z * 2 + 1 - x, t)
    y_mate = (dp, (1 - y) * 2 + c)
    c_mate = (dp, y * 2 + 1 - c)
    peer_window = (1 - y) * 2 + c
    token_total = lax.axis_size("dp") * 4 * WIN_TOK

    started = []

    def send(src, dst, mate):
        i = len(started)
        copy = pltpu.make_async_remote_copy(
            src_ref=src,
            dst_ref=dst,
            send_sem=send_sem.at[i],
            recv_sem=recv_sem.at[i],
            device_id=mate,
            device_id_type=MESH,
        )
        copy.start()
        started.append(copy)
        return copy

    barrier = pltpu.get_barrier_semaphore()
    for mate in z_mates + [x_mate, y_mate, c_mate]:
        pl.semaphore_signal(barrier, inc=1, device_id=mate, device_id_type=MESH)

    loads = []

    def load(src, dst):
        copy = pltpu.make_async_copy(src, dst, load_sem.at[len(loads)])
        copy.start()
        loads.append(copy)
        return copy

    first_loads = [load(triple_hbm, triple_in), load(out_w_hbm, out_w_in)]
    group_loads = [load(we_hbm, we_in), load(ws_hbm, ws_in)]
    x_load = load(x_in, xt)
    side_loads = [
        load(src, dst)
        for src, dst in (
            (expand_bias_hbm, expand_bias_in),
            (qv_bias_hbm, qv_bias_in),
            (valid_hbm, valid_in),
            (gain1_hbm, gain1_in),
            (shift1_hbm, shift1_in),
            (bias_out_hbm, bias_out_in),
            (gain2_hbm, gain2_in),
            (shift2_hbm, shift2_in),
            (bias_shrink_hbm, bias_shrink_in),
            (rows_hbm, rows_in),
            (columns_hbm, columns_in),
        )
    ]
    target_load = load(target_in, tt)

    w_in = (wa_in, we_in, ws_in)
    w_full = (wa, we, ws)
    from_z = {}
    from_x = {}
    from_p = {}
    from_c = {}

    def row_of(k, xx):
        return z_mate(z, k) * 2 + xx

    first = pl.ds(0, 640)
    last = pl.ds(640, 128)

    def gather_start(g):
        full = w_full[g]
        from_p[g, 0] = send(w_in[g].at[:, last], full.at[0, dp, :, last], x_mate)
        for k in (3, 1):
            from_z[g, k] = send(w_in[g].at[:, first], full.at[0, dp, :, first], z_mates[k - 1])
        from_x[g, 0] = send(w_in[g].at[:, first], full.at[0, dp, :, first], x_mate)
        from_c[g, 0] = send(w_in[g], full.at[1, dp], c_mate)
        full[0, dp] = w_in[g][...]

    def to_core(g, i, *at):
        from_c[g, i] = send(w_full[g].at[(0,) + at], w_full[g].at[(1,) + at], c_mate)

    def gather_pair(g, k):
        from_p[g, k].wait_recv()
        pair = (pl.ds(2 * z_mate(z, k), 2), slice(None), last)
        block = w_full[g].at[(0,) + pair]
        if k == 0:
            for m in (3, 1):
                from_p[g, m] = send(block, block, z_mates[m - 1])
            to_core(g, 8, row_of(0, 1 - x), slice(None), last)
        else:
            if k == 3:
                from_p[g, 2] = send(block, block, z_mates[0])
            to_core(g, 8 + k, *pair)

    def gather_z(g, k):
        from_z[g, k].wait_recv()
        block = w_full[g].at[0, row_of(k, x), :, first]
        if k == 3:
            from_z[g, 2] = send(block, block, z_mates[0])
        else:
            from_x[g, k] = send(block, block, x_mate)
        to_core(g, k, row_of(k, x), slice(None), first)

    def gather_far(g):
        block = w_full[g].at[0, row_of(3, x), :, first]
        from_x[g, 3] = send(block, block, x_mate)

    def gather_x(g, k):
        from_x[g, k].wait_recv()
        to_core(g, 4 + k, row_of(k, 1 - x), slice(None), first)

    def gather_end(g, far):
        for k in (2, 3, 6, 7, 10, 11) if far else (0, 1, 4, 5, 8, 9):
            from_c[g, k].wait_recv()

    tasks = []
    done = set()
    plan = iter(PLAN)

    def add(key, step, *args):
        tasks.append((key, step, args))
        tasks.sort(key=lambda task: ORDER.index(task[0]))

    def serve():
        key, step, args = tasks.pop(0)
        step(*args)
        done.add(key)

    def point():
        for _ in range(next(plan, 0)):
            if tasks:
                serve()

    def need(key):
        while key not in done:
            serve()

    def gather_add(g):
        add(("pair", g, 0), gather_pair, g, 0)
        add(("z", g, 3), gather_z, g, 3)
        if g == 0:
            add(("start", 1), gather_start, 1)
        add(("z", g, 1), gather_z, g, 1)
        add(("far", g), gather_far, g)
        add(("pair", g, 3), gather_pair, g, 3)
        add(("x", g, 0), gather_x, g, 0)
        add(("pair", g, 1), gather_pair, g, 1)
        add(("z", g, 2), gather_z, g, 2)
        if g == 0:
            add(("count",), count_spread)
            add(("start", 2), gather_start, 2)
        add(("x", g, 1), gather_x, g, 1)
        add(("near", g), gather_end, g, False)
        add(("x", g, 3), gather_x, g, 3)
        add(("pair", g, 2), gather_pair, g, 2)
        add(("x", g, 2), gather_x, g, 2)
        add(("all", g), gather_end, g, True)

    cnt_z = []

    def count_spread():
        cnt_x.wait_recv()
        cnt[1] = cnt[0] + cntr[0]
        cnt_z.extend(send(cnt.at[1], cntr.at[k], z_mates[k - 1]) for k in (1, 2, 3))

    for copy in first_loads:
        copy.wait()
    for i in range(3):
        wa_in[:, 128 * i : 128 * i + 128] = triple_in[i, :, 0:128]
    source = lax.broadcasted_iota(jnp.int32, (192, 256), 0)
    column = lax.broadcasted_iota(jnp.int32, (192, 256), 1)
    tail = sum(
        dot_nn(
            triple_in[i],
            ((source >= 128) & (source - 128 == column - 64 * i)).astype(F32).astype(BF16),
        )
        for i in range(3)
    )
    out_w = out_w_in[...]
    tail = tail + dot_tn(
        out_w, ((source >= 128) & (source + 64 == column)).astype(F32).astype(BF16)
    )
    wa_in[:, 384:640] = tail.astype(BF16)
    wa_in[:, 640:768] = dot_tn(
        out_w, (source == column).astype(F32).astype(BF16)[:, 0:128]
    ).astype(BF16)
    def fourteens(at):
        whole = jnp.floor((at + 0.5) * (1.0 / WIN))
        return whole, at - WIN * whole

    def grid(shape, dim):
        return lax.broadcasted_iota(jnp.int32, shape, dim).astype(F32)

    def entries(shape, dim):
        at = grid(shape, dim)
        side = (at >= 256.0).astype(F32)
        at = at - 256.0 * side
        main, other = fourteens(at)
        return side, main, other, at < float(WIN_TOK)

    side_of, main, other, valid = entries((512, 64), 0)
    slot = main - other + (WIN - 1) + 32.0 * side_of
    onehot[...] = jnp.where(valid & (grid((512, 64), 1) == slot), 1.0, 0.0).astype(BF16)
    side_of, main, other, valid = entries((ROWS, 512), 1)
    token = grid((ROWS, 512), 0)
    down, across = fourteens(token)
    hit = valid & (main == jnp.where(side_of > 0.5, across, down)) & (token < float(WIN_TOK))
    place[...] = jnp.where(hit, 1.0, 0.0).astype(BF16)
    side_of, main, other, valid = entries((512, KEYS), 0)
    token = grid((512, KEYS), 1)
    down, across = fourteens(token)
    hit = valid & (other == jnp.where(side_of > 0.5, across, down)) & (token < float(WIN_TOK))
    pick[...] = jnp.where(hit, 1.0, 0.0).astype(BF16)
    pl.semaphore_wait(barrier, 6)
    gather_start(0)
    for copy in group_loads + side_loads:
        copy.wait()
    side[0] = jnp.zeros((8, D), F32)
    side[0, 0:1, :] = expand_bias_in[...].reshape(1, D)
    side[0, 1:2, 0:128] = qv_bias_in[0:1, 0:128]
    side[0, 1:2, 256:384] = qv_bias_in[1:2, 0:128]
    side[0, 1:2, 384:448] = qv_bias_in[0:1, 128:192]
    side[0, 1:2, 512:576] = qv_bias_in[1:2, 128:192]
    side_copy = send(side.at[0], side.at[1], c_mate)
    marks_all = valid_in[...].astype(F32)
    cnt[0] = jnp.full((8, 128), jnp.sum(marks_all), F32)
    cnt_x = send(cnt.at[0], cntr.at[0], x_mate)
    for g in range(3):
        gather_add(g)

    gain1 = gain1_in[...].reshape(1, D)
    shift1 = shift1_in[...].reshape(1, D)
    bias_out = bias_out_in[...].reshape(1, D)
    gain2 = gain2_in[...].reshape(1, D)
    shift2 = shift2_in[...].reshape(1, D)
    shrink_row[...] = bias_shrink_in[...].reshape(1, D)

    lane = lax.broadcasted_iota(jnp.int32, (1, 128), 1)
    half = ((lane < 64).astype(F32), (lane >= 64).astype(F32))
    key_mask = [(m * 0.125).astype(BF16) for m in half]
    half = [m.astype(BF16) for m in half]
    key_lane = lax.broadcasted_iota(jnp.int32, (1, KEYS), 1)
    key_bias = jnp.where(key_lane < WIN_TOK, 0.0, -1e30).astype(F32)

    row_ids = lax.broadcasted_iota(jnp.int32, (4, WIN_TOK), 0)
    own_marks = column_sum(jnp.where(row_ids == t, marks_all, 0.0))
    eye = lax.broadcasted_iota(jnp.int32, (ROWS, WIN_TOK), 0) == lax.broadcasted_iota(
        jnp.int32, (ROWS, WIN_TOK), 1
    )
    live = jnp.sum(jnp.where(eye, own_marks, 0.0), axis=1, keepdims=True)

    window_ids = lax.broadcasted_iota(jnp.int32, (1, 4, 1), 1)

    def window_of(ref, window):
        return jnp.sum(ref[...].astype(F32) * (window_ids == window).astype(F32), axis=1)

    xf[...] = jnp.zeros_like(xf)
    x_load.wait()
    for w in range(2):
        xf[w, 0:WIN_TOK, :] = window_of(xt, peer_window if w else t)
        point()
        unit, inverse = normalize(xf[w])
        n1[0, w] = (unit * gain1 + shift1).astype(BF16)
        if w == 0:
            unit1[...] = unit
            inv1[...] = inverse
    n1_copy = send(n1.at[0], n1.at[1], c_mate)
    tabs[...] = jnp.zeros_like(tabs)
    tabs[0:27, 0:64] = rows_in[...]
    tabs[32:59, 0:64] = columns_in[...]
    t2[0] = dot_nn(onehot[...], tabs[...].astype(BF16)).astype(BF16)
    t2[1] = dot_nn(onehot[...], pltpu.roll(tabs[...], 64, 1).astype(BF16)).astype(BF16)
    pj[:, :, ROWS:, :] = jnp.zeros((2, 2, KEYS - ROWS, 896), BF16)
    tg[...] = jnp.zeros_like(tg)

    def project(w):
        def body(j, carry):
            value = dot_nn(n1[0, w], wa[j, :, :, 0:640].reshape(D, 640)) + side[j, 1:2, 0:640]
            pj[w, j, 0:ROWS, 0:640] = value.astype(BF16)
            rolled = pltpu.roll(value[:, 384:512], 64, 1)
            pj[w, j, 0:ROWS, 640:768] = rolled.astype(BF16)
            rolled = pltpu.roll(value[:, 512:640], 64, 1)
            pj[w, j, 0:ROWS, 768:896] = rolled.astype(BF16)
            return carry

        lax.fori_loop(0, 2, body, 0)

    def unit_of(w, j, h):
        q, k, v, p, pv = UNITS[h]
        query = pj[w, j, 0:ROWS, 128 * q : 128 * q + 128]
        key = pj[w, j, :, 128 * k : 128 * k + 128] * key_mask[p]
        value = pj[w, j, :, 128 * v : 128 * v + 128] * half[pv]
        return query, key, value

    def attend(w):
        def body(j, carry):
            mixes = []
            for h in range(3):
                query, key, value = unit_of(w, j, h)
                along = dot_nt(query, t2[UNITS[h][3]])
                high = along.astype(BF16)
                low = (along - high.astype(F32)).astype(BF16) * place[...]
                high = high * place[...]
                scores = dot_nt(query, key) + dot_nn(high, pick[...]) + dot_nn(low, pick[...])
                scores = scores + key_bias
                raised = jnp.exp(scores - jnp.max(scores, axis=-1, keepdims=True))
                soft = raised * (1.0 / jnp.sum(raised, axis=-1, keepdims=True))
                ps[w, j, h] = soft
                mixes.append(dot_nn(soft.astype(BF16), value))
            mx[j, w, :, 0:128] = mixes[2].astype(BF16)
            mx[j, w, :, 128:256] = (mixes[0] + mixes[1]).astype(BF16)
            return carry

        lax.fori_loop(0, 2, body, 0)
        point()

    def attended(w, lo, n):
        return dot_nt(mx[0, w, lo : lo + n, :], wa[0, :, :, 512:768].reshape(D, 256)) + dot_nt(
            mx[1, w, lo : lo + n, :], wa[1, :, :, 512:768].reshape(D, 256)
        )

    side_copy.wait_recv()
    need(("all", 0))
    project(1)
    point()
    attend(1)
    e1 = []
    for lo, n in CHUNKS:
        es[0, lo : lo + n, :] = attended(1, lo, n).astype(BF16)
        e1.append(send(es.at[0, pl.ds(lo, n)], er.at[0, pl.ds(lo, n)], y_mate))
    point()
    project(0)
    point()
    attend(0)
    mx_copy = send(mx.at[1], mxr, c_mate)
    mid[...] = xf[0] + bias_out + attended(0, 0, ROWS)
    point()

    e2 = []
    n2_c = []
    for i, (lo, n) in enumerate(CHUNKS):
        point()
        e1[i].wait_recv()
        middle = mid[lo : lo + n, :] + er[0, lo : lo + n, :].astype(F32)
        mid[lo : lo + n, :] = middle
        unit, inverse = normalize(middle)
        unit2[lo : lo + n, :] = unit
        inv2[lo : lo + n, :] = inverse
        n2[0, 0, lo : lo + n, :] = (unit * gain2 + shift2).astype(BF16)
        rows = pl.ds(lo, n)
        e2.append(send(n2.at[0, 0, rows], n2.at[0, 1, rows], y_mate))
        n2_c.append(send(n2.at[0, 0, rows], n2.at[1, 0, rows], c_mate))

    def feed(w, lo, n):
        def body(j, carry):
            before = dot_nn(n2[0, w, lo : lo + n, :], we[j].reshape(D, D)) + side[j, 0:1, :]
            phi = 0.5 * (1.0 + lax.erf(before * math.sqrt(0.5)))
            hid[j, w, lo : lo + n, :] = (before * phi).astype(BF16)
            bell = jnp.exp(-0.5 * before * before) * (1.0 / math.sqrt(2.0 * math.pi))
            slope[j, w, lo : lo + n, :] = phi + before * bell
            return carry

        lax.fori_loop(0, 2, body, 0)
        point()

    zone = z // 2
    zones = (zone, 1 - zone)
    halves = [pl.ds(pl.multiple_of(q * 384, 128), 384) for q in zones]

    def shrunk(w, i):
        rows = pl.ds(zones[i] * 4, 4)
        return dot_nt(hid[0, w], ws[0, rows].reshape(384, D)) + dot_nt(
            hid[1, w], ws[1, rows].reshape(384, D)
        )

    need(("all", 1))
    for lo, n in CHUNKS:
        feed(0, lo, n)
    for i, (lo, n) in enumerate(CHUNKS):
        rows = pl.ds(lo, n)
        point()
        e2[i].wait_recv()
        n2_c.append(send(n2.at[0, 1, rows], n2.at[1, 1, rows], c_mate))
        feed(1, lo, n)
    hid_copy = send(hid.at[1], hidr, c_mate)
    target_load.wait()
    xf[1, 0:WIN_TOK, :] = window_of(tt, t)
    point()
    xf[1, WIN_TOK:, :] = jnp.zeros((ROWS - WIN_TOK, D), F32)
    need(("near", 2))
    for copy in cnt_z:
        copy.wait_recv()
    count = (cnt[1] + cntr[1]) + (cntr[2] + cntr[3])
    count = count[0:1, 0:1]
    scaled_live = live * (token_total / count)
    pieces = [(0, 0, ROWS)] + [(1, lo, n) for lo, n in CHUNKS]
    e3 = []
    for i in range(2):
        if i == 1:
            need(("all", 2))
        es3[i] = shrunk(1, i).astype(BF16)
        for half_at, lo, n in pieces[:1] if i == 0 else pieces[1:]:
            at = (i, pl.ds(lo, n))
            e3.append(send(es3.at[at], er3.at[at], y_mate))
        acc[:, halves[i]] = mid[:, halves[i]] + shrink_row[:, halves[i]] + shrunk(0, i)

    e4 = []
    gr_c = []
    for i, (half_at, lo, n) in enumerate(pieces):
        cols = halves[half_at]
        part = slice(lo, lo + n)
        rows = pl.ds(lo, n)
        e3[i].wait_recv()
        result = acc[part, cols] + er3[half_at, part, :].astype(F32)
        gap = result - xf[1, part, cols]
        grad = gap * scaled_live[part, :]
        acc[part, cols] = grad
        gr[0, 0, part, cols] = grad.astype(BF16)
        e4.append(send(gr.at[0, 0, rows, cols], gr.at[0, 1, rows, cols], y_mate))
        gr_c.append(send(gr.at[0, 0, rows, cols], gr.at[1, 0, rows, cols], c_mate))
        bo[t, part, cols] = result.astype(BF16)
        lost = column_sum(gap * gap * live[part, :])
        bias = column_sum(grad)
        sums[6:7, cols] = lost if lo == 0 else sums[6:7, cols] + lost
        sums[0:1, cols] = bias if lo == 0 else sums[0:1, cols] + bias
    sb[0] = jnp.zeros((16, D), F32)
    sb[0, 6:7, :] = sums[6:7, :]
    sb[0, 0:1, :] = sums[0:1, :]

    def feed_back(w, lo, n):
        def body(j, carry):
            grad = dot_nn(gr[0, w, lo : lo + n, :], ws[j].reshape(D, D))
            grad = grad * slope[j, w, lo : lo + n, :]
            gb[j, w, lo : lo + n, :] = grad.astype(BF16)
            return carry

        lax.fori_loop(0, 2, body, 0)

    def expanded_back(w, lo, n):
        return dot_nt(gb[0, w, lo : lo + n, :], we[0].reshape(D, D)) + dot_nt(
            gb[1, w, lo : lo + n, :], we[1].reshape(D, D)
        )

    def rows_of(ref, width):
        return ref[...].reshape(2 * ROWS, width)

    def weight_grad(g, left, mine, theirs, width, at):
        def body(m, carry):
            cols = pl.ds(pl.multiple_of(m * 384, 128), 384)
            rows = pl.ds(m * 4, 4)
            value = dot_tn(left[0, :, :, cols].reshape(2 * ROWS, 384), mine.reshape(2 * ROWS, width))
            value = value + dot_tn(
                left[1, :, :, cols].reshape(2 * ROWS, 384), theirs.reshape(2 * ROWS, width)
            )
            gw[g, rows, :, at : at + width] = value.reshape(4, 96, width)
            return carry

        lax.fori_loop(0, 2, body, 0)

    to_x = {}
    to_z = {}

    pair_of = {}

    def pair_rows(k):
        return pl.ds(2 * z_mate(z, k), 2)

    def scatter_pairs(g):
        for i, k in enumerate((2, 1)):
            ps2[g, i] = gw[g, pair_rows(k), :, 640:768].astype(BF16)
            pair_of[g, i] = send(ps2.at[g, i], pr2.at[g, i], z_mates[0])

    parts = {0: ((0, 384), (384, 256)), 1: ((0, 640),), 2: ((0, 640),)}

    def scatter_blocks(g, i, blocks):
        lo, n = parts[g][i]
        for k in blocks:
            xs[g, k, :, lo : lo + n] = gw[g, row_of(k, 1 - x), :, lo : lo + n].astype(BF16)
            at = (g, k, slice(None), pl.ds(lo, n))
            to_x[g, k, i] = send(xs.at[at], xr.at[at], x_mate)

    def scatter_pair(g):
        pair_of[g, 0].wait_recv()
        total = gw[g, pair_rows(3), :, 640:768] + pr2[g, 0].astype(F32)
        ps2[g, 2] = total.astype(BF16)
        pair_of[g, 2] = send(ps2.at[g, 2], pr2.at[g, 2], z_mates[2])

    def scatter_turn(g):
        pair_of[g, 1].wait_recv()
        pair_of[g, 2].wait_recv()
        total = gw[g, pair_rows(0), :, 640:768] + pr2[g, 1].astype(F32)
        ptotal[g] = total + pr2[g, 2].astype(F32)
        pxs[g] = ptotal[g, 1 - x].astype(BF16)
        pair_of[g, 3] = send(pxs.at[g], pxr.at[g], x_mate)

    def scatter_z(g, k, i):
        lo, n = parts[g][i]
        cols = slice(lo, lo + n)
        to_x[g, k, i].wait_recv()
        total = gw[g, row_of(k, x), :, cols] + xr[g, k, :, cols].astype(F32)
        if k == 3:
            to_z[g, 2, i].wait_recv()
            total = total + zr[g, 1, :, cols].astype(F32)
        zs[g, k - 1, :, cols] = total.astype(BF16)
        at = (g, k - 1, slice(None), pl.ds(lo, n))
        to_z[g, k, i] = send(zs.at[at], zr.at[at], z_mates[2 if k == 3 else 0])

    def scatter_end(g, i, out):
        lo, n = parts[g][i]
        cols = slice(lo, lo + n)
        to_x[g, 0, i].wait_recv()
        to_z[g, 1, i].wait_recv()
        to_z[g, 3, i].wait_recv()
        total = gw[g, dp, :, cols] + xr[g, 0, :, cols].astype(F32)
        out[:, cols] = total + zr[g, 0, :, cols].astype(F32) + zr[g, 2, :, cols].astype(F32)

    def scatter_last(g, out):
        pair_of[g, 3].wait_recv()
        out[:, 640:768] = ptotal[g, x] + pxr[g].astype(F32)

    def scatter_add(g, *keys):
        steps = {"pair": scatter_pair, "turn": scatter_turn}
        for key in keys:
            if key in steps:
                add((key + "s", g), steps[key], g)
            else:
                add(("zs", g, *key), scatter_z, g, *key)

    for lo, n in CHUNKS:
        feed_back(0, lo, n)
    e5 = []
    for i, (half_at, lo, n) in enumerate(pieces):
        rows = pl.ds(lo, n)
        cols = halves[half_at]
        e4[i].wait_recv()
        gr_c.append(send(gr.at[0, 1, rows, cols], gr.at[1, 1, rows, cols], c_mate))
        if i == 0:
            continue
        feed_back(1, lo, n)
        es[1, lo : lo + n, :] = expanded_back(1, lo, n).astype(BF16)
        e5.append(send(es.at[1, rows], er.at[1, rows], y_mate))
    gb_copy = send(gb.at[1], gbr, c_mate)
    mid[...] = expanded_back(0, 0, ROWS)
    for copy in gr_c:
        copy.wait_recv()
    hid_copy.wait_recv()
    weight_grad(2, gr, hid[0], hidr[...], D, 0)
    scatter_pairs(2)
    scatter_blocks(2, 0, (2, 3, 1, 0))
    scatter_add(2, "pair", (2, 0), "turn", (3, 0), (1, 0))
    point()

    e6 = []
    gm_c = []
    gain_part = jnp.zeros((1, D), F32)
    shift_part = jnp.zeros((1, D), F32)
    bias_part = jnp.zeros((1, D), F32)
    for i, (lo, n) in enumerate(CHUNKS):
        rows = pl.ds(lo, n)
        point()
        e5[i].wait_recv()
        grad = mid[lo : lo + n, :] + er[1, lo : lo + n, :].astype(F32)
        unit = unit2[lo : lo + n, :]
        gain_part = gain_part + column_sum(grad * unit)
        shift_part = shift_part + column_sum(grad)
        grad = acc[lo : lo + n, :] + normalize_back(grad, unit, inv2[lo : lo + n, :], gain2)
        acc[lo : lo + n, :] = grad
        gm[0, 0, lo : lo + n, :] = grad.astype(BF16)
        e6.append(send(gm.at[0, 0, rows], gm.at[0, 1, rows], y_mate))
        gm_c.append(send(gm.at[0, 0, rows], gm.at[1, 0, rows], c_mate))
        bias_part = bias_part + column_sum(grad)
    sb[0, 1:2, :] = gain_part
    sb[0, 2:3, :] = shift_part
    sb[0, 3:4, :] = bias_part

    bo_y = send(bo.at[t], bo.at[t], y_mate)
    bo_c = [send(bo.at[t], bo.at[t], c_mate)]

    def block_pass():
        bo_y.wait_recv()
        bo_c.append(send(bo.at[peer_window], bo.at[peer_window], c_mate))

    def block_mix():
        for copy in bo_c:
            copy.wait_recv()
        for w in range(4):
            mix[:, w, :] = bo[w, 0:WIN_TOK, :].astype(F32)
        xt[...] = mix[...].astype(BF16)
        stores.append(load(xt, block_out))

    stores = []
    gb_copy.wait_recv()
    for copy in n2_c:
        copy.wait_recv()
    weight_grad(1, n2, gb[0], gbr[...], D, 0)
    ones = jnp.ones((8, 2 * ROWS), BF16)
    sb[0, 8:9, :] = (dot_nn(ones, rows_of(gb.at[0], D)) + dot_nn(ones, rows_of(gbr, D)))[0:1]
    scatter_pairs(1)
    scatter_blocks(1, 0, (2, 3, 1, 0))
    scatter_add(1, "pair", (2, 0), "turn", (3, 0), (1, 0))
    point()

    def mixed_back(w, lo, n):
        for j in range(2):
            grad = dot_nn(gm[0, w, lo : lo + n, :], wa[j, :, :, 512:768].reshape(D, 256))
            gmx[j, w, lo : lo + n, :] = grad.astype(BF16)

    def unit_back(w, j, h):
        query, key, value = unit_of(w, j, h)
        p, pv = UNITS[h][3:]
        grad = gmx[j, w, :, 0:128] if h == 2 else gmx[j, w, :, 128:256]
        soft = ps[w, j, h]
        grad_soft = dot_nt(grad, value)
        delta = jnp.sum(soft * grad_soft, axis=-1, keepdims=True)
        grad_scores = (soft * (grad_soft - delta)).astype(BF16)
        grad_v = dot_tn(soft.astype(BF16), grad * half[pv])[0:ROWS]
        grad_k = dot_tn(grad_scores, query * key_mask[p])[0:ROWS]
        part = dot_nt(grad_scores, pick[...]).astype(BF16) * place[...]
        grad_q = dot_nn(grad_scores, key) + dot_nn(part, t2[p])
        spread = dot_tn(query * half[p], part)
        return grad_q, grad_k, grad_v, spread

    def attend_back_pair(w, j):
        one, two = unit_back(w, j, 0), unit_back(w, j, 1)
        for i in range(3):
            gp[j, w, :, 128 * i : 128 * i + 128] = (one[i] + two[i]).astype(BF16)
        tg[...] += one[3] + two[3]

    def attend_back_last(w, j):
        grad_q, grad_k, grad_v, spread = unit_back(w, j, 2)
        tg[...] += spread
        gp[j, w, :, 384:512] = (grad_q + pltpu.roll(grad_k, 64, 1)).astype(BF16)
        gp[j, w, :, 512:640] = pltpu.roll(grad_v, 64, 1).astype(BF16)

    def projected_back(w, lo, n):
        return dot_nt(gp[0, w, lo : lo + n, :], wa[0, :, :, 0:640].reshape(D, 640)) + dot_nt(
            gp[1, w, lo : lo + n, :], wa[1, :, :, 0:640].reshape(D, 640)
        )

    for i, (lo, n) in enumerate(CHUNKS):
        rows = pl.ds(lo, n)
        point()
        e6[i].wait_recv()
        gm_c.append(send(gm.at[0, 1, rows], gm.at[1, 1, rows], c_mate))
        mixed_back(1, lo, n)
    point()
    add(("block pass",), block_pass)
    add(("block mix",), block_mix)
    def both_back(j, carry):
        attend_back_pair(1, j)
        attend_back_last(1, j)
        return carry

    lax.fori_loop(0, 2, both_back, 0)
    point()
    gp_copies = [send(gp.at[1, 1], gpr.at[1], c_mate)]
    e7 = []
    for lo, n in CHUNKS:
        rows = pl.ds(lo, n)
        es[2, lo : lo + n, :] = projected_back(1, lo, n).astype(BF16)
        e7.append(send(es.at[2, rows], er.at[2, rows], y_mate))
    point()
    for copy in gm_c:
        copy.wait_recv()
    mx_copy.wait_recv()
    weight_grad(0, gm, mx[0], mxr[...], 256, 512)
    scatter_pairs(0)
    scatter_add(0, "pair", "turn")
    point()
    mixed_back(0, 0, ROWS)
    def pair_back(j, carry):
        attend_back_pair(0, j)
        return carry

    lax.fori_loop(0, 2, pair_back, 0)
    point()
    gp_copies.append(send(gp.at[1, 0, :, pl.ds(0, 384)], gpr.at[0, :, pl.ds(0, 384)], c_mate))
    attend_back_last(0, 0)
    point()
    n1_copy.wait_recv()
    for copy in gp_copies:
        copy.wait_recv()

    weight_grad(0, n1, gp[0, :, :, 0:384], gpr[:, :, 0:384], 384, 0)
    scatter_blocks(0, 0, (2, 3, 1, 0))
    scatter_add(0, (2, 0))
    attend_back_last(0, 1)
    last_copy = send(gp.at[1, 0, :, pl.ds(384, 256)], gpr.at[0, :, pl.ds(384, 256)], c_mate)
    mid[...] = projected_back(0, 0, ROWS)
    last_copy.wait_recv()
    held = gw[0, :, :, 512:640]
    weight_grad(0, n1, gp[0, :, :, 384:640], gpr[:, :, 384:640], 256, 384)
    gw[0, :, :, 512:640] += held
    need(("turns", 0))
    scatter_blocks(0, 1, (2, 3, 1, 0))

    small = {}

    def small_first():
        bias = dot_nn(ones, rows_of(gp.at[0], 640)) + dot_nn(ones, rows_of(gpr, 640))
        sb[0, 9:10, 0:640] = bias[0:1]
        spread = tg[...]
        spread_high = spread.astype(BF16)
        spread_low = (spread - spread_high.astype(F32)).astype(BF16)
        table = dot_nn(spread_high, onehot[...]) + dot_nn(spread_low, onehot[...])
        tb[0] = table[0:64] + table[64:128]

    top = pl.ds(0, 8)

    def small_send(stage, dst, mate, rows):
        return [
            send(sb.at[stage, rows], sbr.at[dst, rows], mate),
            send(tb.at[stage], tbr.at[dst], mate),
        ]

    def small_wait(stage):
        for copy in small[stage]:
            copy.wait_recv()

    def small_z():
        small[0] = sum((small_send(0, k - 1, z_mates[k - 1], pl.ds(0, 16)) for k in (1, 2, 3)), [])

    def small_c():
        small_wait(0)
        sb[1] = (sb[0] + sbr[0]) + (sbr[1] + sbr[2])
        tb[1] = (tb[0] + tbr[0]) + (tbr[1] + tbr[2])
        small[1] = small_send(1, 3, c_mate, top)

    def small_next(stage, mate, rows):
        small_wait(stage - 1)
        sb[stage] = sb[stage - 1]
        sb[stage, 0:8, :] = sb[stage - 1, 0:8, :] + sbr[stage + 1, 0:8, :]
        tb[stage] = tb[stage - 1] + tbr[stage + 1]
        small[stage] = small_send(stage, stage + 2, mate, rows)

    def small_end():
        small_wait(3)
        total = sb[3] + sbr[5]
        small_out[...] = total
        small_out[6:7, :] = jnp.broadcast_to(
            jnp.sum(total[6:7, :], axis=1, keepdims=True) / (count * float(D)), (1, D)
        )
        table_out[...] = (tb[3] + tbr[5]).T

    e8 = {}
    ig_c = {}

    def mix_in(window, i):
        lo, n = CHUNKS[i]
        top = min(lo + n, WIN_TOK)
        mix[lo:top, pl.ds(window, 1), :] = (
            ig[window, lo:top, :].astype(F32).reshape(top - lo, 1, D)
        )

    def own_grad(i):
        lo, n = CHUNKS[i]
        e7[i].wait_recv()
        grad = mid[lo : lo + n, :] + er[2, lo : lo + n, :].astype(F32)
        unit = unit1[lo : lo + n, :]
        gain_part = column_sum(grad * unit)
        shift_part = column_sum(grad)
        sb[0, 4:5, :] = gain_part if i == 0 else sb[0, 4:5, :] + gain_part
        sb[0, 5:6, :] = shift_part if i == 0 else sb[0, 5:6, :] + shift_part
        grad = acc[lo : lo + n, :] + normalize_back(grad, unit, inv1[lo : lo + n, :], gain1)
        ig[t, lo : lo + n, :] = grad.astype(BF16)
        rows = pl.ds(lo, n)
        ig_c[i, 0] = send(ig.at[t, rows], ig.at[t, rows], c_mate)
        e8[i] = send(ig.at[t, rows], ig.at[t, rows], y_mate)
        mix_in(t, i)

    def side_grad(i):
        ig_c[i, 0].wait_recv()
        mix_in(t + 1 - 2 * c, i)

    def peer_grad(i):
        lo, n = CHUNKS[i]
        rows = pl.ds(lo, n)
        e8[i].wait_recv()
        ig_c[i, 1] = send(ig.at[peer_window, rows], ig.at[peer_window, rows], c_mate)
        mix_in(peer_window, i)

    def last_grad(i):
        lo, n = CHUNKS[i]
        ig_c[i, 1].wait_recv()
        mix_in(peer_window + 1 - 2 * c, i)
        rows = pl.ds(lo, min(n, WIN_TOK - lo))
        stores.append(load(mix.at[rows], grad_out.at[rows]))

    def scatter_out(g, held, out):
        if g > 0:
            scatter_end(g, 0, held)
        else:
            scatter_end(0, 1, held)
        scatter_last(g, held)
        stores.append(load(held, out))

    need(("block mix",))
    add(("own", 0), own_grad, 0)
    add(("small first",), small_first)
    add(("own", 1), own_grad, 1)
    add(("small z",), small_z)
    scatter_add(0, (3, 0), (2, 1), (1, 0))
    add(("side", 0), side_grad, 0)
    add(("side", 1), side_grad, 1)
    add(("small c",), small_c)
    add(("out", 2), scatter_out, 2, gs, gs_out)
    add(("out", 1), scatter_out, 1, ge, ge_out)
    add(("small y",), small_next, 2, y_mate, top)
    add(("peer", 0), peer_grad, 0)
    scatter_add(0, (3, 1), (1, 1))
    add(("last", 0), last_grad, 0)
    add(("small x",), small_next, 3, x_mate, pl.ds(0, 16))
    add(("peer", 1), peer_grad, 1)
    add(("last", 1), last_grad, 1)
    add(("end", 0), scatter_end, 0, 0, ga)
    add(("out", 0), scatter_out, 0, ga, ga_out)
    add(("small end",), small_end)
    need(("small end",))
    for copy in started:
        copy.wait_send()
    for copy in stores:
        copy.wait()


def finish_kernel(*refs):
    block_in, grad_in, ga_in, ge, gs, small_in, table_in = refs[:7]
    outs = refs[7:24]
    block_hold, grad_hold, ge_hold, gs_hold, ga, small, table = refs[24:31]
    held = refs[31:44]
    sems = refs[44]
    count = [0]

    def move(src, dst):
        copy = pltpu.make_async_copy(src, dst, sems.at[count[0]])
        count[0] += 1
        copy.start()
        return copy

    little = [move(src, dst) for src, dst in ((ga_in, ga), (small_in, small), (table_in, table))]
    arrivals = []
    for src, hold, dst, step in (
        (grad_in, grad_hold, outs[2], 49),
        (block_in, block_hold, outs[0], 98),
        (ge, ge_hold, outs[11], 96),
        (gs, gs_hold, outs[13], 96),
    ):
        for lo in range(0, src.shape[0], step):
            rows = pl.ds(lo, step)
            arrivals.append((move(src.at[rows], hold.at[rows]), hold.at[rows], dst.at[rows]))
    for copy in little:
        copy.wait()
    loss, gain1, shift1, triple, qv, out_w, out_b, gain2, shift2, expand_bias, shrink_bias, by_row, by_column = held
    for i in range(3):
        triple[i, :, 0:128] = ga[:, 128 * i : 128 * i + 128]
    triple[0, :, 128:192] = ga[:, 384:448]
    triple[1, :, 128:192] = pltpu.roll(ga[:, 384:512], 64, 1)[:, 0:64]
    triple[2, :, 128:192] = ga[:, 512:576]
    out_w[0:128, :] = ga[:, 640:768].T
    out_w[128:192, :] = ga[:, 512:640].T[64:128]
    loss[...] = small[6:7, 0:1]
    for i, out in enumerate((shrink_bias, gain2, shift2, out_b, gain1, shift1)):
        out[...] = small[i]
    expand_bias[...] = small[8]
    for i in range(2):
        qv[i : i + 1, 0:128] = small[9:10, 256 * i : 256 * i + 128]
        qv[i : i + 1, 128:192] = small[9:10, 384 + 128 * i : 448 + 128 * i]
    by_row[...] = table[0:27]
    by_column[...] = table[32:59]
    others = [out for i, out in enumerate(outs) if i not in (0, 2, 11, 13)]
    leaving = [move(src, dst) for src, dst in zip(held, others, strict=True)]
    for copy, hold, dst in arrivals:
        copy.wait()
        leaving.append(move(hold, dst))
    for copy in leaving:
        copy.wait()


def fused(
    inputs,
    target,
    valid,
    first_gain,
    first_shift,
    triple_weight,
    query_value_bias,
    output_weight,
    output_bias,
    second_gain,
    second_shift,
    expand_weight,
    expand_bias,
    shrink_weight,
    shrink_bias,
    rows_table,
    columns_table,
):
    vmem = pl.BlockSpec(memory_space=pltpu.VMEM)
    anywhere = pl.BlockSpec(memory_space=pl.ANY)
    mixed_shape = (WIN_TOK, 4, D)
    part = jax.ShapeDtypeStruct((96, D), F32)
    copies = 224
    parts = pl.pallas_call(
        block_kernel,
        out_shape=[
            jax.ShapeDtypeStruct(mixed_shape, BF16),
            jax.ShapeDtypeStruct(mixed_shape, F32),
            part,
            part,
            part,
            jax.ShapeDtypeStruct((16, D), F32),
            jax.ShapeDtypeStruct((64, 64), F32),
        ],
        in_specs=[anywhere] * 17,
        out_specs=[anywhere] * 5 + [vmem] * 2,
        scratch_shapes=[
            pltpu.VMEM(valid.shape, jnp.int32),
            pltpu.VMEM((D,), F32),
            pltpu.VMEM((D,), F32),
            pltpu.VMEM(triple_weight.shape, BF16),
            pltpu.VMEM(query_value_bias.shape, F32),
            pltpu.VMEM(output_weight.shape, BF16),
            pltpu.VMEM((D,), F32),
            pltpu.VMEM((D,), F32),
            pltpu.VMEM((D,), F32),
            pltpu.VMEM(expand_weight.shape, BF16),
            pltpu.VMEM(expand_bias.shape, F32),
            pltpu.VMEM(expand_weight.shape, BF16),
            pltpu.VMEM((D,), F32),
            pltpu.VMEM(rows_table.shape, F32),
            pltpu.VMEM(columns_table.shape, F32),
            pltpu.VMEM((96, D), BF16),
            pltpu.VMEM((2, 8, 96, D), BF16),
            pltpu.VMEM((2, 8, 96, D), BF16),
            pltpu.VMEM((2, 8, 96, D), BF16),
            pltpu.VMEM(mixed_shape, BF16),
            pltpu.VMEM(mixed_shape, BF16),
            pltpu.VMEM((512, 64), BF16),
            pltpu.VMEM((ROWS, 512), BF16),
            pltpu.VMEM((512, KEYS), BF16),
            pltpu.VMEM((64, 128), F32),
            pltpu.VMEM((4, ROWS, D), BF16),
            pltpu.VMEM((4, ROWS, D), BF16),
            pltpu.VMEM(mixed_shape, F32),
            pltpu.VMEM((96, D), F32),
            pltpu.VMEM((96, D), F32),
            pltpu.VMEM((96, D), F32),
            pltpu.VMEM((2, 8, D), F32),
            pltpu.VMEM((2, ROWS, D), F32),
            pltpu.VMEM((ROWS, D), F32),
            pltpu.VMEM((ROWS, D), F32),
            pltpu.VMEM((ROWS, 1), F32),
            pltpu.VMEM((ROWS, 1), F32),
            pltpu.VMEM((ROWS, D), F32),
            pltpu.VMEM((ROWS, D), F32),
            pltpu.VMEM((2, 2, ROWS, D), BF16),
            pltpu.VMEM((2, 2, ROWS, D), BF16),
            pltpu.VMEM((2, 2, ROWS, D), BF16),
            pltpu.VMEM((2, 2, ROWS, D), BF16),
            pltpu.VMEM((2, 2, KEYS, 896), BF16),
            pltpu.VMEM((2, 2, 3, ROWS, KEYS), F32),
            pltpu.VMEM((2, 2, ROWS, 256), BF16),
            pltpu.VMEM((2, ROWS, 256), BF16),
            pltpu.VMEM((2, 2, ROWS, D), BF16),
            pltpu.VMEM((2, ROWS, D), BF16),
            pltpu.VMEM((2, 2, ROWS, D), F32),
            pltpu.VMEM((2, 2, ROWS, D), BF16),
            pltpu.VMEM((2, ROWS, D), BF16),
            pltpu.VMEM((2, 2, ROWS, 256), BF16),
            pltpu.VMEM((2, 2, ROWS, 640), BF16),
            pltpu.VMEM((2, ROWS, 640), BF16),
            pltpu.VMEM((2, 512, 128), BF16),
            pltpu.VMEM((128, 512), F32),
            pltpu.VMEM((3, ROWS, D), BF16),
            pltpu.VMEM((3, ROWS, D), BF16),
            pltpu.VMEM((2, ROWS, 384), BF16),
            pltpu.VMEM((2, ROWS, 384), BF16),
            pltpu.VMEM((8, D), F32),
            pltpu.VMEM((1, D), F32),
            pltpu.VMEM((3, 8, 96, D), F32),
            pltpu.VMEM((3, 4, 96, 640), BF16),
            pltpu.VMEM((3, 4, 96, 640), BF16),
            pltpu.VMEM((3, 3, 96, 640), BF16),
            pltpu.VMEM((3, 3, 96, 640), BF16),
            pltpu.VMEM((3, 3, 2, 96, 128), BF16),
            pltpu.VMEM((3, 3, 2, 96, 128), BF16),
            pltpu.VMEM((3, 2, 96, 128), F32),
            pltpu.VMEM((3, 96, 128), BF16),
            pltpu.VMEM((3, 96, 128), BF16),
            pltpu.VMEM((2, 8, 128), F32),
            pltpu.VMEM((4, 8, 128), F32),
            pltpu.VMEM((4, 16, D), F32),
            pltpu.VMEM((6, 16, D), F32),
            pltpu.VMEM((4, 64, 64), F32),
            pltpu.VMEM((6, 64, 64), F32),
            pltpu.SemaphoreType.DMA((32,)),
            pltpu.SemaphoreType.DMA((copies,)),
            pltpu.SemaphoreType.DMA((copies,)),
        ],
        compiler_params=pltpu.CompilerParams(
            collective_id=0, has_side_effects=True, vmem_limit_bytes=60 << 20
        ),
    )(
        inputs.transpose(1, 0, 2),
        target.transpose(1, 0, 2),
        valid,
        first_gain,
        first_shift,
        triple_weight,
        query_value_bias,
        output_weight,
        output_bias,
        second_gain,
        second_shift,
        expand_weight,
        expand_bias,
        shrink_weight.T,
        shrink_bias,
        rows_table,
        columns_table,
    )
    vector = jax.ShapeDtypeStruct((D,), F32)
    relative = jax.ShapeDtypeStruct(rows_table.shape, F32)
    shapes = [
        jax.ShapeDtypeStruct(mixed_shape, BF16),
        jax.ShapeDtypeStruct((1, 1), F32),
        jax.ShapeDtypeStruct(mixed_shape, F32),
        vector,
        vector,
        jax.ShapeDtypeStruct(triple_weight.shape, F32),
        jax.ShapeDtypeStruct(query_value_bias.shape, F32),
        jax.ShapeDtypeStruct(output_weight.shape, F32),
        vector,
        vector,
        vector,
        part,
        jax.ShapeDtypeStruct(expand_bias.shape, F32),
        part,
        vector,
        relative,
        relative,
    ]
    small_shapes = [shape for i, shape in enumerate(shapes) if i not in (0, 2, 11, 13)]
    outs = pl.pallas_call(
        finish_kernel,
        out_shape=shapes,
        in_specs=[anywhere] * 7,
        out_specs=[anywhere] * 17,
        scratch_shapes=[
            pltpu.VMEM(mixed_shape, BF16),
            pltpu.VMEM(mixed_shape, F32),
            pltpu.VMEM((96, D), F32),
            pltpu.VMEM((96, D), F32),
            pltpu.VMEM((96, D), F32),
            pltpu.VMEM((16, D), F32),
            pltpu.VMEM((64, 64), F32),
        ]
        + [pltpu.VMEM(shape.shape, shape.dtype) for shape in small_shapes]
        + [pltpu.SemaphoreType.DMA((40,))],
    )(*parts)
    outs = list(outs)
    outs[0] = outs[0].transpose(1, 0, 2)
    outs[1] = outs[1].reshape(())
    outs[2] = outs[2].transpose(1, 0, 2)
    outs[13] = outs[13].T
    return tuple(outs)


def solution(mesh):
    placed = (
        P("dp", None, None),
        P("dp", None, None),
        P("dp", None),
        P(),
        P(),
        P(None, "dp", "tensor"),
        P(None, "tensor"),
        P("tensor", "dp"),
        P(),
        P(),
        P(),
        P("dp", "tensor"),
        P("tensor"),
        P("tensor", "dp"),
        P(),
        P(),
        P(),
    )
    on_slice = mesh.shape["dp"] == 8 and mesh.shape["tensor"] == 4
    return jax.shard_map(
        fused if on_slice else shards,
        mesh=mesh,
        in_specs=placed,
        out_specs=(
            P("dp", None, None),
            P(),
            P("dp", None, None),
            P(),
            P(),
            P(None, "dp", "tensor"),
            P(None, "tensor"),
            P("tensor", "dp"),
            P(),
            P(),
            P(),
            P("dp", "tensor"),
            P("tensor"),
            P("tensor", "dp"),
            P(),
            P(),
            P(),
        ),
        check_vma=False,
    )
```
